128 devices in a mesh: mp: 8 (over z, core), dp: 16 (over y, x).
Axes of the slice: x: 4, y: 4, z: 4, core: 2. Of those that a mesh axis runs over, the one named last changes fastest.
Arguments:
- token_ids: int32 [16, 1024], P('dp'), may hold values from 0 to 49151
- targets: int32 [16, 256], replicated, may hold values from 0 to 49151
- loss_rows: int32 [16, 256], P('dp'), may hold values from 0 to 1023, as said below
- selections: int32 [3, 16, 1024], replicated, may hold values from 0 to 1, as said below
- boundary: int32 [16], replicated, may hold values from 0 to 768, as said below
- pack_master: float32 [2463360], P(('mp', 'dp')), may hold values from -2 to 2
- pack_first: float32 [2463360], P(('mp', 'dp')), may hold values from -0.00021362305 to 0.00021362305
- pack_second: float32 [2463360], P(('mp', 'dp')), may hold values from 9.294645e-10 to 3.6827839e-09
- mlp_master: float32 [3, 2560, 960], P(None, ('mp', 'dp')), may hold values from -1 to 1
- mlp_first: float32 [3, 2560, 960], P(None, ('mp', 'dp')), may hold values from -0.00021362305 to 0.00021362305
- mlp_second: float32 [3, 2560, 960], P(None, ('mp', 'dp')), may hold values from 9.294645e-10 to 3.6827839e-09
- table_master: float32 [49152, 960], P(('mp', 'dp')), may hold values from -0.387298335 to 0.387298335
- table_first: float32 [49152, 960], P(('mp', 'dp')), may hold values from -0.00021362305 to 0.00021362305
- table_second: float32 [49152, 960], P(('mp', 'dp')), may hold values from 9.294645e-10 to 3.6827839e-09
Outputs:
- pack_new: float32 [2463360], P(('mp', 'dp'))
- pack_first_new: float32 [2463360], P(('mp', 'dp'))
- pack_second_new: float32 [2463360], P(('mp', 'dp'))
- mlp_new: float32 [3, 2560, 960], P(None, ('mp', 'dp'))
- mlp_first_new: float32 [3, 2560, 960], P(None, ('mp', 'dp'))
- mlp_second_new: float32 [3, 2560, 960], P(None, ('mp', 'dp'))
- table_new: float32 [49152, 960], P(('mp', 'dp'))
- table_first_new: float32 [49152, 960], P(('mp', 'dp'))
- table_second_new: float32 [49152, 960], P(('mp', 'dp'))
- loss_sum: float32 [], replicated
- grad_norm: float32 [], replicated
The draws below stay inside these ranges and needn't reach their ends.
Inputs may be any that keep to these rules, and one draw needn't show every extreme that they name: `loss_rows`: sorted distinct rows of the group, 256 of them. `selections`: the selection of each recursion is contained in that of the recursion before. boundary[0] is 0; every other entry lies between 256 and 768.
All inputs are finite; a program needn't handle non-finite values.
Results may differ from the reference program's by a relative error of at most 0.018.
Values may be sent and summed in bfloat16 or wider, within the bound.
No kernel may reach another device: no remote copies, remote signals or barrier semaphores. Data moves between devices by JAX's collectives and lax.ppermute only.
A program may use at most 320 MiB of HBM per device.

```python
import math
import jax
import jax.numpy as jnp
import numpy as np
from jax import lax

D = 960
HEADS = 15
KV_HEADS = 5
HEAD_DIM = 64
FF = 2560
VOCAB = 49152
RECUR = 3
STEP = 10
TOK_DEV = 128
ROWS = 1024
LOSS_ROWS = 256
TOKENS = 16384
PACK = 2463360
PARAMS = 57022080
N_DP = 16


def draw_boundary(key, part):
    key = jax.random.fold_in(key, 1)
    starts = jax.random.randint(key, (N_DP,), ROWS // 4, 3 * ROWS // 4 + 1).astype(jnp.int32)
    starts = starts.at[0].set(0)
    return starts.at[1].set(3 * ROWS // 4)


def draw_selections(key, part):
    key = jax.random.fold_in(key, 2)
    base = jax.random.randint(key, (N_DP, ROWS), 0, 100)
    levels = jnp.array([75, 55, 35], dtype=jnp.int32)[:RECUR]
    return (base[None] < levels[:, None, None]).astype(jnp.int32)


def draw_loss_rows(key, part):
    key = jax.random.fold_in(key, 3)
    keys = jax.random.split(key, N_DP)

    def one_group(subkey):
        order = jax.random.permutation(subkey, ROWS)
        return jnp.sort(order[:LOSS_ROWS]).astype(jnp.int32)
    return jax.vmap(one_group)(keys)


def draw_pack_master(key, part):
    key = jax.random.fold_in(key, 4)
    keys = jax.random.split(key, 6)
    query_cols = HEADS * HEAD_DIM
    kv_cols = KV_HEADS * HEAD_DIM
    pieces = [jnp.clip(jax.random.normal(keys[0], (D * query_cols,), jnp.float32), -4.0, 4.0) * D ** (-0.5), jnp.clip(jax.random.normal(keys[1], (D * kv_cols,), jnp.float32), -4.0, 4.0) * D ** (-0.5), jnp.clip(jax.random.normal(keys[2], (D * kv_cols,), jnp.float32), -4.0, 4.0) * D ** (-0.5), jnp.clip(jax.random.normal(keys[3], (query_cols * D,), jnp.float32), -4.0, 4.0) * (0.45 * query_cols ** (-0.5)), 1.0 + 0.15 * jax.random.uniform(keys[4], (3 * D,), jnp.float32, -1.0, 1.0), jnp.clip(jax.random.normal(keys[5], (RECUR * D,), jnp.float32), -4.0, 4.0) * (0.7 / (0.06 * D ** 0.5))]
    return jnp.clip(jnp.concatenate(pieces), -2.0, 2.0)


def draw_mlp_master(key, part):
    key = jax.random.fold_in(key, 5)
    keys = jax.random.split(key, 2)
    inward = jnp.clip(jax.random.normal(keys[0], (2, FF, D), jnp.float32), -4.0, 4.0) * D ** (-0.5)
    outward = jnp.clip(jax.random.normal(keys[1], (1, FF, D), jnp.float32), -4.0, 4.0) * (0.12 * FF ** (-0.5))
    return jnp.concatenate([inward, outward], axis=0)


def draw_table_master(key, part):
    key = jax.random.fold_in(key, 6)
    place = jnp.arange(VOCAB, dtype=jnp.float32) / (VOCAB - 1)
    base = jnp.clip(jax.random.normal(key, (VOCAB, D), jnp.float32), -4.0, 4.0)
    rise = 3.0 ** place
    return base * (rise * D ** (-0.5))[:, None]


def place_ends(drawn, stream_key, low, top_value):
    index_at = [jax.random.randint(jax.random.fold_in(stream_key, axis), (), 0, length) for axis, length in enumerate(drawn.shape)]
    widest = drawn.shape.index(max(drawn.shape))
    neighbour = index_at[:widest] + [(index_at[widest] + 1) % drawn.shape[widest]] + index_at[widest + 1:]
    return drawn.at[tuple(index_at)].set(low).at[tuple(neighbour)].set(top_value)


def shard_levels(own_key, dims, cuts, low, top_value):
    gain, own = 1.0, jax.random.fold_in(own_key, 6)
    for dim, parts in cuts:
        steps = jnp.exp(jax.random.uniform(jax.random.fold_in(own, dim), (parts,), jnp.float32, low / len(cuts), top_value / len(cuts)))
        gain = gain * jnp.repeat(steps, dims[dim] // parts).reshape([-1 if axis == dim else 1 for axis in range(len(dims))])
    return gain


def cumulative_ranks(amount, lean):
    weights = [(1 << 20) // math.isqrt(grade ** lean) + 1 for grade in range(1, amount + 1)]
    scale = 1 + sum(weights) // (1 << 30)
    return np.cumsum(np.array([max(1, weight // scale) for weight in weights]))


def skewed_ids(rng, shape, count, skew):
    table = cumulative_ranks(count, skew)
    ticket = jax.random.randint(jax.random.fold_in(rng, 1), shape, 0, int(table[count - 1]))
    standing = jnp.searchsorted(jnp.asarray(table, jnp.int32), ticket, side="right")
    return jax.random.permutation(jax.random.fold_in(rng, 2), count)[standing].astype(jnp.int32)


def gaussian(rng, dims, scale, reach, cuts=(), kind=jnp.bfloat16):
    values = jax.random.normal(rng, dims, jnp.float32) * scale
    if len(cuts) > 0:
        values = shard_levels(rng, dims, cuts, -0.22, 0.18) * values
    return jnp.clip(values, min=-reach, max=reach).astype(kind)


def setup_inputs(seed: int = 0) -> dict:
    key_list = jax.random.split(jax.random.key(seed), 15)
    token_ids = place_ends(skewed_ids(key_list[0], (N_DP, ROWS), VOCAB, 2), jax.random.fold_in(key_list[0], 3), 0, VOCAB - 1).astype(jnp.int32)
    targets = place_ends(jax.random.randint(key_list[1], (N_DP, LOSS_ROWS), 0, VOCAB), jax.random.fold_in(key_list[1], 1), 0, VOCAB - 1).astype(jnp.int32)
    loss_rows = draw_loss_rows(jax.random.fold_in(key_list[14], 71), 0)
    selections = draw_selections(jax.random.fold_in(key_list[14], 71), 0)
    boundary = draw_boundary(jax.random.fold_in(key_list[14], 71), 0)
    pack_master = draw_pack_master(jax.random.fold_in(key_list[14], 71), 0)
    pack_first = gaussian(key_list[6], (PACK,), (0.11 / PARAMS ** 0.5), 0.00021362305, ((0, 128),), jnp.float32)
    pack_second = jnp.clip(jnp.exp(math.log(3.6827838556519055e-09) - 1.3768156 * jax.random.uniform(key_list[7], (PACK,), jnp.float32) ** shard_levels(key_list[7], (PACK,), ((0, 128),), -0.2, 0.2)), 9.294645053614659e-10, 3.6827838556519055e-09)
    mlp_master = draw_mlp_master(jax.random.fold_in(key_list[14], 71), 0)
    mlp_first = gaussian(key_list[9], (3, FF, D), (0.11 / PARAMS ** 0.5), 0.00021362305, ((1, 128),), jnp.float32)
    mlp_second = jnp.clip(jnp.exp(math.log(3.6827838556519055e-09) - 1.3768156 * jax.random.uniform(key_list[10], (3, FF, D), jnp.float32) ** shard_levels(key_list[10], (3, FF, D), ((1, 128),), -0.2, 0.2)), 9.294645053614659e-10, 3.6827838556519055e-09)
    table_master = draw_table_master(jax.random.fold_in(key_list[14], 71), 0)
    table_first = gaussian(key_list[12], (VOCAB, D), (0.11 / PARAMS ** 0.5), 0.00021362305, ((0, 128),), jnp.float32)
    table_second = jnp.clip(jnp.exp(math.log(3.6827838556519055e-09) - 1.3768156 * jax.random.uniform(key_list[13], (VOCAB, D), jnp.float32) ** shard_levels(key_list[13], (VOCAB, D), ((0, 128),), -0.2, 0.2)), 9.294645053614659e-10, 3.6827838556519055e-09)
    return dict(token_ids=token_ids, targets=targets, loss_rows=loss_rows, selections=selections, boundary=boundary, pack_master=pack_master, pack_first=pack_first, pack_second=pack_second, mlp_master=mlp_master, mlp_first=mlp_first, mlp_second=mlp_second, table_master=table_master, table_first=table_first, table_second=table_second)


EPS_NORM = 1e-05
ROPE_BASE = 10000.0
ROUTER_LOSS = 0.1
CLIP_NORM = 1.0
LEARN_RATE = 0.05
BETA_ONE = 0.9
BETA_TWO = 0.95
ADAM_EPS = 1e-08
DECAY = 0.1
MASKED = -1e+30
HIGHEST = lax.Precision.HIGHEST

@jax.custom_vjp
def low(v):
    return lax.optimization_barrier(v.astype(jnp.bfloat16)).astype(jnp.float32)

@jax.custom_vjp
def low_back(v):
    return v

def low_keep(v):
    return (low(v), None)

def low_pass(kept, grad):
    return (grad,)

def back_keep(v):
    return (v, None)

def back_low(kept, grad):
    return (low(grad),)
low.defvjp(low_keep, low_pass)
low_back.defvjp(back_keep, back_low)

def matmul(left, right):
    return jnp.dot(left, right, precision=HIGHEST)

def rms_scale(values, weight):
    return values * lax.rsqrt(lax.optimization_barrier(jnp.mean(values * values, axis=-1, keepdims=True)) + EPS_NORM) * weight

def rotate(values, positions):
    half = HEAD_DIM // 2
    freqs = ROPE_BASE ** (-jnp.arange(half, dtype=jnp.float32) / half)
    angles = positions.astype(jnp.float32)[:, None] * freqs[None, :]
    cosine = jnp.cos(angles)[:, None, :]
    sine = jnp.sin(angles)[:, None, :]
    first = values[..., :half]
    second = values[..., half:]
    return jnp.concatenate([first * cosine - second * sine, second * cosine + first * sine], axis=-1)

def unpack(packed):
    query_cols = HEADS * HEAD_DIM
    kv_cols = KV_HEADS * HEAD_DIM
    shapes = [(D, query_cols), (D, kv_cols), (D, kv_cols), (query_cols, D), (3, D), (RECUR, D)]
    pieces = []
    offset = 0
    for piece_shape in shapes:
        length = piece_shape[0] * piece_shape[1]
        pieces.append(packed[offset:offset + length].reshape(piece_shape))
        offset = offset + length
    return pieces

def doc_ids(rows, boundary, group_rows):
    group = jnp.floor_divide(rows, group_rows)
    start = boundary[jnp.clip(group, 0, boundary.shape[0] - 1)]
    return group - (rows - group * group_rows < start).astype(jnp.int32)

def visible(query_rows, key_rows, key_sel, boundary, group_rows):
    same = doc_ids(query_rows, boundary, group_rows)[:, None] == doc_ids(key_rows, boundary, group_rows)[None, :]
    earlier = key_rows[None, :] <= query_rows[:, None]
    picked = (key_sel[None, :] > 0) | (key_rows[None, :] == query_rows[:, None])
    return same & earlier & picked & (key_rows[None, :] >= 0)

def recursion(hidden, step, weights, mlp_low, chosen, boundary, positions):
    w_query, w_key, w_value, w_out, gains, router = weights
    groups_per = HEADS // KV_HEADS
    normed = low(rms_scale(hidden, gains[0]))
    queries = low(rotate(low_back(matmul(normed, w_query)).reshape(TOKENS, HEADS, HEAD_DIM), positions))
    keys = low(rotate(low_back(matmul(normed, w_key)).reshape(TOKENS, KV_HEADS, HEAD_DIM), positions))
    values = low(low_back(matmul(normed, w_value))).reshape(TOKENS, KV_HEADS, HEAD_DIM)

    def with_prev(array):
        grouped = array.reshape((N_DP, ROWS) + array.shape[1:])
        shifted = jnp.concatenate([jnp.zeros_like(grouped[:1]), grouped[:-1]], axis=0)
        return jnp.concatenate([shifted, grouped], axis=1)

    def attend_group(args):
        group, group_queries, group_keys, group_values, group_sel = args
        query_rows = group * ROWS + jnp.arange(ROWS, dtype=jnp.int32)
        key_rows = (group - 1) * ROWS + jnp.arange(2 * ROWS, dtype=jnp.int32)
        mask = visible(query_rows, key_rows, group_sel, boundary, ROWS)
        grouped_q = group_queries.reshape(ROWS, KV_HEADS, groups_per, HEAD_DIM)
        scores = low_back(jnp.einsum('tkgd,skd->kgts', grouped_q, group_keys, precision=HIGHEST) * HEAD_DIM ** (-0.5))
        scores = jnp.where(mask[None, None], scores, MASKED)
        top = lax.optimization_barrier(jnp.max(scores, axis=-1, keepdims=True))
        expo = jnp.exp(scores - top)
        probs = low(expo / lax.optimization_barrier(jnp.sum(expo, axis=-1, keepdims=True)))
        return jnp.einsum('kgts,skd->tkgd', probs, group_values, precision=HIGHEST)
    attended = lax.map(jax.checkpoint(attend_group), (jnp.arange(N_DP, dtype=jnp.int32), queries.reshape(N_DP, ROWS, HEADS, HEAD_DIM), with_prev(keys), with_prev(values), with_prev(chosen)))
    attended = low_back(low(attended.reshape(TOKENS, HEADS * HEAD_DIM)))
    mixed = hidden + low_back(matmul(attended, w_out))
    normed_two = low(rms_scale(mixed, gains[1]))
    gate_pre = low_back(matmul(normed_two, mlp_low[0].T))
    up_pre = low_back(matmul(normed_two, mlp_low[1].T))
    inner = low(jax.nn.silu(gate_pre) * up_pre)
    branch = mixed + low_back(matmul(inner, mlp_low[2]))
    logit = jnp.dot(hidden, router[step], precision=HIGHEST)
    chosen_float = chosen.astype(jnp.float32)
    weight_sel = chosen_float * jax.nn.sigmoid(logit)
    new_hidden = hidden + weight_sel[:, None] * (branch - hidden)
    return (new_hidden, jnp.sum(jax.nn.softplus(logit) - chosen_float * logit))

def forward(pack, mlp, table_full, token_ids, targets, loss_rows, selections, boundary):
    weights = unpack(low(pack))
    gains = weights[4]
    mlp_low = low(mlp)
    table = low(table_full)
    positions = jnp.arange(TOKENS, dtype=jnp.int32)
    hidden = low_back(jnp.take(table, token_ids.reshape(-1), axis=0))
    flat_sel = selections.reshape(RECUR, TOKENS)
    penalty = jnp.zeros((), jnp.float32)
    for step in range(RECUR):
        hidden, part = recursion(hidden, step, weights, mlp_low, flat_sel[step], boundary, positions)
        penalty = penalty + part
    normed_final = low(rms_scale(hidden, gains[2])).reshape(N_DP, ROWS, D)

    def head_group(args):
        normed_group, rows_used, target = args
        picked = jnp.take(normed_group, rows_used, axis=0)
        logits = low_back(jnp.dot(picked, table.T, precision=HIGHEST))
        top = lax.optimization_barrier(jnp.max(logits, axis=-1, keepdims=True))
        lse = top[:, 0] + jnp.log(lax.optimization_barrier(jnp.sum(jnp.exp(logits - top), axis=-1)))
        hit = jnp.take_along_axis(logits, target[:, None], axis=1)[:, 0]
        return jnp.sum(lse - hit)
    cross = lax.map(jax.checkpoint(head_group), (normed_final, loss_rows, targets))
    total = jnp.sum(cross) + ROUTER_LOSS * penalty
    return (total / TOK_DEV, total)

def adam_update(master, first, second, grad, clip):
    grad = grad * clip
    first_new = BETA_ONE * first + (1.0 - BETA_ONE) * grad
    second_new = BETA_TWO * second + (1.0 - BETA_TWO) * grad * grad
    corr_one = 1.0 - BETA_ONE ** STEP
    corr_two = 1.0 - BETA_TWO ** STEP
    master_new = master - LEARN_RATE * (first_new / corr_one / (jnp.sqrt(second_new / corr_two) + ADAM_EPS) + DECAY * master)
    return (master_new, first_new, second_new)

def reference(token_ids, targets, loss_rows, selections, boundary, pack_master, pack_first, pack_second, mlp_master, mlp_first, mlp_second, table_master, table_first, table_second):

    def objective(pack, mlp, table):
        return forward(pack, mlp, table, token_ids, targets, loss_rows, selections, boundary)
    loss_value, pullback, total = jax.vjp(objective, pack_master, mlp_master, table_master, has_aux=True)
    grad_pack, grad_mlp, grad_table = pullback(jnp.ones_like(loss_value))
    squares = jnp.sum(grad_pack * grad_pack) + jnp.sum(grad_mlp * grad_mlp) + jnp.sum(grad_table * grad_table)
    grad_norm = jnp.sqrt(squares)
    clip = CLIP_NORM / jnp.maximum(grad_norm, CLIP_NORM)
    pack_new, pack_first_new, pack_second_new = adam_update(pack_master, pack_first, pack_second, grad_pack, clip)
    mlp_new, mlp_first_new, mlp_second_new = adam_update(mlp_master, mlp_first, mlp_second, grad_mlp, clip)
    table_new, table_first_new, table_second_new = adam_update(table_master, table_first, table_second, grad_table, clip)
    return (pack_new, pack_first_new, pack_second_new, mlp_new, mlp_first_new, mlp_second_new, table_new, table_first_new, table_second_new, total, grad_norm)
```

```python
import functools

import jax
import jax.numpy as jnp
from jax import lax
from jax.experimental import pallas as pl
from jax.experimental.pallas import tpu as pltpu
from jax.sharding import Mesh
from jax.sharding import PartitionSpec as P

D = 960
HEADS = 15
KV_HEADS = 5
HEAD_DIM = 64
FF = 2560
RECUR = 3
STEP = 10
TOK_DEV = 128
ROWS = 1024
MP = 8
DP = 16
VOCAB_MP = 6144
VOCAB_DEV = 384
UNITS = 20
PACK_DEV = 19245
PACK_ROWS = 2566
PACK_PAD = 2688
CAP = 24

EPS_NORM = 1e-05
ROPE_BASE = 10000.0
ROUTER_LOSS = 0.1
CLIP_NORM = 1.0
LEARN_RATE = 0.05
BETA_ONE = 0.9
BETA_TWO = 0.95
ADAM_EPS = 1e-08
DECAY = 0.1
MASKED = -1e30
HIGHEST = lax.Precision.HIGHEST
BFLOAT = jnp.bfloat16
FLOAT = jnp.float32
DP_AXES = ("y", "x")
ALL_AXES = ("z", "core", "y", "x")


def shift(value, axis, steps):
    return lax.ppermute(value, axis, [(i, (i + steps) % 4) for i in range(4)])


def swap(value):
    return lax.ppermute(value, "core", [(0, 1), (1, 0)])


def shift_group(value, steps):
    pairs = [(i, i + steps) for i in range(DP) if 0 <= i + steps < DP]
    return lax.ppermute(value, DP_AXES, pairs)


def gather_group(value):
    parts = jnp.stack([value] + [shift(value, "z", -k) for k in (1, 2, 3)])
    return jnp.stack([parts, swap(parts)])


def scatter_group(blocks, kind=BFLOAT):
    half = (blocks[0].astype(FLOAT) + swap(blocks[1].astype(BFLOAT)).astype(FLOAT)).astype(BFLOAT)
    total = half[0].astype(FLOAT)
    for k in (1, 2, 3):
        total = total + shift(half[k], "z", k).astype(FLOAT)
    return total.astype(kind)


def sum_all(value):
    value = value + swap(value)
    for axis in ("z", "y", "x"):
        value = value + shift(value, axis, 1) + shift(value, axis, 2) + shift(value, axis, 3)
    return value


def rms_scale(values, weight):
    return values * lax.rsqrt(jnp.mean(values * values, axis=-1, keepdims=True) + EPS_NORM) * weight


def rms_back(values, weight, grad_out):
    inverse = lax.rsqrt(jnp.mean(values * values, axis=-1, keepdims=True) + EPS_NORM)
    weighted = grad_out * weight
    grad_values = inverse * weighted - values * (inverse * inverse * inverse) * jnp.mean(
        weighted * values, axis=-1, keepdims=True
    )
    return (grad_values, jnp.sum(grad_out * values * inverse, axis=0))


def rotation(positions):
    half = HEAD_DIM // 2
    freqs = ROPE_BASE ** (-jnp.arange(half, dtype=FLOAT) / half)
    angles = positions.astype(FLOAT)[:, None] * freqs[None, :]
    return jnp.cos(angles)[:, None, :], jnp.sin(angles)[:, None, :]


def rotate(values, cosine, sine):
    half = HEAD_DIM // 2
    first = values[..., :half]
    second = values[..., half:]
    return jnp.concatenate(
        [first * cosine - second * sine, second * cosine + first * sine], axis=-1
    )


def mm(left, right):
    return jnp.dot(left, right, preferred_element_type=FLOAT)


def contract_rows(left, right):
    return lax.dot_general(left, right, (((0,), (0,)), ((), ())), preferred_element_type=FLOAT)


def contract_cols(left, right):
    return lax.dot_general(left, right, (((1,), (1,)), ((), ())), preferred_element_type=FLOAT)


def reorder(blocks, order):
    hit = order[:, None] == jnp.arange(MP)[None, :]
    return jnp.sum(jnp.where(hit[:, :, None], blocks[..., None, :, :], 0), axis=-2)


def tie(*values):
    return lax.optimization_barrier(values)


def group_gather(pair):
    own = [pair]
    for k in (1, 2, 3):
        own.append(lax.ppermute(pair, "z", [((i + k) % 4, i) for i in range(4) if (i + k) % 4 < i]))
    prev = []
    for k in range(4):
        pairs = []
        for i in range(3):
            for g in range(1, DP):
                pairs.append((((i + k) % 4) * DP + g - 1, i * DP + g))
        prev.append(lax.ppermute(pair, ("z",) + DP_AXES, pairs))
    own = jnp.concatenate(own, axis=0)
    prev = jnp.concatenate(prev, axis=0)
    return prev, own, swap(prev), swap(own)


def group_scatter(prev, own, prev_far, own_far):
    own = (own.astype(FLOAT) + swap(own_far).astype(FLOAT)).astype(BFLOAT).reshape(4, TOK_DEV, -1)
    prev = (prev.astype(FLOAT) + swap(prev_far).astype(FLOAT)).astype(BFLOAT).reshape(4, TOK_DEV, -1)
    total = own[0].astype(FLOAT)
    for k in (1, 2, 3):
        pairs = [(i, (i + k) % 4) for i in range(4) if (i + k) % 4 < i]
        total = total + lax.ppermute(own[k], "z", pairs).astype(FLOAT)
    for k in range(4):
        pairs = []
        for i in range(3):
            for g in range(1, DP):
                pairs.append((i * DP + g, ((i + k) % 4) * DP + g - 1))
        total = total + lax.ppermute(prev[k], ("z",) + DP_AXES, pairs).astype(FLOAT)
    return total


def nn(left, right):
    return jnp.dot(left, right, preferred_element_type=FLOAT)


def head_rows(ref, head):
    return jnp.concatenate(
        [ref[:, 64 * (3 * head + i) : 64 * (3 * head + i) + 64] for i in range(3)], axis=0
    )


def attend_kernel(query_ref, kv0, kv1, kv2, kv3, bias_ref, out_ref, log_ref):
    for head in range(KV_HEADS):
        queries = head_rows(query_ref, head)
        top = None
        for part, kv_ref in enumerate((kv0, kv1, kv2, kv3)):
            keys = kv_ref[:, 64 * head : 64 * head + 64]
            values = kv_ref[:, 320 + 64 * head : 320 + 64 * head + 64]
            bias = bias_ref[512 * part : 512 * part + 512, :]
            scores = contract_cols(keys, queries) + jnp.concatenate([bias, bias, bias], axis=1)
            part_top = jnp.max(scores, axis=0, keepdims=True)
            new_top = part_top if top is None else jnp.maximum(top, part_top)
            expo = jnp.exp(scores - new_top)
            part_total = jnp.sum(expo, axis=0, keepdims=True)
            part_out = contract_rows(values, expo.astype(BFLOAT))
            if top is None:
                total, out = part_total, part_out
            else:
                shrink = jnp.exp(top - new_top)
                total, out = total * shrink + part_total, out * shrink + part_out
            top = new_top
        out = (out / total).T.astype(BFLOAT)
        for i in range(3):
            place = 64 * (3 * head + i)
            out_ref[:, place : place + 64] = out[128 * i : 128 * i + 128]
        log_ref[head : head + 1, :] = top + jnp.log(total)


def attend(queries, pairs, bias):
    return pl.pallas_call(
        attend_kernel,
        out_shape=(
            jax.ShapeDtypeStruct((TOK_DEV, HEADS * HEAD_DIM), BFLOAT),
            jax.ShapeDtypeStruct((8, 3 * TOK_DEV), FLOAT),
        ),
        cost_estimate=pl.CostEstimate(
            flops=12_000_000_000, bytes_accessed=5_000_000, transcendentals=4_000_000
        ),
        compiler_params=pltpu.CompilerParams(vmem_limit_bytes=32 * 1024 * 1024),
    )(queries, *pairs, bias)


def attend_back_kernel(
    query_ref, kv0, kv1, kv2, kv3, bias_ref, log_ref, att_ref, grad_ref, dq_ref, d0, d1, d2, d3
):
    for head in range(KV_HEADS):
        queries = head_rows(query_ref, head)
        grads = head_rows(grad_ref, head)
        outs = head_rows(att_ref, head)
        delta = jnp.sum((grads.astype(FLOAT) * outs.astype(FLOAT)).T, axis=0, keepdims=True)
        log_total = log_ref[head : head + 1, :]
        back = None
        for part, (kv_ref, d_ref) in enumerate(((kv0, d0), (kv1, d1), (kv2, d2), (kv3, d3))):
            keys = kv_ref[:, 64 * head : 64 * head + 64]
            values = kv_ref[:, 320 + 64 * head : 320 + 64 * head + 64]
            bias = bias_ref[512 * part : 512 * part + 512, :]
            probs = jnp.exp(
                contract_cols(keys, queries) + jnp.concatenate([bias, bias, bias], axis=1) - log_total
            )
            grad_scores = (probs * (contract_cols(values, grads) - delta)).astype(BFLOAT)
            d_ref[:, 64 * head : 64 * head + 64] = nn(grad_scores, queries).astype(BFLOAT)
            d_ref[:, 320 + 64 * head : 320 + 64 * head + 64] = nn(
                probs.astype(BFLOAT), grads
            ).astype(BFLOAT)
            part_back = contract_rows(keys, grad_scores)
            back = part_back if back is None else back + part_back
        back = back.T * (HEAD_DIM**-0.5)
        for i in range(3):
            place = 64 * (3 * head + i)
            dq_ref[:, place : place + 64] = back[128 * i : 128 * i + 128]


def attend_back(queries, pairs, bias, log_total, attended, grads):
    side = jax.ShapeDtypeStruct((4 * TOK_DEV, 640), BFLOAT)
    return pl.pallas_call(
        attend_back_kernel,
        out_shape=(jax.ShapeDtypeStruct((TOK_DEV, HEADS * HEAD_DIM), FLOAT), side, side, side, side),
        cost_estimate=pl.CostEstimate(
            flops=20_000_000_000, bytes_accessed=9_000_000, transcendentals=4_000_000
        ),
        compiler_params=pltpu.CompilerParams(vmem_limit_bytes=32 * 1024 * 1024),
    )(queries, *pairs, bias, log_total, attended, grads)


HEAD_BLOCK = 512


def head_kernel(rows_ref, near_ref, final_ref, target_ref, table_ref, logit_ref, pick_ref, stat_ref):
    step = pl.program_id(0)

    @pl.when(step == 0)
    def first():
        hot = (rows_ref[...] == near_ref[...]).astype(FLOAT).astype(BFLOAT)
        pick_ref[...] = nn(hot, final_ref[...]).astype(BFLOAT)
        lane = lax.broadcasted_iota(jnp.int32, (256, 128), 1)
        stat_ref[...] = jnp.where(lane == 0, MASKED, 0.0)

    logits = contract_cols(pick_ref[...], table_ref[...])
    logit_ref[...] = logits
    place = step * HEAD_BLOCK + lax.broadcasted_iota(jnp.int32, (256, HEAD_BLOCK), 1)
    hit = jnp.sum(jnp.where(place == target_ref[...], logits, 0.0), axis=1, keepdims=True)
    old = stat_ref[:, 0:1]
    top = jnp.maximum(old, jnp.max(logits, axis=1, keepdims=True))
    total = stat_ref[:, 1:2] * jnp.exp(old - top) + jnp.sum(
        jnp.exp(logits - top), axis=1, keepdims=True
    )
    stat_ref[:, 1:2] = total
    stat_ref[:, 2:3] = stat_ref[:, 2:3] + hit
    stat_ref[:, 0:1] = top


def head(loss_rows, near_rows, final_rows, local_targets, table):
    def whole(shape):
        return pl.BlockSpec(shape, lambda i: (0, 0))

    return pl.pallas_call(
        head_kernel,
        grid=(VOCAB_MP // HEAD_BLOCK,),
        in_specs=[
            whole((256, 1)),
            whole((1, ROWS)),
            whole((ROWS, D)),
            whole((256, 1)),
            pl.BlockSpec((HEAD_BLOCK, D), lambda i: (i, 0)),
        ],
        out_specs=[
            pl.BlockSpec((256, HEAD_BLOCK), lambda i: (0, i)),
            whole((256, D)),
            whole((256, 128)),
        ],
        out_shape=(
            jax.ShapeDtypeStruct((256, VOCAB_MP), FLOAT),
            jax.ShapeDtypeStruct((256, D), BFLOAT),
            jax.ShapeDtypeStruct((256, 128), FLOAT),
        ),
        compiler_params=pltpu.CompilerParams(vmem_limit_bytes=32 * 1024 * 1024),
    )(loss_rows, near_rows, final_rows, local_targets, table)


def head_back_kernel(
    rows_ref, near_ref, target_ref, norm_ref, logit_ref, pick_ref, table_ref, grad_ref, out_ref, sum_ref
):
    step = pl.program_id(0)
    place = step * HEAD_BLOCK + lax.broadcasted_iota(jnp.int32, (256, HEAD_BLOCK), 1)
    probs = jnp.exp(logit_ref[...] - norm_ref[...])
    hit = jnp.where(place == target_ref[...], 1.0, 0.0)
    grads = ((probs - hit) * (1.0 / TOK_DEV)).astype(BFLOAT)
    grad_ref[...] = contract_rows(grads, pick_ref[...]).astype(BFLOAT)
    part = nn(grads, table_ref[...])

    @pl.when(step == 0)
    def first():
        sum_ref[...] = part

    @pl.when(step > 0)
    def later():
        sum_ref[...] += part

    @pl.when(step == pl.num_programs(0) - 1)
    def last():
        hot = (rows_ref[...] == near_ref[...]).astype(FLOAT).astype(BFLOAT)
        out_ref[...] = contract_rows(hot, sum_ref[...].astype(BFLOAT)).astype(BFLOAT)


def head_back(loss_rows, near_rows, local_targets, log_norm, logits, picked, table):
    def whole(shape):
        return pl.BlockSpec(shape, lambda i: (0, 0))

    return pl.pallas_call(
        head_back_kernel,
        grid=(VOCAB_MP // HEAD_BLOCK,),
        in_specs=[
            whole((256, 1)),
            whole((1, ROWS)),
            whole((256, 1)),
            whole((256, 1)),
            pl.BlockSpec((256, HEAD_BLOCK), lambda i: (0, i)),
            whole((256, D)),
            pl.BlockSpec((HEAD_BLOCK, D), lambda i: (i, 0)),
        ],
        out_specs=[pl.BlockSpec((HEAD_BLOCK, D), lambda i: (i, 0)), whole((ROWS, D))],
        out_shape=(
            jax.ShapeDtypeStruct((VOCAB_MP, D), BFLOAT),
            jax.ShapeDtypeStruct((ROWS, D), BFLOAT),
        ),
        scratch_shapes=[pltpu.VMEM((256, D), FLOAT)],
        compiler_params=pltpu.CompilerParams(vmem_limit_bytes=32 * 1024 * 1024),
    )(loss_rows, near_rows, local_targets, log_norm, logits, picked, table)


def mlp_grad_kernel(added, which_ref, *refs):
    lefts, rights, refs = refs[0:3], refs[3:6], refs[6:]
    for i in range(3):
        total = contract_rows(lefts[i][...], rights[i][...])
        if added:
            total = total + refs[0][i].astype(FLOAT)
        refs[-1][i] = total.astype(BFLOAT)


def mlp_grads(which, lefts, rights, received=None):
    added = received is not None
    block = 256
    rows = lefts[0].shape[0]
    steps = FF // 2 // block
    out_spec = pl.BlockSpec((3, block, D), lambda i, half: (0, i, 0))
    return pl.pallas_call(
        functools.partial(mlp_grad_kernel, added),
        grid_spec=pltpu.PrefetchScalarGridSpec(
            num_scalar_prefetch=1,
            grid=(steps,),
            in_specs=[pl.BlockSpec((rows, block), lambda i, half: (0, half[0] * steps + i))] * 3
            + [pl.BlockSpec((rows, D), lambda i, half: (0, 0))] * 3
            + [out_spec] * added,
            out_specs=out_spec,
        ),
        out_shape=jax.ShapeDtypeStruct((3, FF // 2, D), BFLOAT),
        compiler_params=pltpu.CompilerParams(vmem_limit_bytes=32 * 1024 * 1024),
    )(which.reshape(1), *lefts, *rights, *([received] if added else []))


def pack_grad_kernel(
    starts_ref, normed_ref, dq_ref, dk_ref, dv_ref, att_ref, grad_ref, rows_ref, mine_ref, other_ref, buf
):
    buf[0:960, :] = contract_rows(normed_ref[...], dq_ref[...]).astype(BFLOAT)
    buf[1600:2560, :] = contract_rows(att_ref[...], grad_ref[...]).astype(BFLOAT)
    buf[2560:2576, :] = rows_ref[...].astype(BFLOAT)
    buf[2576:2688, :] = jnp.zeros((112, D), BFLOAT)
    line = lax.broadcasted_iota(jnp.int32, (960, 320), 0)
    place = lax.broadcasted_iota(jnp.int32, (960, 320), 1)
    for first, ref in ((960, dk_ref), (1280, dv_ref)):
        full = contract_rows(normed_ref[...], ref[...]).astype(BFLOAT)
        for i in range(3):
            chosen = (line == 3 * place + i).astype(FLOAT).astype(BFLOAT)
            buf[first : first + 320, 320 * i : 320 * i + 320] = contract_rows(chosen, full).astype(
                BFLOAT
            )
    for i in range(4):
        mine_ref[i] = buf[pl.ds(pl.multiple_of(starts_ref[i], 16), 352), :]
        other_ref[i] = buf[pl.ds(pl.multiple_of(starts_ref[4 + i], 16), 352), :]


def pack_grads(starts, *parts):
    side = jax.ShapeDtypeStruct((4, 352, D), BFLOAT)
    return pl.pallas_call(
        pack_grad_kernel,
        in_specs=[pl.BlockSpec(memory_space=pltpu.SMEM)]
        + [pl.BlockSpec(memory_space=pltpu.VMEM)] * len(parts),
        out_shape=(side, side),
        scratch_shapes=[pltpu.VMEM((PACK_PAD, D), BFLOAT)],
        compiler_params=pltpu.CompilerParams(vmem_limit_bytes=40 * 1024 * 1024),
    )(starts, *parts)


def adam_update(master, first, second, grad, clip):
    grad = grad * clip
    first_new = BETA_ONE * first + (1.0 - BETA_ONE) * grad
    second_new = BETA_TWO * second + (1.0 - BETA_TWO) * grad * grad
    corr_one = 1.0 - BETA_ONE**STEP
    corr_two = 1.0 - BETA_TWO**STEP
    master_new = master - LEARN_RATE * (
        first_new / corr_one / (jnp.sqrt(second_new / corr_two) + ADAM_EPS) + DECAY * master
    )
    return (master_new, first_new, second_new)


def pack_row(device):
    return (1283 * device) // 64


def join_kernel(blocks_ref, out_ref):
    step = pl.program_id(0)
    first = jnp.minimum((step * (128 * 64)) // 1283, 118)
    first = (first // 2) * 2
    window = blocks_ref[pl.ds(pl.multiple_of(first * 24, 48), 240), :]
    row = step * 128 + lax.broadcasted_iota(jnp.int32, (128, 240), 0)
    place = lax.broadcasted_iota(jnp.int32, (128, 240), 1)
    device = (place * 2731) >> 16
    source = ((1283 * (first + device)) >> 6) + place - 24 * device
    chosen = (source == row).astype(FLOAT).astype(BFLOAT)
    out_ref[...] = jnp.dot(chosen, window, preferred_element_type=FLOAT).astype(BFLOAT)


def join_pack(blocks):
    return pl.pallas_call(
        join_kernel,
        grid=(PACK_PAD // 128,),
        in_specs=[pl.BlockSpec((128 * 24, D), lambda i: (0, 0))],
        out_specs=pl.BlockSpec((128, D), lambda i: (i, 0)),
        out_shape=jax.ShapeDtypeStruct((PACK_PAD, D), BFLOAT),
        compiler_params=pltpu.CompilerParams(vmem_limit_bytes=32 * 1024 * 1024),
    )(blocks)


def stage(value, axis, index):
    total = lax.dynamic_index_in_dim(value, index, 0, False).astype(FLOAT)
    for k in (1, 2, 3):
        sent = lax.dynamic_index_in_dim(value, (index + k) % 4, 0, False)
        total = total + shift(sent, axis, k).astype(FLOAT)
    return total


def stage_near(value, axis):
    total = value[0].astype(FLOAT)
    for k in (1, 2, 3):
        total = total + shift(value[k], axis, -k).astype(FLOAT)
    return total


def shards(
    token_ids,
    targets,
    loss_rows,
    selections,
    boundary,
    pack_master,
    pack_first,
    pack_second,
    mlp_master,
    mlp_first,
    mlp_second,
    table_master,
    table_first,
    table_second,
):
    z = lax.axis_index("z")
    core = lax.axis_index("core")
    y = lax.axis_index("y")
    x = lax.axis_index("x")
    model_index = z * 2 + core
    data_index = y * 4 + x
    device = model_index * DP + data_index
    groups_per = HEADS // KV_HEADS
    scale = HEAD_DIM ** (-0.5)
    own_table = table_master.astype(BFLOAT)

    near = jnp.stack([((z + k) % 4) * 2 + (core ^ j) for j in (0, 1) for k in range(4)])
    near_rows = (near[:, None] * TOK_DEV + jnp.arange(TOK_DEV, dtype=jnp.int32)[None, :]).reshape(-1)

    pack_offset = PACK_DEV * device - D * pack_row(device)
    pack_block = lax.dynamic_update_slice(
        jnp.zeros((24 * D,), BFLOAT), pack_master.astype(BFLOAT), (pack_offset,)
    ).reshape(24, D)
    pack_blocks = lax.all_gather(pack_block, ALL_AXES, axis=0, tiled=True)
    mlp_own = mlp_master.astype(BFLOAT)
    mlp_quad = jnp.concatenate([mlp_own] + [shift(mlp_own, "z", k) for k in (1, 2, 3)], axis=1)
    mlp_blocks = lax.all_gather(mlp_quad.reshape(3 * 80, D), ("core", "y", "x"), axis=0, tiled=True)
    table = lax.all_gather(own_table, DP_AXES, axis=0, tiled=True)

    group_ids = token_ids[0]
    near_ids = reorder(group_ids.reshape(MP, TOK_DEV), near).reshape(-1)
    local_ids = near_ids - model_index * VOCAB_MP
    inside = (local_ids >= 0) & (local_ids < VOCAB_MP)
    high = local_ids >> 7
    low = local_ids & 127
    high_hot = (high[:, None] == jnp.arange(48)[None, :]).astype(BFLOAT)
    low_hot = (low[:, None] == jnp.arange(128)[None, :]).astype(BFLOAT)
    present = (contract_rows(high_hot, low_hot) > 0).reshape(DP, VOCAB_DEV)
    before = (jnp.arange(VOCAB_DEV)[:, None] < jnp.arange(VOCAB_DEV)[None, :]).astype(BFLOAT)
    slots = mm(present.astype(BFLOAT), before)
    asked = present & (slots < CAP)
    over = jnp.max(jnp.where(present & (slots >= CAP), 1.0, 0.0))
    over = sum_all(jnp.full((1, 128), over, FLOAT))[0, 0] > 0
    slot_table = jnp.where(asked, slots, 255.0).reshape(48, 128).astype(BFLOAT)
    token_slot = jnp.sum(mm(high_hot, slot_table) * low_hot.astype(FLOAT), axis=-1)
    token_place = jnp.where(
        inside & (token_slot < CAP), (high // 3) * CAP + token_slot.astype(jnp.int32), -1
    )
    place_hot = (token_place[:, None] == jnp.arange(DP * CAP)[None, :]).astype(BFLOAT)
    match = asked[:, None, :] & (slots[:, None, :] == jnp.arange(CAP, dtype=FLOAT)[None, :, None])
    request = (
        jnp.sum(jnp.where(match, jnp.arange(1, VOCAB_DEV + 1, dtype=FLOAT)[None, None, :], 0.0), axis=-1)
        - 1.0
    )
    request = lax.all_to_all(request, DP_AXES, 0, 0, tiled=True)
    owner_hot = (
        request.reshape(-1)[:, None] == jnp.arange(VOCAB_DEV, dtype=FLOAT)[None, :]
    ).astype(BFLOAT)
    sent_rows = mm(owner_hot, own_table).astype(BFLOAT)
    asked_rows = lax.all_to_all(sent_rows, DP_AXES, 0, 0, tiled=True)

    def looked_sparse():
        return mm(place_hot, asked_rows).astype(BFLOAT)

    def looked_dense():
        full = lax.all_gather(own_table, DP_AXES, axis=0, tiled=True)
        rows = jnp.take(full, jnp.clip(local_ids, 0, VOCAB_MP - 1), axis=0)
        return jnp.where(inside[:, None], rows, jnp.zeros_like(rows))

    looked = lax.cond(over, looked_dense, looked_sparse)
    looked, pack_blocks = tie(looked, pack_blocks)
    hidden = scatter_group(looked.reshape(2, 4, TOK_DEV, D), FLOAT)

    pack_weights = join_pack(pack_blocks)
    w_query = pack_weights[:960]
    w_key = pack_weights[960:1280].reshape(D, KV_HEADS * HEAD_DIM)
    w_value = pack_weights[1280:1600].reshape(D, KV_HEADS * HEAD_DIM)
    w_out = pack_weights[1600:2560]
    gains = pack_weights[2560:2563].astype(FLOAT)
    router = pack_weights[2563:2566].astype(FLOAT)
    mlp_weights = (
        mlp_blocks.reshape(2, 4, 4, 3, 80, D).transpose(3, 0, 2, 1, 4, 5).reshape(3, FF, D)
    )
    gate_w = mlp_weights[0]
    up_w = mlp_weights[1]
    down_w = mlp_weights[2]

    first_row = data_index * ROWS + model_index * TOK_DEV
    query_rows = first_row + jnp.arange(TOK_DEV, dtype=jnp.int32)
    cosine, sine = rotation(query_rows)
    group_sel = selections.reshape(RECUR, DP, MP, TOK_DEV)
    prev_index = jnp.maximum(data_index - 1, 0)
    here_sel = lax.dynamic_index_in_dim(group_sel, data_index, 1, False)
    own_sel = lax.dynamic_index_in_dim(here_sel, model_index, 1, False)
    near_sel = reorder(here_sel, near).reshape(RECUR, ROWS)
    prev_sel = reorder(lax.dynamic_index_in_dim(group_sel, prev_index, 1, False), near)
    prev_sel = prev_sel.reshape(RECUR, ROWS)
    start = lax.dynamic_index_in_dim(boundary, data_index, 0, False)
    prev_start = lax.dynamic_index_in_dim(boundary, prev_index, 0, False)
    place = (model_index * TOK_DEV + jnp.arange(TOK_DEV, dtype=jnp.int32))[None, None, :]
    key_place = near_rows[None, :, None]
    own_seen = (
        (key_place <= place)
        & ((key_place < start) == (place < start))
        & ((near_sel[:, :, None] > 0) | (key_place == place))
    )
    prev_seen = (
        (data_index > 0) & (place < start) & (key_place >= prev_start) & (prev_sel[:, :, None] > 0)
    )
    biases = jnp.concatenate(
        [prev_seen[:, :512], own_seen[:, :512], prev_seen[:, 512:], own_seen[:, 512:]], axis=1
    )
    biases = jnp.where(biases, 0.0, MASKED)

    saves = []
    penalty_total = jnp.zeros((), FLOAT)
    for step in range(RECUR):
        normed = rms_scale(hidden, gains[0]).astype(BFLOAT)
        keys_own = rotate(mm(normed, w_key).reshape(TOK_DEV, KV_HEADS, HEAD_DIM), cosine, sine)
        values_own = mm(normed, w_value)
        pair = jnp.concatenate([keys_own.reshape(TOK_DEV, -1), values_own], axis=1).astype(BFLOAT)
        pairs = group_gather(pair)
        queries = (
            rotate(mm(normed, w_query).reshape(TOK_DEV, HEADS, HEAD_DIM), cosine, sine) * scale
        ).astype(BFLOAT)
        attended, log_total = attend(queries.reshape(TOK_DEV, -1), pairs, biases[step])
        mixed = hidden + mm(attended, w_out)
        mlp_input = rms_scale(mixed, gains[1]).astype(BFLOAT)
        gate_pre = contract_cols(mlp_input, gate_w)
        up_pre = contract_cols(mlp_input, up_w)
        inner = (jax.nn.silu(gate_pre) * up_pre).astype(BFLOAT)
        branch = mixed + mm(inner, down_w)
        logit = jnp.dot(hidden, router[step], precision=HIGHEST)
        chosen = own_sel[step].astype(FLOAT)
        weight_sel = chosen * jax.nn.sigmoid(logit)
        new_hidden = hidden + weight_sel[:, None] * (branch - hidden)
        penalty_total = penalty_total + jnp.sum(jax.nn.softplus(logit) - chosen * logit)
        saves.append(
            (
                hidden,
                normed,
                queries,
                pairs,
                log_total,
                attended,
                mixed,
                mlp_input,
                gate_pre,
                up_pre,
                inner,
                branch,
                logit,
            )
        )
        hidden = new_hidden

    normed_final = rms_scale(hidden, gains[2]).astype(BFLOAT)
    final_rows = gather_group(normed_final).reshape(ROWS, D)
    row_targets = lax.dynamic_index_in_dim(targets, data_index, 0, keepdims=False)
    head_args = (loss_rows[0][:, None], near_rows[None, :])
    local_targets = (row_targets - model_index * VOCAB_MP)[:, None]
    logits, picked, stats = head(*head_args, final_rows, local_targets, table)
    stats = stats[:, :3].T

    def join_stats(parts):
        top = parts[0][0]
        for part in parts[1:]:
            top = jnp.maximum(top, part[0])
        total = sum(part[1] * jnp.exp(part[0] - top) for part in parts)
        return jnp.stack([top, total, sum(part[2] for part in parts)])

    stats = join_stats([stats, swap(stats)])
    stats = join_stats([stats] + [shift(stats, "z", k) for k in (1, 2, 3)])
    log_norm = stats[0] + jnp.log(stats[1])
    cross = log_norm - stats[2]
    per_device = cross.shape[0] // MP
    loss_part = (
        jnp.sum(lax.dynamic_slice_in_dim(cross, model_index * per_device, per_device))
        + ROUTER_LOSS * penalty_total
    )
    head_grad, scattered = head_back(
        *head_args, local_targets, log_norm[:, None], logits, picked, table
    )
    grad_final = scatter_group(scattered.reshape(2, 4, TOK_DEV, D), FLOAT)
    grad_hidden, grad_gain_final = rms_back(hidden, gains[2], grad_final)
    head_grad = lax.psum_scatter(head_grad, DP_AXES, scatter_dimension=0, tiled=True)

    kept = []
    mlp_parts = []
    router_rows = [None] * RECUR
    gain_one = jnp.zeros((D,), FLOAT)
    gain_two = jnp.zeros((D,), FLOAT)
    for step in reversed(range(RECUR)):
        grad_new = grad_hidden
        (
            hidden_in,
            normed,
            queries,
            pairs,
            log_total,
            attended,
            mixed,
            mlp_input,
            gate_pre,
            up_pre,
            inner,
            branch,
            logit,
        ) = saves[step]
        chosen = own_sel[step].astype(FLOAT)
        sigma = jax.nn.sigmoid(logit)
        weight_sel = chosen * sigma
        grad_branch = weight_sel[:, None] * grad_new
        grad_weight = jnp.sum(grad_new * (branch - hidden_in), axis=-1)
        grad_logit = grad_weight * chosen * sigma * (1.0 - sigma) + ROUTER_LOSS / TOK_DEV * (
            sigma - chosen
        )
        grad_in = (
            grad_new - weight_sel[:, None] * grad_new + grad_logit[:, None] * router[step][None, :]
        )
        router_rows[step] = jnp.dot(grad_logit, hidden_in, precision=HIGHEST)
        grad_rows = grad_branch.astype(BFLOAT)
        grad_inner = contract_cols(grad_rows, down_w)
        sigma_gate = jax.nn.sigmoid(gate_pre)
        grad_gate = (
            grad_inner * up_pre * sigma_gate * (1.0 + gate_pre * (1.0 - sigma_gate))
        ).astype(BFLOAT)
        grad_up = (grad_inner * gate_pre * sigma_gate).astype(BFLOAT)
        mlp_parts.append((grad_gate, grad_up, inner, mlp_input, mlp_input, grad_rows))
        grad_normed_two = mm(grad_gate, gate_w) + mm(grad_up, up_w)
        grad_mixed_norm, part_two = rms_back(mixed, gains[1], grad_normed_two)
        gain_two = gain_two + part_two
        grad_mixed = grad_branch + grad_mixed_norm
        grad_in = grad_in + grad_mixed
        grad_attn = grad_mixed.astype(BFLOAT)
        grad_attended = (
            contract_cols(grad_attn, w_out).astype(BFLOAT)
        )
        if step == 0:
            mlp_kept = [jnp.concatenate(parts, axis=0) for parts in zip(*mlp_parts)]
            far = mlp_grads(1 - core, mlp_kept[:3], mlp_kept[3:])
            grad_attended, far, head_grad = tie(grad_attended, far, head_grad)
            far = swap(far)
        grad_queries, *grad_sides = attend_back(
            queries.reshape(TOK_DEV, -1), pairs, biases[step], log_total, attended, grad_attended
        )
        if step == 0:
            far, *grad_sides = tie(far, *grad_sides)
            mlp_half = mlp_grads(core, mlp_kept[:3], mlp_kept[3:], far)
        grad_own = group_scatter(*grad_sides)
        grad_query_pre = (
            rotate(grad_queries.reshape(TOK_DEV, HEADS, HEAD_DIM), cosine, -sine)
            .reshape(TOK_DEV, -1)
            .astype(BFLOAT)
        )
        grad_key_pre = (
            rotate(grad_own[:, :320].reshape(TOK_DEV, KV_HEADS, HEAD_DIM), cosine, -sine)
            .reshape(TOK_DEV, -1)
            .astype(BFLOAT)
        )
        grad_value_pre = grad_own[:, 320:].astype(BFLOAT)
        grad_normed = (
            contract_cols(grad_query_pre, w_query)
            + contract_cols(grad_key_pre, w_key)
            + contract_cols(grad_value_pre, w_value)
        )
        grad_hidden_norm, part_one = rms_back(hidden_in, gains[0], grad_normed)
        gain_one = gain_one + part_one
        grad_hidden = grad_in + grad_hidden_norm
        kept.append(
            (
                normed,
                grad_query_pre,
                grad_key_pre,
                grad_value_pre,
                attended,
                grad_attn,
            )
        )
    (
        normed_all,
        grad_query_all,
        grad_key_all,
        grad_value_all,
        attended_all,
        grad_attn_all,
    ) = [jnp.concatenate(parts, axis=0) for parts in zip(*kept)]

    mlp_half = mlp_half.reshape(3, 4, 4, 80, D)
    cols = mlp_half[..., :512].transpose(1, 2, 0, 3, 4)
    part = stage(stage(cols, "x", x).astype(BFLOAT), "y", y).astype(BFLOAT)
    left = stage_near(part.reshape(3, 4, UNITS, -1).transpose(1, 0, 2, 3), "z")
    cols = mlp_half[..., 512:].transpose(2, 1, 0, 3, 4)
    part = stage(stage(cols, "y", y).astype(BFLOAT), "x", x).astype(BFLOAT)
    right = stage_near(part.reshape(3, 4, UNITS, -1).transpose(1, 0, 2, 3), "z")
    mlp_grad = jnp.concatenate([left, right], axis=-1)

    def aligned_row(which):
        return (pack_row(which) // 16) * 16

    small = jnp.concatenate(
        [
            jnp.stack([gain_one, gain_two, grad_gain_final] + router_rows),
            jnp.zeros((10, D), FLOAT),
        ]
    )
    starts = jnp.stack(
        [aligned_row(DP * (2 * i + c)) for c in (core, 1 - core) for i in range(4)]
    ).astype(jnp.int32)
    mine, other = pack_grads(
        starts,
        normed_all,
        grad_query_all,
        grad_key_all,
        grad_value_all,
        attended_all,
        grad_attn_all,
        small,
    )
    half = (mine.astype(FLOAT) + swap(other).astype(FLOAT)).astype(BFLOAT)

    def y_windows(value):
        return jnp.stack([value[..., 80 * i : 80 * i + 112, :] for i in range(4)])

    def x_windows(value):
        return jnp.stack([value[..., i : i + 48, :] for i in (0, 16, 40, 56)])

    part = stage(y_windows(half[..., :512]), "y", y).astype(BFLOAT)
    part = stage(part, "z", z).astype(BFLOAT)
    left = stage(x_windows(part), "x", x)
    part = stage(half[..., 512:], "z", z).astype(BFLOAT)
    part = stage(y_windows(part), "y", y).astype(BFLOAT)
    right = stage(x_windows(part), "x", x)
    part = jnp.concatenate([left, right], axis=-1).reshape(-1)
    begin = aligned_row(DP * model_index) + 80 * y + (20 * x) // 8 * 8
    pack_grad = lax.dynamic_slice(part, (PACK_DEV * device - D * begin,), (PACK_DEV,))

    grad_embed = gather_group(grad_hidden.astype(BFLOAT)).reshape(ROWS, D)

    unique = contract_rows(place_hot, grad_embed).astype(BFLOAT)
    unique = lax.all_to_all(unique, DP_AXES, 0, 0, tiled=True)

    def embed_sparse():
        return contract_rows(owner_hot, unique)

    def embed_dense():
        kept_rows = grad_embed.astype(FLOAT) * inside.astype(FLOAT)[:, None]
        sums = jax.ops.segment_sum(
            kept_rows, jnp.clip(local_ids, 0, VOCAB_MP - 1), num_segments=VOCAB_MP
        )
        return lax.psum_scatter(
            sums.astype(BFLOAT), DP_AXES, scatter_dimension=0, tiled=True
        ).astype(FLOAT)

    table_grad = head_grad.astype(FLOAT) + lax.cond(over, embed_dense, embed_sparse)

    squares = (
        jnp.sum(pack_grad * pack_grad)
        + jnp.sum(mlp_grad * mlp_grad)
        + jnp.sum(table_grad * table_grad)
    )
    lane = lax.broadcasted_iota(jnp.int32, (1, 128), 1)
    sums = sum_all(jnp.where(lane == 0, squares, loss_part))
    total_squares = sums[0, 0]
    loss_sum = sums[0, 1]
    grad_norm = jnp.sqrt(total_squares)
    clip = CLIP_NORM / jnp.maximum(grad_norm, CLIP_NORM)
    pack_new, pack_first_new, pack_second_new = adam_update(
        pack_master, pack_first, pack_second, pack_grad, clip
    )
    mlp_new, mlp_first_new, mlp_second_new = adam_update(
        mlp_master, mlp_first, mlp_second, mlp_grad, clip
    )
    table_new, table_first_new, table_second_new = adam_update(
        table_master, table_first, table_second, table_grad, clip
    )
    return (
        pack_new,
        pack_first_new,
        pack_second_new,
        mlp_new,
        mlp_first_new,
        mlp_second_new,
        table_new,
        table_first_new,
        table_second_new,
        loss_sum,
        grad_norm,
    )


def solution(mesh):
    grid = Mesh(mesh.devices.reshape(4, 2, 4, 4), ALL_AXES)
    owners = (P(ALL_AXES), P(None, ALL_AXES, None), P(ALL_AXES, None))
    group = P(DP_AXES, None)
    masters = tuple(spec for spec in owners for _ in range(3))
    return jax.shard_map(
        shards,
        mesh=grid,
        in_specs=(group, P(), group, P(), P()) + masters,
        out_specs=masters + (P(), P()),
        check_vma=False,
    )
```

```python
import functools

import jax
import jax.numpy as jnp
from jax import lax
from jax.experimental import pallas as pl
from jax.experimental.layout import Layout, with_layout_constraint
from jax.experimental.pallas import tpu as pltpu
from jax.sharding import Mesh
from jax.sharding import PartitionSpec as P

D = 960
HEADS = 15
KV_HEADS = 5
HEAD_DIM = 64
FF = 2560
RECUR = 3
STEP = 10
TOK_DEV = 128
ROWS = 1024
MP = 8
DP = 16
VOCAB_MP = 6144
VOCAB_DEV = 384
UNITS = 20
PACK_DEV = 19245
PACK_ROWS = 2566
PACK_PAD = 2688
CAP = 24

EPS_NORM = 1e-05
ROPE_BASE = 10000.0
ROUTER_LOSS = 0.1
CLIP_NORM = 1.0
LEARN_RATE = 0.05
BETA_ONE = 0.9
BETA_TWO = 0.95
ADAM_EPS = 1e-08
DECAY = 0.1
MASKED = -1e30
HIGHEST = lax.Precision.HIGHEST
BFLOAT = jnp.bfloat16
FLOAT = jnp.float32
DP_AXES = ("y", "x")
ALL_AXES = ("z", "core", "y", "x")


def shift(value, axis, steps):
    return lax.ppermute(value, axis, [(i, (i + steps) % 4) for i in range(4)])


def swap(value):
    return lax.ppermute(value, "core", [(0, 1), (1, 0)])


def gather_group(value):
    parts = jnp.stack([value] + [shift(value, "z", -k) for k in (1, 2, 3)])
    return jnp.stack([parts, swap(parts)])


def scatter_group(blocks, kind=BFLOAT):
    half = (blocks[0].astype(FLOAT) + swap(blocks[1].astype(BFLOAT)).astype(FLOAT)).astype(BFLOAT)
    total = half[0].astype(FLOAT)
    for k in (1, 2, 3):
        total = total + shift(half[k], "z", k).astype(FLOAT)
    return total.astype(kind)


def sum_all(value):
    value = value + swap(value)
    for axis in ("z", "y", "x"):
        value = value + shift(value, axis, 1) + shift(value, axis, 2) + shift(value, axis, 3)
    return value


def rms_scale(values, weight):
    return values * lax.rsqrt(jnp.mean(values * values, axis=-1, keepdims=True) + EPS_NORM) * weight


def rms_back(values, weight, grad_out):
    inverse = lax.rsqrt(jnp.mean(values * values, axis=-1, keepdims=True) + EPS_NORM)
    weighted = grad_out * weight
    grad_values = inverse * weighted - values * (inverse * inverse * inverse) * jnp.mean(
        weighted * values, axis=-1, keepdims=True
    )
    return (grad_values, jnp.sum(grad_out * values * inverse, axis=0))


def mm(left, right):
    return jnp.dot(left, right, preferred_element_type=FLOAT)


def contract_rows(left, right):
    return lax.dot_general(left, right, (((0,), (0,)), ((), ())), preferred_element_type=FLOAT)


def contract_cols(left, right):
    return lax.dot_general(left, right, (((1,), (1,)), ((), ())), preferred_element_type=FLOAT)


def reorder(blocks, order):
    hit = order[:, None] == jnp.arange(MP)[None, :]
    return jnp.sum(jnp.where(hit[:, :, None], blocks[..., None, :, :], 0), axis=-2)


def by_rows(value):
    return with_layout_constraint(value, Layout(tuple(range(value.ndim))))


def by_cols(value):
    return with_layout_constraint(value, Layout((1, 0)))


def tie(*values):
    return lax.optimization_barrier(values)


def group_gather(pair):
    own = [pair]
    for k in (1, 2, 3):
        own.append(lax.ppermute(pair, "z", [((i + k) % 4, i) for i in range(4) if (i + k) % 4 < i]))
    prev = []
    for k in range(4):
        pairs = []
        for i in range(3):
            for g in range(1, DP):
                pairs.append((((i + k) % 4) * DP + g - 1, i * DP + g))
        prev.append(lax.ppermute(pair, ("z",) + DP_AXES, pairs))
    own = jnp.concatenate(own, axis=0)
    prev = jnp.concatenate(prev, axis=0)
    return prev, own, swap(prev), swap(own)


def group_scatter(prev, own, prev_far, own_far):
    own = (own.astype(FLOAT) + swap(own_far).astype(FLOAT)).astype(BFLOAT).reshape(4, TOK_DEV, -1)
    prev = (prev.astype(FLOAT) + swap(prev_far).astype(FLOAT)).astype(BFLOAT).reshape(4, TOK_DEV, -1)
    total = own[0].astype(FLOAT)
    for k in (1, 2, 3):
        pairs = [(i, (i + k) % 4) for i in range(4) if (i + k) % 4 < i]
        total = total + lax.ppermute(own[k], "z", pairs).astype(FLOAT)
    for k in range(4):
        pairs = []
        for i in range(3):
            for g in range(1, DP):
                pairs.append((i * DP + g, ((i + k) % 4) * DP + g - 1))
        total = total + lax.ppermute(prev[k], ("z",) + DP_AXES, pairs).astype(FLOAT)
    return total


def nn(left, right):
    return jnp.dot(left, right, preferred_element_type=FLOAT)


def head_rows(ref, head):
    return jnp.concatenate(
        [ref[:, 64 * (3 * head + i) : 64 * (3 * head + i) + 64] for i in range(3)], axis=0
    )


def head_lanes(ref, head):
    return jnp.concatenate(
        [ref[64 * (3 * head + i) : 64 * (3 * head + i) + 64, :] for i in range(3)], axis=1
    )


def turn(value, cosine, sine):
    parts = []
    for head in range(value.shape[0] // 64):
        first = value[64 * head : 64 * head + 32]
        second = value[64 * head + 32 : 64 * head + 64]
        parts.append(first * cosine - second * sine)
        parts.append(second * cosine + first * sine)
    return jnp.concatenate(parts, axis=0)


def normalize(values, weight):
    return values * lax.rsqrt(jnp.mean(values * values, axis=-1, keepdims=True) + EPS_NORM) * weight


def normalize_back(values, weight, grad_out):
    inverse = lax.rsqrt(jnp.mean(values * values, axis=-1, keepdims=True) + EPS_NORM)
    weighted = grad_out * weight
    grad_values = inverse * weighted - values * (inverse * inverse * inverse) * jnp.mean(
        weighted * values, axis=-1, keepdims=True
    )
    return grad_values, jnp.sum(grad_out * values * inverse, axis=0, keepdims=True)


def attend_kernel(query_ref, kv0, kv1, kv2, kv3, bias_ref, out_ref, log_ref):
    for head in range(KV_HEADS):
        queries = head_lanes(query_ref, head)
        top = None
        for part, kv_ref in enumerate((kv0, kv1, kv2, kv3)):
            keys = kv_ref[:, 64 * head : 64 * head + 64]
            values = kv_ref[:, 320 + 64 * head : 320 + 64 * head + 64]
            bias = bias_ref[512 * part : 512 * part + 512, :]
            scores = nn(keys, queries) + jnp.concatenate([bias, bias, bias], axis=1)
            part_top = jnp.max(scores, axis=0, keepdims=True)
            new_top = part_top if top is None else jnp.maximum(top, part_top)
            expo = jnp.exp(scores - new_top)
            part_total = jnp.sum(expo, axis=0, keepdims=True)
            part_out = contract_rows(values, expo.astype(BFLOAT))
            if top is None:
                total, out = part_total, part_out
            else:
                shrink = jnp.exp(top - new_top)
                total, out = total * shrink + part_total, out * shrink + part_out
            top = new_top
        out = (out / total).T.astype(BFLOAT)
        for i in range(3):
            place = 64 * (3 * head + i)
            out_ref[:, place : place + 64] = out[128 * i : 128 * i + 128]
        log_ref[head : head + 1, :] = top + jnp.log(total)


def params(mib):
    return pltpu.CompilerParams(vmem_limit_bytes=mib * 1024 * 1024)


def whole(*shape):
    return pl.BlockSpec(shape, lambda i: (0,) * len(shape))


def struct(kind, *shape):
    return jax.ShapeDtypeStruct(shape, kind)


def attend(queries, pairs, bias):
    return pl.pallas_call(
        attend_kernel,
        out_shape=(struct(BFLOAT, TOK_DEV, D), struct(FLOAT, 8, 3 * TOK_DEV)),
        cost_estimate=pl.CostEstimate(
            flops=12_000_000_000, bytes_accessed=5_000_000, transcendentals=4_000_000
        ),
        compiler_params=params(24),
    )(queries, *pairs, bias)


def attend_back_kernel(
    query_ref, kv0, kv1, kv2, kv3, bias_ref, log_ref, att_ref, grad_ref, cos_ref, sin_ref,
    dq_ref, d0, d1, d2, d3
):
    cosine = jnp.concatenate([cos_ref[...]] * 3, axis=1)
    sine = jnp.concatenate([sin_ref[...]] * 3, axis=1)
    for head in range(KV_HEADS):
        queries = head_lanes(query_ref, head)
        grads = head_rows(grad_ref, head)
        outs = head_rows(att_ref, head)
        delta = jnp.sum((grads.astype(FLOAT) * outs.astype(FLOAT)).T, axis=0, keepdims=True)
        log_total = log_ref[head : head + 1, :]
        back = None
        for part, (kv_ref, d_ref) in enumerate(((kv0, d0), (kv1, d1), (kv2, d2), (kv3, d3))):
            keys = kv_ref[:, 64 * head : 64 * head + 64]
            values = kv_ref[:, 320 + 64 * head : 320 + 64 * head + 64]
            bias = bias_ref[512 * part : 512 * part + 512, :]
            probs = jnp.exp(
                nn(keys, queries) + jnp.concatenate([bias, bias, bias], axis=1) - log_total
            )
            grad_scores = (probs * (contract_cols(values, grads) - delta)).astype(BFLOAT)
            d_ref[:, 64 * head : 64 * head + 64] = contract_cols(grad_scores, queries).astype(BFLOAT)
            d_ref[:, 320 + 64 * head : 320 + 64 * head + 64] = nn(
                probs.astype(BFLOAT), grads
            ).astype(BFLOAT)
            part_back = contract_rows(keys, grad_scores)
            back = part_back if back is None else back + part_back
        back = turn(back * (HEAD_DIM**-0.5), cosine, -sine).T.astype(BFLOAT)
        for i in range(3):
            place = 64 * (3 * head + i)
            dq_ref[:, place : place + 64] = back[128 * i : 128 * i + 128]


def attend_back(queries, pairs, bias, log_total, attended, grads, cosine, sine):
    side = struct(BFLOAT, 4 * TOK_DEV, 640)
    return pl.pallas_call(
        attend_back_kernel,
        out_shape=(struct(BFLOAT, TOK_DEV, D), side, side, side, side),
        cost_estimate=pl.CostEstimate(
            flops=20_000_000_000, bytes_accessed=9_000_000, transcendentals=4_000_000
        ),
        compiler_params=params(24),
    )(queries, *pairs, bias, log_total, attended, grads, cosine, sine)


def project(hidden, gain, wq_ref, wk_ref, wv_ref, cos_ref, sin_ref, normed_ref, query_ref, pair_ref):
    normed = normalize(hidden, gain).astype(BFLOAT)
    normed_ref[...] = normed
    cosine, sine = cos_ref[...], sin_ref[...]
    keys = turn(nn(normed, wk_ref[...]).T, cosine, sine).T
    pair_ref[:, 0:320] = keys.astype(BFLOAT)
    pair_ref[:, 320:640] = nn(normed, wv_ref[...]).astype(BFLOAT)
    queries = turn(nn(normed, wq_ref[...]).T, cosine, sine)
    query_ref[...] = (queries * (HEAD_DIM**-0.5)).astype(BFLOAT)


PROJECTED = (
    struct(BFLOAT, TOK_DEV, D),
    struct(BFLOAT, D, TOK_DEV),
    struct(BFLOAT, TOK_DEV, 640),
)


def enter_kernel(hidden_ref, gain_ref, *refs):
    project(hidden_ref[...], gain_ref[0:1, :], *refs)


def enter(hidden, gains, wq, wk, wv, cosine, sine):
    return pl.pallas_call(enter_kernel, out_shape=PROJECTED, compiler_params=params(24))(
        hidden, gains, wq, wk, wv, cosine, sine
    )


FF_BLOCK = 640
FF_STEPS = FF // FF_BLOCK


def block_kernel(
    more, att_ref, hidden_ref, sel_ref, gain_ref, router_ref, wo_ref, weight_ref, *refs
):
    proj_in, refs = (refs[:5], refs[5:]) if more else ((), refs)
    mixed_ref, input_ref, gate_ref, up_ref, inner_ref, branch_ref, logit_ref, new_ref = refs[:8]
    acc_ref = refs[-1]
    step = pl.program_id(0)

    @pl.when(step == 0)
    def first():
        mixed = hidden_ref[...] + nn(att_ref[...], wo_ref[...])
        mixed_ref[...] = mixed
        input_ref[...] = normalize(mixed, gain_ref[1:2, :]).astype(BFLOAT)
        acc_ref[...] = mixed

    rows = input_ref[...]
    gate = contract_cols(rows, weight_ref[0])
    up = contract_cols(rows, weight_ref[1])
    gate_ref[...] = gate
    up_ref[...] = up
    inner = (gate * jax.nn.sigmoid(gate) * up).astype(BFLOAT)
    inner_ref[...] = inner
    acc_ref[...] += nn(inner, weight_ref[2])

    @pl.when(step == FF_STEPS - 1)
    def last():
        hidden = hidden_ref[...]
        branch = acc_ref[...]
        branch_ref[...] = branch
        logit = jnp.sum(hidden * router_ref[...], axis=1, keepdims=True)
        logit_ref[...] = logit
        new = hidden + sel_ref[...] * jax.nn.sigmoid(logit) * (branch - hidden)
        new_ref[...] = new
        if more:
            project(new, gain_ref[0:1, :], *proj_in, *refs[8:11])


def block(att, hidden, sel, gains, router, wo, weights, projections):
    more = projections is not None
    proj_specs = [whole(D, D), whole(D, 320), whole(D, 320), whole(32, 128), whole(32, 128)]
    rows = pl.BlockSpec((TOK_DEV, FF_BLOCK), lambda i: (0, i))
    return pl.pallas_call(
        functools.partial(block_kernel, more),
        grid=(FF_STEPS,),
        in_specs=[
            whole(TOK_DEV, D),
            whole(TOK_DEV, D),
            whole(TOK_DEV, 1),
            whole(8, D),
            whole(1, D),
            whole(D, D),
            pl.BlockSpec((3, FF_BLOCK, D), lambda i: (0, i, 0)),
        ]
        + proj_specs * more,
        out_specs=[
            whole(TOK_DEV, D),
            whole(TOK_DEV, D),
            rows,
            rows,
            rows,
            whole(TOK_DEV, D),
            whole(TOK_DEV, 1),
            whole(TOK_DEV, D),
        ]
        + [whole(TOK_DEV, D), whole(D, TOK_DEV), whole(TOK_DEV, 640)] * more,
        out_shape=(
            struct(FLOAT, TOK_DEV, D),
            struct(BFLOAT, TOK_DEV, D),
            struct(FLOAT, TOK_DEV, FF),
            struct(FLOAT, TOK_DEV, FF),
            struct(BFLOAT, TOK_DEV, FF),
            struct(FLOAT, TOK_DEV, D),
            struct(FLOAT, TOK_DEV, 1),
            struct(FLOAT, TOK_DEV, D),
        )
        + (PROJECTED if more else ()),
        scratch_shapes=[pltpu.VMEM((TOK_DEV, D), FLOAT)],
        cost_estimate=pl.CostEstimate(
            flops=4_000_000_000, bytes_accessed=20_000_000, transcendentals=400_000
        ),
        compiler_params=params(32),
    )(att, hidden, sel, gains, router, wo, weights, *(projections if more else ()))


def block_back_kernel(
    new_ref, sel_ref, logit_ref, hidden_ref, branch_ref, mixed_ref, gain_ref, router_ref, wo_ref,
    gate_ref, up_ref, weight_ref,
    rows_ref, dgate_ref, dup_ref, in_ref, attn_ref, back_ref, small_ref, acc_ref
):
    step = pl.program_id(0)
    sigma = jax.nn.sigmoid(logit_ref[...])
    weight = sel_ref[...] * sigma

    @pl.when(step == 0)
    def first():
        rows_ref[...] = (weight * new_ref[...]).astype(BFLOAT)
        acc_ref[...] = jnp.zeros_like(acc_ref)

    inner = contract_cols(rows_ref[...], weight_ref[2])
    gate = gate_ref[...]
    shape = jax.nn.sigmoid(gate)
    dgate = (inner * up_ref[...] * shape * (1.0 + gate * (1.0 - shape))).astype(BFLOAT)
    dup = (inner * gate * shape).astype(BFLOAT)
    dgate_ref[...] = dgate
    dup_ref[...] = dup
    acc_ref[...] += nn(dgate, weight_ref[0]) + nn(dup, weight_ref[1])

    @pl.when(step == FF_STEPS - 1)
    def last():
        grad_new = new_ref[...]
        hidden = hidden_ref[...]
        grad_branch = weight * grad_new
        grad_weight = jnp.sum(grad_new * (branch_ref[...] - hidden), axis=1, keepdims=True)
        grad_logit = grad_weight * sel_ref[...] * sigma * (1.0 - sigma) + ROUTER_LOSS / TOK_DEV * (
            sigma - sel_ref[...]
        )
        grad_norm, gain_row = normalize_back(mixed_ref[...], gain_ref[1:2, :], acc_ref[...])
        grad_mixed = grad_branch + grad_norm
        in_ref[...] = grad_new - grad_branch + grad_logit * router_ref[...] + grad_mixed
        attn = grad_mixed.astype(BFLOAT)
        attn_ref[...] = attn
        back_ref[...] = contract_cols(attn, wo_ref[...]).astype(BFLOAT)
        small_ref[0:1, :] = gain_row
        small_ref[1:2, :] = jnp.sum(grad_logit * hidden, axis=0, keepdims=True)
        small_ref[2:8, :] = jnp.zeros((6, D), FLOAT)


def block_back(new, sel, logit, hidden, branch, mixed, gains, router, wo, gate, up, weights):
    rows = pl.BlockSpec((TOK_DEV, FF_BLOCK), lambda i: (0, i))
    full = whole(TOK_DEV, D)
    return pl.pallas_call(
        block_back_kernel,
        grid=(FF_STEPS,),
        in_specs=[
            full,
            whole(TOK_DEV, 1),
            whole(TOK_DEV, 1),
            full,
            full,
            full,
            whole(8, D),
            whole(1, D),
            whole(D, D),
            rows,
            rows,
            pl.BlockSpec((3, FF_BLOCK, D), lambda i: (0, i, 0)),
        ],
        out_specs=[full, rows, rows, full, full, full, whole(8, D)],
        out_shape=(
            struct(BFLOAT, TOK_DEV, D),
            struct(BFLOAT, TOK_DEV, FF),
            struct(BFLOAT, TOK_DEV, FF),
            struct(FLOAT, TOK_DEV, D),
            struct(BFLOAT, TOK_DEV, D),
            struct(BFLOAT, TOK_DEV, D),
            struct(FLOAT, 8, D),
        ),
        scratch_shapes=[pltpu.VMEM((TOK_DEV, D), FLOAT)],
        cost_estimate=pl.CostEstimate(
            flops=4_000_000_000, bytes_accessed=20_000_000, transcendentals=400_000
        ),
        compiler_params=params(32),
    )(new, sel, logit, hidden, branch, mixed, gains, router, wo, gate, up, weights)


def enter_back_kernel(
    in_ref, dq_ref, own_ref, hidden_ref, gain_ref, wq_ref, wk_ref, wv_ref, cos_ref, sin_ref,
    pair_ref, out_ref, small_ref
):
    keys = turn(own_ref[:, 0:320].T, cos_ref[...], -sin_ref[...]).T.astype(BFLOAT)
    values = own_ref[:, 320:640].astype(BFLOAT)
    pair_ref[:, 0:320] = keys
    pair_ref[:, 320:640] = values
    grad_normed = (
        contract_cols(dq_ref[...], wq_ref[...])
        + contract_cols(keys, wk_ref[...])
        + contract_cols(values, wv_ref[...])
    )
    grad_hidden, gain_row = normalize_back(hidden_ref[...], gain_ref[0:1, :], grad_normed)
    out_ref[...] = in_ref[...] + grad_hidden
    small_ref[...] = jnp.concatenate([gain_row, jnp.zeros((7, D), FLOAT)], axis=0)


def enter_back(grad_in, dq, own, hidden, gains, wq, wk, wv, cosine, sine):
    return pl.pallas_call(
        enter_back_kernel,
        out_shape=(
            struct(BFLOAT, TOK_DEV, 640),
            struct(FLOAT, TOK_DEV, D),
            struct(FLOAT, 8, D),
        ),
        compiler_params=params(24),
    )(grad_in, dq, own, hidden, gains, wq, wk, wv, cosine, sine)


HEAD_BLOCK = 512


def head_kernel(rows_ref, near_ref, final_ref, target_ref, table_ref, logit_ref, pick_ref, stat_ref):
    step = pl.program_id(0)

    @pl.when(step == 0)
    def first():
        hot = (rows_ref[...] == near_ref[...]).astype(FLOAT).astype(BFLOAT)
        pick_ref[...] = nn(hot, final_ref[...]).astype(BFLOAT)
        lane = lax.broadcasted_iota(jnp.int32, (256, 128), 1)
        stat_ref[...] = jnp.where(lane == 0, MASKED, 0.0)

    logits = contract_cols(pick_ref[...], table_ref[...])
    logit_ref[...] = logits
    place = step * HEAD_BLOCK + lax.broadcasted_iota(jnp.int32, (256, HEAD_BLOCK), 1)
    hit = jnp.sum(jnp.where(place == target_ref[...], logits, 0.0), axis=1, keepdims=True)
    old = stat_ref[:, 0:1]
    top = jnp.maximum(old, jnp.max(logits, axis=1, keepdims=True))
    total = stat_ref[:, 1:2] * jnp.exp(old - top) + jnp.sum(
        jnp.exp(logits - top), axis=1, keepdims=True
    )
    stat_ref[:, 1:2] = total
    stat_ref[:, 2:3] = stat_ref[:, 2:3] + hit
    stat_ref[:, 0:1] = top


def head(loss_rows, near_rows, final_rows, local_targets, table):
    return pl.pallas_call(
        head_kernel,
        grid=(VOCAB_MP // HEAD_BLOCK,),
        in_specs=[
            whole(256, 1),
            whole(1, ROWS),
            whole(ROWS, D),
            whole(256, 1),
            pl.BlockSpec((HEAD_BLOCK, D), lambda i: (i, 0)),
        ],
        out_specs=[
            pl.BlockSpec((256, HEAD_BLOCK), lambda i: (0, i)),
            whole(256, D),
            whole(256, 128),
        ],
        out_shape=(
            jax.ShapeDtypeStruct((256, VOCAB_MP), FLOAT),
            jax.ShapeDtypeStruct((256, D), BFLOAT),
            jax.ShapeDtypeStruct((256, 128), FLOAT),
        ),
        compiler_params=pltpu.CompilerParams(vmem_limit_bytes=32 * 1024 * 1024),
    )(loss_rows, near_rows, final_rows, local_targets, table)


def head_back_kernel(
    rows_ref, near_ref, target_ref, norm_ref, logit_ref, pick_ref, table_ref, grad_ref, out_ref, sum_ref
):
    step = pl.program_id(0)
    place = step * HEAD_BLOCK + lax.broadcasted_iota(jnp.int32, (256, HEAD_BLOCK), 1)
    probs = jnp.exp(logit_ref[...] - norm_ref[...])
    hit = jnp.where(place == target_ref[...], 1.0, 0.0)
    grads = ((probs - hit) * (1.0 / TOK_DEV)).astype(BFLOAT)
    grad_ref[...] = contract_rows(grads, pick_ref[...]).astype(BFLOAT)
    part = nn(grads, table_ref[...])

    @pl.when(step == 0)
    def first():
        sum_ref[...] = part

    @pl.when(step > 0)
    def later():
        sum_ref[...] += part

    @pl.when(step == pl.num_programs(0) - 1)
    def last():
        hot = (rows_ref[...] == near_ref[...]).astype(FLOAT).astype(BFLOAT)
        out_ref[...] = contract_rows(hot, sum_ref[...].astype(BFLOAT)).astype(BFLOAT)


def head_back(loss_rows, near_rows, local_targets, log_norm, logits, picked, table):
    return pl.pallas_call(
        head_back_kernel,
        grid=(VOCAB_MP // HEAD_BLOCK,),
        in_specs=[
            whole(256, 1),
            whole(1, ROWS),
            whole(256, 1),
            whole(256, 1),
            pl.BlockSpec((256, HEAD_BLOCK), lambda i: (0, i)),
            whole(256, D),
            pl.BlockSpec((HEAD_BLOCK, D), lambda i: (i, 0)),
        ],
        out_specs=[pl.BlockSpec((HEAD_BLOCK, D), lambda i: (i, 0)), whole(ROWS, D)],
        out_shape=(
            jax.ShapeDtypeStruct((VOCAB_MP, D), BFLOAT),
            jax.ShapeDtypeStruct((ROWS, D), BFLOAT),
        ),
        scratch_shapes=[pltpu.VMEM((256, D), FLOAT)],
        compiler_params=pltpu.CompilerParams(vmem_limit_bytes=32 * 1024 * 1024),
    )(loss_rows, near_rows, local_targets, log_norm, logits, picked, table)


def mlp_grad_kernel(added, which_ref, *refs):
    lefts, rights, refs = refs[0:3], refs[3:6], refs[6:]
    for i in range(3):
        total = contract_rows(lefts[i][...], rights[i][...]).reshape(8, 80, D)
        if added:
            total = total + refs[0][:, i].astype(FLOAT)
        refs[-1][:, i] = total.astype(BFLOAT)


def mlp_grads(which, lefts, rights, received=None):
    added = received is not None
    rows = lefts[0].shape[0]
    out_spec = pl.BlockSpec((8, 3, 80, D), lambda i, half: (i, 0, 0, 0))
    return pl.pallas_call(
        functools.partial(mlp_grad_kernel, added),
        grid_spec=pltpu.PrefetchScalarGridSpec(
            num_scalar_prefetch=1,
            grid=(2,),
            in_specs=[pl.BlockSpec((rows, 640), lambda i, half: (0, half[0] * 2 + i))] * 3
            + [pl.BlockSpec((rows, D), lambda i, half: (0, 0))] * 3
            + [out_spec] * added,
            out_specs=out_spec,
        ),
        out_shape=struct(BFLOAT, 16, 3, 80, D),
        compiler_params=params(40),
    )(which.reshape(1), *lefts, *rights, *([received] if added else []))


def pack_grad_kernel(
    starts_ref, normed_ref, dq_ref, dk_ref, dv_ref, att_ref, grad_ref, rows_ref, mine_ref, other_ref, buf
):
    buf[0:960, :] = contract_rows(normed_ref[...], dq_ref[...]).astype(BFLOAT)
    buf[1600:2560, :] = contract_rows(att_ref[...], grad_ref[...]).astype(BFLOAT)
    buf[2560:2576, :] = rows_ref[...].astype(BFLOAT)
    buf[2576:2688, :] = jnp.zeros((112, D), BFLOAT)
    line = lax.broadcasted_iota(jnp.int32, (960, 320), 0)
    place = lax.broadcasted_iota(jnp.int32, (960, 320), 1)
    for first, ref in ((960, dk_ref), (1280, dv_ref)):
        full = contract_rows(normed_ref[...], ref[...]).astype(BFLOAT)
        for i in range(3):
            chosen = (line == 3 * place + i).astype(FLOAT).astype(BFLOAT)
            buf[first : first + 320, 320 * i : 320 * i + 320] = contract_rows(chosen, full).astype(
                BFLOAT
            )
    for i in range(4):
        mine_ref[i] = buf[pl.ds(pl.multiple_of(starts_ref[i], 16), 352), :]
        other_ref[i] = buf[pl.ds(pl.multiple_of(starts_ref[4 + i], 16), 352), :]


def pack_grads(starts, *parts):
    side = jax.ShapeDtypeStruct((4, 352, D), BFLOAT)
    return pl.pallas_call(
        pack_grad_kernel,
        in_specs=[pl.BlockSpec(memory_space=pltpu.SMEM)]
        + [pl.BlockSpec(memory_space=pltpu.VMEM)] * len(parts),
        out_shape=(side, side),
        scratch_shapes=[pltpu.VMEM((PACK_PAD, D), BFLOAT)],
        compiler_params=pltpu.CompilerParams(vmem_limit_bytes=40 * 1024 * 1024),
    )(starts, *parts)


def adam_update(master, first, second, grad, clip):
    grad = grad * clip
    first_new = BETA_ONE * first + (1.0 - BETA_ONE) * grad
    second_new = BETA_TWO * second + (1.0 - BETA_TWO) * grad * grad
    corr_one = 1.0 - BETA_ONE**STEP
    corr_two = 1.0 - BETA_TWO**STEP
    master_new = master - LEARN_RATE * (
        first_new / corr_one / (jnp.sqrt(second_new / corr_two) + ADAM_EPS) + DECAY * master
    )
    return (master_new, first_new, second_new)


def pack_row(device):
    return (1283 * device) // 64


def join_kernel(blocks_ref, out_ref):
    step = pl.program_id(0)
    first = jnp.minimum((step * (128 * 64)) // 1283, 118)
    first = (first // 2) * 2
    window = blocks_ref[pl.ds(pl.multiple_of(first * 24, 48), 240), :]
    row = step * 128 + lax.broadcasted_iota(jnp.int32, (128, 240), 0)
    place = lax.broadcasted_iota(jnp.int32, (128, 240), 1)
    device = (place * 2731) >> 16
    source = ((1283 * (first + device)) >> 6) + place - 24 * device
    chosen = (source == row).astype(FLOAT).astype(BFLOAT)
    out_ref[...] = jnp.dot(chosen, window, preferred_element_type=FLOAT).astype(BFLOAT)


def join_pack(blocks):
    return pl.pallas_call(
        join_kernel,
        grid=(PACK_PAD // 128,),
        in_specs=[pl.BlockSpec((128 * 24, D), lambda i: (0, 0))],
        out_specs=pl.BlockSpec((128, D), lambda i: (i, 0)),
        out_shape=jax.ShapeDtypeStruct((PACK_PAD, D), BFLOAT),
        compiler_params=pltpu.CompilerParams(vmem_limit_bytes=32 * 1024 * 1024),
    )(blocks)


def stage(value, axis, index):
    total = lax.dynamic_index_in_dim(value, index, 0, False).astype(FLOAT)
    for k in (1, 2, 3):
        sent = lax.dynamic_index_in_dim(value, (index + k) % 4, 0, False)
        total = total + shift(sent, axis, k).astype(FLOAT)
    return total


def stage_near(value, axis):
    total = value[0].astype(FLOAT)
    for k in (1, 2, 3):
        total = total + shift(value[k], axis, -k).astype(FLOAT)
    return total


def shards(
    token_ids,
    targets,
    loss_rows,
    selections,
    boundary,
    pack_master,
    pack_first,
    pack_second,
    mlp_master,
    mlp_first,
    mlp_second,
    table_master,
    table_first,
    table_second,
):
    z = lax.axis_index("z")
    core = lax.axis_index("core")
    y = lax.axis_index("y")
    x = lax.axis_index("x")
    model_index = z * 2 + core
    data_index = y * 4 + x
    device = model_index * DP + data_index
    own_table = table_master.astype(BFLOAT)

    near = jnp.stack([((z + k) % 4) * 2 + (core ^ j) for j in (0, 1) for k in range(4)])
    near_rows = (near[:, None] * TOK_DEV + jnp.arange(TOK_DEV, dtype=jnp.int32)[None, :]).reshape(-1)

    pack_offset = PACK_DEV * device - D * pack_row(device)
    pack_block = lax.dynamic_update_slice(
        jnp.zeros((24 * D,), BFLOAT), pack_master.astype(BFLOAT), (pack_offset,)
    ).reshape(24, D)
    pack_blocks = lax.all_gather(pack_block, ALL_AXES, axis=0, tiled=True)
    mlp_own = mlp_master.astype(BFLOAT)
    mlp_quad = jnp.concatenate([mlp_own] + [shift(mlp_own, "z", k) for k in (1, 2, 3)], axis=1)
    mlp_blocks = lax.all_gather(mlp_quad.reshape(3 * 80, D), ("core", "y", "x"), axis=0, tiled=True)
    table = lax.all_gather(own_table, DP_AXES, axis=0, tiled=True)

    group_ids = token_ids[0]
    near_ids = reorder(group_ids.reshape(MP, TOK_DEV), near).reshape(-1)
    local_ids = near_ids - model_index * VOCAB_MP
    inside = (local_ids >= 0) & (local_ids < VOCAB_MP)
    high = local_ids >> 7
    low = local_ids & 127
    high_hot = (high[:, None] == jnp.arange(48)[None, :]).astype(BFLOAT)
    low_hot = (low[:, None] == jnp.arange(128)[None, :]).astype(BFLOAT)
    present = (contract_rows(high_hot, low_hot) > 0).reshape(DP, VOCAB_DEV)
    before = (jnp.arange(VOCAB_DEV)[:, None] < jnp.arange(VOCAB_DEV)[None, :]).astype(BFLOAT)
    slots = mm(present.astype(BFLOAT), before)
    asked = present & (slots < CAP)
    over = jnp.max(jnp.where(present & (slots >= CAP), 1.0, 0.0))
    over = sum_all(jnp.full((1, 128), over, FLOAT))[0, 0] > 0
    slot_table = jnp.where(asked, slots, 255.0).reshape(48, 128).astype(BFLOAT)
    token_slot = jnp.sum(mm(high_hot, slot_table) * low_hot.astype(FLOAT), axis=-1)
    token_place = jnp.where(
        inside & (token_slot < CAP), (high // 3) * CAP + token_slot.astype(jnp.int32), -1
    )
    place_hot = (token_place[:, None] == jnp.arange(DP * CAP)[None, :]).astype(BFLOAT)
    match = asked[:, None, :] & (slots[:, None, :] == jnp.arange(CAP, dtype=FLOAT)[None, :, None])
    request = (
        jnp.sum(jnp.where(match, jnp.arange(1, VOCAB_DEV + 1, dtype=FLOAT)[None, None, :], 0.0), axis=-1)
        - 1.0
    )
    request = lax.all_to_all(request, DP_AXES, 0, 0, tiled=True)
    owner_hot = (
        request.reshape(-1)[:, None] == jnp.arange(VOCAB_DEV, dtype=FLOAT)[None, :]
    ).astype(BFLOAT)
    sent_rows = mm(owner_hot, own_table).astype(BFLOAT)
    asked_rows = lax.all_to_all(sent_rows, DP_AXES, 0, 0, tiled=True)

    def looked_sparse():
        return mm(place_hot, asked_rows).astype(BFLOAT)

    def looked_dense():
        full = lax.all_gather(own_table, DP_AXES, axis=0, tiled=True)
        rows = jnp.take(full, jnp.clip(local_ids, 0, VOCAB_MP - 1), axis=0)
        return jnp.where(inside[:, None], rows, jnp.zeros_like(rows))

    asked_rows, pack_blocks = tie(asked_rows, pack_blocks)
    looked = lax.cond(over, looked_dense, looked_sparse)
    hidden = scatter_group(looked.reshape(2, 4, TOK_DEV, D), FLOAT)

    pack_weights = join_pack(pack_blocks)
    w_query = pack_weights[:960]
    w_key = pack_weights[960:1280].reshape(D, KV_HEADS * HEAD_DIM)
    w_value = pack_weights[1280:1600].reshape(D, KV_HEADS * HEAD_DIM)
    w_out = pack_weights[1600:2560]
    gains = jnp.concatenate([pack_weights[2560:2563].astype(FLOAT), jnp.zeros((5, D), FLOAT)])
    router = pack_weights[2563:2566].astype(FLOAT)
    mlp_weights = mlp_blocks.reshape(32, 3, 80, D).transpose(1, 0, 2, 3).reshape(3, FF, D)

    half_dim = HEAD_DIM // 2
    freqs = ROPE_BASE ** (-jnp.arange(half_dim, dtype=FLOAT) / half_dim)
    first_row = data_index * ROWS + model_index * TOK_DEV
    angles = freqs[:, None] * (first_row + jnp.arange(TOK_DEV, dtype=jnp.int32)).astype(FLOAT)[None, :]
    turns = (jnp.cos(angles), jnp.sin(angles))
    projections = (w_query, w_key, w_value) + turns
    group_sel = selections.reshape(RECUR, DP, MP, TOK_DEV)
    prev_index = jnp.maximum(data_index - 1, 0)
    here_sel = lax.dynamic_index_in_dim(group_sel, data_index, 1, False)
    own_sel = lax.dynamic_index_in_dim(here_sel, model_index, 1, False)
    near_sel = reorder(here_sel, near).reshape(RECUR, ROWS)
    prev_sel = reorder(lax.dynamic_index_in_dim(group_sel, prev_index, 1, False), near)
    prev_sel = prev_sel.reshape(RECUR, ROWS)
    start = lax.dynamic_index_in_dim(boundary, data_index, 0, False)
    prev_start = lax.dynamic_index_in_dim(boundary, prev_index, 0, False)
    place = (model_index * TOK_DEV + jnp.arange(TOK_DEV, dtype=jnp.int32))[None, None, :]
    key_place = near_rows[None, :, None]
    own_seen = (
        (key_place <= place)
        & ((key_place < start) == (place < start))
        & ((near_sel[:, :, None] > 0) | (key_place == place))
    )
    prev_seen = (
        (data_index > 0) & (place < start) & (key_place >= prev_start) & (prev_sel[:, :, None] > 0)
    )
    biases = jnp.concatenate(
        [prev_seen[:, :512], own_seen[:, :512], prev_seen[:, 512:], own_seen[:, 512:]], axis=1
    )
    biases = jnp.where(biases, 0.0, MASKED)

    sel_cols = own_sel.astype(FLOAT)[:, :, None]
    saves = []
    logits_all = []
    normed, queries, pair = enter(hidden, gains, *projections)
    for step in range(RECUR):
        pairs = group_gather(pair)
        attended, log_total = attend(queries, pairs, biases[step])
        mixed, mlp_input, gate, up, inner, branch, logit, new_hidden, *nexts = block(
            attended,
            hidden,
            sel_cols[step],
            gains,
            router[step : step + 1],
            w_out,
            mlp_weights,
            projections if step < RECUR - 1 else None,
        )
        logits_all.append(logit[:, 0])
        saves.append(
            (
                hidden,
                normed,
                queries,
                pairs,
                attended,
                log_total,
                mixed,
                mlp_input,
                gate,
                up,
                inner,
                branch,
                logit,
            )
        )
        hidden = new_hidden
        if nexts:
            normed, queries, pair = nexts
    logits_all = jnp.stack(logits_all)
    penalty_total = jnp.sum(jax.nn.softplus(logits_all) - own_sel.astype(FLOAT) * logits_all)

    normed_final = rms_scale(hidden, gains[2]).astype(BFLOAT)
    final_rows = gather_group(normed_final).reshape(ROWS, D)
    row_targets = lax.dynamic_index_in_dim(targets, data_index, 0, keepdims=False)
    head_args = (loss_rows[0][:, None], near_rows[None, :])
    local_targets = (row_targets - model_index * VOCAB_MP)[:, None]
    logits, picked, stats = head(*head_args, final_rows, local_targets, table)
    stats = stats[:, :3].T

    def join_stats(parts):
        top = parts[0][0]
        for part in parts[1:]:
            top = jnp.maximum(top, part[0])
        total = sum(part[1] * jnp.exp(part[0] - top) for part in parts)
        return jnp.stack([top, total, sum(part[2] for part in parts)])

    stats = join_stats([stats, swap(stats)])
    stats = join_stats([stats] + [shift(stats, "z", k) for k in (1, 2, 3)])
    log_norm = stats[0] + jnp.log(stats[1])
    cross = log_norm - stats[2]
    per_device = cross.shape[0] // MP
    loss_part = (
        jnp.sum(lax.dynamic_slice_in_dim(cross, model_index * per_device, per_device))
        + ROUTER_LOSS * penalty_total
    )
    head_grad, scattered = head_back(
        *head_args, local_targets, log_norm[:, None], logits, picked, table
    )
    grad_final = scatter_group(scattered.reshape(2, 4, TOK_DEV, D), FLOAT)
    grad_hidden, grad_gain_final = rms_back(hidden, gains[2], grad_final)
    head_grad = lax.psum_scatter(head_grad, DP_AXES, scatter_dimension=0, tiled=True)

    kept = []
    mlp_parts = []
    router_rows = [None] * RECUR
    gain_one = jnp.zeros((1, D), FLOAT)
    gain_two = jnp.zeros((1, D), FLOAT)
    for step in reversed(range(RECUR)):
        (
            hidden_in,
            normed,
            queries,
            pairs,
            attended,
            log_total,
            mixed,
            mlp_input,
            gate,
            up,
            inner,
            branch,
            logit,
        ) = saves[step]
        grad_rows, grad_gate, grad_up, grad_in, grad_attn, grad_attended, small = block_back(
            grad_hidden,
            sel_cols[step],
            logit,
            hidden_in,
            branch,
            mixed,
            gains,
            router[step : step + 1],
            w_out,
            gate,
            up,
            mlp_weights,
        )
        gain_two = gain_two + small[0:1]
        router_rows[step] = small[1:2]
        mlp_parts.append((grad_gate, grad_up, inner, mlp_input, mlp_input, grad_rows))
        if step == 0:
            mlp_kept = [jnp.concatenate(parts, axis=0) for parts in zip(*mlp_parts)]
            far = mlp_grads(1 - core, mlp_kept[:3], mlp_kept[3:])
            far, grad_attended, head_grad = tie(by_rows(far), grad_attended, head_grad)
            far = by_rows(swap(far))
        grad_query, *grad_sides = attend_back(
            queries, pairs, biases[step], log_total, attended, grad_attended, *turns
        )
        if step == 0:
            far, *grad_sides = tie(far, *grad_sides)
            mlp_half = mlp_grads(core, mlp_kept[:3], mlp_kept[3:], far)
            mlp_sum = lax.psum_scatter(
                mlp_half.reshape(16 * 240, D), DP_AXES, scatter_dimension=0, tiled=True
            )
        grad_own = group_scatter(*grad_sides)
        grad_pair, grad_hidden, small = enter_back(
            grad_in, grad_query, grad_own, hidden_in, gains, *projections
        )
        gain_one = gain_one + small[0:1]
        kept.append((normed, grad_query, grad_pair, attended, grad_attn))
    normed_all, grad_query_all, grad_pair_all, attended_all, grad_attn_all = [
        jnp.concatenate(parts, axis=0) for parts in zip(*kept)
    ]

    def aligned_row(which):
        return (pack_row(which) // 16) * 16

    small = jnp.concatenate(
        [
            gain_one,
            gain_two,
            grad_gain_final[None],
            *router_rows,
            jnp.zeros((10, D), FLOAT),
        ]
    )
    starts = jnp.stack(
        [aligned_row(DP * (2 * i + c)) for c in (core, 1 - core) for i in range(4)]
    ).astype(jnp.int32)
    mine, other = pack_grads(
        starts,
        normed_all,
        grad_query_all,
        grad_pair_all[:, :320],
        grad_pair_all[:, 320:],
        attended_all,
        grad_attn_all,
        small,
    )
    half = (mine.astype(FLOAT) + swap(other).astype(FLOAT)).astype(BFLOAT)

    def y_windows(value):
        return jnp.stack([value[..., 80 * i : 80 * i + 112, :] for i in range(4)])

    def x_windows(value):
        return jnp.stack([value[..., i : i + 48, :] for i in (0, 16, 40, 56)])

    part = stage(half, "z", z).astype(BFLOAT)
    part = stage(y_windows(part), "y", y).astype(BFLOAT)
    part = stage(x_windows(part), "x", x).reshape(-1)
    begin = aligned_row(DP * model_index) + 80 * y + (20 * x) // 8 * 8
    pack_grad = lax.dynamic_slice(part, (PACK_DEV * device - D * begin,), (PACK_DEV,))

    grad_embed = gather_group(grad_hidden.astype(BFLOAT)).reshape(ROWS, D)

    unique = contract_rows(place_hot, grad_embed).astype(BFLOAT)
    unique = lax.all_to_all(unique, DP_AXES, 0, 0, tiled=True)

    sparse = contract_rows(owner_hot, unique)

    mlp_sum = mlp_sum.reshape(3, 4, UNITS, D).transpose(1, 0, 2, 3)
    mlp_grad = stage_near(mlp_sum, "z")

    def embed_dense():
        kept_rows = grad_embed.astype(FLOAT) * inside.astype(FLOAT)[:, None]
        sums = jax.ops.segment_sum(
            kept_rows, jnp.clip(local_ids, 0, VOCAB_MP - 1), num_segments=VOCAB_MP
        )
        return lax.psum_scatter(
            sums.astype(BFLOAT), DP_AXES, scatter_dimension=0, tiled=True
        ).astype(FLOAT)

    sparse, mlp_grad, pack_grad = tie(sparse, mlp_grad, pack_grad)
    table_grad = head_grad.astype(FLOAT) + lax.cond(over, embed_dense, lambda: sparse)
    table_grad = by_cols(table_grad)

    squares = (
        jnp.sum(pack_grad * pack_grad)
        + jnp.sum(mlp_grad * mlp_grad)
        + jnp.sum(table_grad * table_grad)
    )
    lane = lax.broadcasted_iota(jnp.int32, (1, 128), 1)
    sums = sum_all(jnp.where(lane == 0, squares, loss_part))
    total_squares = sums[0, 0]
    loss_sum = sums[0, 1]
    grad_norm = jnp.sqrt(total_squares)
    clip = CLIP_NORM / jnp.maximum(grad_norm, CLIP_NORM)
    pack_new, pack_first_new, pack_second_new = adam_update(
        pack_master, pack_first, pack_second, pack_grad, clip
    )
    mlp_new, mlp_first_new, mlp_second_new = adam_update(
        mlp_master, mlp_first, mlp_second, mlp_grad, clip
    )
    table_new, table_first_new, table_second_new = adam_update(
        table_master, table_first, table_second, table_grad, clip
    )
    return (
        pack_new,
        pack_first_new,
        pack_second_new,
        mlp_new,
        mlp_first_new,
        mlp_second_new,
        table_new,
        table_first_new,
        table_second_new,
        loss_sum,
        grad_norm,
    )


def solution(mesh):
    grid = Mesh(mesh.devices.reshape(4, 2, 4, 4), ALL_AXES)
    owners = (P(ALL_AXES), P(None, ALL_AXES, None), P(ALL_AXES, None))
    group = P(DP_AXES, None)
    masters = tuple(spec for spec in owners for _ in range(3))
    return jax.shard_map(
        shards,
        mesh=grid,
        in_specs=(group, P(), group, P(), P()) + masters,
        out_specs=masters + (P(), P()),
        check_vma=False,
    )
```

```python
import functools

import jax
import jax.numpy as jnp
from jax import lax
from jax.experimental import pallas as pl
from jax.experimental.layout import Layout, with_layout_constraint
from jax.experimental.pallas import tpu as pltpu
from jax.sharding import Mesh
from jax.sharding import PartitionSpec as P

D = 960
HEADS = 15
KV_HEADS = 5
HEAD_DIM = 64
FF = 2560
RECUR = 3
STEP = 10
TOK_DEV = 128
ROWS = 1024
MP = 8
DP = 16
VOCAB_MP = 6144
VOCAB_DEV = 384
UNITS = 20
PACK_DEV = 19245
PACK_ROWS = 2566
PACK_PAD = 2688
CAP = 24

EPS_NORM = 1e-05
ROPE_BASE = 10000.0
ROUTER_LOSS = 0.1
CLIP_NORM = 1.0
LEARN_RATE = 0.05
BETA_ONE = 0.9
BETA_TWO = 0.95
ADAM_EPS = 1e-08
DECAY = 0.1
MASKED = -1e30
HIGHEST = lax.Precision.HIGHEST
BFLOAT = jnp.bfloat16
FLOAT = jnp.float32
DP_AXES = ("y", "x")
ALL_AXES = ("z", "core", "y", "x")


def shift(value, axis, steps):
    return lax.ppermute(value, axis, [(i, (i + steps) % 4) for i in range(4)])


def swap(value):
    return lax.ppermute(value, "core", [(0, 1), (1, 0)])


def gather_group(value):
    near = by_rows(jnp.concatenate([value] + [shift(value, "z", -k) for k in (1, 2, 3)], axis=0))
    return near, by_rows(swap(near))


def scatter_group(near, far):
    half = (near.astype(FLOAT) + by_rows(swap(by_rows(far))).astype(FLOAT)).astype(BFLOAT)
    half = half.reshape(4, TOK_DEV, -1)
    total = half[0].astype(FLOAT)
    for k in (1, 2, 3):
        total = total + shift(half[k], "z", k).astype(FLOAT)
    return total


def sum_all(value):
    value = value + swap(value)
    for axis in ("z", "y", "x"):
        value = value + shift(value, axis, 1) + shift(value, axis, 2) + shift(value, axis, 3)
    return value


def rms_scale(values, weight):
    return values * lax.rsqrt(jnp.mean(values * values, axis=-1, keepdims=True) + EPS_NORM) * weight


def rms_back(values, weight, grad_out):
    inverse = lax.rsqrt(jnp.mean(values * values, axis=-1, keepdims=True) + EPS_NORM)
    weighted = grad_out * weight
    grad_values = inverse * weighted - values * (inverse * inverse * inverse) * jnp.mean(
        weighted * values, axis=-1, keepdims=True
    )
    return (grad_values, jnp.sum(grad_out * values * inverse, axis=0))


def mm(left, right):
    return jnp.dot(left, right, preferred_element_type=FLOAT)


def contract_rows(left, right):
    return lax.dot_general(left, right, (((0,), (0,)), ((), ())), preferred_element_type=FLOAT)


def contract_cols(left, right):
    return lax.dot_general(left, right, (((1,), (1,)), ((), ())), preferred_element_type=FLOAT)


def reorder(blocks, order):
    hit = order[:, None] == jnp.arange(MP)[None, :]
    return jnp.sum(jnp.where(hit[:, :, None], blocks[..., None, :, :], 0), axis=-2)


def by_rows(value):
    return with_layout_constraint(value, Layout(tuple(range(value.ndim))))


def by_cols(value):
    return with_layout_constraint(value, Layout((1, 0)))


def tie(*values):
    return lax.optimization_barrier(values)


def group_gather(pair):
    own = [pair]
    for k in (1, 2, 3):
        own.append(lax.ppermute(pair, "z", [((i + k) % 4, i) for i in range(4) if (i + k) % 4 < i]))
    prev = []
    for k in range(4):
        pairs = []
        for i in range(3):
            for g in range(1, DP):
                pairs.append((((i + k) % 4) * DP + g - 1, i * DP + g))
        prev.append(lax.ppermute(pair, ("z",) + DP_AXES, pairs))
    own = jnp.concatenate(own, axis=0)
    prev = jnp.concatenate(prev, axis=0)
    return prev, own, swap(prev), swap(own)


def group_scatter(prev, own, prev_far, own_far):
    own = (own.astype(FLOAT) + swap(own_far).astype(FLOAT)).astype(BFLOAT).reshape(4, TOK_DEV, -1)
    prev = (prev.astype(FLOAT) + swap(prev_far).astype(FLOAT)).astype(BFLOAT).reshape(4, TOK_DEV, -1)
    total = own[0].astype(FLOAT)
    for k in (1, 2, 3):
        pairs = [(i, (i + k) % 4) for i in range(4) if (i + k) % 4 < i]
        total = total + lax.ppermute(own[k], "z", pairs).astype(FLOAT)
    for k in range(4):
        pairs = []
        for i in range(3):
            for g in range(1, DP):
                pairs.append((i * DP + g, ((i + k) % 4) * DP + g - 1))
        total = total + lax.ppermute(prev[k], ("z",) + DP_AXES, pairs).astype(FLOAT)
    return total


def nn(left, right):
    return jnp.dot(left, right, preferred_element_type=FLOAT)


def head_rows(ref, head):
    return jnp.concatenate(
        [ref[:, 64 * (3 * head + i) : 64 * (3 * head + i) + 64] for i in range(3)], axis=0
    )


def head_lanes(ref, head):
    return jnp.concatenate(
        [ref[64 * (3 * head + i) : 64 * (3 * head + i) + 64, :] for i in range(3)], axis=1
    )


def turn(value, cosine, sine):
    parts = []
    for head in range(value.shape[0] // 64):
        first = value[64 * head : 64 * head + 32]
        second = value[64 * head + 32 : 64 * head + 64]
        parts.append(first * cosine - second * sine)
        parts.append(second * cosine + first * sine)
    return jnp.concatenate(parts, axis=0)


def normalize(values, weight):
    return values * lax.rsqrt(jnp.mean(values * values, axis=-1, keepdims=True) + EPS_NORM) * weight


def normalize_back(values, weight, grad_out):
    inverse = lax.rsqrt(jnp.mean(values * values, axis=-1, keepdims=True) + EPS_NORM)
    weighted = grad_out * weight
    grad_values = inverse * weighted - values * (inverse * inverse * inverse) * jnp.mean(
        weighted * values, axis=-1, keepdims=True
    )
    return grad_values, jnp.sum(grad_out * values * inverse, axis=0, keepdims=True)


def attend_kernel(query_ref, kv0, kv1, kv2, kv3, bias_ref, out_ref, log_ref):
    for head in range(KV_HEADS):
        queries = head_lanes(query_ref, head)
        top = None
        for part, kv_ref in enumerate((kv0, kv1, kv2, kv3)):
            keys = kv_ref[:, 64 * head : 64 * head + 64]
            values = kv_ref[:, 320 + 64 * head : 320 + 64 * head + 64]
            bias = bias_ref[512 * part : 512 * part + 512, :]
            scores = nn(keys, queries) + jnp.concatenate([bias, bias, bias], axis=1)
            part_top = jnp.max(scores, axis=0, keepdims=True)
            new_top = part_top if top is None else jnp.maximum(top, part_top)
            expo = jnp.exp(scores - new_top)
            part_total = jnp.sum(expo, axis=0, keepdims=True)
            part_out = contract_rows(values, expo.astype(BFLOAT))
            if top is None:
                total, out = part_total, part_out
            else:
                shrink = jnp.exp(top - new_top)
                total, out = total * shrink + part_total, out * shrink + part_out
            top = new_top
        out = (out / total).T.astype(BFLOAT)
        for i in range(3):
            place = 64 * (3 * head + i)
            out_ref[:, place : place + 64] = out[128 * i : 128 * i + 128]
        log_ref[head : head + 1, :] = top + jnp.log(total)


def params(mib):
    return pltpu.CompilerParams(vmem_limit_bytes=mib * 1024 * 1024)


def whole(*shape):
    return pl.BlockSpec(shape, lambda i: (0,) * len(shape))


def struct(kind, *shape):
    return jax.ShapeDtypeStruct(shape, kind)


def attend(queries, pairs, bias):
    return pl.pallas_call(
        attend_kernel,
        out_shape=(struct(BFLOAT, TOK_DEV, D), struct(FLOAT, 8, 3 * TOK_DEV)),
        cost_estimate=pl.CostEstimate(
            flops=12_000_000_000, bytes_accessed=5_000_000, transcendentals=4_000_000
        ),
        compiler_params=params(24),
    )(queries, *pairs, bias)


def attend_back_kernel(
    query_ref, kv0, kv1, kv2, kv3, bias_ref, log_ref, att_ref, grad_ref, cos_ref, sin_ref,
    dq_ref, d0, d1, d2, d3
):
    cosine = jnp.concatenate([cos_ref[...]] * 3, axis=1)
    sine = jnp.concatenate([sin_ref[...]] * 3, axis=1)
    for head in range(KV_HEADS):
        queries = head_lanes(query_ref, head)
        grads = head_rows(grad_ref, head)
        outs = head_rows(att_ref, head)
        delta = jnp.sum((grads.astype(FLOAT) * outs.astype(FLOAT)).T, axis=0, keepdims=True)
        log_total = log_ref[head : head + 1, :]
        back = None
        for part, (kv_ref, d_ref) in enumerate(((kv0, d0), (kv1, d1), (kv2, d2), (kv3, d3))):
            keys = kv_ref[:, 64 * head : 64 * head + 64]
            values = kv_ref[:, 320 + 64 * head : 320 + 64 * head + 64]
            bias = bias_ref[512 * part : 512 * part + 512, :]
            probs = jnp.exp(
                nn(keys, queries) + jnp.concatenate([bias, bias, bias], axis=1) - log_total
            )
            grad_scores = (probs * (contract_cols(values, grads) - delta)).astype(BFLOAT)
            d_ref[:, 64 * head : 64 * head + 64] = contract_cols(grad_scores, queries).astype(BFLOAT)
            d_ref[:, 320 + 64 * head : 320 + 64 * head + 64] = nn(
                probs.astype(BFLOAT), grads
            ).astype(BFLOAT)
            part_back = contract_rows(keys, grad_scores)
            back = part_back if back is None else back + part_back
        back = turn(back * (HEAD_DIM**-0.5), cosine, -sine).T.astype(BFLOAT)
        for i in range(3):
            place = 64 * (3 * head + i)
            dq_ref[:, place : place + 64] = back[128 * i : 128 * i + 128]


def attend_back(queries, pairs, bias, log_total, attended, grads, cosine, sine):
    side = struct(BFLOAT, 4 * TOK_DEV, 640)
    return pl.pallas_call(
        attend_back_kernel,
        out_shape=(struct(BFLOAT, TOK_DEV, D), side, side, side, side),
        cost_estimate=pl.CostEstimate(
            flops=20_000_000_000, bytes_accessed=9_000_000, transcendentals=4_000_000
        ),
        compiler_params=params(24),
    )(queries, *pairs, bias, log_total, attended, grads, cosine, sine)


def project(hidden, gain, wq_ref, wk_ref, wv_ref, cos_ref, sin_ref, normed_ref, query_ref, pair_ref):
    normed = normalize(hidden, gain).astype(BFLOAT)
    normed_ref[...] = normed
    cosine, sine = cos_ref[...], sin_ref[...]
    keys = turn(nn(normed, wk_ref[...]).T, cosine, sine).T
    pair_ref[:, 0:320] = keys.astype(BFLOAT)
    pair_ref[:, 320:640] = nn(normed, wv_ref[...]).astype(BFLOAT)
    queries = turn(nn(normed, wq_ref[...]).T, cosine, sine)
    query_ref[...] = (queries * (HEAD_DIM**-0.5)).astype(BFLOAT)


PROJECTED = (
    struct(BFLOAT, TOK_DEV, D),
    struct(BFLOAT, D, TOK_DEV),
    struct(BFLOAT, TOK_DEV, 640),
)


def spread_kernel(place_ref, rows_ref, near_ref, far_ref):
    place = lax.broadcasted_iota(jnp.int32, (512, DP * CAP), 1)
    for part, ref in enumerate((near_ref, far_ref)):
        hot = (place_ref[512 * part : 512 * part + 512, :] == place).astype(FLOAT).astype(BFLOAT)
        ref[...] = nn(hot, rows_ref[...]).astype(BFLOAT)


def spread(place, rows):
    return pl.pallas_call(
        spread_kernel,
        out_shape=(struct(BFLOAT, 512, D), struct(BFLOAT, 512, D)),
        compiler_params=params(24),
    )(place, rows)


def collect_kernel(place_ref, near_ref, far_ref, out_ref):
    place = lax.broadcasted_iota(jnp.int32, (512, DP * CAP), 1)
    total = None
    for part, ref in enumerate((near_ref, far_ref)):
        hot = (place_ref[512 * part : 512 * part + 512, :] == place).astype(FLOAT).astype(BFLOAT)
        sums = contract_rows(hot, ref[...])
        total = sums if total is None else total + sums
    out_ref[...] = total.astype(BFLOAT)


def collect(place, near, far):
    return pl.pallas_call(
        collect_kernel, out_shape=struct(BFLOAT, DP * CAP, D), compiler_params=params(24)
    )(place, near, far)


def enter_kernel(hidden_ref, gain_ref, *refs):
    project(hidden_ref[...], gain_ref[0:1, :], *refs)


def enter(hidden, gains, wq, wk, wv, cosine, sine):
    return pl.pallas_call(enter_kernel, out_shape=PROJECTED, compiler_params=params(24))(
        hidden, gains, wq, wk, wv, cosine, sine
    )


BIG = 56
FF_BLOCK = 640
FF_STEPS = FF // FF_BLOCK


def weight(ref, which):
    return ref[:, which].reshape(FF_BLOCK, D)


def block_kernel(
    more, att_ref, hidden_ref, sel_ref, gain_ref, router_ref, wo_ref, weight_ref, *refs
):
    proj_in, refs = (refs[:5], refs[5:]) if more else ((), refs)
    mixed_ref, input_ref, gate_ref, up_ref, inner_ref, branch_ref, logit_ref, new_ref = refs[:8]
    proj_out, refs = (refs[8:11], refs[11:]) if more else ((), refs[8:])
    acc_ref = refs[0]
    step = pl.program_id(0)
    copies = [
        pltpu.make_async_copy(source, target, refs[4].at[i])
        for i, (source, target) in enumerate(zip(proj_in[:3], refs[1:4]))
    ]

    @pl.when(step == 0)
    def first():
        for copy in copies:
            copy.start()
        mixed = hidden_ref[...] + nn(att_ref[...], wo_ref[...])
        mixed_ref[...] = mixed
        input_ref[...] = normalize(mixed, gain_ref[1:2, :]).astype(BFLOAT)
        acc_ref[...] = mixed

    rows = input_ref[...]
    gate = contract_cols(rows, weight(weight_ref, 0))
    up = contract_cols(rows, weight(weight_ref, 1))
    gate_ref[...] = gate
    up_ref[...] = up
    inner = (gate * jax.nn.sigmoid(gate) * up).astype(BFLOAT)
    inner_ref[...] = inner
    acc_ref[...] += nn(inner, weight(weight_ref, 2))

    @pl.when(step == FF_STEPS - 1)
    def last():
        hidden = hidden_ref[...]
        branch = acc_ref[...]
        branch_ref[...] = branch
        logit = jnp.sum(hidden * router_ref[...], axis=1, keepdims=True)
        logit_ref[...] = logit
        new = hidden + sel_ref[...] * jax.nn.sigmoid(logit) * (branch - hidden)
        new_ref[...] = new
        for copy in copies:
            copy.wait()
        if more:
            project(new, gain_ref[0:1, :], *refs[1:4], *proj_in[3:], *proj_out)


WEIGHT_SPEC = pl.BlockSpec((FF_BLOCK // 80, 3, 80, D), lambda i: (i, 0, 0, 0))


def block(att, hidden, sel, gains, router, wo, weights, projections):
    more = projections is not None
    proj_specs = [pl.BlockSpec(memory_space=pl.ANY)] * 3 + [whole(32, 128), whole(32, 128)]
    rows = pl.BlockSpec((TOK_DEV, FF_BLOCK), lambda i: (0, i))
    return pl.pallas_call(
        functools.partial(block_kernel, more),
        grid=(FF_STEPS,),
        in_specs=[
            whole(TOK_DEV, D),
            whole(TOK_DEV, D),
            whole(TOK_DEV, 1),
            whole(8, D),
            whole(1, D),
            whole(D, D),
            WEIGHT_SPEC,
        ]
        + proj_specs * more,
        out_specs=[
            whole(TOK_DEV, D),
            whole(TOK_DEV, D),
            rows,
            rows,
            rows,
            whole(TOK_DEV, D),
            whole(TOK_DEV, 1),
            whole(TOK_DEV, D),
        ]
        + [whole(TOK_DEV, D), whole(D, TOK_DEV), whole(TOK_DEV, 640)] * more,
        out_shape=(
            struct(FLOAT, TOK_DEV, D),
            struct(BFLOAT, TOK_DEV, D),
            struct(FLOAT, TOK_DEV, FF),
            struct(FLOAT, TOK_DEV, FF),
            struct(BFLOAT, TOK_DEV, FF),
            struct(FLOAT, TOK_DEV, D),
            struct(FLOAT, TOK_DEV, 1),
            struct(FLOAT, TOK_DEV, D),
        )
        + (PROJECTED if more else ()),
        scratch_shapes=[pltpu.VMEM((TOK_DEV, D), FLOAT)]
        + [
            pltpu.VMEM((D, D), BFLOAT),
            pltpu.VMEM((D, 320), BFLOAT),
            pltpu.VMEM((D, 320), BFLOAT),
            pltpu.SemaphoreType.DMA((3,)),
        ]
        * more,
        cost_estimate=pl.CostEstimate(
            flops=4_000_000_000, bytes_accessed=20_000_000, transcendentals=400_000
        ),
        compiler_params=params(BIG),
    )(att, hidden, sel, gains, router, wo, weights, *(projections if more else ()))


def block_back_kernel(
    new_ref, sel_ref, logit_ref, hidden_ref, branch_ref, mixed_ref, gain_ref, router_ref, wo_ref,
    gate_ref, up_ref, weight_ref,
    rows_ref, dgate_ref, dup_ref, in_ref, attn_ref, back_ref, small_ref, acc_ref, held_ref, sem
):
    step = pl.program_id(0)
    sigma = jax.nn.sigmoid(logit_ref[...])
    chosen = sel_ref[...] * sigma
    copy = pltpu.make_async_copy(wo_ref, held_ref, sem)

    @pl.when(step == 0)
    def first():
        copy.start()
        rows_ref[...] = (chosen * new_ref[...]).astype(BFLOAT)
        acc_ref[...] = jnp.zeros_like(acc_ref)

    inner = contract_cols(rows_ref[...], weight(weight_ref, 2))
    gate = gate_ref[...]
    shape = jax.nn.sigmoid(gate)
    dgate = (inner * up_ref[...] * shape * (1.0 + gate * (1.0 - shape))).astype(BFLOAT)
    dup = (inner * gate * shape).astype(BFLOAT)
    dgate_ref[...] = dgate
    dup_ref[...] = dup
    acc_ref[...] += nn(dgate, weight(weight_ref, 0)) + nn(dup, weight(weight_ref, 1))

    @pl.when(step == FF_STEPS - 1)
    def last():
        grad_new = new_ref[...]
        hidden = hidden_ref[...]
        grad_branch = chosen * grad_new
        grad_weight = jnp.sum(grad_new * (branch_ref[...] - hidden), axis=1, keepdims=True)
        grad_logit = grad_weight * sel_ref[...] * sigma * (1.0 - sigma) + ROUTER_LOSS / TOK_DEV * (
            sigma - sel_ref[...]
        )
        grad_norm, gain_row = normalize_back(mixed_ref[...], gain_ref[1:2, :], acc_ref[...])
        grad_mixed = grad_branch + grad_norm
        in_ref[...] = grad_new - grad_branch + grad_logit * router_ref[...] + grad_mixed
        attn = grad_mixed.astype(BFLOAT)
        attn_ref[...] = attn
        copy.wait()
        back_ref[...] = contract_cols(attn, held_ref[...]).astype(BFLOAT)
        small_ref[0:1, :] = gain_row
        small_ref[1:2, :] = jnp.sum(grad_logit * hidden, axis=0, keepdims=True)
        small_ref[2:8, :] = jnp.zeros((6, D), FLOAT)


def block_back(new, sel, logit, hidden, branch, mixed, gains, router, wo, gate, up, weights):
    rows = pl.BlockSpec((TOK_DEV, FF_BLOCK), lambda i: (0, i))
    full = whole(TOK_DEV, D)
    return pl.pallas_call(
        block_back_kernel,
        grid=(FF_STEPS,),
        in_specs=[
            full,
            whole(TOK_DEV, 1),
            whole(TOK_DEV, 1),
            full,
            full,
            full,
            whole(8, D),
            whole(1, D),
            pl.BlockSpec(memory_space=pl.ANY),
            rows,
            rows,
            WEIGHT_SPEC,
        ],
        out_specs=[full, rows, rows, full, full, full, whole(8, D)],
        out_shape=(
            struct(BFLOAT, TOK_DEV, D),
            struct(BFLOAT, TOK_DEV, FF),
            struct(BFLOAT, TOK_DEV, FF),
            struct(FLOAT, TOK_DEV, D),
            struct(BFLOAT, TOK_DEV, D),
            struct(BFLOAT, TOK_DEV, D),
            struct(FLOAT, 8, D),
        ),
        scratch_shapes=[
            pltpu.VMEM((TOK_DEV, D), FLOAT),
            pltpu.VMEM((D, D), BFLOAT),
            pltpu.SemaphoreType.DMA,
        ],
        cost_estimate=pl.CostEstimate(
            flops=4_000_000_000, bytes_accessed=20_000_000, transcendentals=400_000
        ),
        compiler_params=params(BIG),
    )(new, sel, logit, hidden, branch, mixed, gains, router, wo, gate, up, weights)


def enter_back_kernel(
    in_ref, dq_ref, own_ref, hidden_ref, gain_ref, wq_ref, wk_ref, wv_ref, cos_ref, sin_ref,
    pair_ref, out_ref, small_ref
):
    keys = turn(own_ref[:, 0:320].T, cos_ref[...], -sin_ref[...]).T.astype(BFLOAT)
    values = own_ref[:, 320:640].astype(BFLOAT)
    pair_ref[:, 0:320] = keys
    pair_ref[:, 320:640] = values
    grad_normed = (
        contract_cols(dq_ref[...], wq_ref[...])
        + contract_cols(keys, wk_ref[...])
        + contract_cols(values, wv_ref[...])
    )
    grad_hidden, gain_row = normalize_back(hidden_ref[...], gain_ref[0:1, :], grad_normed)
    out_ref[...] = in_ref[...] + grad_hidden
    small_ref[...] = jnp.concatenate([gain_row, jnp.zeros((7, D), FLOAT)], axis=0)


def enter_back(grad_in, dq, own, hidden, gains, wq, wk, wv, cosine, sine):
    return pl.pallas_call(
        enter_back_kernel,
        out_shape=(
            struct(BFLOAT, TOK_DEV, 640),
            struct(FLOAT, TOK_DEV, D),
            struct(FLOAT, 8, D),
        ),
        compiler_params=params(24),
    )(grad_in, dq, own, hidden, gains, wq, wk, wv, cosine, sine)


HEAD_BLOCK = 512


def head_kernel(rows_ref, near_ref, side_ref, far_ref, target_ref, table_ref, logit_ref, pick_ref, stat_ref):
    step = pl.program_id(0)

    @pl.when(step == 0)
    def first():
        hot = (rows_ref[...] == near_ref[...]).astype(FLOAT).astype(BFLOAT)
        pick_ref[...] = (nn(hot[:, :512], side_ref[...]) + nn(hot[:, 512:], far_ref[...])).astype(
            BFLOAT
        )
        lane = lax.broadcasted_iota(jnp.int32, (256, 128), 1)
        stat_ref[...] = jnp.where(lane == 0, MASKED, 0.0)

    logits = contract_cols(pick_ref[...], table_ref[...])
    logit_ref[...] = logits
    place = step * HEAD_BLOCK + lax.broadcasted_iota(jnp.int32, (256, HEAD_BLOCK), 1)
    hit = jnp.sum(jnp.where(place == target_ref[...], logits, 0.0), axis=1, keepdims=True)
    old = stat_ref[:, 0:1]
    top = jnp.maximum(old, jnp.max(logits, axis=1, keepdims=True))
    total = stat_ref[:, 1:2] * jnp.exp(old - top) + jnp.sum(
        jnp.exp(logits - top), axis=1, keepdims=True
    )
    stat_ref[:, 1:2] = total
    stat_ref[:, 2:3] = stat_ref[:, 2:3] + hit
    stat_ref[:, 0:1] = top


def head(loss_rows, near_rows, near, far, local_targets, table):
    return pl.pallas_call(
        head_kernel,
        grid=(VOCAB_MP // HEAD_BLOCK,),
        in_specs=[
            whole(256, 1),
            whole(1, ROWS),
            whole(512, D),
            whole(512, D),
            whole(256, 1),
            pl.BlockSpec((HEAD_BLOCK, D), lambda i: (i, 0)),
        ],
        out_specs=[
            pl.BlockSpec((256, HEAD_BLOCK), lambda i: (0, i)),
            whole(256, D),
            whole(256, 128),
        ],
        out_shape=(
            jax.ShapeDtypeStruct((256, VOCAB_MP), FLOAT),
            jax.ShapeDtypeStruct((256, D), BFLOAT),
            jax.ShapeDtypeStruct((256, 128), FLOAT),
        ),
        compiler_params=params(BIG),
    )(loss_rows, near_rows, near, far, local_targets, table)


def head_back_kernel(
    rows_ref, near_ref, target_ref, norm_ref, logit_ref, pick_ref, table_ref, grad_ref, side_ref, far_ref, sum_ref
):
    step = pl.program_id(0)
    place = step * HEAD_BLOCK + lax.broadcasted_iota(jnp.int32, (256, HEAD_BLOCK), 1)
    probs = jnp.exp(logit_ref[...] - norm_ref[...])
    hit = jnp.where(place == target_ref[...], 1.0, 0.0)
    grads = ((probs - hit) * (1.0 / TOK_DEV)).astype(BFLOAT)
    grad_ref[...] = contract_rows(grads, pick_ref[...]).astype(BFLOAT)
    part = nn(grads, table_ref[...])

    @pl.when(step == 0)
    def first():
        sum_ref[...] = part

    @pl.when(step > 0)
    def later():
        sum_ref[...] += part

    @pl.when(step == pl.num_programs(0) - 1)
    def last():
        hot = (rows_ref[...] == near_ref[...]).astype(FLOAT).astype(BFLOAT)
        total = sum_ref[...].astype(BFLOAT)
        side_ref[...] = contract_rows(hot[:, :512], total).astype(BFLOAT)
        far_ref[...] = contract_rows(hot[:, 512:], total).astype(BFLOAT)


def head_back(loss_rows, near_rows, local_targets, log_norm, logits, picked, table):
    return pl.pallas_call(
        head_back_kernel,
        grid=(VOCAB_MP // HEAD_BLOCK,),
        in_specs=[
            whole(256, 1),
            whole(1, ROWS),
            whole(256, 1),
            whole(256, 1),
            pl.BlockSpec((256, HEAD_BLOCK), lambda i: (0, i)),
            whole(256, D),
            pl.BlockSpec((HEAD_BLOCK, D), lambda i: (i, 0)),
        ],
        out_specs=[pl.BlockSpec((HEAD_BLOCK, D), lambda i: (i, 0)), whole(512, D), whole(512, D)],
        out_shape=(
            struct(BFLOAT, VOCAB_MP, D),
            struct(BFLOAT, 512, D),
            struct(BFLOAT, 512, D),
        ),
        scratch_shapes=[pltpu.VMEM((256, D), FLOAT)],
        compiler_params=params(BIG),
    )(loss_rows, near_rows, local_targets, log_norm, logits, picked, table)


def mlp_grad_kernel(which_ref, *refs):
    out_ref = refs[-1]

    def joined(first):
        return jnp.concatenate([ref[...] for ref in refs[first:-1:10]], axis=0)

    def both(first):
        return jnp.concatenate([joined(first), joined(first + 5)], axis=0)

    rights = both(3), both(3), both(4)
    for i in range(3):
        out_ref[:, i] = contract_rows(both(i), rights[i]).reshape(8, 80, D).astype(BFLOAT)


def mlp_grads(which, kept, received):
    def cols(width, place):
        return pl.BlockSpec((TOK_DEV, width), place)

    own = [cols(640, lambda i, half: (0, half[0] * 2 + i))] * 3 + [cols(D, lambda i, half: (0, 0))] * 2
    far = [cols(640, lambda i, half, n=n: (0, 2 * n + i)) for n in range(3)] + [
        cols(D, lambda i, half, n=n: (n, 0)) for n in (0, 1)
    ]
    args = []
    for parts, other in zip(kept, received):
        args += [*parts, *[other[0]] * 3, *[other[1]] * 2]
    return pl.pallas_call(
        mlp_grad_kernel,
        grid_spec=pltpu.PrefetchScalarGridSpec(
            num_scalar_prefetch=1,
            grid=(2,),
            in_specs=(own + far) * RECUR,
            out_specs=pl.BlockSpec((8, 3, 80, D), lambda i, half: (i, 0, 0, 0)),
        ),
        out_shape=struct(BFLOAT, 16, 3, 80, D),
        compiler_params=params(40),
    )(which.reshape(1), *args)


def square_grad_kernel(*refs):
    wq_ref, wo_ref = refs[-2:]
    ins = refs[:-2]

    def joined(first):
        return jnp.concatenate([ref[...] for ref in ins[first::8]], axis=0)

    def both(first):
        return jnp.concatenate([joined(first), joined(first + 4)], axis=0)

    wq_ref[...] = contract_rows(both(2), both(3)).astype(BFLOAT)
    wo_ref[...] = contract_rows(both(0), both(1)).astype(BFLOAT)


def square_grads(kept, received, queries):
    full = whole(TOK_DEV, D)
    far = [pl.BlockSpec((TOK_DEV, D), lambda i, n=n: (n, 0)) for n in (2, 3, 4)] + [full]
    args = []
    for parts, other, query in zip(kept, received, queries):
        args += [*parts, *[other[1]] * 3, query]
    return pl.pallas_call(
        square_grad_kernel,
        grid=(1,),
        in_specs=([full] * 4 + far) * RECUR,
        out_specs=[whole(D, D), whole(D, D)],
        out_shape=(struct(BFLOAT, D, D), struct(BFLOAT, D, D)),
        compiler_params=params(40),
    )(*args)


def pack_grad_kernel(starts_ref, *refs):
    wq_ref, wo_ref, rows_ref = refs[:3]
    ins = refs[3:-3]
    left_ref, right_ref, buf = refs[-3:]
    buf[0:960, :] = wq_ref[...]
    buf[1600:2560, :] = wo_ref[...]
    buf[2560:2576, :] = rows_ref[...].astype(BFLOAT)
    buf[2576:2688, :] = jnp.zeros((112, D), BFLOAT)
    normed = jnp.concatenate([ref[...] for ref in ins[0::4] + ins[1::4]], axis=0)
    grads = jnp.concatenate([ref[...] for ref in ins[2::4] + ins[3::4]], axis=0)
    line = lax.broadcasted_iota(jnp.int32, (960, 320), 0)
    place = lax.broadcasted_iota(jnp.int32, (960, 320), 1)
    full = contract_rows(normed, grads).astype(BFLOAT)
    for i in range(3):
        chosen = (line == 3 * place + i).astype(FLOAT).astype(BFLOAT)
        rows = contract_rows(chosen, full).astype(BFLOAT)
        buf[960:1280, 320 * i : 320 * i + 320] = rows[:, 0:320]
        buf[1280:1600, 320 * i : 320 * i + 320] = rows[:, 320:640]
    for i in range(4):
        start = pl.multiple_of(starts_ref[i], 16)
        left_ref[i] = buf[pl.ds(start, 352), 0:512]
        right_ref[i] = buf[pl.ds(start, 352), 512:960]


def pack_grads(starts, wq, wo, small, kept, received, pairs):
    args = []
    for (normed, pair), other, far in zip(kept, received, pairs):
        args += [normed, other[1], pair, far]
    specs = [
        whole(TOK_DEV, D),
        pl.BlockSpec((TOK_DEV, D), lambda i: (4, 0)),
        whole(TOK_DEV, 640),
        whole(TOK_DEV, 640),
    ]
    return pl.pallas_call(
        pack_grad_kernel,
        grid=(1,),
        in_specs=[pl.BlockSpec(memory_space=pltpu.SMEM), whole(D, D), whole(D, D), whole(16, D)]
        + specs * RECUR,
        out_specs=[whole(4, 352, 512), whole(4, 352, 448)],
        out_shape=(struct(BFLOAT, 4, 352, 512), struct(BFLOAT, 4, 352, 448)),
        scratch_shapes=[pltpu.VMEM((PACK_PAD, D), BFLOAT)],
        compiler_params=params(40),
    )(starts, wq, wo, small, *args)


def adam_update(master, first, second, grad, clip):
    grad = grad * clip
    first_new = BETA_ONE * first + (1.0 - BETA_ONE) * grad
    second_new = BETA_TWO * second + (1.0 - BETA_TWO) * grad * grad
    corr_one = 1.0 - BETA_ONE**STEP
    corr_two = 1.0 - BETA_TWO**STEP
    master_new = master - LEARN_RATE * (
        first_new / corr_one / (jnp.sqrt(second_new / corr_two) + ADAM_EPS) + DECAY * master
    )
    return (master_new, first_new, second_new)


def pack_row(device):
    return (1283 * device) // 64


def join_kernel(blocks_ref, out_ref):
    step = pl.program_id(0)
    first = jnp.minimum((step * (128 * 64)) // 1283, 118)
    first = (first // 2) * 2
    window = blocks_ref[pl.ds(pl.multiple_of(first * 24, 48), 240), :]
    row = step * 128 + lax.broadcasted_iota(jnp.int32, (128, 240), 0)
    place = lax.broadcasted_iota(jnp.int32, (128, 240), 1)
    device = (place * 2731) >> 16
    source = ((1283 * (first + device)) >> 6) + place - 24 * device
    chosen = (source == row).astype(FLOAT).astype(BFLOAT)
    out_ref[...] = jnp.dot(chosen, window, preferred_element_type=FLOAT).astype(BFLOAT)


def join_pack(blocks):
    return pl.pallas_call(
        join_kernel,
        grid=(PACK_PAD // 128,),
        in_specs=[pl.BlockSpec((128 * 24, D), lambda i: (0, 0))],
        out_specs=pl.BlockSpec((128, D), lambda i: (i, 0)),
        out_shape=jax.ShapeDtypeStruct((PACK_PAD, D), BFLOAT),
        compiler_params=pltpu.CompilerParams(vmem_limit_bytes=32 * 1024 * 1024),
    )(blocks)


def stage(value, axis, index):
    total = lax.dynamic_index_in_dim(value, index, 0, False).astype(FLOAT)
    for k in (1, 2, 3):
        sent = lax.dynamic_index_in_dim(value, (index + k) % 4, 0, False)
        total = total + shift(sent, axis, k).astype(FLOAT)
    return total


def stage_near(value, axis):
    total = value[0].astype(FLOAT)
    for k in (1, 2, 3):
        total = total + shift(value[k], axis, -k).astype(FLOAT)
    return total


def gradients(
    dense,
    token_ids,
    targets,
    loss_rows,
    selections,
    boundary,
    pack_master,
    mlp_master,
    table_master,
):
    z = lax.axis_index("z")
    core = lax.axis_index("core")
    y = lax.axis_index("y")
    x = lax.axis_index("x")
    model_index = z * 2 + core
    data_index = y * 4 + x
    device = model_index * DP + data_index
    own_table = table_master.astype(BFLOAT)

    near = jnp.stack([((z + k) % 4) * 2 + (core ^ j) for j in (0, 1) for k in range(4)])
    near_rows = (near[:, None] * TOK_DEV + jnp.arange(TOK_DEV, dtype=jnp.int32)[None, :]).reshape(-1)

    pack_offset = PACK_DEV * device - D * pack_row(device)
    pack_block = lax.dynamic_update_slice(
        jnp.zeros((24 * D,), BFLOAT), pack_master.astype(BFLOAT), (pack_offset,)
    ).reshape(24, D)
    own = jnp.concatenate([pack_block, mlp_master.astype(BFLOAT).reshape(3 * UNITS, D)], axis=0)
    ring = [own] + [shift(own, "z", k) for k in (1, 2, 3)]
    pack_quad = []
    for i in range(4):
        part = ring[3][:24]
        for k in (2, 1, 0):
            part = jnp.where(z == (i + k) % 4, ring[k][:24], part)
        pack_quad.append(part)
    pack_quad = jnp.concatenate(pack_quad, axis=0)
    mlp_quad = jnp.concatenate([part[24:].reshape(3, UNITS, D) for part in ring], axis=1)
    near_axes = ("core", "y", "x")
    pack_blocks = lax.all_gather(pack_quad, near_axes, axis=0, tiled=True)
    pack_blocks = (
        pack_blocks.reshape(2, DP, 4, 24, D).transpose(2, 0, 1, 3, 4).reshape(128 * 24, D)
    )

    group_ids = token_ids[0]
    near_ids = reorder(group_ids.reshape(MP, TOK_DEV), near).reshape(-1)
    local_ids = near_ids - model_index * VOCAB_MP
    inside = (local_ids >= 0) & (local_ids < VOCAB_MP)
    high = local_ids >> 7
    low = local_ids & 127
    high_hot = (high[:, None] == jnp.arange(48)[None, :]).astype(BFLOAT)
    low_hot = (low[:, None] == jnp.arange(128)[None, :]).astype(BFLOAT)
    present = (contract_rows(high_hot, low_hot) > 0).reshape(DP, VOCAB_DEV)
    before = (jnp.arange(VOCAB_DEV)[:, None] < jnp.arange(VOCAB_DEV)[None, :]).astype(BFLOAT)
    slots = mm(present.astype(BFLOAT), before)
    asked = present & (slots < CAP)
    over = jnp.max(jnp.where(present & (slots >= CAP), 1.0, 0.0))
    slot_table = jnp.where(asked, slots, 255.0).reshape(48, 128).astype(BFLOAT)
    token_slot = jnp.sum(mm(high_hot, slot_table) * low_hot.astype(FLOAT), axis=-1)
    token_place = jnp.where(
        inside & (token_slot < CAP), (high // 3) * CAP + token_slot.astype(jnp.int32), -1
    )
    token_place = token_place[:, None]
    match = asked[:, None, :] & (slots[:, None, :] == jnp.arange(CAP, dtype=FLOAT)[None, :, None])
    request = (
        jnp.sum(jnp.where(match, jnp.arange(1, VOCAB_DEV + 1, dtype=FLOAT)[None, None, :], 0.0), axis=-1)
        - 1.0
    )
    request = jnp.concatenate([request, jnp.full((DP, 8), over, FLOAT)], axis=1)
    request = lax.all_to_all(request, DP_AXES, 0, 0, tiled=True)
    over = jnp.max(request[:, CAP:])
    owner_hot = (
        request[:, :CAP].reshape(-1)[:, None] == jnp.arange(VOCAB_DEV, dtype=FLOAT)[None, :]
    ).astype(BFLOAT)
    mlp_quad, owner_hot = tie(mlp_quad, owner_hot)
    mlp_weights = lax.all_gather(mlp_quad.reshape(3 * 80, D), near_axes, axis=0, tiled=True)
    mlp_weights = mlp_weights.reshape(32, 3, 80, D)
    asked_rows = lax.all_to_all(mm(owner_hot, own_table).astype(BFLOAT), DP_AXES, 0, 0, tiled=True)
    own_table, asked_rows = tie(own_table, asked_rows)
    table = lax.all_gather(own_table, DP_AXES, axis=0, tiled=True)
    if dense:
        rows = jnp.take(table, jnp.clip(local_ids, 0, VOCAB_MP - 1), axis=0)
        looked = jnp.where(inside[:, None], rows, jnp.zeros_like(rows))
        looked = looked[:512], looked[512:]
    else:
        looked = spread(token_place, asked_rows)
    hidden = scatter_group(*looked)

    pack_weights = join_pack(pack_blocks)
    w_query = pack_weights[:960]
    w_key = pack_weights[960:1280].reshape(D, KV_HEADS * HEAD_DIM)
    w_value = pack_weights[1280:1600].reshape(D, KV_HEADS * HEAD_DIM)
    w_out = pack_weights[1600:2560]
    gains = jnp.concatenate([pack_weights[2560:2563].astype(FLOAT), jnp.zeros((5, D), FLOAT)])
    router = pack_weights[2563:2566].astype(FLOAT)
    half_dim = HEAD_DIM // 2
    freqs = ROPE_BASE ** (-jnp.arange(half_dim, dtype=FLOAT) / half_dim)
    first_row = data_index * ROWS + model_index * TOK_DEV
    angles = freqs[:, None] * (first_row + jnp.arange(TOK_DEV, dtype=jnp.int32)).astype(FLOAT)[None, :]
    turns = (jnp.cos(angles), jnp.sin(angles))
    projections = (w_query, w_key, w_value) + turns
    group_sel = selections.reshape(RECUR, DP, MP, TOK_DEV)
    prev_index = jnp.maximum(data_index - 1, 0)
    here_sel = lax.dynamic_index_in_dim(group_sel, data_index, 1, False)
    own_sel = lax.dynamic_index_in_dim(here_sel, model_index, 1, False)
    near_sel = reorder(here_sel, near).reshape(RECUR, ROWS)
    prev_sel = reorder(lax.dynamic_index_in_dim(group_sel, prev_index, 1, False), near)
    prev_sel = prev_sel.reshape(RECUR, ROWS)
    start = lax.dynamic_index_in_dim(boundary, data_index, 0, False)
    prev_start = lax.dynamic_index_in_dim(boundary, prev_index, 0, False)
    place = (model_index * TOK_DEV + jnp.arange(TOK_DEV, dtype=jnp.int32))[None, :]
    key_place = near_rows[:, None]
    biases = []
    for step in range(RECUR):
        own_seen = (
            (key_place <= place)
            & ((key_place < start) == (place < start))
            & ((near_sel[step][:, None] > 0) | (key_place == place))
        )
        prev_seen = (
            (data_index > 0)
            & (place < start)
            & (key_place >= prev_start)
            & (prev_sel[step][:, None] > 0)
        )
        seen = [prev_seen[:512], own_seen[:512], prev_seen[512:], own_seen[512:]]
        biases.append(jnp.where(jnp.concatenate(seen, axis=0), 0.0, MASKED))

    sel_cols = own_sel.astype(FLOAT)[:, :, None]
    saves = []
    logits_all = []
    normed, queries, pair = enter(hidden, gains, *projections)
    for step in range(RECUR):
        pairs = group_gather(pair)
        attended, log_total = attend(queries, pairs, biases[step])
        mixed, mlp_input, gate, up, inner, branch, logit, new_hidden, *nexts = block(
            attended,
            hidden,
            sel_cols[step],
            gains,
            router[step : step + 1],
            w_out,
            mlp_weights,
            projections if step < RECUR - 1 else None,
        )
        logits_all.append(logit[:, 0])
        saves.append(
            (
                hidden,
                normed,
                queries,
                pairs,
                attended,
                log_total,
                mixed,
                mlp_input,
                gate,
                up,
                inner,
                branch,
                logit,
            )
        )
        hidden = new_hidden
        if nexts:
            normed, queries, pair = nexts
    logits_all = jnp.stack(logits_all)
    penalty_total = jnp.sum(jax.nn.softplus(logits_all) - own_sel.astype(FLOAT) * logits_all)

    normed_final = rms_scale(hidden, gains[2]).astype(BFLOAT)
    final_rows = gather_group(normed_final)
    row_targets = lax.dynamic_index_in_dim(targets, data_index, 0, keepdims=False)
    head_args = (loss_rows[0][:, None], near_rows[None, :])
    local_targets = (row_targets - model_index * VOCAB_MP)[:, None]
    logits, picked, stats = head(*head_args, *final_rows, local_targets, table)
    stats = jnp.concatenate([stats[:, :3].T, jnp.full((1, 256), over)])

    def join_stats(parts):
        top = parts[0][0]
        for part in parts[1:]:
            top = jnp.maximum(top, part[0])
        total = sum(part[1] * jnp.exp(part[0] - top) for part in parts)
        over = parts[0][3]
        for part in parts[1:]:
            over = jnp.maximum(over, part[3])
        return jnp.stack([top, total, sum(part[2] for part in parts), over])

    stats = join_stats([stats, swap(stats)])
    stats = join_stats([stats] + [shift(stats, "z", k) for k in (1, 2, 3)])
    log_norm = stats[0] + jnp.log(stats[1])
    cross = log_norm - stats[2]
    per_device = cross.shape[0] // MP
    loss_part = (
        jnp.sum(lax.dynamic_slice_in_dim(cross, model_index * per_device, per_device))
        + ROUTER_LOSS * penalty_total
    )
    head_grad, *scattered = head_back(
        *head_args, local_targets, log_norm[:, None], logits, picked, table
    )
    grad_final = scatter_group(*scattered)
    grad_hidden, grad_gain_final = rms_back(hidden, gains[2], grad_final)
    if not dense:
        head_grad = lax.psum_scatter(head_grad, DP_AXES, scatter_dimension=0, tiled=True)

    mlp_kept, far_kept, square_kept, far_queries, pack_kept, far_pairs = [], [], [], [], [], []
    router_rows = [None] * RECUR
    gain_one = jnp.zeros((1, D), FLOAT)
    gain_two = jnp.zeros((1, D), FLOAT)
    for step in reversed(range(RECUR)):
        (
            hidden_in,
            normed,
            queries,
            pairs,
            attended,
            log_total,
            mixed,
            mlp_input,
            gate,
            up,
            inner,
            branch,
            logit,
        ) = saves[step]
        grad_rows, grad_gate, grad_up, grad_in, grad_attn, grad_attended, small = block_back(
            grad_hidden,
            sel_cols[step],
            logit,
            hidden_in,
            branch,
            mixed,
            gains,
            router[step : step + 1],
            w_out,
            gate,
            up,
            mlp_weights,
        )
        gain_two = gain_two + small[0:1]
        router_rows[step] = small[1:2]
        mlp_kept.append((grad_gate, grad_up, inner, mlp_input, grad_rows))

        def far_half(value):
            return lax.dynamic_slice_in_dim(value, (1 - core) * (FF // 2), FF // 2, 1)

        sent = jnp.concatenate([far_half(grad_gate), far_half(grad_up), far_half(inner)], axis=1)
        rows = jnp.concatenate([mlp_input, grad_rows, attended, grad_attn, normed], axis=0)
        far_kept.append((swap(sent), by_rows(swap(by_rows(rows)))))
        grad_query, *grad_sides = attend_back(
            queries, pairs, biases[step], log_total, attended, grad_attended, *turns
        )
        square_kept.append((attended, grad_attn, normed, grad_query))
        far_queries.append(by_rows(swap(grad_query)))
        grad_own = group_scatter(*grad_sides)
        if step == 0:
            mlp_half = mlp_grads(core.astype(jnp.int32), mlp_kept, far_kept)
            mlp_sum = lax.psum_scatter(
                mlp_half.reshape(16 * 240, D), DP_AXES, scatter_dimension=0, tiled=True
            )
            squares = square_grads(square_kept, far_kept, far_queries)
            grad_own, mlp_half, *squares = tie(grad_own, mlp_half, *squares)
        grad_pair, grad_hidden, small = enter_back(
            grad_in, grad_query, grad_own, hidden_in, gains, *projections
        )
        gain_one = gain_one + small[0:1]
        pack_kept.append((normed, grad_pair))
        far_pairs.append(swap(grad_pair))

    def aligned_row(which):
        return (pack_row(which) // 16) * 16

    small = jnp.concatenate(
        [
            gain_one,
            gain_two,
            grad_gain_final[None],
            *router_rows,
            jnp.zeros((10, D), FLOAT),
        ]
    )
    small = small + swap(small)
    starts = jnp.stack([aligned_row(DP * (2 * i + core)) for i in range(4)]).astype(jnp.int32)
    left, right = pack_grads(starts, *squares, small, pack_kept, far_kept, far_pairs)

    def y_windows(value):
        return jnp.stack([value[..., 80 * i : 80 * i + 112, :] for i in range(4)])

    def x_windows(value):
        return jnp.stack([value[..., i : i + 48, :] for i in (0, 16, 40, 56)])

    left = stage(y_windows(left), "y", y).astype(BFLOAT)
    right = stage(right, "z", z).astype(BFLOAT)
    left = stage(left, "z", z).astype(BFLOAT)
    right = stage(y_windows(right), "y", y).astype(BFLOAT)
    part = jnp.concatenate([left, right], axis=-1)
    part, mlp_sum = tie(part, mlp_sum)
    part = stage(x_windows(part), "x", x).reshape(-1)
    begin = aligned_row(DP * model_index) + 80 * y + (20 * x) // 8 * 8
    pack_grad = lax.dynamic_slice(part, (PACK_DEV * device - D * begin,), (PACK_DEV,))

    mlp_sum = mlp_sum.reshape(3, 4, UNITS, D).transpose(1, 0, 2, 3)
    mlp_grad = stage_near(mlp_sum, "z")

    grad_embed = gather_group(grad_hidden.astype(BFLOAT))
    if dense:
        kept_rows = jnp.concatenate(grad_embed).astype(FLOAT) * inside.astype(FLOAT)[:, None]
        sums = jax.ops.segment_sum(
            kept_rows, jnp.clip(local_ids, 0, VOCAB_MP - 1), num_segments=VOCAB_MP
        )
        table_grad = lax.psum_scatter(
            (head_grad.astype(FLOAT) + sums).astype(BFLOAT),
            DP_AXES,
            scatter_dimension=0,
            tiled=True,
        ).astype(FLOAT)
    else:
        unique = collect(token_place, *grad_embed)
        unique = lax.all_to_all(unique, DP_AXES, 0, 0, tiled=True)
        table_grad = head_grad.astype(FLOAT) + contract_rows(owner_hot, unique)
    return pack_grad, mlp_grad, by_cols(table_grad), loss_part, stats[3, 0]


def shards(
    token_ids,
    targets,
    loss_rows,
    selections,
    boundary,
    pack_master,
    pack_first,
    pack_second,
    mlp_master,
    mlp_first,
    mlp_second,
    table_master,
    table_first,
    table_second,
):
    args = (
        token_ids,
        targets,
        loss_rows,
        selections,
        boundary,
        pack_master,
        mlp_master,
        table_master,
    )
    *found, over = gradients(False, *args)
    pack_grad, mlp_grad, table_grad, loss_part = lax.cond(
        over > 0, lambda: gradients(True, *args)[:4], lambda: tuple(found)
    )
    squares = (
        jnp.sum(pack_grad * pack_grad)
        + jnp.sum(mlp_grad * mlp_grad)
        + jnp.sum(table_grad * table_grad)
    )
    lane = lax.broadcasted_iota(jnp.int32, (1, 128), 1)
    sums = sum_all(jnp.where(lane == 0, squares, loss_part))
    total_squares = sums[0, 0]
    loss_sum = sums[0, 1]
    grad_norm = jnp.sqrt(total_squares)
    clip = CLIP_NORM / jnp.maximum(grad_norm, CLIP_NORM)
    pack_new, pack_first_new, pack_second_new = adam_update(
        pack_master, pack_first, pack_second, pack_grad, clip
    )
    mlp_new, mlp_first_new, mlp_second_new = adam_update(
        mlp_master, mlp_first, mlp_second, mlp_grad, clip
    )
    table_new, table_first_new, table_second_new = adam_update(
        table_master, table_first, table_second, table_grad, clip
    )
    return (
        pack_new,
        pack_first_new,
        pack_second_new,
        mlp_new,
        mlp_first_new,
        mlp_second_new,
        table_new,
        table_first_new,
        table_second_new,
        loss_sum,
        grad_norm,
    )


def solution(mesh):
    grid = Mesh(mesh.devices.reshape(4, 2, 4, 4), ALL_AXES)
    owners = (P(ALL_AXES), P(None, ALL_AXES, None), P(ALL_AXES, None))
    group = P(DP_AXES, None)
    masters = tuple(spec for spec in owners for _ in range(3))
    return jax.shard_map(
        shards,
        mesh=grid,
        in_specs=(group, P(), group, P(), P()) + masters,
        out_specs=masters + (P(), P()),
        check_vma=False,
    )
```

```python
import functools

import jax
import jax.numpy as jnp
from jax import lax
from jax.experimental import pallas as pl
from jax.experimental.layout import Layout, with_layout_constraint
from jax.experimental.pallas import tpu as pltpu
from jax.sharding import Mesh
from jax.sharding import PartitionSpec as P

D = 960
HEADS = 15
KV_HEADS = 5
HEAD_DIM = 64
FF = 2560
RECUR = 3
STEP = 10
TOK_DEV = 128
ROWS = 1024
MP = 8
DP = 16
VOCAB_MP = 6144
VOCAB_DEV = 384
UNITS = 20
PACK_DEV = 19245
PACK_ROWS = 2566
PACK_PAD = 2688
CAP = 24

EPS_NORM = 1e-05
ROPE_BASE = 10000.0
ROUTER_LOSS = 0.1
CLIP_NORM = 1.0
LEARN_RATE = 0.05
BETA_ONE = 0.9
BETA_TWO = 0.95
ADAM_EPS = 1e-08
DECAY = 0.1
MASKED = -1e30
HIGHEST = lax.Precision.HIGHEST
BFLOAT = jnp.bfloat16
FLOAT = jnp.float32
DP_AXES = ("y", "x")
ALL_AXES = ("z", "core", "y", "x")


def shift(value, axis, steps):
    return lax.ppermute(value, axis, [(i, (i + steps) % 4) for i in range(4)])


def swap(value):
    return lax.ppermute(value, "core", [(0, 1), (1, 0)])


def gather_group(value):
    near = [value] + [shift(value, "z", -k) for k in (1, 2, 3)]
    return near + [swap(part) for part in near]


def scatter_group(blocks):
    half = [near.astype(FLOAT) + swap(far).astype(FLOAT) for near, far in zip(blocks[:4], blocks[4:])]
    total = half[0]
    for k in (1, 2, 3):
        total = total + shift(half[k].astype(BFLOAT), "z", k).astype(FLOAT)
    return total


def sum_all(value):
    value = value + swap(value)
    for axis in ("z", "y", "x"):
        value = value + shift(value, axis, 1) + shift(value, axis, 2) + shift(value, axis, 3)
    return value


def rms_scale(values, weight):
    return values * lax.rsqrt(jnp.mean(values * values, axis=-1, keepdims=True) + EPS_NORM) * weight


def rms_back(values, weight, grad_out):
    inverse = lax.rsqrt(jnp.mean(values * values, axis=-1, keepdims=True) + EPS_NORM)
    weighted = grad_out * weight
    grad_values = inverse * weighted - values * (inverse * inverse * inverse) * jnp.mean(
        weighted * values, axis=-1, keepdims=True
    )
    return (grad_values, jnp.sum(grad_out * values * inverse, axis=0))


def mm(left, right):
    return jnp.dot(left, right, preferred_element_type=FLOAT)


def contract_rows(left, right):
    return lax.dot_general(left, right, (((0,), (0,)), ((), ())), preferred_element_type=FLOAT)


def contract_cols(left, right):
    return lax.dot_general(left, right, (((1,), (1,)), ((), ())), preferred_element_type=FLOAT)


def reorder(blocks, order):
    hit = order[:, None] == jnp.arange(MP)[None, :]
    return jnp.sum(jnp.where(hit[:, :, None], blocks[..., None, :, :], 0), axis=-2)


def by_cols(value):
    return with_layout_constraint(value, Layout((1, 0)))


def tie(*values):
    return lax.optimization_barrier(values)


def group_gather(pair):
    own = [pair]
    for k in (1, 2, 3):
        own.append(lax.ppermute(pair, "z", [((i + k) % 4, i) for i in range(4) if (i + k) % 4 < i]))
    prev = []
    for k in range(4):
        pairs = []
        for i in range(3):
            for g in range(1, DP):
                pairs.append((((i + k) % 4) * DP + g - 1, i * DP + g))
        prev.append(lax.ppermute(pair, ("z",) + DP_AXES, pairs))
    return prev + own + [swap(part) for part in prev] + [swap(part) for part in own]


def group_scatter(prev, own, prev_far, own_far):
    own = (own.astype(FLOAT) + swap(own_far).astype(FLOAT)).astype(BFLOAT).reshape(4, TOK_DEV, -1)
    prev = (prev.astype(FLOAT) + swap(prev_far).astype(FLOAT)).astype(BFLOAT).reshape(4, TOK_DEV, -1)
    total = own[0].astype(FLOAT)
    for k in (1, 2, 3):
        pairs = [(i, (i + k) % 4) for i in range(4) if (i + k) % 4 < i]
        total = total + lax.ppermute(own[k], "z", pairs).astype(FLOAT)
    for k in range(4):
        pairs = []
        for i in range(3):
            for g in range(1, DP):
                pairs.append((i * DP + g, ((i + k) % 4) * DP + g - 1))
        total = total + lax.ppermute(prev[k], ("z",) + DP_AXES, pairs).astype(FLOAT)
    return total


def nn(left, right):
    return jnp.dot(left, right, preferred_element_type=FLOAT)


def head_rows(ref, head):
    return jnp.concatenate(
        [ref[:, 64 * (3 * head + i) : 64 * (3 * head + i) + 64] for i in range(3)], axis=0
    )


def head_lanes(ref, head):
    return jnp.concatenate(
        [ref[64 * (3 * head + i) : 64 * (3 * head + i) + 64, :] for i in range(3)], axis=1
    )


def turn(value, cosine, sine):
    parts = []
    for head in range(value.shape[0] // 64):
        first = value[64 * head : 64 * head + 32]
        second = value[64 * head + 32 : 64 * head + 64]
        parts.append(first * cosine - second * sine)
        parts.append(second * cosine + first * sine)
    return jnp.concatenate(parts, axis=0)


def normalize(values, weight):
    return values * lax.rsqrt(jnp.mean(values * values, axis=-1, keepdims=True) + EPS_NORM) * weight


def normalize_back(values, weight, grad_out):
    inverse = lax.rsqrt(jnp.mean(values * values, axis=-1, keepdims=True) + EPS_NORM)
    weighted = grad_out * weight
    grad_values = inverse * weighted - values * (inverse * inverse * inverse) * jnp.mean(
        weighted * values, axis=-1, keepdims=True
    )
    return grad_values, jnp.sum(grad_out * values * inverse, axis=0, keepdims=True)


def joined(refs, part, first):
    return jnp.concatenate(
        [ref[:, first : first + 64] for ref in refs[4 * part : 4 * part + 4]], axis=0
    )


def attend_kernel(query_ref, *refs):
    kv_refs, (bias_ref, out_ref, log_ref) = refs[:16], refs[16:]
    for head in range(KV_HEADS):
        queries = head_lanes(query_ref, head)
        top = None
        for part in range(4):
            keys = joined(kv_refs, part, 64 * head)
            values = joined(kv_refs, part, 320 + 64 * head)
            bias = bias_ref[512 * part : 512 * part + 512, :]
            scores = nn(keys, queries) + jnp.concatenate([bias, bias, bias], axis=1)
            part_top = jnp.max(scores, axis=0, keepdims=True)
            new_top = part_top if top is None else jnp.maximum(top, part_top)
            expo = jnp.exp(scores - new_top)
            part_total = jnp.sum(expo, axis=0, keepdims=True)
            part_out = contract_rows(values, expo.astype(BFLOAT))
            if top is None:
                total, out = part_total, part_out
            else:
                shrink = jnp.exp(top - new_top)
                total, out = total * shrink + part_total, out * shrink + part_out
            top = new_top
        out = (out / total).T.astype(BFLOAT)
        for i in range(3):
            place = 64 * (3 * head + i)
            out_ref[:, place : place + 64] = out[128 * i : 128 * i + 128]
        log_ref[head : head + 1, :] = top + jnp.log(total)


def params(mib):
    return pltpu.CompilerParams(vmem_limit_bytes=mib * 1024 * 1024)


def whole(*shape):
    return pl.BlockSpec(shape, lambda i: (0,) * len(shape))


def struct(kind, *shape):
    return jax.ShapeDtypeStruct(shape, kind)


def attend(queries, pairs, bias):
    return pl.pallas_call(
        attend_kernel,
        out_shape=(struct(BFLOAT, TOK_DEV, D), struct(FLOAT, 8, 3 * TOK_DEV)),
        cost_estimate=pl.CostEstimate(
            flops=12_000_000_000, bytes_accessed=5_000_000, transcendentals=4_000_000
        ),
        compiler_params=params(BIG),
    )(queries, *pairs, bias)


def attend_back_kernel(query_ref, *refs):
    kv_refs, refs = refs[:16], refs[16:]
    bias_ref, log_ref, att_ref, grad_ref, cos_ref, sin_ref, dq_ref = refs[:7]
    d_refs = refs[7:]
    cosine = jnp.concatenate([cos_ref[...]] * 3, axis=1)
    sine = jnp.concatenate([sin_ref[...]] * 3, axis=1)
    for head in range(KV_HEADS):
        queries = head_lanes(query_ref, head)
        grads = head_rows(grad_ref, head)
        outs = head_rows(att_ref, head)
        delta = jnp.sum((grads.astype(FLOAT) * outs.astype(FLOAT)).T, axis=0, keepdims=True)
        log_total = log_ref[head : head + 1, :]
        back = None
        for part, d_ref in enumerate(d_refs):
            keys = joined(kv_refs, part, 64 * head)
            values = joined(kv_refs, part, 320 + 64 * head)
            bias = bias_ref[512 * part : 512 * part + 512, :]
            probs = jnp.exp(
                nn(keys, queries) + jnp.concatenate([bias, bias, bias], axis=1) - log_total
            )
            grad_scores = (probs * (contract_cols(values, grads) - delta)).astype(BFLOAT)
            d_ref[:, 64 * head : 64 * head + 64] = contract_cols(grad_scores, queries).astype(BFLOAT)
            d_ref[:, 320 + 64 * head : 320 + 64 * head + 64] = nn(
                probs.astype(BFLOAT), grads
            ).astype(BFLOAT)
            part_back = contract_rows(keys, grad_scores)
            back = part_back if back is None else back + part_back
        back = turn(back * (HEAD_DIM**-0.5), cosine, -sine).T.astype(BFLOAT)
        for i in range(3):
            place = 64 * (3 * head + i)
            dq_ref[:, place : place + 64] = back[128 * i : 128 * i + 128]


def attend_back(queries, pairs, bias, log_total, attended, grads, cosine, sine):
    side = struct(BFLOAT, 4 * TOK_DEV, 640)
    return pl.pallas_call(
        attend_back_kernel,
        out_shape=(struct(BFLOAT, TOK_DEV, D), side, side, side, side),
        cost_estimate=pl.CostEstimate(
            flops=20_000_000_000, bytes_accessed=9_000_000, transcendentals=4_000_000
        ),
        compiler_params=params(BIG),
    )(queries, *pairs, bias, log_total, attended, grads, cosine, sine)


def project(hidden, gain, wq_ref, wk_ref, wv_ref, cos_ref, sin_ref, normed_ref, query_ref, pair_ref):
    normed = normalize(hidden, gain).astype(BFLOAT)
    normed_ref[...] = normed
    cosine, sine = cos_ref[...], sin_ref[...]
    keys = turn(nn(normed, wk_ref[...]).T, cosine, sine).T
    pair_ref[:, 0:320] = keys.astype(BFLOAT)
    pair_ref[:, 320:640] = nn(normed, wv_ref[...]).astype(BFLOAT)
    queries = turn(nn(normed, wq_ref[...]).T, cosine, sine)
    query_ref[...] = (queries * (HEAD_DIM**-0.5)).astype(BFLOAT)


PROJECTED = (
    struct(BFLOAT, TOK_DEV, D),
    struct(BFLOAT, D, TOK_DEV),
    struct(BFLOAT, TOK_DEV, 640),
)


def spread_kernel(place_ref, rows_ref, *out_refs):
    place = lax.broadcasted_iota(jnp.int32, (TOK_DEV, DP * CAP), 1)
    for part, ref in enumerate(out_refs):
        hot = (place_ref[128 * part : 128 * part + 128, :] == place).astype(FLOAT).astype(BFLOAT)
        ref[...] = nn(hot, rows_ref[...]).astype(BFLOAT)


def spread(place, rows):
    return pl.pallas_call(
        spread_kernel,
        out_shape=[struct(BFLOAT, TOK_DEV, D)] * MP,
        compiler_params=params(BIG),
    )(place, rows)


def collect_kernel(place_ref, *refs):
    place = lax.broadcasted_iota(jnp.int32, (TOK_DEV, DP * CAP), 1)
    total = None
    for part, ref in enumerate(refs[:-1]):
        hot = (place_ref[128 * part : 128 * part + 128, :] == place).astype(FLOAT).astype(BFLOAT)
        sums = contract_rows(hot, ref[...])
        total = sums if total is None else total + sums
    refs[-1][...] = total.astype(BFLOAT)


def collect(place, blocks):
    return pl.pallas_call(
        collect_kernel, out_shape=struct(BFLOAT, DP * CAP, D), compiler_params=params(BIG)
    )(place, *blocks)


def enter_kernel(hidden_ref, gain_ref, *refs):
    project(hidden_ref[...], gain_ref[0:1, :], *refs)


def enter(hidden, gains, wq, wk, wv, cosine, sine):
    return pl.pallas_call(enter_kernel, out_shape=PROJECTED, compiler_params=params(BIG))(
        hidden, gains, wq, wk, wv, cosine, sine
    )


BIG = 56
FF_BLOCK = 640
FF_STEPS = FF // FF_BLOCK


def weight(ref, which):
    return ref[:, which].reshape(FF_BLOCK, D)


def block_kernel(
    more, att_ref, hidden_ref, sel_ref, gain_ref, router_ref, wo_ref, weight_ref, *refs
):
    proj_in, refs = (refs[:5], refs[5:]) if more else ((), refs)
    mixed_ref, input_ref, gate_ref, up_ref, inner_ref, branch_ref, logit_ref, new_ref = refs[:8]
    proj_out, refs = (refs[8:11], refs[11:]) if more else ((), refs[8:])
    acc_ref = refs[0]
    step = pl.program_id(0)
    copies = [
        pltpu.make_async_copy(source, target, refs[4].at[i])
        for i, (source, target) in enumerate(zip(proj_in[:3], refs[1:4]))
    ]

    @pl.when(step == 0)
    def first():
        for copy in copies:
            copy.start()
        mixed = hidden_ref[...] + nn(att_ref[...], wo_ref[...])
        mixed_ref[...] = mixed
        input_ref[...] = normalize(mixed, gain_ref[1:2, :]).astype(BFLOAT)
        acc_ref[...] = mixed

    rows = input_ref[...]
    gate = contract_cols(rows, weight(weight_ref, 0))
    up = contract_cols(rows, weight(weight_ref, 1))
    gate_ref[...] = gate
    up_ref[...] = up
    inner = (gate * jax.nn.sigmoid(gate) * up).astype(BFLOAT)
    inner_ref[...] = inner
    acc_ref[...] += nn(inner, weight(weight_ref, 2))

    @pl.when(step == FF_STEPS - 1)
    def last():
        hidden = hidden_ref[...]
        branch = acc_ref[...]
        branch_ref[...] = branch
        logit = jnp.sum(hidden * router_ref[...], axis=1, keepdims=True)
        logit_ref[...] = logit
        new = hidden + sel_ref[...] * jax.nn.sigmoid(logit) * (branch - hidden)
        new_ref[...] = new
        for copy in copies:
            copy.wait()
        if more:
            project(new, gain_ref[0:1, :], *refs[1:4], *proj_in[3:], *proj_out)


WEIGHT_SPEC = pl.BlockSpec((FF_BLOCK // 80, 3, 80, D), lambda i: (i, 0, 0, 0))


def block(att, hidden, sel, gains, router, wo, weights, projections):
    more = projections is not None
    proj_specs = [pl.BlockSpec(memory_space=pl.ANY)] * 3 + [whole(32, 128), whole(32, 128)]
    rows = pl.BlockSpec((TOK_DEV, FF_BLOCK), lambda i: (0, i))
    return pl.pallas_call(
        functools.partial(block_kernel, more),
        grid=(FF_STEPS,),
        in_specs=[
            whole(TOK_DEV, D),
            whole(TOK_DEV, D),
            whole(TOK_DEV, 1),
            whole(8, D),
            whole(1, D),
            whole(D, D),
            WEIGHT_SPEC,
        ]
        + proj_specs * more,
        out_specs=[
            whole(TOK_DEV, D),
            whole(TOK_DEV, D),
            rows,
            rows,
            rows,
            whole(TOK_DEV, D),
            whole(TOK_DEV, 1),
            whole(TOK_DEV, D),
        ]
        + [whole(TOK_DEV, D), whole(D, TOK_DEV), whole(TOK_DEV, 640)] * more,
        out_shape=(
            struct(FLOAT, TOK_DEV, D),
            struct(BFLOAT, TOK_DEV, D),
            struct(FLOAT, TOK_DEV, FF),
            struct(FLOAT, TOK_DEV, FF),
            struct(BFLOAT, TOK_DEV, FF),
            struct(FLOAT, TOK_DEV, D),
            struct(FLOAT, TOK_DEV, 1),
            struct(FLOAT, TOK_DEV, D),
        )
        + (PROJECTED if more else ()),
        scratch_shapes=[pltpu.VMEM((TOK_DEV, D), FLOAT)]
        + [
            pltpu.VMEM((D, D), BFLOAT),
            pltpu.VMEM((D, 320), BFLOAT),
            pltpu.VMEM((D, 320), BFLOAT),
            pltpu.SemaphoreType.DMA((3,)),
        ]
        * more,
        cost_estimate=pl.CostEstimate(
            flops=4_000_000_000, bytes_accessed=20_000_000, transcendentals=400_000
        ),
        compiler_params=params(BIG),
    )(att, hidden, sel, gains, router, wo, weights, *(projections if more else ()))


def block_back_kernel(
    new_ref, sel_ref, logit_ref, hidden_ref, branch_ref, mixed_ref, gain_ref, router_ref, wo_ref,
    gate_ref, up_ref, weight_ref,
    rows_ref, dgate_ref, dup_ref, in_ref, attn_ref, back_ref, small_ref, acc_ref, held_ref, sem
):
    step = pl.program_id(0)
    sigma = jax.nn.sigmoid(logit_ref[...])
    chosen = sel_ref[...] * sigma
    copy = pltpu.make_async_copy(wo_ref, held_ref, sem)

    @pl.when(step == 0)
    def first():
        copy.start()
        rows_ref[...] = (chosen * new_ref[...]).astype(BFLOAT)
        acc_ref[...] = jnp.zeros_like(acc_ref)

    inner = contract_cols(rows_ref[...], weight(weight_ref, 2))
    gate = gate_ref[...]
    shape = jax.nn.sigmoid(gate)
    dgate = (inner * up_ref[...] * shape * (1.0 + gate * (1.0 - shape))).astype(BFLOAT)
    dup = (inner * gate * shape).astype(BFLOAT)
    dgate_ref[...] = dgate
    dup_ref[...] = dup
    acc_ref[...] += nn(dgate, weight(weight_ref, 0)) + nn(dup, weight(weight_ref, 1))

    @pl.when(step == FF_STEPS - 1)
    def last():
        grad_new = new_ref[...]
        hidden = hidden_ref[...]
        grad_branch = chosen * grad_new
        grad_weight = jnp.sum(grad_new * (branch_ref[...] - hidden), axis=1, keepdims=True)
        grad_logit = grad_weight * sel_ref[...] * sigma * (1.0 - sigma) + ROUTER_LOSS / TOK_DEV * (
            sigma - sel_ref[...]
        )
        grad_norm, gain_row = normalize_back(mixed_ref[...], gain_ref[1:2, :], acc_ref[...])
        grad_mixed = grad_branch + grad_norm
        in_ref[...] = grad_new - grad_branch + grad_logit * router_ref[...] + grad_mixed
        attn = grad_mixed.astype(BFLOAT)
        attn_ref[...] = attn
        copy.wait()
        back_ref[...] = contract_cols(attn, held_ref[...]).astype(BFLOAT)
        small_ref[0:1, :] = gain_row
        small_ref[1:2, :] = jnp.sum(grad_logit * hidden, axis=0, keepdims=True)
        small_ref[2:8, :] = jnp.zeros((6, D), FLOAT)


def block_back(new, sel, logit, hidden, branch, mixed, gains, router, wo, gate, up, weights):
    rows = pl.BlockSpec((TOK_DEV, FF_BLOCK), lambda i: (0, i))
    full = whole(TOK_DEV, D)
    return pl.pallas_call(
        block_back_kernel,
        grid=(FF_STEPS,),
        in_specs=[
            full,
            whole(TOK_DEV, 1),
            whole(TOK_DEV, 1),
            full,
            full,
            full,
            whole(8, D),
            whole(1, D),
            pl.BlockSpec(memory_space=pl.ANY),
            rows,
            rows,
            WEIGHT_SPEC,
        ],
        out_specs=[full, rows, rows, full, full, full, whole(8, D)],
        out_shape=(
            struct(BFLOAT, TOK_DEV, D),
            struct(BFLOAT, TOK_DEV, FF),
            struct(BFLOAT, TOK_DEV, FF),
            struct(FLOAT, TOK_DEV, D),
            struct(BFLOAT, TOK_DEV, D),
            struct(BFLOAT, TOK_DEV, D),
            struct(FLOAT, 8, D),
        ),
        scratch_shapes=[
            pltpu.VMEM((TOK_DEV, D), FLOAT),
            pltpu.VMEM((D, D), BFLOAT),
            pltpu.SemaphoreType.DMA,
        ],
        cost_estimate=pl.CostEstimate(
            flops=4_000_000_000, bytes_accessed=20_000_000, transcendentals=400_000
        ),
        compiler_params=params(BIG),
    )(new, sel, logit, hidden, branch, mixed, gains, router, wo, gate, up, weights)


def enter_back_kernel(
    in_ref, dq_ref, own_ref, hidden_ref, gain_ref, wq_ref, wk_ref, wv_ref, cos_ref, sin_ref,
    pair_ref, out_ref, small_ref
):
    keys = turn(own_ref[:, 0:320].T, cos_ref[...], -sin_ref[...]).T.astype(BFLOAT)
    values = own_ref[:, 320:640].astype(BFLOAT)
    pair_ref[:, 0:320] = keys
    pair_ref[:, 320:640] = values
    grad_normed = (
        contract_cols(dq_ref[...], wq_ref[...])
        + contract_cols(keys, wk_ref[...])
        + contract_cols(values, wv_ref[...])
    )
    grad_hidden, gain_row = normalize_back(hidden_ref[...], gain_ref[0:1, :], grad_normed)
    out_ref[...] = in_ref[...] + grad_hidden
    small_ref[...] = jnp.concatenate([gain_row, jnp.zeros((7, D), FLOAT)], axis=0)


def enter_back(grad_in, dq, own, hidden, gains, wq, wk, wv, cosine, sine):
    return pl.pallas_call(
        enter_back_kernel,
        out_shape=(
            struct(BFLOAT, TOK_DEV, 640),
            struct(FLOAT, TOK_DEV, D),
            struct(FLOAT, 8, D),
        ),
        compiler_params=params(BIG),
    )(grad_in, dq, own, hidden, gains, wq, wk, wv, cosine, sine)


HEAD_BLOCK = 1024


def head_kernel(rows_ref, near_ref, *refs):
    block_refs, (target_ref, table_ref, logit_ref, pick_ref, out_ref, stat_ref) = refs[:8], refs[8:]
    step = pl.program_id(0)

    @pl.when(step == 0)
    def first():
        picked = None
        for i, ref in enumerate(block_refs):
            hot = rows_ref[...] == near_ref[:, 128 * i : 128 * i + 128]
            part = nn(hot.astype(FLOAT).astype(BFLOAT), ref[...])
            picked = part if picked is None else picked + part
        pick_ref[...] = picked.astype(BFLOAT)
        lane = lax.broadcasted_iota(jnp.int32, (256, 128), 1)
        stat_ref[...] = jnp.where(lane == 0, MASKED, 0.0)

    logits = contract_cols(pick_ref[...], table_ref[...])
    logit_ref[...] = logits
    place = step * HEAD_BLOCK + lax.broadcasted_iota(jnp.int32, (256, HEAD_BLOCK), 1)
    hit = jnp.sum(jnp.where(place == target_ref[...], logits, 0.0), axis=1, keepdims=True)
    old = stat_ref[:, 0:1]
    top = jnp.maximum(old, jnp.max(logits, axis=1, keepdims=True))
    total = stat_ref[:, 1:2] * jnp.exp(old - top) + jnp.sum(
        jnp.exp(logits - top), axis=1, keepdims=True
    )
    stat_ref[:, 1:2] = total
    stat_ref[:, 2:3] = stat_ref[:, 2:3] + hit
    stat_ref[:, 0:1] = top

    @pl.when(step == pl.num_programs(0) - 1)
    def last():
        out_ref[...] = stat_ref[...].T[0:8]


def head(loss_rows, near_rows, blocks, local_targets, table):
    return pl.pallas_call(
        head_kernel,
        grid=(VOCAB_MP // HEAD_BLOCK,),
        in_specs=[whole(256, 1), whole(1, ROWS)]
        + [whole(TOK_DEV, D)] * MP
        + [whole(256, 1), pl.BlockSpec((HEAD_BLOCK, D), lambda i: (i, 0))],
        out_specs=[
            pl.BlockSpec((256, HEAD_BLOCK), lambda i: (0, i)),
            whole(256, D),
            whole(8, 256),
        ],
        out_shape=(
            struct(FLOAT, 256, VOCAB_MP),
            struct(BFLOAT, 256, D),
            struct(FLOAT, 8, 256),
        ),
        scratch_shapes=[pltpu.VMEM((256, 128), FLOAT)],
        compiler_params=params(BIG),
    )(loss_rows, near_rows, *blocks, local_targets, table)


def head_back_kernel(
    rows_ref, near_ref, target_ref, stat_ref, logit_ref, pick_ref, table_ref, grad_ref, *refs
):
    block_refs, (sum_ref, norm_ref) = refs[:8], refs[8:]
    step = pl.program_id(0)

    @pl.when(step == 0)
    def first():
        norm = stat_ref[0:1, :] + jnp.log(stat_ref[1:2, :])
        norm_ref[:, 0:8] = jnp.concatenate([norm] * 8, axis=0).T
        sum_ref[...] = jnp.zeros((256, D), FLOAT)

    place = step * HEAD_BLOCK + lax.broadcasted_iota(jnp.int32, (256, HEAD_BLOCK), 1)
    probs = jnp.exp(logit_ref[...] - norm_ref[:, 0:1])
    hit = jnp.where(place == target_ref[...], 1.0, 0.0)
    grads = ((probs - hit) * (1.0 / TOK_DEV)).astype(BFLOAT)
    grad_ref[...] = contract_rows(grads, pick_ref[...]).astype(BFLOAT)
    sum_ref[...] += nn(grads, table_ref[...])

    @pl.when(step == pl.num_programs(0) - 1)
    def last():
        total = sum_ref[...].astype(BFLOAT)
        for i, ref in enumerate(block_refs):
            hot = rows_ref[...] == near_ref[:, 128 * i : 128 * i + 128]
            ref[...] = contract_rows(hot.astype(FLOAT).astype(BFLOAT), total).astype(BFLOAT)


def head_back(loss_rows, near_rows, local_targets, stats, logits, picked, table):
    return pl.pallas_call(
        head_back_kernel,
        grid=(VOCAB_MP // HEAD_BLOCK,),
        in_specs=[
            whole(256, 1),
            whole(1, ROWS),
            whole(256, 1),
            whole(8, 256),
            pl.BlockSpec((256, HEAD_BLOCK), lambda i: (0, i)),
            whole(256, D),
            pl.BlockSpec((HEAD_BLOCK, D), lambda i: (i, 0)),
        ],
        out_specs=[pl.BlockSpec((HEAD_BLOCK, D), lambda i: (i, 0))] + [whole(TOK_DEV, D)] * MP,
        out_shape=[struct(BFLOAT, VOCAB_MP, D)] + [struct(BFLOAT, TOK_DEV, D)] * MP,
        scratch_shapes=[pltpu.VMEM((256, D), FLOAT), pltpu.VMEM((256, 128), FLOAT)],
        compiler_params=params(BIG),
    )(loss_rows, near_rows, local_targets, stats, logits, picked, table)


def mlp_grad_kernel(which_ref, *refs):
    out_ref = refs[-1]

    def joined(first):
        return jnp.concatenate([ref[...] for ref in refs[first:-1:10]], axis=0)

    def both(first):
        return jnp.concatenate([joined(first), joined(first + 5)], axis=0)

    rights = both(3), both(3), both(4)
    for i in range(3):
        out_ref[:, i] = contract_rows(both(i), rights[i]).reshape(8, 80, D).astype(BFLOAT)


def mlp_grads(which, kept, received):
    def cols(width, place):
        return pl.BlockSpec((TOK_DEV, width), place)

    rights = [cols(D, lambda i, half: (0, 0))] * 2
    own = [cols(640, lambda i, half: (0, half[0] * 2 + i))] * 3 + rights
    far = [cols(640, lambda i, half: (0, i))] * 3 + rights
    args = []
    for parts, other in zip(kept, received):
        args += [*parts, *other]
    return pl.pallas_call(
        mlp_grad_kernel,
        grid_spec=pltpu.PrefetchScalarGridSpec(
            num_scalar_prefetch=1,
            grid=(2,),
            in_specs=(own + far) * RECUR,
            out_specs=pl.BlockSpec((8, 3, 80, D), lambda i, half: (i, 0, 0, 0)),
        ),
        out_shape=struct(BFLOAT, 16, 3, 80, D),
        compiler_params=params(BIG),
    )(which.reshape(1), *args)


def square_grad_kernel(*refs):
    wq_ref, wo_ref = refs[-2:]
    ins = refs[:-2]

    def joined(first):
        return jnp.concatenate([ref[...] for ref in ins[first::8]], axis=0)

    def both(first):
        return jnp.concatenate([joined(first), joined(first + 4)], axis=0)

    wq_ref[...] = contract_rows(both(2), both(3)).astype(BFLOAT)
    wo_ref[...] = contract_rows(both(0), both(1)).astype(BFLOAT)


def square_grads(kept, received):
    args = []
    for parts, other in zip(kept, received):
        args += [*parts, *other]
    return pl.pallas_call(
        square_grad_kernel,
        grid=(1,),
        in_specs=[whole(TOK_DEV, D)] * (8 * RECUR),
        out_specs=[whole(D, D), whole(D, D)],
        out_shape=(struct(BFLOAT, D, D), struct(BFLOAT, D, D)),
        compiler_params=params(BIG),
    )(*args)


def pack_grad_kernel(starts_ref, *refs):
    wq_ref, wo_ref, rows_ref = refs[:3]
    ins = refs[3:-3]
    left_ref, right_ref, buf = refs[-3:]
    buf[0:960, :] = wq_ref[...]
    buf[1600:2560, :] = wo_ref[...]
    buf[2560:2576, :] = rows_ref[...].astype(BFLOAT)
    buf[2576:2688, :] = jnp.zeros((112, D), BFLOAT)
    normed = jnp.concatenate([ref[...] for ref in ins[0::4] + ins[1::4]], axis=0)
    grads = jnp.concatenate([ref[...] for ref in ins[2::4] + ins[3::4]], axis=0)
    line = lax.broadcasted_iota(jnp.int32, (960, 320), 0)
    place = lax.broadcasted_iota(jnp.int32, (960, 320), 1)
    full = contract_rows(normed, grads).astype(BFLOAT)
    for i in range(3):
        chosen = (line == 3 * place + i).astype(FLOAT).astype(BFLOAT)
        rows = contract_rows(chosen, full).astype(BFLOAT)
        buf[960:1280, 320 * i : 320 * i + 320] = rows[:, 0:320]
        buf[1280:1600, 320 * i : 320 * i + 320] = rows[:, 320:640]
    for i in range(4):
        start = pl.multiple_of(starts_ref[i], 16)
        left_ref[i] = buf[pl.ds(start, 352), 0:512]
        right_ref[i] = buf[pl.ds(start, 352), 512:960]


def pack_grads(starts, wq, wo, small, kept, received):
    args = []
    for (normed, pair), (far_normed, far_pair) in zip(kept, received):
        args += [normed, far_normed, pair, far_pair]
    specs = [whole(TOK_DEV, D)] * 2 + [whole(TOK_DEV, 640)] * 2
    return pl.pallas_call(
        pack_grad_kernel,
        grid=(1,),
        in_specs=[pl.BlockSpec(memory_space=pltpu.SMEM), whole(D, D), whole(D, D), whole(16, D)]
        + specs * RECUR,
        out_specs=[whole(4, 352, 512), whole(4, 352, 448)],
        out_shape=(struct(BFLOAT, 4, 352, 512), struct(BFLOAT, 4, 352, 448)),
        scratch_shapes=[pltpu.VMEM((PACK_PAD, D), BFLOAT)],
        compiler_params=params(BIG),
    )(starts, wq, wo, small, *args)


def adam_update(master, first, second, grad, clip):
    grad = grad * clip
    first_new = BETA_ONE * first + (1.0 - BETA_ONE) * grad
    second_new = BETA_TWO * second + (1.0 - BETA_TWO) * grad * grad
    corr_one = 1.0 - BETA_ONE**STEP
    corr_two = 1.0 - BETA_TWO**STEP
    master_new = master - LEARN_RATE * (
        first_new / corr_one / (jnp.sqrt(second_new / corr_two) + ADAM_EPS) + DECAY * master
    )
    return (master_new, first_new, second_new)


def pack_row(device):
    return (1283 * device) // 64


def join_kernel(blocks_ref, out_ref):
    step = pl.program_id(0)
    first = jnp.minimum((step * (128 * 64)) // 1283, 118)
    first = (first // 2) * 2
    window = blocks_ref[pl.ds(pl.multiple_of(first * 24, 48), 240), :]
    row = step * 128 + lax.broadcasted_iota(jnp.int32, (128, 240), 0)
    place = lax.broadcasted_iota(jnp.int32, (128, 240), 1)
    device = (place * 2731) >> 16
    source = ((1283 * (first + device)) >> 6) + place - 24 * device
    chosen = (source == row).astype(FLOAT).astype(BFLOAT)
    out_ref[...] = jnp.dot(chosen, window, preferred_element_type=FLOAT).astype(BFLOAT)


def join_pack(blocks):
    return pl.pallas_call(
        join_kernel,
        grid=(PACK_PAD // 128,),
        in_specs=[pl.BlockSpec((128 * 24, D), lambda i: (0, 0))],
        out_specs=pl.BlockSpec((128, D), lambda i: (i, 0)),
        out_shape=jax.ShapeDtypeStruct((PACK_PAD, D), BFLOAT),
        compiler_params=pltpu.CompilerParams(vmem_limit_bytes=32 * 1024 * 1024),
    )(blocks)


def stage(value, axis, index):
    total = lax.dynamic_index_in_dim(value, index, 0, False).astype(FLOAT)
    for k in (1, 2, 3):
        sent = lax.dynamic_index_in_dim(value, (index + k) % 4, 0, False)
        total = total + shift(sent, axis, k).astype(FLOAT)
    return total


def stage_near(value, axis):
    total = value[0].astype(FLOAT)
    for k in (1, 2, 3):
        total = total + shift(value[k], axis, -k).astype(FLOAT)
    return total


def gradients(
    dense,
    token_ids,
    targets,
    loss_rows,
    selections,
    boundary,
    pack_master,
    mlp_master,
    table_master,
):
    z = lax.axis_index("z")
    core = lax.axis_index("core")
    y = lax.axis_index("y")
    x = lax.axis_index("x")
    model_index = z * 2 + core
    data_index = y * 4 + x
    device = model_index * DP + data_index
    own_table = table_master.astype(BFLOAT)

    near = jnp.stack([((z + k) % 4) * 2 + (core ^ j) for j in (0, 1) for k in range(4)])
    near_rows = (near[:, None] * TOK_DEV + jnp.arange(TOK_DEV, dtype=jnp.int32)[None, :]).reshape(-1)

    pack_offset = PACK_DEV * device - D * pack_row(device)
    pack_block = lax.dynamic_update_slice(
        jnp.zeros((24 * D,), BFLOAT), pack_master.astype(BFLOAT), (pack_offset,)
    ).reshape(24, D)
    own = jnp.concatenate([pack_block, mlp_master.astype(BFLOAT).reshape(3 * UNITS, D)], axis=0)
    ring = [own] + [shift(own, "z", k) for k in (1, 2, 3)]
    pack_quad = []
    for i in range(4):
        part = ring[3][:24]
        for k in (2, 1, 0):
            part = jnp.where(z == (i + k) % 4, ring[k][:24], part)
        pack_quad.append(part)
    pack_quad = jnp.concatenate(pack_quad, axis=0)
    mlp_quad = jnp.concatenate([part[24:].reshape(3, UNITS, D) for part in ring], axis=1)
    near_axes = ("core", "y", "x")
    pack_blocks = lax.all_gather(pack_quad, near_axes, axis=0, tiled=True)
    pack_blocks = (
        pack_blocks.reshape(2, DP, 4, 24, D).transpose(2, 0, 1, 3, 4).reshape(128 * 24, D)
    )

    group_ids = token_ids[0]
    near_ids = reorder(group_ids.reshape(MP, TOK_DEV), near).reshape(-1)
    local_ids = near_ids - model_index * VOCAB_MP
    inside = (local_ids >= 0) & (local_ids < VOCAB_MP)
    high = local_ids >> 7
    low = local_ids & 127
    high_hot = (high[:, None] == jnp.arange(48)[None, :]).astype(BFLOAT)
    low_hot = (low[:, None] == jnp.arange(128)[None, :]).astype(BFLOAT)
    present = (contract_rows(high_hot, low_hot) > 0).reshape(DP, VOCAB_DEV)
    before = (jnp.arange(VOCAB_DEV)[:, None] < jnp.arange(VOCAB_DEV)[None, :]).astype(BFLOAT)
    slots = mm(present.astype(BFLOAT), before)
    asked = present & (slots < CAP)
    over = jnp.max(jnp.where(present & (slots >= CAP), 1.0, 0.0))
    slot_table = jnp.where(asked, slots, 255.0).reshape(48, 128).astype(BFLOAT)
    token_slot = jnp.sum(mm(high_hot, slot_table) * low_hot.astype(FLOAT), axis=-1)
    token_place = jnp.where(
        inside & (token_slot < CAP), (high // 3) * CAP + token_slot.astype(jnp.int32), -1
    )
    token_place = token_place[:, None]
    match = asked[:, None, :] & (slots[:, None, :] == jnp.arange(CAP, dtype=FLOAT)[None, :, None])
    request = (
        jnp.sum(jnp.where(match, jnp.arange(1, VOCAB_DEV + 1, dtype=FLOAT)[None, None, :], 0.0), axis=-1)
        - 1.0
    )
    request = jnp.concatenate([request, jnp.full((DP, 8), over, FLOAT)], axis=1)
    request = lax.all_to_all(request, DP_AXES, 0, 0, tiled=True)
    over = jnp.max(request[:, CAP:])
    owner_hot = (
        request[:, :CAP].reshape(-1)[:, None] == jnp.arange(VOCAB_DEV, dtype=FLOAT)[None, :]
    ).astype(BFLOAT)
    mlp_quad, owner_hot = tie(mlp_quad, owner_hot)
    mlp_weights = lax.all_gather(mlp_quad.reshape(3 * 80, D), near_axes, axis=0, tiled=True)
    mlp_weights = mlp_weights.reshape(32, 3, 80, D)
    asked_rows = lax.all_to_all(mm(owner_hot, own_table).astype(BFLOAT), DP_AXES, 0, 0, tiled=True)
    own_table, asked_rows = tie(own_table, asked_rows)
    table = lax.all_gather(own_table, DP_AXES, axis=0, tiled=True)
    if dense:
        rows = jnp.take(table, jnp.clip(local_ids, 0, VOCAB_MP - 1), axis=0)
        looked = jnp.where(inside[:, None], rows, jnp.zeros_like(rows))
        looked = [looked[128 * i : 128 * i + 128] for i in range(MP)]
    else:
        looked = spread(token_place, asked_rows)
    hidden = scatter_group(looked)

    pack_weights = join_pack(pack_blocks)
    w_query = pack_weights[:960]
    w_key = pack_weights[960:1280].reshape(D, KV_HEADS * HEAD_DIM)
    w_value = pack_weights[1280:1600].reshape(D, KV_HEADS * HEAD_DIM)
    w_out = pack_weights[1600:2560]
    gains = jnp.concatenate([pack_weights[2560:2563].astype(FLOAT), jnp.zeros((5, D), FLOAT)])
    router = pack_weights[2563:2566].astype(FLOAT)
    half_dim = HEAD_DIM // 2
    freqs = ROPE_BASE ** (-jnp.arange(half_dim, dtype=FLOAT) / half_dim)
    first_row = data_index * ROWS + model_index * TOK_DEV
    angles = freqs[:, None] * (first_row + jnp.arange(TOK_DEV, dtype=jnp.int32)).astype(FLOAT)[None, :]
    turns = (jnp.cos(angles), jnp.sin(angles))
    projections = (w_query, w_key, w_value) + turns
    group_sel = selections.reshape(RECUR, DP, MP, TOK_DEV)
    prev_index = jnp.maximum(data_index - 1, 0)
    here_sel = lax.dynamic_index_in_dim(group_sel, data_index, 1, False)
    own_sel = lax.dynamic_index_in_dim(here_sel, model_index, 1, False)
    near_sel = reorder(here_sel, near).reshape(RECUR, ROWS)
    prev_sel = reorder(lax.dynamic_index_in_dim(group_sel, prev_index, 1, False), near)
    prev_sel = prev_sel.reshape(RECUR, ROWS)
    start = lax.dynamic_index_in_dim(boundary, data_index, 0, False)
    prev_start = lax.dynamic_index_in_dim(boundary, prev_index, 0, False)
    place = (model_index * TOK_DEV + jnp.arange(TOK_DEV, dtype=jnp.int32))[None, :]
    key_place = near_rows[:, None]
    biases = []
    for step in range(RECUR):
        own_seen = (
            (key_place <= place)
            & ((key_place < start) == (place < start))
            & ((near_sel[step][:, None] > 0) | (key_place == place))
        )
        prev_seen = (
            (data_index > 0)
            & (place < start)
            & (key_place >= prev_start)
            & (prev_sel[step][:, None] > 0)
        )
        seen = [prev_seen[:512], own_seen[:512], prev_seen[512:], own_seen[512:]]
        biases.append(jnp.where(jnp.concatenate(seen, axis=0), 0.0, MASKED))

    sel_cols = own_sel.astype(FLOAT)[:, :, None]
    saves = []
    logits_all = []
    normed, queries, pair = enter(hidden, gains, *projections)
    for step in range(RECUR):
        pairs = group_gather(pair)
        attended, log_total = attend(queries, pairs, biases[step])
        mixed, mlp_input, gate, up, inner, branch, logit, new_hidden, *nexts = block(
            attended,
            hidden,
            sel_cols[step],
            gains,
            router[step : step + 1],
            w_out,
            mlp_weights,
            projections if step < RECUR - 1 else None,
        )
        logits_all.append(logit[:, 0])
        saves.append(
            (
                hidden,
                normed,
                queries,
                pairs,
                attended,
                log_total,
                mixed,
                mlp_input,
                gate,
                up,
                inner,
                branch,
                logit,
            )
        )
        hidden = new_hidden
        if nexts:
            normed, queries, pair = nexts
    logits_all = jnp.stack(logits_all)
    penalty_total = jnp.sum(jax.nn.softplus(logits_all) - own_sel.astype(FLOAT) * logits_all)

    normed_final = rms_scale(hidden, gains[2]).astype(BFLOAT)
    final_rows = gather_group(normed_final)
    row_targets = lax.dynamic_index_in_dim(targets, data_index, 0, keepdims=False)
    head_args = (loss_rows[0][:, None], near_rows[None, :])
    local_targets = (row_targets - model_index * VOCAB_MP)[:, None]
    logits, picked, stats = head(*head_args, final_rows, local_targets, table)
    flag_row = lax.broadcasted_iota(jnp.int32, (8, 256), 0) == 3
    stats = jnp.where(flag_row, over, stats)

    def join_stats(parts):
        top = parts[0][0]
        for part in parts[1:]:
            top = jnp.maximum(top, part[0])
        total = sum(part[1] * jnp.exp(part[0] - top) for part in parts)
        over = parts[0][3]
        for part in parts[1:]:
            over = jnp.maximum(over, part[3])
        rest = [jnp.zeros_like(top)] * 4
        return jnp.stack([top, total, sum(part[2] for part in parts), over] + rest)

    stats = join_stats([stats, swap(stats)])
    stats = join_stats([stats] + [shift(stats, "z", k) for k in (1, 2, 3)])
    log_norm = stats[0] + jnp.log(stats[1])
    cross = log_norm - stats[2]
    per_device = cross.shape[0] // MP
    loss_part = (
        jnp.sum(lax.dynamic_slice_in_dim(cross, model_index * per_device, per_device))
        + ROUTER_LOSS * penalty_total
    )
    head_grad, *scattered = head_back(*head_args, local_targets, stats, logits, picked, table)
    grad_final = scatter_group(scattered)
    grad_hidden, grad_gain_final = rms_back(hidden, gains[2], grad_final)
    if not dense:
        head_grad = lax.psum_scatter(head_grad, DP_AXES, scatter_dimension=0, tiled=True)

    mlp_kept, mlp_far, square_kept, square_far, pack_kept, pack_far = [], [], [], [], [], []
    loss_part, flag, grad_hidden = tie(loss_part, stats[3, 0], grad_hidden)
    router_rows = [None] * RECUR
    gain_one = jnp.zeros((1, D), FLOAT)
    gain_two = jnp.zeros((1, D), FLOAT)
    for step in reversed(range(RECUR)):
        (
            hidden_in,
            normed,
            queries,
            pairs,
            attended,
            log_total,
            mixed,
            mlp_input,
            gate,
            up,
            inner,
            branch,
            logit,
        ) = saves[step]
        grad_rows, grad_gate, grad_up, grad_in, grad_attn, grad_attended, small = block_back(
            grad_hidden,
            sel_cols[step],
            logit,
            hidden_in,
            branch,
            mixed,
            gains,
            router[step : step + 1],
            w_out,
            gate,
            up,
            mlp_weights,
        )
        gain_two = gain_two + small[0:1]
        router_rows[step] = small[1:2]
        mlp_kept.append((grad_gate, grad_up, inner, mlp_input, grad_rows))

        def far_half(value):
            return lax.dynamic_slice_in_dim(value, (1 - core) * (FF // 2), FF // 2, 1)

        mlp_far.append(
            [swap(far_half(part)) for part in (grad_gate, grad_up, inner)]
            + [swap(mlp_input), swap(grad_rows)]
        )
        grad_query, *grad_sides = attend_back(
            queries, pairs, biases[step], log_total, attended, grad_attended, *turns
        )
        far_normed = swap(normed)
        square_kept.append((attended, grad_attn, normed, grad_query))
        square_far.append((swap(attended), swap(grad_attn), far_normed, swap(grad_query)))
        if step == 0:
            tied = tie(*grad_sides, *mlp_kept[-1])
            grad_sides, mlp_kept[-1] = tied[:4], tied[4:]
        grad_own = group_scatter(*grad_sides)
        if step == 0:
            mlp_half = mlp_grads(core.astype(jnp.int32), mlp_kept, mlp_far)
            mlp_sum = lax.psum_scatter(
                mlp_half.reshape(16 * 240, D), DP_AXES, scatter_dimension=0, tiled=True
            )
            squares = square_grads(square_kept, square_far)
            grad_own, mlp_half, *squares = tie(grad_own, mlp_half, *squares)
        grad_pair, grad_hidden, small = enter_back(
            grad_in, grad_query, grad_own, hidden_in, gains, *projections
        )
        gain_one = gain_one + small[0:1]
        pack_kept.append((normed, grad_pair))
        pack_far.append((far_normed, swap(grad_pair)))
        if step == 1 and not dense:
            head_grad, grad_hidden = tie(head_grad, grad_hidden)

    def aligned_row(which):
        return (pack_row(which) // 16) * 16

    small = jnp.concatenate(
        [
            gain_one,
            gain_two,
            grad_gain_final[None],
            *router_rows,
            jnp.zeros((10, D), FLOAT),
        ]
    )
    small = small + swap(small)
    starts = jnp.stack([aligned_row(DP * (2 * i + core)) for i in range(4)]).astype(jnp.int32)
    left, right = pack_grads(starts, *squares, small, pack_kept, pack_far)

    def y_windows(value):
        return jnp.stack([value[..., 80 * i : 80 * i + 112, :] for i in range(4)])

    def x_windows(value):
        return jnp.stack([value[..., i : i + 48, :] for i in (0, 16, 40, 56)])

    left = stage(y_windows(left), "y", y).astype(BFLOAT)
    right = stage(right, "z", z).astype(BFLOAT)
    left = stage(left, "z", z).astype(BFLOAT)
    right = stage(y_windows(right), "y", y).astype(BFLOAT)
    part = jnp.concatenate([left, right], axis=-1)
    part, mlp_sum = tie(part, mlp_sum)
    part = stage(x_windows(part), "x", x).reshape(-1)
    begin = aligned_row(DP * model_index) + 80 * y + (20 * x) // 8 * 8
    pack_grad = lax.dynamic_slice(part, (PACK_DEV * device - D * begin,), (PACK_DEV,))

    mlp_sum = mlp_sum.reshape(3, 4, UNITS, D).transpose(1, 0, 2, 3)
    mlp_grad = stage_near(mlp_sum, "z")

    grad_embed = gather_group(grad_hidden.astype(BFLOAT))
    if dense:
        kept_rows = jnp.concatenate(grad_embed).astype(FLOAT) * inside.astype(FLOAT)[:, None]
        sums = jax.ops.segment_sum(
            kept_rows, jnp.clip(local_ids, 0, VOCAB_MP - 1), num_segments=VOCAB_MP
        )
        table_grad = lax.psum_scatter(
            (head_grad.astype(FLOAT) + sums).astype(BFLOAT),
            DP_AXES,
            scatter_dimension=0,
            tiled=True,
        ).astype(FLOAT)
    else:
        unique = collect(token_place, grad_embed)
        unique = lax.all_to_all(unique, DP_AXES, 0, 0, tiled=True)
        table_grad = head_grad.astype(FLOAT) + contract_rows(owner_hot, unique)
    return pack_grad, mlp_grad, by_cols(table_grad), loss_part, flag


def shards(
    token_ids,
    targets,
    loss_rows,
    selections,
    boundary,
    pack_master,
    pack_first,
    pack_second,
    mlp_master,
    mlp_first,
    mlp_second,
    table_master,
    table_first,
    table_second,
):
    args = (
        token_ids,
        targets,
        loss_rows,
        selections,
        boundary,
        pack_master,
        mlp_master,
        table_master,
    )
    *found, over = tie(*gradients(False, *args))
    pack_grad, mlp_grad, table_grad, loss_part = lax.cond(
        over > 0, lambda: gradients(True, *args)[:4], lambda: tuple(found)
    )
    squares = (
        jnp.sum(pack_grad * pack_grad)
        + jnp.sum(mlp_grad * mlp_grad)
        + jnp.sum(table_grad * table_grad)
    )
    lane = lax.broadcasted_iota(jnp.int32, (1, 128), 1)
    sums = sum_all(jnp.where(lane == 0, squares, loss_part))
    total_squares = sums[0, 0]
    loss_sum = sums[0, 1]
    grad_norm = jnp.sqrt(total_squares)
    clip = CLIP_NORM / jnp.maximum(grad_norm, CLIP_NORM)
    pack_new, pack_first_new, pack_second_new = adam_update(
        pack_master, pack_first, pack_second, pack_grad, clip
    )
    mlp_new, mlp_first_new, mlp_second_new = adam_update(
        mlp_master, mlp_first, mlp_second, mlp_grad, clip
    )
    table_new, table_first_new, table_second_new = adam_update(
        table_master, table_first, table_second, table_grad, clip
    )
    return (
        pack_new,
        pack_first_new,
        pack_second_new,
        mlp_new,
        mlp_first_new,
        mlp_second_new,
        table_new,
        table_first_new,
        table_second_new,
        loss_sum,
        grad_norm,
    )


def solution(mesh):
    grid = Mesh(mesh.devices.reshape(4, 2, 4, 4), ALL_AXES)
    owners = (P(ALL_AXES), P(None, ALL_AXES, None), P(ALL_AXES, None))
    group = P(DP_AXES, None)
    masters = tuple(spec for spec in owners for _ in range(3))
    return jax.shard_map(
        shards,
        mesh=grid,
        in_specs=(group, P(), group, P(), P()) + masters,
        out_specs=masters + (P(), P()),
        check_vma=False,
    )
```

```python
import functools

import jax
import jax.numpy as jnp
from jax import lax
from jax.experimental import pallas as pl
from jax.experimental.layout import Layout, with_layout_constraint
from jax.experimental.pallas import tpu as pltpu
from jax.sharding import Mesh
from jax.sharding import PartitionSpec as P

D = 960
HEADS = 15
KV_HEADS = 5
HEAD_DIM = 64
FF = 2560
RECUR = 3
STEP = 10
TOK_DEV = 128
ROWS = 1024
MP = 8
DP = 16
VOCAB_MP = 6144
VOCAB_DEV = 384
UNITS = 20
PACK_DEV = 19245
PACK_ROWS = 2566
PACK_PAD = 2688
CAP = 24

EPS_NORM = 1e-05
ROPE_BASE = 10000.0
ROUTER_LOSS = 0.1
CLIP_NORM = 1.0
LEARN_RATE = 0.05
BETA_ONE = 0.9
BETA_TWO = 0.95
ADAM_EPS = 1e-08
DECAY = 0.1
MASKED = -1e30
HIGHEST = lax.Precision.HIGHEST
BFLOAT = jnp.bfloat16
FLOAT = jnp.float32
DP_AXES = ("y", "x")
ALL_AXES = ("z", "core", "y", "x")


def shift(value, axis, steps):
    return lax.ppermute(value, axis, [(i, (i + steps) % 4) for i in range(4)])


def swap(value):
    return lax.ppermute(value, "core", [(0, 1), (1, 0)])


def gather_group(value):
    near = [value] + [shift(value, "z", -k) for k in (1, 2, 3)]
    return near + [swap(part) for part in near]


def scatter_group(blocks, other=None):
    half = [near.astype(FLOAT) + swap(far).astype(FLOAT) for near, far in zip(blocks[:4], blocks[4:])]
    total = half[0]
    sent = [part.astype(BFLOAT) for part in half[1:]]
    if other is not None:
        *sent, other = tie(*sent, other)
    for k in (1, 2, 3):
        total = total + shift(sent[k - 1], "z", k).astype(FLOAT)
    return total if other is None else (total, other)


def rms_scale(values, weight):
    return values * lax.rsqrt(jnp.mean(values * values, axis=-1, keepdims=True) + EPS_NORM) * weight


def rms_back(values, weight, grad_out):
    inverse = lax.rsqrt(jnp.mean(values * values, axis=-1, keepdims=True) + EPS_NORM)
    weighted = grad_out * weight
    grad_values = inverse * weighted - values * (inverse * inverse * inverse) * jnp.mean(
        weighted * values, axis=-1, keepdims=True
    )
    return (grad_values, jnp.sum(grad_out * values * inverse, axis=0))


def mm(left, right):
    return jnp.dot(left, right, preferred_element_type=FLOAT)


def contract_rows(left, right):
    return lax.dot_general(left, right, (((0,), (0,)), ((), ())), preferred_element_type=FLOAT)


def contract_cols(left, right):
    return lax.dot_general(left, right, (((1,), (1,)), ((), ())), preferred_element_type=FLOAT)


def reorder(blocks, order):
    hit = order[:, None] == jnp.arange(MP)[None, :]
    return jnp.sum(jnp.where(hit[:, :, None], blocks[..., None, :, :], 0), axis=-2)


def by_cols(value):
    return with_layout_constraint(value, Layout((1, 0)))


def tie(*values):
    return lax.optimization_barrier(values)


def group_gather(pair):
    own = [pair]
    for k in (1, 2, 3):
        own.append(lax.ppermute(pair, "z", [((i + k) % 4, i) for i in range(4) if (i + k) % 4 < i]))
    prev = []
    for k in range(4):
        pairs = []
        for i in range(3):
            for g in range(1, DP):
                pairs.append((((i + k) % 4) * DP + g - 1, i * DP + g))
        prev.append(lax.ppermute(pair, ("z",) + DP_AXES, pairs))
    return prev + own + [swap(part) for part in prev] + [swap(part) for part in own]


def group_scatter(prev, own, prev_far, own_far):
    own = (own.astype(FLOAT) + swap(own_far).astype(FLOAT)).astype(BFLOAT).reshape(4, TOK_DEV, -1)
    prev = (prev.astype(FLOAT) + swap(prev_far).astype(FLOAT)).astype(BFLOAT).reshape(4, TOK_DEV, -1)
    total = own[0].astype(FLOAT)
    for k in (1, 2, 3):
        pairs = [(i, (i + k) % 4) for i in range(4) if (i + k) % 4 < i]
        total = total + lax.ppermute(own[k], "z", pairs).astype(FLOAT)
    for k in range(4):
        pairs = []
        for i in range(3):
            for g in range(1, DP):
                pairs.append((i * DP + g, ((i + k) % 4) * DP + g - 1))
        total = total + lax.ppermute(prev[k], ("z",) + DP_AXES, pairs).astype(FLOAT)
    return total


def nn(left, right):
    return jnp.dot(left, right, preferred_element_type=FLOAT)


def head_rows(ref, head):
    return jnp.concatenate(
        [ref[:, 64 * (3 * head + i) : 64 * (3 * head + i) + 64] for i in range(3)], axis=0
    )


def head_lanes(ref, head):
    return jnp.concatenate(
        [ref[64 * (3 * head + i) : 64 * (3 * head + i) + 64, :] for i in range(3)], axis=1
    )


def turn(value, cosine, sine):
    parts = []
    for head in range(value.shape[0] // 64):
        first = value[64 * head : 64 * head + 32]
        second = value[64 * head + 32 : 64 * head + 64]
        parts.append(first * cosine - second * sine)
        parts.append(second * cosine + first * sine)
    return jnp.concatenate(parts, axis=0)


def normalize(values, weight):
    return values * lax.rsqrt(jnp.mean(values * values, axis=-1, keepdims=True) + EPS_NORM) * weight


def normalize_back(values, weight, grad_out):
    inverse = lax.rsqrt(jnp.mean(values * values, axis=-1, keepdims=True) + EPS_NORM)
    weighted = grad_out * weight
    grad_values = inverse * weighted - values * (inverse * inverse * inverse) * jnp.mean(
        weighted * values, axis=-1, keepdims=True
    )
    return grad_values, jnp.sum(grad_out * values * inverse, axis=0, keepdims=True)


def joined(refs, part, first):
    return jnp.concatenate(
        [ref[:, first : first + 64] for ref in refs[4 * part : 4 * part + 4]], axis=0
    )


def attend_kernel(query_ref, *refs):
    kv_refs, (bias_ref, out_ref, log_ref) = refs[:16], refs[16:]
    for head in range(KV_HEADS):
        queries = head_lanes(query_ref, head)
        top = None
        for part in range(4):
            keys = joined(kv_refs, part, 64 * head)
            values = joined(kv_refs, part, 320 + 64 * head)
            bias = bias_ref[512 * part : 512 * part + 512, :]
            scores = nn(keys, queries) + jnp.concatenate([bias, bias, bias], axis=1)
            part_top = jnp.max(scores, axis=0, keepdims=True)
            new_top = part_top if top is None else jnp.maximum(top, part_top)
            expo = jnp.exp(scores - new_top)
            part_total = jnp.sum(expo, axis=0, keepdims=True)
            part_out = contract_rows(values, expo.astype(BFLOAT))
            if top is None:
                total, out = part_total, part_out
            else:
                shrink = jnp.exp(top - new_top)
                total, out = total * shrink + part_total, out * shrink + part_out
            top = new_top
        out = (out / total).T.astype(BFLOAT)
        for i in range(3):
            place = 64 * (3 * head + i)
            out_ref[:, place : place + 64] = out[128 * i : 128 * i + 128]
        log_ref[head : head + 1, :] = top + jnp.log(total)


def params(mib):
    return pltpu.CompilerParams(vmem_limit_bytes=mib * 1024 * 1024)


def whole(*shape):
    return pl.BlockSpec(shape, lambda i: (0,) * len(shape))


def struct(kind, *shape):
    return jax.ShapeDtypeStruct(shape, kind)


def attend(queries, pairs, bias):
    return pl.pallas_call(
        attend_kernel,
        out_shape=(struct(BFLOAT, TOK_DEV, D), struct(FLOAT, 8, 3 * TOK_DEV)),
        cost_estimate=pl.CostEstimate(
            flops=12_000_000_000, bytes_accessed=5_000_000, transcendentals=4_000_000
        ),
        compiler_params=params(24),
    )(queries, *pairs, bias)


def attend_back_kernel(query_ref, *refs):
    kv_refs, refs = refs[:16], refs[16:]
    bias_ref, log_ref, att_ref, grad_ref, cos_ref, sin_ref, dq_ref = refs[:7]
    d_refs = refs[7:]
    cosine = jnp.concatenate([cos_ref[...]] * 3, axis=1)
    sine = jnp.concatenate([sin_ref[...]] * 3, axis=1)
    for head in range(KV_HEADS):
        queries = head_lanes(query_ref, head)
        grads = head_rows(grad_ref, head)
        outs = head_rows(att_ref, head)
        delta = jnp.sum((grads.astype(FLOAT) * outs.astype(FLOAT)).T, axis=0, keepdims=True)
        log_total = log_ref[head : head + 1, :]
        back = None
        for part, d_ref in enumerate(d_refs):
            keys = joined(kv_refs, part, 64 * head)
            values = joined(kv_refs, part, 320 + 64 * head)
            bias = bias_ref[512 * part : 512 * part + 512, :]
            probs = jnp.exp(
                nn(keys, queries) + jnp.concatenate([bias, bias, bias], axis=1) - log_total
            )
            grad_scores = (probs * (contract_cols(values, grads) - delta)).astype(BFLOAT)
            d_ref[:, 64 * head : 64 * head + 64] = contract_cols(grad_scores, queries).astype(BFLOAT)
            d_ref[:, 320 + 64 * head : 320 + 64 * head + 64] = nn(
                probs.astype(BFLOAT), grads
            ).astype(BFLOAT)
            part_back = contract_rows(keys, grad_scores)
            back = part_back if back is None else back + part_back
        back = turn(back * (HEAD_DIM**-0.5), cosine, -sine).T.astype(BFLOAT)
        for i in range(3):
            place = 64 * (3 * head + i)
            dq_ref[:, place : place + 64] = back[128 * i : 128 * i + 128]


def attend_back(queries, pairs, bias, log_total, attended, grads, cosine, sine):
    side = struct(BFLOAT, 4 * TOK_DEV, 640)
    return pl.pallas_call(
        attend_back_kernel,
        out_shape=(struct(BFLOAT, TOK_DEV, D), side, side, side, side),
        cost_estimate=pl.CostEstimate(
            flops=20_000_000_000, bytes_accessed=9_000_000, transcendentals=4_000_000
        ),
        compiler_params=params(24),
    )(queries, *pairs, bias, log_total, attended, grads, cosine, sine)


def project(hidden, gain, wq_ref, wk_ref, wv_ref, cos_ref, sin_ref, normed_ref, query_ref, pair_ref):
    normed = normalize(hidden, gain).astype(BFLOAT)
    normed_ref[...] = normed
    cosine, sine = cos_ref[...], sin_ref[...]
    keys = turn(nn(normed, wk_ref[...]).T, cosine, sine).T
    pair_ref[:, 0:320] = keys.astype(BFLOAT)
    pair_ref[:, 320:640] = nn(normed, wv_ref[...]).astype(BFLOAT)
    queries = turn(nn(normed, wq_ref[...]).T, cosine, sine)
    query_ref[...] = (queries * (HEAD_DIM**-0.5)).astype(BFLOAT)


PROJECTED = (
    struct(BFLOAT, TOK_DEV, D),
    struct(BFLOAT, D, TOK_DEV),
    struct(BFLOAT, TOK_DEV, 640),
)


def spread_kernel(place_ref, rows_ref, *out_refs):
    place = lax.broadcasted_iota(jnp.int32, (TOK_DEV, DP * CAP), 1)
    for part, ref in enumerate(out_refs):
        hot = (place_ref[128 * part : 128 * part + 128, :] == place).astype(FLOAT).astype(BFLOAT)
        ref[...] = nn(hot, rows_ref[...]).astype(BFLOAT)


def spread(place, rows):
    return pl.pallas_call(
        spread_kernel,
        out_shape=[struct(BFLOAT, TOK_DEV, D)] * MP,
        compiler_params=params(24),
    )(place, rows)


def collect_kernel(place_ref, *refs):
    place = lax.broadcasted_iota(jnp.int32, (TOK_DEV, DP * CAP), 1)
    total = None
    for part, ref in enumerate(refs[:-1]):
        hot = (place_ref[128 * part : 128 * part + 128, :] == place).astype(FLOAT).astype(BFLOAT)
        sums = contract_rows(hot, ref[...])
        total = sums if total is None else total + sums
    refs[-1][...] = total.astype(BFLOAT)


def collect(place, blocks):
    return pl.pallas_call(
        collect_kernel, out_shape=struct(BFLOAT, DP * CAP, D), compiler_params=params(24)
    )(place, *blocks)


def enter_kernel(hidden_ref, gain_ref, *refs):
    project(hidden_ref[...], gain_ref[0:1, :], *refs)


def enter(hidden, gains, wq, wk, wv, cosine, sine):
    return pl.pallas_call(enter_kernel, out_shape=PROJECTED, compiler_params=params(24))(
        hidden, gains, wq, wk, wv, cosine, sine
    )


BIG = 56
FF_BLOCK = 640
FF_STEPS = FF // FF_BLOCK


def weight(ref, which):
    return ref[:, which].reshape(FF_BLOCK, D)


def block_kernel(
    more, att_ref, hidden_ref, sel_ref, gain_ref, router_ref, wo_ref, weight_ref, *refs
):
    proj_in, refs = (refs[:5], refs[5:]) if more else ((), refs)
    mixed_ref, input_ref, gate_ref, up_ref, inner_ref, branch_ref, logit_ref, new_ref = refs[:8]
    proj_out, refs = (refs[8:11], refs[11:]) if more else ((), refs[8:])
    acc_ref = refs[0]
    step = pl.program_id(0)
    copies = [
        pltpu.make_async_copy(source, target, refs[4].at[i])
        for i, (source, target) in enumerate(zip(proj_in[:3], refs[1:4]))
    ]

    @pl.when(step == 0)
    def first():
        for copy in copies:
            copy.start()
        mixed = hidden_ref[...] + nn(att_ref[...], wo_ref[...])
        mixed_ref[...] = mixed
        input_ref[...] = normalize(mixed, gain_ref[1:2, :]).astype(BFLOAT)
        acc_ref[...] = mixed

    rows = input_ref[...]
    gate = contract_cols(rows, weight(weight_ref, 0))
    up = contract_cols(rows, weight(weight_ref, 1))
    gate_ref[...] = gate
    up_ref[...] = up
    inner = (gate * jax.nn.sigmoid(gate) * up).astype(BFLOAT)
    inner_ref[...] = inner
    acc_ref[...] += nn(inner, weight(weight_ref, 2))

    @pl.when(step == FF_STEPS - 1)
    def last():
        hidden = hidden_ref[...]
        branch = acc_ref[...]
        branch_ref[...] = branch
        logit = jnp.sum(hidden * router_ref[...], axis=1, keepdims=True)
        logit_ref[...] = logit
        new = hidden + sel_ref[...] * jax.nn.sigmoid(logit) * (branch - hidden)
        new_ref[...] = new
        for copy in copies:
            copy.wait()
        if more:
            project(new, gain_ref[0:1, :], *refs[1:4], *proj_in[3:], *proj_out)


WEIGHT_SPEC = pl.BlockSpec((FF_BLOCK // 80, 3, 80, D), lambda i: (i, 0, 0, 0))


def block(att, hidden, sel, gains, router, wo, weights, projections):
    more = projections is not None
    proj_specs = [pl.BlockSpec(memory_space=pl.ANY)] * 3 + [whole(32, 128), whole(32, 128)]
    rows = pl.BlockSpec((TOK_DEV, FF_BLOCK), lambda i: (0, i))
    return pl.pallas_call(
        functools.partial(block_kernel, more),
        grid=(FF_STEPS,),
        in_specs=[
            whole(TOK_DEV, D),
            whole(TOK_DEV, D),
            whole(TOK_DEV, 1),
            whole(8, D),
            whole(1, D),
            whole(D, D),
            WEIGHT_SPEC,
        ]
        + proj_specs * more,
        out_specs=[
            whole(TOK_DEV, D),
            whole(TOK_DEV, D),
            rows,
            rows,
            rows,
            whole(TOK_DEV, D),
            whole(TOK_DEV, 1),
            whole(TOK_DEV, D),
        ]
        + [whole(TOK_DEV, D), whole(D, TOK_DEV), whole(TOK_DEV, 640)] * more,
        out_shape=(
            struct(FLOAT, TOK_DEV, D),
            struct(BFLOAT, TOK_DEV, D),
            struct(FLOAT, TOK_DEV, FF),
            struct(FLOAT, TOK_DEV, FF),
            struct(BFLOAT, TOK_DEV, FF),
            struct(FLOAT, TOK_DEV, D),
            struct(FLOAT, TOK_DEV, 1),
            struct(FLOAT, TOK_DEV, D),
        )
        + (PROJECTED if more else ()),
        scratch_shapes=[pltpu.VMEM((TOK_DEV, D), FLOAT)]
        + [
            pltpu.VMEM((D, D), BFLOAT),
            pltpu.VMEM((D, 320), BFLOAT),
            pltpu.VMEM((D, 320), BFLOAT),
            pltpu.SemaphoreType.DMA((3,)),
        ]
        * more,
        cost_estimate=pl.CostEstimate(
            flops=4_000_000_000, bytes_accessed=20_000_000, transcendentals=400_000
        ),
        compiler_params=params(BIG),
    )(att, hidden, sel, gains, router, wo, weights, *(projections if more else ()))


def block_back_kernel(
    new_ref, sel_ref, logit_ref, hidden_ref, branch_ref, mixed_ref, gain_ref, router_ref, wo_ref,
    gate_ref, up_ref, weight_ref,
    rows_ref, dgate_ref, dup_ref, in_ref, attn_ref, back_ref, small_ref, acc_ref, held_ref, sem
):
    step = pl.program_id(0)
    sigma = jax.nn.sigmoid(logit_ref[...])
    chosen = sel_ref[...] * sigma
    copy = pltpu.make_async_copy(wo_ref, held_ref, sem)

    @pl.when(step == 0)
    def first():
        copy.start()
        rows_ref[...] = (chosen * new_ref[...]).astype(BFLOAT)
        acc_ref[...] = jnp.zeros_like(acc_ref)

    inner = contract_cols(rows_ref[...], weight(weight_ref, 2))
    gate = gate_ref[...]
    shape = jax.nn.sigmoid(gate)
    dgate = (inner * up_ref[...] * shape * (1.0 + gate * (1.0 - shape))).astype(BFLOAT)
    dup = (inner * gate * shape).astype(BFLOAT)
    dgate_ref[...] = dgate
    dup_ref[...] = dup
    acc_ref[...] += nn(dgate, weight(weight_ref, 0)) + nn(dup, weight(weight_ref, 1))

    @pl.when(step == FF_STEPS - 1)
    def last():
        grad_new = new_ref[...]
        hidden = hidden_ref[...]
        grad_branch = chosen * grad_new
        grad_weight = jnp.sum(grad_new * (branch_ref[...] - hidden), axis=1, keepdims=True)
        grad_logit = grad_weight * sel_ref[...] * sigma * (1.0 - sigma) + ROUTER_LOSS / TOK_DEV * (
            sigma - sel_ref[...]
        )
        grad_norm, gain_row = normalize_back(mixed_ref[...], gain_ref[1:2, :], acc_ref[...])
        grad_mixed = grad_branch + grad_norm
        in_ref[...] = grad_new - grad_branch + grad_logit * router_ref[...] + grad_mixed
        attn = grad_mixed.astype(BFLOAT)
        attn_ref[...] = attn
        copy.wait()
        back_ref[...] = contract_cols(attn, held_ref[...]).astype(BFLOAT)
        small_ref[0:1, :] = gain_row
        small_ref[1:2, :] = jnp.sum(grad_logit * hidden, axis=0, keepdims=True)
        small_ref[2:8, :] = jnp.zeros((6, D), FLOAT)


def block_back(new, sel, logit, hidden, branch, mixed, gains, router, wo, gate, up, weights):
    rows = pl.BlockSpec((TOK_DEV, FF_BLOCK), lambda i: (0, i))
    full = whole(TOK_DEV, D)
    return pl.pallas_call(
        block_back_kernel,
        grid=(FF_STEPS,),
        in_specs=[
            full,
            whole(TOK_DEV, 1),
            whole(TOK_DEV, 1),
            full,
            full,
            full,
            whole(8, D),
            whole(1, D),
            pl.BlockSpec(memory_space=pl.ANY),
            rows,
            rows,
            WEIGHT_SPEC,
        ],
        out_specs=[full, rows, rows, full, full, full, whole(8, D)],
        out_shape=(
            struct(BFLOAT, TOK_DEV, D),
            struct(BFLOAT, TOK_DEV, FF),
            struct(BFLOAT, TOK_DEV, FF),
            struct(FLOAT, TOK_DEV, D),
            struct(BFLOAT, TOK_DEV, D),
            struct(BFLOAT, TOK_DEV, D),
            struct(FLOAT, 8, D),
        ),
        scratch_shapes=[
            pltpu.VMEM((TOK_DEV, D), FLOAT),
            pltpu.VMEM((D, D), BFLOAT),
            pltpu.SemaphoreType.DMA,
        ],
        cost_estimate=pl.CostEstimate(
            flops=4_000_000_000, bytes_accessed=20_000_000, transcendentals=400_000
        ),
        compiler_params=params(BIG),
    )(new, sel, logit, hidden, branch, mixed, gains, router, wo, gate, up, weights)


def enter_back_kernel(
    in_ref, dq_ref, own_ref, hidden_ref, gain_ref, wq_ref, wk_ref, wv_ref, cos_ref, sin_ref,
    pair_ref, out_ref, small_ref
):
    keys = turn(own_ref[:, 0:320].T, cos_ref[...], -sin_ref[...]).T.astype(BFLOAT)
    values = own_ref[:, 320:640].astype(BFLOAT)
    pair_ref[:, 0:320] = keys
    pair_ref[:, 320:640] = values
    grad_normed = (
        contract_cols(dq_ref[...], wq_ref[...])
        + contract_cols(keys, wk_ref[...])
        + contract_cols(values, wv_ref[...])
    )
    grad_hidden, gain_row = normalize_back(hidden_ref[...], gain_ref[0:1, :], grad_normed)
    out_ref[...] = in_ref[...] + grad_hidden
    small_ref[...] = jnp.concatenate([gain_row, jnp.zeros((7, D), FLOAT)], axis=0)


def enter_back(grad_in, dq, own, hidden, gains, wq, wk, wv, cosine, sine):
    return pl.pallas_call(
        enter_back_kernel,
        out_shape=(
            struct(BFLOAT, TOK_DEV, 640),
            struct(FLOAT, TOK_DEV, D),
            struct(FLOAT, 8, D),
        ),
        compiler_params=params(24),
    )(grad_in, dq, own, hidden, gains, wq, wk, wv, cosine, sine)


HEAD_BLOCK = 1024


def head_kernel(rows_ref, near_ref, *refs):
    block_refs, (target_ref, table_ref, logit_ref, pick_ref, out_ref, stat_ref) = refs[:8], refs[8:]
    step = pl.program_id(0)

    @pl.when(step == 0)
    def first():
        picked = None
        for i, ref in enumerate(block_refs):
            hot = rows_ref[...] == near_ref[:, 128 * i : 128 * i + 128]
            part = nn(hot.astype(FLOAT).astype(BFLOAT), ref[...])
            picked = part if picked is None else picked + part
        pick_ref[...] = picked.astype(BFLOAT)
        lane = lax.broadcasted_iota(jnp.int32, (256, 128), 1)
        stat_ref[...] = jnp.where(lane == 0, MASKED, 0.0)

    logits = contract_cols(pick_ref[...], table_ref[...])
    logit_ref[...] = logits
    place = step * HEAD_BLOCK + lax.broadcasted_iota(jnp.int32, (256, HEAD_BLOCK), 1)
    hit = jnp.sum(jnp.where(place == target_ref[...], logits, 0.0), axis=1, keepdims=True)
    old = stat_ref[:, 0:1]
    top = jnp.maximum(old, jnp.max(logits, axis=1, keepdims=True))
    total = stat_ref[:, 1:2] * jnp.exp(old - top) + jnp.sum(
        jnp.exp(logits - top), axis=1, keepdims=True
    )
    stat_ref[:, 1:2] = total
    stat_ref[:, 2:3] = stat_ref[:, 2:3] + hit
    stat_ref[:, 0:1] = top

    @pl.when(step == pl.num_programs(0) - 1)
    def last():
        out_ref[...] = stat_ref[...].T[0:8]


def head(loss_rows, near_rows, blocks, local_targets, table):
    return pl.pallas_call(
        head_kernel,
        grid=(VOCAB_MP // HEAD_BLOCK,),
        in_specs=[whole(256, 1), whole(1, ROWS)]
        + [whole(TOK_DEV, D)] * MP
        + [whole(256, 1), pl.BlockSpec((HEAD_BLOCK, D), lambda i: (i, 0))],
        out_specs=[
            pl.BlockSpec((256, HEAD_BLOCK), lambda i: (0, i)),
            whole(256, D),
            whole(8, 256),
        ],
        out_shape=(
            struct(FLOAT, 256, VOCAB_MP),
            struct(BFLOAT, 256, D),
            struct(FLOAT, 8, 256),
        ),
        scratch_shapes=[pltpu.VMEM((256, 128), FLOAT)],
        compiler_params=params(BIG),
    )(loss_rows, near_rows, *blocks, local_targets, table)


def head_back_kernel(
    rows_ref, near_ref, target_ref, stat_ref, logit_ref, pick_ref, table_ref, grad_ref, *refs
):
    block_refs, (sum_ref, norm_ref) = refs[:8], refs[8:]
    step = pl.program_id(0)

    @pl.when(step == 0)
    def first():
        norm = stat_ref[0:1, :] + jnp.log(stat_ref[1:2, :])
        norm_ref[:, 0:8] = jnp.concatenate([norm] * 8, axis=0).T
        sum_ref[...] = jnp.zeros((256, D), FLOAT)

    place = step * HEAD_BLOCK + lax.broadcasted_iota(jnp.int32, (256, HEAD_BLOCK), 1)
    probs = jnp.exp(logit_ref[...] - norm_ref[:, 0:1])
    hit = jnp.where(place == target_ref[...], 1.0, 0.0)
    grads = ((probs - hit) * (1.0 / TOK_DEV)).astype(BFLOAT)
    grad_ref[...] = contract_rows(grads, pick_ref[...]).astype(BFLOAT)
    sum_ref[...] += nn(grads, table_ref[...])

    @pl.when(step == pl.num_programs(0) - 1)
    def last():
        total = sum_ref[...].astype(BFLOAT)
        for i, ref in enumerate(block_refs):
            hot = rows_ref[...] == near_ref[:, 128 * i : 128 * i + 128]
            ref[...] = contract_rows(hot.astype(FLOAT).astype(BFLOAT), total).astype(BFLOAT)


def head_back(loss_rows, near_rows, local_targets, stats, logits, picked, table):
    return pl.pallas_call(
        head_back_kernel,
        grid=(VOCAB_MP // HEAD_BLOCK,),
        in_specs=[
            whole(256, 1),
            whole(1, ROWS),
            whole(256, 1),
            whole(8, 256),
            pl.BlockSpec((256, HEAD_BLOCK), lambda i: (0, i)),
            whole(256, D),
            pl.BlockSpec((HEAD_BLOCK, D), lambda i: (i, 0)),
        ],
        out_specs=[pl.BlockSpec((HEAD_BLOCK, D), lambda i: (i, 0))] + [whole(TOK_DEV, D)] * MP,
        out_shape=[struct(BFLOAT, VOCAB_MP, D)] + [struct(BFLOAT, TOK_DEV, D)] * MP,
        scratch_shapes=[pltpu.VMEM((256, D), FLOAT), pltpu.VMEM((256, 128), FLOAT)],
        compiler_params=params(BIG),
    )(loss_rows, near_rows, local_targets, stats, logits, picked, table)


def mlp_grad_kernel(which_ref, *refs):
    out_ref = refs[-1]

    def joined(first):
        return jnp.concatenate([ref[...] for ref in refs[first:-1:10]], axis=0)

    def both(first):
        return jnp.concatenate([joined(first), joined(first + 5)], axis=0)

    rights = both(3), both(3), both(4)
    for i in range(3):
        out_ref[:, i] = contract_rows(both(i), rights[i]).reshape(8, 80, D).astype(BFLOAT)


def mlp_grads(which, kept, received):
    def cols(width, place):
        return pl.BlockSpec((TOK_DEV, width), place)

    rights = [cols(D, lambda i, half: (0, 0))] * 2
    own = [cols(640, lambda i, half: (0, half[0] * 2 + i))] * 3 + rights
    far = [cols(640, lambda i, half: (0, i))] * 3 + rights
    args = []
    for parts, other in zip(kept, received):
        args += [*parts, *other]
    return pl.pallas_call(
        mlp_grad_kernel,
        grid_spec=pltpu.PrefetchScalarGridSpec(
            num_scalar_prefetch=1,
            grid=(2,),
            in_specs=(own + far) * RECUR,
            out_specs=pl.BlockSpec((8, 3, 80, D), lambda i, half: (i, 0, 0, 0)),
        ),
        out_shape=struct(BFLOAT, 16, 3, 80, D),
        compiler_params=params(BIG),
    )(which.reshape(1), *args)


def square_grad_kernel(*refs):
    wq_ref, wo_ref = refs[-2:]
    ins = refs[:-2]

    def joined(first):
        return jnp.concatenate([ref[...] for ref in ins[first::8]], axis=0)

    def both(first):
        return jnp.concatenate([joined(first), joined(first + 4)], axis=0)

    wq_ref[...] = contract_rows(both(2), both(3)).astype(BFLOAT)
    wo_ref[...] = contract_rows(both(0), both(1)).astype(BFLOAT)


def square_grads(kept, received):
    args = []
    for parts, other in zip(kept, received):
        args += [*parts, *other]
    return pl.pallas_call(
        square_grad_kernel,
        grid=(1,),
        in_specs=[whole(TOK_DEV, D)] * (8 * RECUR),
        out_specs=[whole(D, D), whole(D, D)],
        out_shape=(struct(BFLOAT, D, D), struct(BFLOAT, D, D)),
        compiler_params=params(BIG),
    )(*args)


def pack_grad_kernel(starts_ref, *refs):
    wq_ref, wo_ref, rows_ref = refs[:3]
    ins = refs[3:-2]
    out_ref, buf = refs[-2:]
    buf[0:960, :] = wq_ref[...]
    buf[1600:2560, :] = wo_ref[...]
    buf[2560:2576, :] = rows_ref[...].astype(BFLOAT)
    buf[2576:2688, :] = jnp.zeros((112, D), BFLOAT)
    normed = jnp.concatenate([ref[...] for ref in ins[0::4] + ins[1::4]], axis=0)
    grads = jnp.concatenate([ref[...] for ref in ins[2::4] + ins[3::4]], axis=0)
    line = lax.broadcasted_iota(jnp.int32, (960, 320), 0)
    place = lax.broadcasted_iota(jnp.int32, (960, 320), 1)
    full = contract_rows(normed, grads).astype(BFLOAT)
    for i in range(3):
        chosen = (line == 3 * place + i).astype(FLOAT).astype(BFLOAT)
        rows = contract_rows(chosen, full).astype(BFLOAT)
        buf[960:1280, 320 * i : 320 * i + 320] = rows[:, 0:320]
        buf[1280:1600, 320 * i : 320 * i + 320] = rows[:, 320:640]
    for i in range(4):
        start = pl.multiple_of(starts_ref[i], 16)
        out_ref[i] = buf[pl.ds(start, 352), :]


def pack_grads(starts, wq, wo, small, kept, received):
    args = []
    for (normed, pair), (far_normed, far_pair) in zip(kept, received):
        args += [normed, far_normed, pair, far_pair]
    specs = [whole(TOK_DEV, D)] * 2 + [whole(TOK_DEV, 640)] * 2
    return pl.pallas_call(
        pack_grad_kernel,
        grid=(1,),
        in_specs=[pl.BlockSpec(memory_space=pltpu.SMEM), whole(D, D), whole(D, D), whole(16, D)]
        + specs * RECUR,
        out_specs=whole(4, 352, D),
        out_shape=struct(BFLOAT, 4, 352, D),
        scratch_shapes=[pltpu.VMEM((PACK_PAD, D), BFLOAT)],
        compiler_params=params(BIG),
    )(starts, wq, wo, small, *args)


def adam_update(master, first, second, grad, clip):
    grad = grad * clip
    first_new = BETA_ONE * first + (1.0 - BETA_ONE) * grad
    second_new = BETA_TWO * second + (1.0 - BETA_TWO) * grad * grad
    corr_one = 1.0 - BETA_ONE**STEP
    corr_two = 1.0 - BETA_TWO**STEP
    master_new = master - LEARN_RATE * (
        first_new / corr_one / (jnp.sqrt(second_new / corr_two) + ADAM_EPS) + DECAY * master
    )
    return (master_new, first_new, second_new)


def pack_row(device):
    return (1283 * device) // 64


def join_kernel(blocks_ref, wq_ref, wk_ref, wv_ref, wo_ref, small_ref, buf):
    row = lax.broadcasted_iota(jnp.int32, (128, 240), 0)
    place = lax.broadcasted_iota(jnp.int32, (128, 240), 1)
    device = (place * 2731) >> 16
    for step in range(PACK_PAD // 128):
        first = min(step * 128 * 64 // 1283, 118) // 2 * 2
        source = ((1283 * (first + device)) >> 6) + place - 24 * device
        chosen = (source == row + 128 * step).astype(FLOAT).astype(BFLOAT)
        buf[128 * step : 128 * step + 128, :] = nn(
            chosen, blocks_ref[24 * first : 24 * first + 240, :]
        ).astype(BFLOAT)
    wq_ref[...] = buf[0:960, :]
    wo_ref[...] = buf[1600:2560, :]
    small_ref[...] = buf[2560:2576, :]
    line = lax.broadcasted_iota(jnp.int32, (960, 320), 0)
    place = lax.broadcasted_iota(jnp.int32, (960, 320), 1)
    for first, ref in ((960, wk_ref), (1280, wv_ref)):
        total = None
        for i in range(3):
            chosen = (line == 3 * place + i).astype(FLOAT).astype(BFLOAT)
            part = nn(chosen, buf[first : first + 320, 320 * i : 320 * i + 320])
            total = part if total is None else total + part
        ref[...] = total.astype(BFLOAT)


def join_pack(blocks):
    return pl.pallas_call(
        join_kernel,
        out_shape=(
            struct(BFLOAT, D, D),
            struct(BFLOAT, D, 320),
            struct(BFLOAT, D, 320),
            struct(BFLOAT, D, D),
            struct(BFLOAT, 16, D),
        ),
        scratch_shapes=[pltpu.VMEM((PACK_PAD, D), BFLOAT)],
        compiler_params=params(32),
    )(blocks)


def stage(value, axis, index):
    total = lax.dynamic_index_in_dim(value, index, 0, False).astype(FLOAT)
    for k in (1, 2, 3):
        sent = lax.dynamic_index_in_dim(value, (index + k) % 4, 0, False)
        total = total + shift(sent, axis, k).astype(FLOAT)
    return total


def gradients(
    dense,
    token_ids,
    targets,
    loss_rows,
    selections,
    boundary,
    pack_master,
    mlp_master,
    table_master,
):
    z = lax.axis_index("z")
    core = lax.axis_index("core")
    y = lax.axis_index("y")
    x = lax.axis_index("x")
    model_index = z * 2 + core
    data_index = y * 4 + x
    device = model_index * DP + data_index
    own_table = table_master.astype(BFLOAT)

    near = jnp.stack([((z + k) % 4) * 2 + (core ^ j) for j in (0, 1) for k in range(4)])
    near_rows = (near[:, None] * TOK_DEV + jnp.arange(TOK_DEV, dtype=jnp.int32)[None, :]).reshape(-1)

    pack_offset = PACK_DEV * device - D * pack_row(device)
    pack_block = lax.dynamic_update_slice(
        jnp.zeros((24 * D,), BFLOAT), pack_master.astype(BFLOAT), (pack_offset,)
    ).reshape(24, D)
    pack_quad = [pack_block] + [shift(pack_block, "x", k) for k in (1, 2, 3)]
    pack_rows = []
    for i in range(4):
        part = pack_quad[3]
        for k in (2, 1, 0):
            part = jnp.where(x == (i + k) % 4, pack_quad[k], part)
        pack_rows.append(part)
    pack_blocks = lax.all_gather(
        jnp.concatenate(pack_rows, axis=0), ("z", "core", "y"), axis=0, tiled=True
    )
    mlp_own = mlp_master.astype(BFLOAT)
    mlp_quad = jnp.concatenate([mlp_own] + [shift(mlp_own, "x", k) for k in (1, 2, 3)], axis=1)

    group_ids = token_ids[0]
    near_ids = reorder(group_ids.reshape(MP, TOK_DEV), near).reshape(-1)
    local_ids = near_ids - model_index * VOCAB_MP
    inside = (local_ids >= 0) & (local_ids < VOCAB_MP)
    high = local_ids >> 7
    low = local_ids & 127
    high_hot = (high[:, None] == jnp.arange(48)[None, :]).astype(BFLOAT)
    low_hot = (low[:, None] == jnp.arange(128)[None, :]).astype(BFLOAT)
    present = (contract_rows(high_hot, low_hot) > 0).reshape(DP, VOCAB_DEV)
    before = (jnp.arange(VOCAB_DEV)[:, None] < jnp.arange(VOCAB_DEV)[None, :]).astype(BFLOAT)
    slots = mm(present.astype(BFLOAT), before)
    asked = present & (slots < CAP)
    over = jnp.max(jnp.where(present & (slots >= CAP), 1.0, 0.0))
    slot_table = jnp.where(asked, slots, 255.0).reshape(48, 128).astype(BFLOAT)
    token_slot = jnp.sum(mm(high_hot, slot_table) * low_hot.astype(FLOAT), axis=-1)
    token_place = jnp.where(
        inside & (token_slot < CAP), (high // 3) * CAP + token_slot.astype(jnp.int32), -1
    )
    token_place = token_place[:, None]
    match = asked[:, None, :] & (slots[:, None, :] == jnp.arange(CAP, dtype=FLOAT)[None, :, None])
    request = (
        jnp.sum(jnp.where(match, jnp.arange(1, VOCAB_DEV + 1, dtype=FLOAT)[None, None, :], 0.0), axis=-1)
        - 1.0
    )
    request = jnp.concatenate([request, jnp.full((DP, 8), over, FLOAT)], axis=1)
    request = lax.all_to_all(request, DP_AXES, 0, 0, tiled=True)
    over = jnp.max(request[:, CAP:])
    owner_hot = (
        request[:, :CAP].reshape(-1)[:, None] == jnp.arange(VOCAB_DEV, dtype=FLOAT)[None, :]
    ).astype(BFLOAT)
    mlp_quad, owner_hot = tie(mlp_quad, owner_hot)
    mlp_weights = lax.all_gather(
        mlp_quad.reshape(3 * 80, D), ("core", "z", "y"), axis=0, tiled=True
    )
    mlp_weights = mlp_weights.reshape(32, 3, 80, D)
    asked_rows = lax.all_to_all(mm(owner_hot, own_table).astype(BFLOAT), DP_AXES, 0, 0, tiled=True)
    own_table, asked_rows = tie(own_table, asked_rows)
    table = lax.all_gather(own_table, DP_AXES, axis=0, tiled=True)
    if dense:
        rows = jnp.take(table, jnp.clip(local_ids, 0, VOCAB_MP - 1), axis=0)
        looked = jnp.where(inside[:, None], rows, jnp.zeros_like(rows))
        looked = [looked[128 * i : 128 * i + 128] for i in range(MP)]
    else:
        looked = spread(token_place, asked_rows)
    hidden, pack_blocks = scatter_group(looked, pack_blocks)

    w_query, w_key, w_value, w_out, last_rows = join_pack(pack_blocks)
    gains = jnp.concatenate([last_rows[:3].astype(FLOAT), jnp.zeros((5, D), FLOAT)])
    router = last_rows[3:6].astype(FLOAT)

    half_dim = HEAD_DIM // 2
    freqs = ROPE_BASE ** (-jnp.arange(half_dim, dtype=FLOAT) / half_dim)
    first_row = data_index * ROWS + model_index * TOK_DEV
    angles = freqs[:, None] * (first_row + jnp.arange(TOK_DEV, dtype=jnp.int32)).astype(FLOAT)[None, :]
    turns = (jnp.cos(angles), jnp.sin(angles))
    projections = (w_query, w_key, w_value) + turns
    group_sel = selections.reshape(RECUR, DP, MP, TOK_DEV)
    prev_index = jnp.maximum(data_index - 1, 0)
    here_sel = lax.dynamic_index_in_dim(group_sel, data_index, 1, False)
    own_sel = lax.dynamic_index_in_dim(here_sel, model_index, 1, False)
    near_sel = reorder(here_sel, near).reshape(RECUR, ROWS)
    prev_sel = reorder(lax.dynamic_index_in_dim(group_sel, prev_index, 1, False), near)
    prev_sel = prev_sel.reshape(RECUR, ROWS)
    start = lax.dynamic_index_in_dim(boundary, data_index, 0, False)
    prev_start = lax.dynamic_index_in_dim(boundary, prev_index, 0, False)
    place = (model_index * TOK_DEV + jnp.arange(TOK_DEV, dtype=jnp.int32))[None, :]
    key_place = near_rows[:, None]
    biases = []
    for step in range(RECUR):
        own_seen = (
            (key_place <= place)
            & ((key_place < start) == (place < start))
            & ((near_sel[step][:, None] > 0) | (key_place == place))
        )
        prev_seen = (
            (data_index > 0)
            & (place < start)
            & (key_place >= prev_start)
            & (prev_sel[step][:, None] > 0)
        )
        seen = [prev_seen[:512], own_seen[:512], prev_seen[512:], own_seen[512:]]
        biases.append(jnp.where(jnp.concatenate(seen, axis=0), 0.0, MASKED))

    sel_cols = own_sel.astype(FLOAT)[:, :, None]
    saves = []
    logits_all = []
    normed, queries, pair = enter(hidden, gains, *projections)
    for step in range(RECUR):
        pairs = group_gather(pair)
        attended, log_total = attend(queries, pairs, biases[step])
        mixed, mlp_input, gate, up, inner, branch, logit, new_hidden, *nexts = block(
            attended,
            hidden,
            sel_cols[step],
            gains,
            router[step : step + 1],
            w_out,
            mlp_weights,
            projections if step < RECUR - 1 else None,
        )
        logits_all.append(logit[:, 0])
        saves.append(
            (
                hidden,
                normed,
                queries,
                pairs,
                attended,
                log_total,
                mixed,
                mlp_input,
                gate,
                up,
                inner,
                branch,
                logit,
            )
        )
        hidden = new_hidden
        if nexts:
            normed, queries, pair = nexts
    logits_all = jnp.stack(logits_all)
    penalty_total = jnp.sum(jax.nn.softplus(logits_all) - own_sel.astype(FLOAT) * logits_all)

    normed_final = rms_scale(hidden, gains[2]).astype(BFLOAT)
    final_rows = gather_group(normed_final)
    row_targets = lax.dynamic_index_in_dim(targets, data_index, 0, keepdims=False)
    head_args = (loss_rows[0][:, None], near_rows[None, :])
    local_targets = (row_targets - model_index * VOCAB_MP)[:, None]
    logits, picked, stats = head(*head_args, final_rows, local_targets, table)
    flag_row = lax.broadcasted_iota(jnp.int32, (8, 256), 0) == 3
    stats = jnp.where(flag_row, over, stats)

    def join_stats(parts):
        top = parts[0][0]
        for part in parts[1:]:
            top = jnp.maximum(top, part[0])
        total = sum(part[1] * jnp.exp(part[0] - top) for part in parts)
        over = parts[0][3]
        for part in parts[1:]:
            over = jnp.maximum(over, part[3])
        rest = [jnp.zeros_like(top)] * 4
        return jnp.stack([top, total, sum(part[2] for part in parts), over] + rest)

    stats = join_stats([stats, swap(stats)])
    stats = join_stats([stats] + [shift(stats, "z", k) for k in (1, 2, 3)])
    log_norm = stats[0] + jnp.log(stats[1])
    cross = log_norm - stats[2]
    per_device = cross.shape[0] // MP
    loss_part = (
        jnp.sum(lax.dynamic_slice_in_dim(cross, model_index * per_device, per_device))
        + ROUTER_LOSS * penalty_total
    )
    head_grad, *scattered = head_back(*head_args, local_targets, stats, logits, picked, table)
    grad_final = scatter_group(scattered)
    grad_hidden, grad_gain_final = rms_back(hidden, gains[2], grad_final)
    if not dense:
        head_grad = lax.psum_scatter(head_grad, DP_AXES, scatter_dimension=0, tiled=True)

    mlp_kept, mlp_far, square_kept, square_far, pack_kept, pack_far = [], [], [], [], [], []
    loss_part, flag, grad_hidden = tie(loss_part, stats[3, 0], grad_hidden)
    router_rows = [None] * RECUR
    gain_one = jnp.zeros((1, D), FLOAT)
    gain_two = jnp.zeros((1, D), FLOAT)
    for step in reversed(range(RECUR)):
        (
            hidden_in,
            normed,
            queries,
            pairs,
            attended,
            log_total,
            mixed,
            mlp_input,
            gate,
            up,
            inner,
            branch,
            logit,
        ) = saves[step]
        grad_rows, grad_gate, grad_up, grad_in, grad_attn, grad_attended, small = block_back(
            grad_hidden,
            sel_cols[step],
            logit,
            hidden_in,
            branch,
            mixed,
            gains,
            router[step : step + 1],
            w_out,
            gate,
            up,
            mlp_weights,
        )
        gain_two = gain_two + small[0:1]
        router_rows[step] = small[1:2]
        mlp_kept.append((grad_gate, grad_up, inner, mlp_input, grad_rows))

        def far_half(value):
            return lax.dynamic_slice_in_dim(value, (1 - core) * (FF // 2), FF // 2, 1)

        mlp_far.append(
            [swap(far_half(part)) for part in (grad_gate, grad_up, inner)]
            + [swap(mlp_input), swap(grad_rows)]
        )
        grad_query, *grad_sides = attend_back(
            queries, pairs, biases[step], log_total, attended, grad_attended, *turns
        )
        far_normed = swap(normed)
        square_kept.append((attended, grad_attn, normed, grad_query))
        square_far.append((swap(attended), swap(grad_attn), far_normed, swap(grad_query)))
        if step == 0:
            tied = tie(*grad_sides, *mlp_kept[-1])
            grad_sides, mlp_kept[-1] = tied[:4], tied[4:]
        grad_own = group_scatter(*grad_sides)
        if step == 0:
            mlp_half = mlp_grads(core.astype(jnp.int32), mlp_kept, mlp_far)
            mlp_sum = lax.psum_scatter(
                mlp_half.reshape(16 * 240, D), ("z", "y"), scatter_dimension=0, tiled=True
            )
            squares = square_grads(square_kept, square_far)
            grad_own, mlp_half, *squares = tie(grad_own, mlp_half, *squares)
        grad_pair, grad_hidden, small = enter_back(
            grad_in, grad_query, grad_own, hidden_in, gains, *projections
        )
        gain_one = gain_one + small[0:1]
        pack_kept.append((normed, grad_pair))
        pack_far.append((far_normed, swap(grad_pair)))
        if step == 1 and not dense:
            head_grad, grad_hidden = tie(head_grad, grad_hidden)

    def aligned_row(which):
        return (pack_row(which) // 16) * 16

    small = jnp.concatenate(
        [
            gain_one,
            gain_two,
            grad_gain_final[None],
            *router_rows,
            jnp.zeros((10, D), FLOAT),
        ]
    )
    small = small + swap(small)
    starts = jnp.stack([aligned_row(DP * (2 * i + core)) for i in range(4)]).astype(jnp.int32)
    part = pack_grads(starts, *squares, small, pack_kept, pack_far)

    def y_windows(value):
        return jnp.stack([value[..., 80 * i : 80 * i + 112, :] for i in range(4)])

    def x_windows(value):
        return jnp.stack([value[..., i : i + 48, :] for i in (0, 16, 40, 56)])

    part = stage(part, "z", z).astype(BFLOAT)
    part = stage(y_windows(part), "y", y).astype(BFLOAT)
    part, mlp_sum = tie(x_windows(part), mlp_sum)
    mlp_sum = mlp_sum.reshape(3, 4, UNITS, D).transpose(1, 0, 2, 3).reshape(4, 3 * UNITS, D)

    def toward(k):
        mine = lax.dynamic_index_in_dim(part, (x + k) % 4, 0, False)
        return jnp.concatenate([mine, mlp_sum[(4 - k) % 4]], axis=0)

    total = toward(0).astype(FLOAT)
    for k in (1, 2, 3):
        total = total + shift(toward(k), "x", k).astype(FLOAT)
    part = total[:48].reshape(-1)
    mlp_grad = total[48:].reshape(3, UNITS, D)
    begin = aligned_row(DP * model_index) + 80 * y + (20 * x) // 8 * 8
    pack_grad = lax.dynamic_slice(part, (PACK_DEV * device - D * begin,), (PACK_DEV,))

    grad_embed = gather_group(grad_hidden.astype(BFLOAT))
    if dense:
        kept_rows = jnp.concatenate(grad_embed).astype(FLOAT) * inside.astype(FLOAT)[:, None]
        sums = jax.ops.segment_sum(
            kept_rows, jnp.clip(local_ids, 0, VOCAB_MP - 1), num_segments=VOCAB_MP
        )
        table_grad = lax.psum_scatter(
            (head_grad.astype(FLOAT) + sums).astype(BFLOAT),
            DP_AXES,
            scatter_dimension=0,
            tiled=True,
        ).astype(FLOAT)
    else:
        unique = collect(token_place, grad_embed)
        unique = lax.all_to_all(unique, DP_AXES, 0, 0, tiled=True)
        table_grad = head_grad.astype(FLOAT) + contract_rows(owner_hot, unique)
    table_grad = by_cols(table_grad)
    squares = (
        jnp.sum(pack_grad * pack_grad)
        + jnp.sum(mlp_grad * mlp_grad)
        + jnp.sum(table_grad * table_grad)
    )
    return pack_grad, mlp_grad, table_grad, squares, loss_part, flag


def shards(
    token_ids,
    targets,
    loss_rows,
    selections,
    boundary,
    pack_master,
    pack_first,
    pack_second,
    mlp_master,
    mlp_first,
    mlp_second,
    table_master,
    table_first,
    table_second,
):
    args = (
        token_ids,
        targets,
        loss_rows,
        selections,
        boundary,
        pack_master,
        mlp_master,
        table_master,
    )
    *found, over = tie(*gradients(False, *args))
    pack_grad, mlp_grad, table_grad, squares, loss_part = lax.cond(
        over > 0, lambda: gradients(True, *args)[:5], lambda: tuple(found)
    )
    lane = lax.broadcasted_iota(jnp.int32, (128, 128), 1)
    sums = lax.all_to_all(
        jnp.where(lane == 0, squares, loss_part), ALL_AXES, 0, 0, tiled=True
    )
    sums = jnp.sum(sums, axis=0, keepdims=True)
    total_squares = sums[0, 0]
    loss_sum = sums[0, 1]
    grad_norm = jnp.sqrt(total_squares)
    clip = CLIP_NORM / jnp.maximum(grad_norm, CLIP_NORM)
    pack_new, pack_first_new, pack_second_new = adam_update(
        pack_master, pack_first, pack_second, pack_grad, clip
    )
    mlp_new, mlp_first_new, mlp_second_new = adam_update(
        mlp_master, mlp_first, mlp_second, mlp_grad, clip
    )
    table_new, table_first_new, table_second_new = adam_update(
        table_master, table_first, table_second, table_grad, clip
    )
    return (
        pack_new,
        pack_first_new,
        pack_second_new,
        mlp_new,
        mlp_first_new,
        mlp_second_new,
        table_new,
        table_first_new,
        table_second_new,
        loss_sum,
        grad_norm,
    )


def solution(mesh):
    grid = Mesh(mesh.devices.reshape(4, 2, 4, 4), ALL_AXES)
    owners = (P(ALL_AXES), P(None, ALL_AXES, None), P(ALL_AXES, None))
    group = P(DP_AXES, None)
    masters = tuple(spec for spec in owners for _ in range(3))
    return jax.shard_map(
        shards,
        mesh=grid,
        in_specs=(group, P(), group, P(), P()) + masters,
        out_specs=masters + (P(), P()),
        check_vma=False,
    )
```

```python
import functools

import jax
import jax.numpy as jnp
from jax import lax
from jax.experimental import pallas as pl
from jax.experimental.layout import Layout, with_layout_constraint
from jax.experimental.pallas import tpu as pltpu
from jax.sharding import Mesh
from jax.sharding import PartitionSpec as P

D = 960
HEADS = 15
KV_HEADS = 5
HEAD_DIM = 64
FF = 2560
RECUR = 3
STEP = 10
TOK_DEV = 128
ROWS = 1024
MP = 8
DP = 16
VOCAB_MP = 6144
VOCAB_DEV = 384
UNITS = 20
PACK_DEV = 19245
PACK_ROWS = 2566
PACK_PAD = 2688
CAP = 24

EPS_NORM = 1e-05
ROPE_BASE = 10000.0
ROUTER_LOSS = 0.1
CLIP_NORM = 1.0
LEARN_RATE = 0.05
BETA_ONE = 0.9
BETA_TWO = 0.95
ADAM_EPS = 1e-08
DECAY = 0.1
MASKED = -1e30
HIGHEST = lax.Precision.HIGHEST
BFLOAT = jnp.bfloat16
FLOAT = jnp.float32
DP_AXES = ("y", "x")
ALL_AXES = ("z", "core", "y", "x")


def shift(value, axis, steps):
    return lax.ppermute(value, axis, [(i, (i + steps) % 4) for i in range(4)])


def swap(value):
    return lax.ppermute(value, "core", [(0, 1), (1, 0)])


def gather_group(value):
    near = [value] + [shift(value, "z", -k) for k in (1, 2, 3)]
    return near + [swap(part) for part in near]


def scatter_group(blocks, other=None):
    half = [near.astype(FLOAT) + swap(far).astype(FLOAT) for near, far in zip(blocks[:4], blocks[4:])]
    total = half[0]
    sent = [part.astype(BFLOAT) for part in half[1:]]
    if other is not None:
        *sent, other = tie(*sent, other)
    for k in (1, 2, 3):
        total = total + shift(sent[k - 1], "z", k).astype(FLOAT)
    return total if other is None else (total, other)


def rms_scale(values, weight):
    return values * lax.rsqrt(jnp.mean(values * values, axis=-1, keepdims=True) + EPS_NORM) * weight


def rms_back(values, weight, grad_out):
    inverse = lax.rsqrt(jnp.mean(values * values, axis=-1, keepdims=True) + EPS_NORM)
    weighted = grad_out * weight
    grad_values = inverse * weighted - values * (inverse * inverse * inverse) * jnp.mean(
        weighted * values, axis=-1, keepdims=True
    )
    return (grad_values, jnp.sum(grad_out * values * inverse, axis=0))


def mm(left, right):
    return jnp.dot(left, right, preferred_element_type=FLOAT)


def contract_rows(left, right):
    return lax.dot_general(left, right, (((0,), (0,)), ((), ())), preferred_element_type=FLOAT)


def contract_cols(left, right):
    return lax.dot_general(left, right, (((1,), (1,)), ((), ())), preferred_element_type=FLOAT)


def reorder(blocks, order):
    hit = order[:, None] == jnp.arange(MP)[None, :]
    return jnp.sum(jnp.where(hit[:, :, None], blocks[..., None, :, :], 0), axis=-2)


def by_cols(value):
    return with_layout_constraint(value, Layout((1, 0)))


def tie(*values):
    return lax.optimization_barrier(values)


def group_gather(pair):
    own = [pair]
    for k in (1, 2, 3):
        own.append(lax.ppermute(pair, "z", [((i + k) % 4, i) for i in range(4) if (i + k) % 4 < i]))
    prev = []
    for k in range(4):
        pairs = []
        for i in range(3):
            for g in range(1, DP):
                pairs.append((((i + k) % 4) * DP + g - 1, i * DP + g))
        prev.append(lax.ppermute(pair, ("z",) + DP_AXES, pairs))
    return prev + own + [swap(part) for part in prev] + [swap(part) for part in own]


def group_scatter(prev, own, prev_far, own_far):
    own = (own.astype(FLOAT) + swap(own_far).astype(FLOAT)).astype(BFLOAT).reshape(4, TOK_DEV, -1)
    prev = (prev.astype(FLOAT) + swap(prev_far).astype(FLOAT)).astype(BFLOAT).reshape(4, TOK_DEV, -1)
    total = own[0].astype(FLOAT)
    for k in (1, 2, 3):
        pairs = [(i, (i + k) % 4) for i in range(4) if (i + k) % 4 < i]
        total = total + lax.ppermute(own[k], "z", pairs).astype(FLOAT)
    for k in range(4):
        pairs = []
        for i in range(3):
            for g in range(1, DP):
                pairs.append((i * DP + g, ((i + k) % 4) * DP + g - 1))
        total = total + lax.ppermute(prev[k], ("z",) + DP_AXES, pairs).astype(FLOAT)
    return total


def nn(left, right):
    return jnp.dot(left, right, preferred_element_type=FLOAT)


def head_rows(ref, head):
    return jnp.concatenate(
        [ref[:, 64 * (3 * head + i) : 64 * (3 * head + i) + 64] for i in range(3)], axis=0
    )


def head_lanes(ref, head):
    return jnp.concatenate(
        [ref[64 * (3 * head + i) : 64 * (3 * head + i) + 64, :] for i in range(3)], axis=1
    )


def turn(value, cosine, sine):
    parts = []
    for head in range(value.shape[0] // 64):
        first = value[64 * head : 64 * head + 32]
        second = value[64 * head + 32 : 64 * head + 64]
        parts.append(first * cosine - second * sine)
        parts.append(second * cosine + first * sine)
    return jnp.concatenate(parts, axis=0)


def normalize(values, weight):
    return values * lax.rsqrt(jnp.mean(values * values, axis=-1, keepdims=True) + EPS_NORM) * weight


def normalize_back(values, weight, grad_out):
    inverse = lax.rsqrt(jnp.mean(values * values, axis=-1, keepdims=True) + EPS_NORM)
    weighted = grad_out * weight
    grad_values = inverse * weighted - values * (inverse * inverse * inverse) * jnp.mean(
        weighted * values, axis=-1, keepdims=True
    )
    return grad_values, jnp.sum(grad_out * values * inverse, axis=0, keepdims=True)


def joined(refs, part, first):
    return jnp.concatenate(
        [ref[:, first : first + 64] for ref in refs[4 * part : 4 * part + 4]], axis=0
    )


def attend_kernel(query_ref, *refs):
    kv_refs, (bias_ref, out_ref, log_ref) = refs[:16], refs[16:]
    for head in range(KV_HEADS):
        queries = head_lanes(query_ref, head)
        top = None
        for part in range(4):
            keys = joined(kv_refs, part, 64 * head)
            values = joined(kv_refs, part, 320 + 64 * head)
            bias = bias_ref[512 * part : 512 * part + 512, :]
            scores = nn(keys, queries) + jnp.concatenate([bias, bias, bias], axis=1)
            part_top = jnp.max(scores, axis=0, keepdims=True)
            new_top = part_top if top is None else jnp.maximum(top, part_top)
            expo = jnp.exp(scores - new_top)
            part_total = jnp.sum(expo, axis=0, keepdims=True)
            part_out = contract_rows(values, expo.astype(BFLOAT))
            if top is None:
                total, out = part_total, part_out
            else:
                shrink = jnp.exp(top - new_top)
                total, out = total * shrink + part_total, out * shrink + part_out
            top = new_top
        out = (out / total).T.astype(BFLOAT)
        for i in range(3):
            place = 64 * (3 * head + i)
            out_ref[:, place : place + 64] = out[128 * i : 128 * i + 128]
        log_ref[head : head + 1, :] = top + jnp.log(total)


def params(mib):
    return pltpu.CompilerParams(vmem_limit_bytes=mib * 1024 * 1024)


def whole(*shape):
    return pl.BlockSpec(shape, lambda i: (0,) * len(shape))


def struct(kind, *shape):
    return jax.ShapeDtypeStruct(shape, kind)


def attend(queries, pairs, bias):
    return pl.pallas_call(
        attend_kernel,
        out_shape=(struct(BFLOAT, TOK_DEV, D), struct(FLOAT, 8, 3 * TOK_DEV)),
        cost_estimate=pl.CostEstimate(
            flops=12_000_000_000, bytes_accessed=5_000_000, transcendentals=4_000_000
        ),
        compiler_params=params(24),
    )(queries, *pairs, bias)


def attend_back_kernel(query_ref, *refs):
    kv_refs, refs = refs[:16], refs[16:]
    bias_ref, log_ref, att_ref, grad_ref, cos_ref, sin_ref, dq_ref = refs[:7]
    d_refs = refs[7:]
    cosine = jnp.concatenate([cos_ref[...]] * 3, axis=1)
    sine = jnp.concatenate([sin_ref[...]] * 3, axis=1)
    for head in range(KV_HEADS):
        queries = head_lanes(query_ref, head)
        grads = head_rows(grad_ref, head)
        outs = head_rows(att_ref, head)
        delta = jnp.sum((grads.astype(FLOAT) * outs.astype(FLOAT)).T, axis=0, keepdims=True)
        log_total = log_ref[head : head + 1, :]
        back = None
        for part, d_ref in enumerate(d_refs):
            keys = joined(kv_refs, part, 64 * head)
            values = joined(kv_refs, part, 320 + 64 * head)
            bias = bias_ref[512 * part : 512 * part + 512, :]
            probs = jnp.exp(
                nn(keys, queries) + jnp.concatenate([bias, bias, bias], axis=1) - log_total
            )
            grad_scores = (probs * (contract_cols(values, grads) - delta)).astype(BFLOAT)
            d_ref[:, 64 * head : 64 * head + 64] = contract_cols(grad_scores, queries).astype(BFLOAT)
            d_ref[:, 320 + 64 * head : 320 + 64 * head + 64] = nn(
                probs.astype(BFLOAT), grads
            ).astype(BFLOAT)
            part_back = contract_rows(keys, grad_scores)
            back = part_back if back is None else back + part_back
        back = turn(back * (HEAD_DIM**-0.5), cosine, -sine).T.astype(BFLOAT)
        for i in range(3):
            place = 64 * (3 * head + i)
            dq_ref[:, place : place + 64] = back[128 * i : 128 * i + 128]


def attend_back(queries, pairs, bias, log_total, attended, grads, cosine, sine):
    side = struct(BFLOAT, 4 * TOK_DEV, 640)
    return pl.pallas_call(
        attend_back_kernel,
        out_shape=(struct(BFLOAT, TOK_DEV, D), side, side, side, side),
        cost_estimate=pl.CostEstimate(
            flops=20_000_000_000, bytes_accessed=9_000_000, transcendentals=4_000_000
        ),
        compiler_params=params(BIG),
    )(queries, *pairs, bias, log_total, attended, grads, cosine, sine)


def project(hidden, gain, wq_ref, wk_ref, wv_ref, cos_ref, sin_ref, normed_ref, query_ref, pair_ref):
    normed = normalize(hidden, gain).astype(BFLOAT)
    normed_ref[...] = normed
    cosine, sine = cos_ref[...], sin_ref[...]
    keys = turn(nn(normed, wk_ref[...]).T, cosine, sine).T
    pair_ref[:, 0:320] = keys.astype(BFLOAT)
    pair_ref[:, 320:640] = nn(normed, wv_ref[...]).astype(BFLOAT)
    queries = turn(nn(normed, wq_ref[...]).T, cosine, sine)
    query_ref[...] = (queries * (HEAD_DIM**-0.5)).astype(BFLOAT)


PROJECTED = (
    struct(BFLOAT, TOK_DEV, D),
    struct(BFLOAT, D, TOK_DEV),
    struct(BFLOAT, TOK_DEV, 640),
)


def spread_kernel(place_ref, rows_ref, *out_refs):
    place = lax.broadcasted_iota(jnp.int32, (TOK_DEV, DP * CAP), 1)
    for part, ref in enumerate(out_refs):
        hot = (place_ref[128 * part : 128 * part + 128, :] == place).astype(FLOAT).astype(BFLOAT)
        ref[...] = nn(hot, rows_ref[...]).astype(BFLOAT)


def spread(place, rows):
    return pl.pallas_call(
        spread_kernel,
        out_shape=[struct(BFLOAT, TOK_DEV, D)] * MP,
        compiler_params=params(24),
    )(place, rows)


def collect_kernel(place_ref, *refs):
    place = lax.broadcasted_iota(jnp.int32, (TOK_DEV, DP * CAP), 1)
    total = None
    for part, ref in enumerate(refs[:-1]):
        hot = (place_ref[128 * part : 128 * part + 128, :] == place).astype(FLOAT).astype(BFLOAT)
        sums = contract_rows(hot, ref[...])
        total = sums if total is None else total + sums
    refs[-1][...] = total.astype(BFLOAT)


def collect(place, blocks):
    return pl.pallas_call(
        collect_kernel, out_shape=struct(BFLOAT, DP * CAP, D), compiler_params=params(24)
    )(place, *blocks)


def enter_kernel(hidden_ref, gain_ref, *refs):
    project(hidden_ref[...], gain_ref[0:1, :], *refs)


def enter(hidden, gains, wq, wk, wv, cosine, sine):
    return pl.pallas_call(enter_kernel, out_shape=PROJECTED, compiler_params=params(24))(
        hidden, gains, wq, wk, wv, cosine, sine
    )


BIG = 56
FF_BLOCK = 640
FF_STEPS = FF // FF_BLOCK


def weight(ref, which):
    return ref[:, which].reshape(FF_BLOCK, D)


def block_kernel(
    more, att_ref, hidden_ref, sel_ref, gain_ref, router_ref, wo_ref, weight_ref, *refs
):
    proj_in, refs = (refs[:5], refs[5:]) if more else ((), refs)
    mixed_ref, input_ref, gate_ref, up_ref, inner_ref, branch_ref, logit_ref, new_ref = refs[:8]
    proj_out, refs = (refs[8:11], refs[11:]) if more else ((), refs[8:])
    acc_ref = refs[0]
    step = pl.program_id(0)
    copies = [
        pltpu.make_async_copy(source, target, refs[4].at[i])
        for i, (source, target) in enumerate(zip(proj_in[:3], refs[1:4]))
    ]

    @pl.when(step == 0)
    def first():
        for copy in copies:
            copy.start()
        mixed = hidden_ref[...] + nn(att_ref[...], wo_ref[...])
        mixed_ref[...] = mixed
        input_ref[...] = normalize(mixed, gain_ref[1:2, :]).astype(BFLOAT)
        acc_ref[...] = mixed

    rows = input_ref[...]
    gate = contract_cols(rows, weight(weight_ref, 0))
    up = contract_cols(rows, weight(weight_ref, 1))
    gate_ref[...] = gate
    up_ref[...] = up
    inner = (gate * jax.nn.sigmoid(gate) * up).astype(BFLOAT)
    inner_ref[...] = inner
    acc_ref[...] += nn(inner, weight(weight_ref, 2))

    @pl.when(step == FF_STEPS - 1)
    def last():
        hidden = hidden_ref[...]
        branch = acc_ref[...]
        branch_ref[...] = branch
        logit = jnp.sum(hidden * router_ref[...], axis=1, keepdims=True)
        logit_ref[...] = logit
        new = hidden + sel_ref[...] * jax.nn.sigmoid(logit) * (branch - hidden)
        new_ref[...] = new
        for copy in copies:
            copy.wait()
        if more:
            project(new, gain_ref[0:1, :], *refs[1:4], *proj_in[3:], *proj_out)


WEIGHT_SPEC = pl.BlockSpec((FF_BLOCK // 80, 3, 80, D), lambda i: (i, 0, 0, 0))


def block(att, hidden, sel, gains, router, wo, weights, projections):
    more = projections is not None
    proj_specs = [pl.BlockSpec(memory_space=pl.ANY)] * 3 + [whole(32, 128), whole(32, 128)]
    rows = pl.BlockSpec((TOK_DEV, FF_BLOCK), lambda i: (0, i))
    return pl.pallas_call(
        functools.partial(block_kernel, more),
        grid=(FF_STEPS,),
        in_specs=[
            whole(TOK_DEV, D),
            whole(TOK_DEV, D),
            whole(TOK_DEV, 1),
            whole(8, D),
            whole(1, D),
            whole(D, D),
            WEIGHT_SPEC,
        ]
        + proj_specs * more,
        out_specs=[
            whole(TOK_DEV, D),
            whole(TOK_DEV, D),
            rows,
            rows,
            rows,
            whole(TOK_DEV, D),
            whole(TOK_DEV, 1),
            whole(TOK_DEV, D),
        ]
        + [whole(TOK_DEV, D), whole(D, TOK_DEV), whole(TOK_DEV, 640)] * more,
        out_shape=(
            struct(FLOAT, TOK_DEV, D),
            struct(BFLOAT, TOK_DEV, D),
            struct(FLOAT, TOK_DEV, FF),
            struct(FLOAT, TOK_DEV, FF),
            struct(BFLOAT, TOK_DEV, FF),
            struct(FLOAT, TOK_DEV, D),
            struct(FLOAT, TOK_DEV, 1),
            struct(FLOAT, TOK_DEV, D),
        )
        + (PROJECTED if more else ()),
        scratch_shapes=[pltpu.VMEM((TOK_DEV, D), FLOAT)]
        + [
            pltpu.VMEM((D, D), BFLOAT),
            pltpu.VMEM((D, 320), BFLOAT),
            pltpu.VMEM((D, 320), BFLOAT),
            pltpu.SemaphoreType.DMA((3,)),
        ]
        * more,
        cost_estimate=pl.CostEstimate(
            flops=4_000_000_000, bytes_accessed=20_000_000, transcendentals=400_000
        ),
        compiler_params=params(BIG),
    )(att, hidden, sel, gains, router, wo, weights, *(projections if more else ()))


def block_back_kernel(
    new_ref, sel_ref, logit_ref, hidden_ref, branch_ref, mixed_ref, gain_ref, router_ref, wo_ref,
    gate_ref, up_ref, weight_ref,
    rows_ref, dgate_ref, dup_ref, in_ref, attn_ref, back_ref, small_ref, acc_ref, held_ref, sem
):
    step = pl.program_id(0)
    sigma = jax.nn.sigmoid(logit_ref[...])
    chosen = sel_ref[...] * sigma
    copy = pltpu.make_async_copy(wo_ref, held_ref, sem)

    @pl.when(step == 0)
    def first():
        copy.start()
        rows_ref[...] = (chosen * new_ref[...]).astype(BFLOAT)
        acc_ref[...] = jnp.zeros_like(acc_ref)

    inner = contract_cols(rows_ref[...], weight(weight_ref, 2))
    gate = gate_ref[...]
    shape = jax.nn.sigmoid(gate)
    dgate = (inner * up_ref[...] * shape * (1.0 + gate * (1.0 - shape))).astype(BFLOAT)
    dup = (inner * gate * shape).astype(BFLOAT)
    dgate_ref[...] = dgate
    dup_ref[...] = dup
    acc_ref[...] += nn(dgate, weight(weight_ref, 0)) + nn(dup, weight(weight_ref, 1))

    @pl.when(step == FF_STEPS - 1)
    def last():
        grad_new = new_ref[...]
        hidden = hidden_ref[...]
        grad_branch = chosen * grad_new
        grad_weight = jnp.sum(grad_new * (branch_ref[...] - hidden), axis=1, keepdims=True)
        grad_logit = grad_weight * sel_ref[...] * sigma * (1.0 - sigma) + ROUTER_LOSS / TOK_DEV * (
            sigma - sel_ref[...]
        )
        grad_norm, gain_row = normalize_back(mixed_ref[...], gain_ref[1:2, :], acc_ref[...])
        grad_mixed = grad_branch + grad_norm
        in_ref[...] = grad_new - grad_branch + grad_logit * router_ref[...] + grad_mixed
        attn = grad_mixed.astype(BFLOAT)
        attn_ref[...] = attn
        copy.wait()
        back_ref[...] = contract_cols(attn, held_ref[...]).astype(BFLOAT)
        small_ref[0:1, :] = gain_row
        small_ref[1:2, :] = jnp.sum(grad_logit * hidden, axis=0, keepdims=True)
        small_ref[2:8, :] = jnp.zeros((6, D), FLOAT)


def block_back(new, sel, logit, hidden, branch, mixed, gains, router, wo, gate, up, weights):
    rows = pl.BlockSpec((TOK_DEV, FF_BLOCK), lambda i: (0, i))
    full = whole(TOK_DEV, D)
    return pl.pallas_call(
        block_back_kernel,
        grid=(FF_STEPS,),
        in_specs=[
            full,
            whole(TOK_DEV, 1),
            whole(TOK_DEV, 1),
            full,
            full,
            full,
            whole(8, D),
            whole(1, D),
            pl.BlockSpec(memory_space=pl.ANY),
            rows,
            rows,
            WEIGHT_SPEC,
        ],
        out_specs=[full, rows, rows, full, full, full, whole(8, D)],
        out_shape=(
            struct(BFLOAT, TOK_DEV, D),
            struct(BFLOAT, TOK_DEV, FF),
            struct(BFLOAT, TOK_DEV, FF),
            struct(FLOAT, TOK_DEV, D),
            struct(BFLOAT, TOK_DEV, D),
            struct(BFLOAT, TOK_DEV, D),
            struct(FLOAT, 8, D),
        ),
        scratch_shapes=[
            pltpu.VMEM((TOK_DEV, D), FLOAT),
            pltpu.VMEM((D, D), BFLOAT),
            pltpu.SemaphoreType.DMA,
        ],
        cost_estimate=pl.CostEstimate(
            flops=4_000_000_000, bytes_accessed=20_000_000, transcendentals=400_000
        ),
        compiler_params=params(BIG),
    )(new, sel, logit, hidden, branch, mixed, gains, router, wo, gate, up, weights)


def enter_back_kernel(
    in_ref, dq_ref, own_ref, hidden_ref, gain_ref, wq_ref, wk_ref, wv_ref, cos_ref, sin_ref,
    pair_ref, out_ref, small_ref
):
    keys = turn(own_ref[:, 0:320].T, cos_ref[...], -sin_ref[...]).T.astype(BFLOAT)
    values = own_ref[:, 320:640].astype(BFLOAT)
    pair_ref[:, 0:320] = keys
    pair_ref[:, 320:640] = values
    grad_normed = (
        contract_cols(dq_ref[...], wq_ref[...])
        + contract_cols(keys, wk_ref[...])
        + contract_cols(values, wv_ref[...])
    )
    grad_hidden, gain_row = normalize_back(hidden_ref[...], gain_ref[0:1, :], grad_normed)
    out_ref[...] = in_ref[...] + grad_hidden
    small_ref[...] = jnp.concatenate([gain_row, jnp.zeros((7, D), FLOAT)], axis=0)


def enter_back(grad_in, dq, own, hidden, gains, wq, wk, wv, cosine, sine):
    return pl.pallas_call(
        enter_back_kernel,
        out_shape=(
            struct(BFLOAT, TOK_DEV, 640),
            struct(FLOAT, TOK_DEV, D),
            struct(FLOAT, 8, D),
        ),
        compiler_params=params(24),
    )(grad_in, dq, own, hidden, gains, wq, wk, wv, cosine, sine)


HEAD_BLOCK = 1024


def head_kernel(rows_ref, near_ref, *refs):
    block_refs, (target_ref, table_ref, logit_ref, pick_ref, out_ref, stat_ref) = refs[:8], refs[8:]
    step = pl.program_id(0)

    @pl.when(step == 0)
    def first():
        picked = None
        for i, ref in enumerate(block_refs):
            hot = rows_ref[...] == near_ref[:, 128 * i : 128 * i + 128]
            part = nn(hot.astype(FLOAT).astype(BFLOAT), ref[...])
            picked = part if picked is None else picked + part
        pick_ref[...] = picked.astype(BFLOAT)
        lane = lax.broadcasted_iota(jnp.int32, (256, 128), 1)
        stat_ref[...] = jnp.where(lane == 0, MASKED, 0.0)

    logits = contract_cols(pick_ref[...], table_ref[...])
    logit_ref[...] = logits
    place = step * HEAD_BLOCK + lax.broadcasted_iota(jnp.int32, (256, HEAD_BLOCK), 1)
    hit = jnp.sum(jnp.where(place == target_ref[...], logits, 0.0), axis=1, keepdims=True)
    old = stat_ref[:, 0:1]
    top = jnp.maximum(old, jnp.max(logits, axis=1, keepdims=True))
    total = stat_ref[:, 1:2] * jnp.exp(old - top) + jnp.sum(
        jnp.exp(logits - top), axis=1, keepdims=True
    )
    stat_ref[:, 1:2] = total
    stat_ref[:, 2:3] = stat_ref[:, 2:3] + hit
    stat_ref[:, 0:1] = top

    @pl.when(step == pl.num_programs(0) - 1)
    def last():
        out_ref[...] = stat_ref[...].T[0:8]


def head(loss_rows, near_rows, blocks, local_targets, table):
    return pl.pallas_call(
        head_kernel,
        grid=(VOCAB_MP // HEAD_BLOCK,),
        in_specs=[whole(256, 1), whole(1, ROWS)]
        + [whole(TOK_DEV, D)] * MP
        + [whole(256, 1), pl.BlockSpec((HEAD_BLOCK, D), lambda i: (i, 0))],
        out_specs=[
            pl.BlockSpec((256, HEAD_BLOCK), lambda i: (0, i)),
            whole(256, D),
            whole(8, 256),
        ],
        out_shape=(
            struct(FLOAT, 256, VOCAB_MP),
            struct(BFLOAT, 256, D),
            struct(FLOAT, 8, 256),
        ),
        scratch_shapes=[pltpu.VMEM((256, 128), FLOAT)],
        compiler_params=params(BIG),
    )(loss_rows, near_rows, *blocks, local_targets, table)


def head_back_kernel(
    rows_ref, near_ref, target_ref, stat_ref, logit_ref, pick_ref, table_ref, grad_ref, *refs
):
    block_refs, (sum_ref, norm_ref) = refs[:8], refs[8:]
    step = pl.program_id(0)

    @pl.when(step == 0)
    def first():
        norm = stat_ref[0:1, :] + jnp.log(stat_ref[1:2, :])
        norm_ref[:, 0:8] = jnp.concatenate([norm] * 8, axis=0).T
        sum_ref[...] = jnp.zeros((256, D), FLOAT)

    place = step * HEAD_BLOCK + lax.broadcasted_iota(jnp.int32, (256, HEAD_BLOCK), 1)
    probs = jnp.exp(logit_ref[...] - norm_ref[:, 0:1])
    hit = jnp.where(place == target_ref[...], 1.0, 0.0)
    grads = ((probs - hit) * (1.0 / TOK_DEV)).astype(BFLOAT)
    grad_ref[...] = contract_rows(grads, pick_ref[...]).astype(BFLOAT)
    sum_ref[...] += nn(grads, table_ref[...])

    @pl.when(step == pl.num_programs(0) - 1)
    def last():
        total = sum_ref[...].astype(BFLOAT)
        for i, ref in enumerate(block_refs):
            hot = rows_ref[...] == near_ref[:, 128 * i : 128 * i + 128]
            ref[...] = contract_rows(hot.astype(FLOAT).astype(BFLOAT), total).astype(BFLOAT)


def head_back(loss_rows, near_rows, local_targets, stats, logits, picked, table):
    return pl.pallas_call(
        head_back_kernel,
        grid=(VOCAB_MP // HEAD_BLOCK,),
        in_specs=[
            whole(256, 1),
            whole(1, ROWS),
            whole(256, 1),
            whole(8, 256),
            pl.BlockSpec((256, HEAD_BLOCK), lambda i: (0, i)),
            whole(256, D),
            pl.BlockSpec((HEAD_BLOCK, D), lambda i: (i, 0)),
        ],
        out_specs=[pl.BlockSpec((HEAD_BLOCK, D), lambda i: (i, 0))] + [whole(TOK_DEV, D)] * MP,
        out_shape=[struct(BFLOAT, VOCAB_MP, D)] + [struct(BFLOAT, TOK_DEV, D)] * MP,
        scratch_shapes=[pltpu.VMEM((256, D), FLOAT), pltpu.VMEM((256, 128), FLOAT)],
        compiler_params=params(BIG),
    )(loss_rows, near_rows, local_targets, stats, logits, picked, table)


def mlp_grad_kernel(which_ref, *refs):
    out_ref = refs[-1]

    def joined(first):
        return jnp.concatenate([ref[...] for ref in refs[first:-1:10]], axis=0)

    def both(first):
        return jnp.concatenate([joined(first), joined(first + 5)], axis=0)

    rights = both(3), both(3), both(4)
    for i in range(3):
        out_ref[:, i] = contract_rows(both(i), rights[i]).reshape(8, 80, D).astype(BFLOAT)


def mlp_grads(which, kept, received):
    def cols(width, place):
        return pl.BlockSpec((TOK_DEV, width), place)

    rights = [cols(D, lambda i, half: (0, 0))] * 2
    own = [cols(640, lambda i, half: (0, half[0] * 2 + i))] * 3 + rights
    far = [cols(640, lambda i, half: (0, i))] * 3 + rights
    args = []
    for parts, other in zip(kept, received):
        args += [*parts, *other]
    return pl.pallas_call(
        mlp_grad_kernel,
        grid_spec=pltpu.PrefetchScalarGridSpec(
            num_scalar_prefetch=1,
            grid=(2,),
            in_specs=(own + far) * RECUR,
            out_specs=pl.BlockSpec((8, 3, 80, D), lambda i, half: (i, 0, 0, 0)),
        ),
        out_shape=struct(BFLOAT, 16, 3, 80, D),
        compiler_params=params(BIG),
    )(which.reshape(1), *args)


def square_grad_kernel(*refs):
    wq_ref, wo_ref = refs[-2:]
    ins = refs[:-2]

    def joined(first):
        return jnp.concatenate([ref[...] for ref in ins[first::8]], axis=0)

    def both(first):
        return jnp.concatenate([joined(first), joined(first + 4)], axis=0)

    wq_ref[...] = contract_rows(both(2), both(3)).astype(BFLOAT)
    wo_ref[...] = contract_rows(both(0), both(1)).astype(BFLOAT)


def square_grads(kept, received):
    args = []
    for parts, other in zip(kept, received):
        args += [*parts, *other]
    return pl.pallas_call(
        square_grad_kernel,
        grid=(1,),
        in_specs=[whole(TOK_DEV, D)] * (8 * RECUR),
        out_specs=[whole(D, D), whole(D, D)],
        out_shape=(struct(BFLOAT, D, D), struct(BFLOAT, D, D)),
        compiler_params=params(BIG),
    )(*args)


def pack_grad_kernel(starts_ref, *refs):
    wq_ref, wo_ref, rows_ref = refs[:3]
    ins = refs[3:-2]
    out_ref, buf = refs[-2:]
    buf[0:960, :] = wq_ref[...]
    buf[1600:2560, :] = wo_ref[...]
    buf[2560:2576, :] = rows_ref[...].astype(BFLOAT)
    buf[2576:2688, :] = jnp.zeros((112, D), BFLOAT)
    normed = jnp.concatenate([ref[...] for ref in ins[0::4] + ins[1::4]], axis=0)
    grads = jnp.concatenate([ref[...] for ref in ins[2::4] + ins[3::4]], axis=0)
    line = lax.broadcasted_iota(jnp.int32, (960, 320), 0)
    place = lax.broadcasted_iota(jnp.int32, (960, 320), 1)
    full = contract_rows(normed, grads).astype(BFLOAT)
    for i in range(3):
        chosen = (line == 3 * place + i).astype(FLOAT).astype(BFLOAT)
        rows = contract_rows(chosen, full).astype(BFLOAT)
        buf[960:1280, 320 * i : 320 * i + 320] = rows[:, 0:320]
        buf[1280:1600, 320 * i : 320 * i + 320] = rows[:, 320:640]
    for i in range(4):
        start = pl.multiple_of(starts_ref[i], 16)
        out_ref[i] = buf[pl.ds(start, 352), :]


def pack_grads(starts, wq, wo, small, kept, received):
    args = []
    for (normed, pair), (far_normed, far_pair) in zip(kept, received):
        args += [normed, far_normed, pair, far_pair]
    specs = [whole(TOK_DEV, D)] * 2 + [whole(TOK_DEV, 640)] * 2
    return pl.pallas_call(
        pack_grad_kernel,
        grid=(1,),
        in_specs=[pl.BlockSpec(memory_space=pltpu.SMEM), whole(D, D), whole(D, D), whole(16, D)]
        + specs * RECUR,
        out_specs=whole(4, 352, D),
        out_shape=struct(BFLOAT, 4, 352, D),
        scratch_shapes=[pltpu.VMEM((PACK_PAD, D), BFLOAT)],
        compiler_params=params(BIG),
    )(starts, wq, wo, small, *args)


def adam_update(master, first, second, grad, clip):
    grad = grad * clip
    first_new = BETA_ONE * first + (1.0 - BETA_ONE) * grad
    second_new = BETA_TWO * second + (1.0 - BETA_TWO) * grad * grad
    corr_one = 1.0 - BETA_ONE**STEP
    corr_two = 1.0 - BETA_TWO**STEP
    master_new = master - LEARN_RATE * (
        first_new / corr_one / (jnp.sqrt(second_new / corr_two) + ADAM_EPS) + DECAY * master
    )
    return (master_new, first_new, second_new)


def pack_row(device):
    return (1283 * device) // 64


def join_kernel(blocks_ref, wq_ref, wk_ref, wv_ref, wo_ref, small_ref, buf):
    row = lax.broadcasted_iota(jnp.int32, (128, 240), 0)
    place = lax.broadcasted_iota(jnp.int32, (128, 240), 1)
    device = (place * 2731) >> 16
    for step in range(PACK_PAD // 128):
        first = min(step * 128 * 64 // 1283, 118) // 2 * 2
        source = ((1283 * (first + device)) >> 6) + place - 24 * device
        chosen = (source == row + 128 * step).astype(FLOAT).astype(BFLOAT)
        buf[128 * step : 128 * step + 128, :] = nn(
            chosen, blocks_ref[24 * first : 24 * first + 240, :]
        ).astype(BFLOAT)
    wq_ref[...] = buf[0:960, :]
    wo_ref[...] = buf[1600:2560, :]
    small_ref[...] = buf[2560:2576, :]
    line = lax.broadcasted_iota(jnp.int32, (960, 320), 0)
    place = lax.broadcasted_iota(jnp.int32, (960, 320), 1)
    for first, ref in ((960, wk_ref), (1280, wv_ref)):
        total = None
        for i in range(3):
            chosen = (line == 3 * place + i).astype(FLOAT).astype(BFLOAT)
            part = nn(chosen, buf[first : first + 320, 320 * i : 320 * i + 320])
            total = part if total is None else total + part
        ref[...] = total.astype(BFLOAT)


def join_pack(blocks):
    return pl.pallas_call(
        join_kernel,
        out_shape=(
            struct(BFLOAT, D, D),
            struct(BFLOAT, D, 320),
            struct(BFLOAT, D, 320),
            struct(BFLOAT, D, D),
            struct(BFLOAT, 16, D),
        ),
        scratch_shapes=[pltpu.VMEM((PACK_PAD, D), BFLOAT)],
        compiler_params=params(32),
    )(blocks)


def stage(value, axis, index):
    total = lax.dynamic_index_in_dim(value, index, 0, False).astype(FLOAT)
    for k in (1, 2, 3):
        sent = lax.dynamic_index_in_dim(value, (index + k) % 4, 0, False)
        total = total + shift(sent, axis, k).astype(FLOAT)
    return total


def gradients(
    dense,
    token_ids,
    targets,
    loss_rows,
    selections,
    boundary,
    pack_master,
    mlp_master,
    table_master,
):
    z = lax.axis_index("z")
    core = lax.axis_index("core")
    y = lax.axis_index("y")
    x = lax.axis_index("x")
    model_index = z * 2 + core
    data_index = y * 4 + x
    device = model_index * DP + data_index
    own_table = table_master.astype(BFLOAT)

    near = jnp.stack([((z + k) % 4) * 2 + (core ^ j) for j in (0, 1) for k in range(4)])
    near_rows = (near[:, None] * TOK_DEV + jnp.arange(TOK_DEV, dtype=jnp.int32)[None, :]).reshape(-1)

    pack_offset = PACK_DEV * device - D * pack_row(device)
    pack_block = lax.dynamic_update_slice(
        jnp.zeros((24 * D,), BFLOAT), pack_master.astype(BFLOAT), (pack_offset,)
    ).reshape(24, D)
    pack_quad = [pack_block] + [shift(pack_block, "x", k) for k in (1, 2, 3)]
    pack_rows = []
    for i in range(4):
        part = pack_quad[3]
        for k in (2, 1, 0):
            part = jnp.where(x == (i + k) % 4, pack_quad[k], part)
        pack_rows.append(part)
    pack_blocks = lax.all_gather(
        jnp.concatenate(pack_rows, axis=0), ("z", "core", "y"), axis=0, tiled=True
    )
    mlp_own = mlp_master.astype(BFLOAT)
    mlp_quad = jnp.concatenate([mlp_own] + [shift(mlp_own, "z", k) for k in (1, 2, 3)], axis=1)

    group_ids = token_ids[0]
    near_ids = reorder(group_ids.reshape(MP, TOK_DEV), near).reshape(-1)
    local_ids = near_ids - model_index * VOCAB_MP
    inside = (local_ids >= 0) & (local_ids < VOCAB_MP)
    high = local_ids >> 7
    low = local_ids & 127
    high_hot = (high[:, None] == jnp.arange(48)[None, :]).astype(BFLOAT)
    low_hot = (low[:, None] == jnp.arange(128)[None, :]).astype(BFLOAT)
    present = (contract_rows(high_hot, low_hot) > 0).reshape(DP, VOCAB_DEV)
    before = (jnp.arange(VOCAB_DEV)[:, None] < jnp.arange(VOCAB_DEV)[None, :]).astype(BFLOAT)
    slots = mm(present.astype(BFLOAT), before)
    asked = present & (slots < CAP)
    over = jnp.max(jnp.where(present & (slots >= CAP), 1.0, 0.0))
    slot_table = jnp.where(asked, slots, 255.0).reshape(48, 128).astype(BFLOAT)
    token_slot = jnp.sum(mm(high_hot, slot_table) * low_hot.astype(FLOAT), axis=-1)
    token_place = jnp.where(
        inside & (token_slot < CAP), (high // 3) * CAP + token_slot.astype(jnp.int32), -1
    )
    token_place = token_place[:, None]
    match = asked[:, None, :] & (slots[:, None, :] == jnp.arange(CAP, dtype=FLOAT)[None, :, None])
    request = (
        jnp.sum(jnp.where(match, jnp.arange(1, VOCAB_DEV + 1, dtype=FLOAT)[None, None, :], 0.0), axis=-1)
        - 1.0
    )
    request = jnp.concatenate([request, jnp.full((DP, 8), over, FLOAT)], axis=1)
    request = lax.all_to_all(request, DP_AXES, 0, 0, tiled=True)
    over = jnp.max(request[:, CAP:])
    owner_hot = (
        request[:, :CAP].reshape(-1)[:, None] == jnp.arange(VOCAB_DEV, dtype=FLOAT)[None, :]
    ).astype(BFLOAT)
    mlp_quad, owner_hot = tie(mlp_quad, owner_hot)
    mlp_weights = lax.all_gather(
        mlp_quad.reshape(3 * 80, D), ("core", "y", "x"), axis=0, tiled=True
    )
    mlp_weights = mlp_weights.reshape(32, 3, 80, D)
    asked_rows = lax.all_to_all(mm(owner_hot, own_table).astype(BFLOAT), DP_AXES, 0, 0, tiled=True)
    own_table, asked_rows = tie(own_table, asked_rows)
    table = lax.all_gather(own_table, DP_AXES, axis=0, tiled=True)
    if dense:
        rows = jnp.take(table, jnp.clip(local_ids, 0, VOCAB_MP - 1), axis=0)
        looked = jnp.where(inside[:, None], rows, jnp.zeros_like(rows))
        looked = [looked[128 * i : 128 * i + 128] for i in range(MP)]
    else:
        looked = spread(token_place, asked_rows)
    hidden, pack_blocks = scatter_group(looked, pack_blocks)

    w_query, w_key, w_value, w_out, last_rows = join_pack(pack_blocks)
    gains = jnp.concatenate([last_rows[:3].astype(FLOAT), jnp.zeros((5, D), FLOAT)])
    router = last_rows[3:6].astype(FLOAT)

    half_dim = HEAD_DIM // 2
    freqs = ROPE_BASE ** (-jnp.arange(half_dim, dtype=FLOAT) / half_dim)
    first_row = data_index * ROWS + model_index * TOK_DEV
    angles = freqs[:, None] * (first_row + jnp.arange(TOK_DEV, dtype=jnp.int32)).astype(FLOAT)[None, :]
    turns = (jnp.cos(angles), jnp.sin(angles))
    projections = (w_query, w_key, w_value) + turns
    group_sel = selections.reshape(RECUR, DP, MP, TOK_DEV)
    prev_index = jnp.maximum(data_index - 1, 0)
    here_sel = lax.dynamic_index_in_dim(group_sel, data_index, 1, False)
    own_sel = lax.dynamic_index_in_dim(here_sel, model_index, 1, False)
    near_sel = reorder(here_sel, near).reshape(RECUR, ROWS)
    prev_sel = reorder(lax.dynamic_index_in_dim(group_sel, prev_index, 1, False), near)
    prev_sel = prev_sel.reshape(RECUR, ROWS)
    start = lax.dynamic_index_in_dim(boundary, data_index, 0, False)
    prev_start = lax.dynamic_index_in_dim(boundary, prev_index, 0, False)
    place = (model_index * TOK_DEV + jnp.arange(TOK_DEV, dtype=jnp.int32))[None, :]
    key_place = near_rows[:, None]
    biases = []
    for step in range(RECUR):
        own_seen = (
            (key_place <= place)
            & ((key_place < start) == (place < start))
            & ((near_sel[step][:, None] > 0) | (key_place == place))
        )
        prev_seen = (
            (data_index > 0)
            & (place < start)
            & (key_place >= prev_start)
            & (prev_sel[step][:, None] > 0)
        )
        seen = [prev_seen[:512], own_seen[:512], prev_seen[512:], own_seen[512:]]
        biases.append(jnp.where(jnp.concatenate(seen, axis=0), 0.0, MASKED))

    sel_cols = own_sel.astype(FLOAT)[:, :, None]
    saves = []
    logits_all = []
    normed, queries, pair = enter(hidden, gains, *projections)
    for step in range(RECUR):
        pairs = group_gather(pair)
        attended, log_total = attend(queries, pairs, biases[step])
        mixed, mlp_input, gate, up, inner, branch, logit, new_hidden, *nexts = block(
            attended,
            hidden,
            sel_cols[step],
            gains,
            router[step : step + 1],
            w_out,
            mlp_weights,
            projections if step < RECUR - 1 else None,
        )
        logits_all.append(logit[:, 0])
        saves.append(
            (
                hidden,
                normed,
                queries,
                pairs,
                attended,
                log_total,
                mixed,
                mlp_input,
                gate,
                up,
                inner,
                branch,
                logit,
            )
        )
        hidden = new_hidden
        if nexts:
            normed, queries, pair = nexts
    logits_all = jnp.stack(logits_all)
    penalty_total = jnp.sum(jax.nn.softplus(logits_all) - own_sel.astype(FLOAT) * logits_all)

    normed_final = rms_scale(hidden, gains[2]).astype(BFLOAT)
    final_rows = gather_group(normed_final)
    row_targets = lax.dynamic_index_in_dim(targets, data_index, 0, keepdims=False)
    head_args = (loss_rows[0][:, None], near_rows[None, :])
    local_targets = (row_targets - model_index * VOCAB_MP)[:, None]
    logits, picked, stats = head(*head_args, final_rows, local_targets, table)
    flag_row = lax.broadcasted_iota(jnp.int32, (8, 256), 0) == 3
    stats = jnp.where(flag_row, over, stats)

    def join_stats(parts):
        top = parts[0][0]
        for part in parts[1:]:
            top = jnp.maximum(top, part[0])
        total = sum(part[1] * jnp.exp(part[0] - top) for part in parts)
        over = parts[0][3]
        for part in parts[1:]:
            over = jnp.maximum(over, part[3])
        rest = [jnp.zeros_like(top)] * 4
        return jnp.stack([top, total, sum(part[2] for part in parts), over] + rest)

    stats = join_stats([stats, swap(stats)])
    stats = join_stats([stats] + [shift(stats, "z", k) for k in (1, 2, 3)])
    log_norm = stats[0] + jnp.log(stats[1])
    cross = log_norm - stats[2]
    per_device = cross.shape[0] // MP
    loss_part = (
        jnp.sum(lax.dynamic_slice_in_dim(cross, model_index * per_device, per_device))
        + ROUTER_LOSS * penalty_total
    )
    head_grad, *scattered = head_back(*head_args, local_targets, stats, logits, picked, table)
    grad_final = scatter_group(scattered)
    grad_hidden, grad_gain_final = rms_back(hidden, gains[2], grad_final)
    if not dense:
        head_grad = lax.psum_scatter(head_grad, DP_AXES, scatter_dimension=0, tiled=True)

    mlp_kept, mlp_far, square_kept, square_far, pack_kept, pack_far = [], [], [], [], [], []
    loss_part, flag, grad_hidden = tie(loss_part, stats[3, 0], grad_hidden)
    router_rows = [None] * RECUR
    gain_one = jnp.zeros((1, D), FLOAT)
    gain_two = jnp.zeros((1, D), FLOAT)
    for step in reversed(range(RECUR)):
        (
            hidden_in,
            normed,
            queries,
            pairs,
            attended,
            log_total,
            mixed,
            mlp_input,
            gate,
            up,
            inner,
            branch,
            logit,
        ) = saves[step]
        grad_rows, grad_gate, grad_up, grad_in, grad_attn, grad_attended, small = block_back(
            grad_hidden,
            sel_cols[step],
            logit,
            hidden_in,
            branch,
            mixed,
            gains,
            router[step : step + 1],
            w_out,
            gate,
            up,
            mlp_weights,
        )
        gain_two = gain_two + small[0:1]
        router_rows[step] = small[1:2]
        mlp_kept.append((grad_gate, grad_up, inner, mlp_input, grad_rows))

        def far_half(value):
            return lax.dynamic_slice_in_dim(value, (1 - core) * (FF // 2), FF // 2, 1)

        mlp_far.append(
            [swap(far_half(part)) for part in (grad_gate, grad_up, inner)]
            + [swap(mlp_input), swap(grad_rows)]
        )
        grad_query, *grad_sides = attend_back(
            queries, pairs, biases[step], log_total, attended, grad_attended, *turns
        )
        far_normed = swap(normed)
        square_kept.append((attended, grad_attn, normed, grad_query))
        square_far.append((swap(attended), swap(grad_attn), far_normed, swap(grad_query)))
        if step == 0:
            tied = tie(*grad_sides, *mlp_kept[-1])
            grad_sides, mlp_kept[-1] = tied[:4], tied[4:]
        grad_own = group_scatter(*grad_sides)
        if step == 0:
            mlp_half = mlp_grads(core.astype(jnp.int32), mlp_kept, mlp_far)
            mlp_sum = lax.psum_scatter(
                mlp_half.reshape(16 * 240, D), DP_AXES, scatter_dimension=0, tiled=True
            )
            squares = square_grads(square_kept, square_far)
            grad_own, mlp_half, *squares = tie(grad_own, mlp_half, *squares)
        grad_pair, grad_hidden, small = enter_back(
            grad_in, grad_query, grad_own, hidden_in, gains, *projections
        )
        gain_one = gain_one + small[0:1]
        pack_kept.append((normed, grad_pair))
        pack_far.append((far_normed, swap(grad_pair)))
        if step == 1 and not dense:
            head_grad, grad_hidden = tie(head_grad, grad_hidden)

    sent = grad_hidden.astype(BFLOAT)
    grad_embed = [sent] + [shift(sent, "z", -k) for k in (1, 2, 3)]
    grad_embed[1], grad_embed[3], gain_one = tie(grad_embed[1], grad_embed[3], gain_one)
    grad_embed += [swap(part) for part in grad_embed]

    def aligned_row(which):
        return (pack_row(which) // 16) * 16

    small = jnp.concatenate(
        [
            gain_one,
            gain_two,
            grad_gain_final[None],
            *router_rows,
            jnp.zeros((10, D), FLOAT),
        ]
    )
    small = small + swap(small)
    starts = jnp.stack([aligned_row(DP * (2 * i + core)) for i in range(4)]).astype(jnp.int32)
    part = pack_grads(starts, *squares, small, pack_kept, pack_far)

    def y_windows(value):
        return jnp.stack([value[..., 80 * i : 80 * i + 112, :] for i in range(4)])

    def x_windows(value):
        return jnp.stack([value[..., i : i + 48, :] for i in (0, 16, 40, 56)])

    part = stage(part, "z", z).astype(BFLOAT)
    part, mlp_sum = tie(y_windows(part), mlp_sum)
    mlp_sum = mlp_sum.reshape(3, 4, UNITS, D).transpose(1, 0, 2, 3)
    mlp_grad = mlp_sum[0].astype(FLOAT)
    for k in (1, 2, 3):
        mlp_grad = mlp_grad + shift(mlp_sum[k], "z", -k).astype(FLOAT)
    part = stage(part, "y", y).astype(BFLOAT)
    part = stage(x_windows(part), "x", x).reshape(-1)
    begin = aligned_row(DP * model_index) + 80 * y + (20 * x) // 8 * 8
    pack_grad = lax.dynamic_slice(part, (PACK_DEV * device - D * begin,), (PACK_DEV,))

    if dense:
        kept_rows = jnp.concatenate(grad_embed).astype(FLOAT) * inside.astype(FLOAT)[:, None]
        sums = jax.ops.segment_sum(
            kept_rows, jnp.clip(local_ids, 0, VOCAB_MP - 1), num_segments=VOCAB_MP
        )
        table_grad = lax.psum_scatter(
            (head_grad.astype(FLOAT) + sums).astype(BFLOAT),
            DP_AXES,
            scatter_dimension=0,
            tiled=True,
        ).astype(FLOAT)
    else:
        unique = collect(token_place, grad_embed)
        unique = lax.all_to_all(unique, DP_AXES, 0, 0, tiled=True)
        table_grad = head_grad.astype(FLOAT) + contract_rows(owner_hot, unique)
    table_grad = by_cols(table_grad)
    squares = (
        jnp.sum(pack_grad * pack_grad)
        + jnp.sum(mlp_grad * mlp_grad)
        + jnp.sum(table_grad * table_grad)
    )
    return pack_grad, mlp_grad, table_grad, squares, loss_part, flag


def shards(
    token_ids,
    targets,
    loss_rows,
    selections,
    boundary,
    pack_master,
    pack_first,
    pack_second,
    mlp_master,
    mlp_first,
    mlp_second,
    table_master,
    table_first,
    table_second,
):
    args = (
        token_ids,
        targets,
        loss_rows,
        selections,
        boundary,
        pack_master,
        mlp_master,
        table_master,
    )
    *found, over = tie(*gradients(False, *args))
    pack_grad, mlp_grad, table_grad, squares, loss_part = lax.cond(
        over > 0, lambda: gradients(True, *args)[:5], lambda: tuple(found)
    )
    lane = lax.broadcasted_iota(jnp.int32, (128, 128), 1)
    sums = lax.all_to_all(
        jnp.where(lane == 0, squares, loss_part), ALL_AXES, 0, 0, tiled=True
    )
    sums = jnp.sum(sums, axis=0, keepdims=True)
    total_squares = sums[0, 0]
    loss_sum = sums[0, 1]
    grad_norm = jnp.sqrt(total_squares)
    clip = CLIP_NORM / jnp.maximum(grad_norm, CLIP_NORM)
    pack_new, pack_first_new, pack_second_new = adam_update(
        pack_master, pack_first, pack_second, pack_grad, clip
    )
    mlp_new, mlp_first_new, mlp_second_new = adam_update(
        mlp_master, mlp_first, mlp_second, mlp_grad, clip
    )
    table_new, table_first_new, table_second_new = adam_update(
        table_master, table_first, table_second, table_grad, clip
    )
    return (
        pack_new,
        pack_first_new,
        pack_second_new,
        mlp_new,
        mlp_first_new,
        mlp_second_new,
        table_new,
        table_first_new,
        table_second_new,
        loss_sum,
        grad_norm,
    )


def solution(mesh):
    grid = Mesh(mesh.devices.reshape(4, 2, 4, 4), ALL_AXES)
    owners = (P(ALL_AXES), P(None, ALL_AXES, None), P(ALL_AXES, None))
    group = P(DP_AXES, None)
    masters = tuple(spec for spec in owners for _ in range(3))
    return jax.shard_map(
        shards,
        mesh=grid,
        in_specs=(group, P(), group, P(), P()) + masters,
        out_specs=masters + (P(), P()),
        check_vma=False,
    )
```

```python
import functools

import jax
import jax.numpy as jnp
from jax import lax
from jax.experimental import pallas as pl
from jax.experimental.layout import Layout, with_layout_constraint
from jax.experimental.pallas import tpu as pltpu
from jax.sharding import Mesh
from jax.sharding import PartitionSpec as P

D = 960
HEADS = 15
KV_HEADS = 5
HEAD_DIM = 64
FF = 2560
RECUR = 3
STEP = 10
TOK_DEV = 128
ROWS = 1024
MP = 8
DP = 16
VOCAB_MP = 6144
VOCAB_DEV = 384
UNITS = 20
PACK_DEV = 19245
PACK_ROWS = 2566
PACK_PAD = 2688
CAP = 24

EPS_NORM = 1e-05
ROPE_BASE = 10000.0
ROUTER_LOSS = 0.1
CLIP_NORM = 1.0
LEARN_RATE = 0.05
BETA_ONE = 0.9
BETA_TWO = 0.95
ADAM_EPS = 1e-08
DECAY = 0.1
MASKED = -1e30
HIGHEST = lax.Precision.HIGHEST
BFLOAT = jnp.bfloat16
FLOAT = jnp.float32
DP_AXES = ("y", "x")
ALL_AXES = ("z", "core", "y", "x")


def shift(value, axis, steps):
    return lax.ppermute(value, axis, [(i, (i + steps) % 4) for i in range(4)])


def swap(value):
    return lax.ppermute(value, "core", [(0, 1), (1, 0)])


def gather_group(value):
    near = [value] + [shift(value, "z", -k) for k in (1, 2, 3)]
    return near + [swap(part) for part in near]


def scatter_group(blocks, other=None):
    half = [near.astype(FLOAT) + swap(far).astype(FLOAT) for near, far in zip(blocks[:4], blocks[4:])]
    total = half[0]
    sent = [part.astype(BFLOAT) for part in half[1:]]
    if other is not None:
        *sent, other = tie(*sent, other)
    for k in (1, 2, 3):
        total = total + shift(sent[k - 1], "z", k).astype(FLOAT)
    return total if other is None else (total, other)


def rms_scale(values, weight):
    return values * lax.rsqrt(jnp.mean(values * values, axis=-1, keepdims=True) + EPS_NORM) * weight


def rms_back(values, weight, grad_out):
    inverse = lax.rsqrt(jnp.mean(values * values, axis=-1, keepdims=True) + EPS_NORM)
    weighted = grad_out * weight
    grad_values = inverse * weighted - values * (inverse * inverse * inverse) * jnp.mean(
        weighted * values, axis=-1, keepdims=True
    )
    return (grad_values, jnp.sum(grad_out * values * inverse, axis=0))


def mm(left, right):
    return jnp.dot(left, right, preferred_element_type=FLOAT)


def contract_rows(left, right):
    return lax.dot_general(left, right, (((0,), (0,)), ((), ())), preferred_element_type=FLOAT)


def contract_cols(left, right):
    return lax.dot_general(left, right, (((1,), (1,)), ((), ())), preferred_element_type=FLOAT)


def reorder(blocks, order):
    hit = order[:, None] == jnp.arange(MP)[None, :]
    return jnp.sum(jnp.where(hit[:, :, None], blocks[..., None, :, :], 0), axis=-2)


def by_cols(value):
    return with_layout_constraint(value, Layout((1, 0)))


def tie(*values):
    return lax.optimization_barrier(values)


def group_gather(pair):
    own = [pair]
    for k in (1, 2, 3):
        own.append(lax.ppermute(pair, "z", [((i + k) % 4, i) for i in range(4) if (i + k) % 4 < i]))
    prev = []
    for k in range(4):
        pairs = []
        for i in range(3):
            for g in range(1, DP):
                pairs.append((((i + k) % 4) * DP + g - 1, i * DP + g))
        prev.append(lax.ppermute(pair, ("z",) + DP_AXES, pairs))
    return prev + own + [swap(part) for part in prev] + [swap(part) for part in own]


def group_scatter(prev, own, prev_far, own_far):
    own = (own.astype(FLOAT) + swap(own_far).astype(FLOAT)).astype(BFLOAT).reshape(4, TOK_DEV, -1)
    prev = (prev.astype(FLOAT) + swap(prev_far).astype(FLOAT)).astype(BFLOAT).reshape(4, TOK_DEV, -1)
    total = own[0].astype(FLOAT)
    for k in (1, 2, 3):
        pairs = [(i, (i + k) % 4) for i in range(4) if (i + k) % 4 < i]
        total = total + lax.ppermute(own[k], "z", pairs).astype(FLOAT)
    for k in range(4):
        pairs = []
        for i in range(3):
            for g in range(1, DP):
                pairs.append((i * DP + g, ((i + k) % 4) * DP + g - 1))
        total = total + lax.ppermute(prev[k], ("z",) + DP_AXES, pairs).astype(FLOAT)
    return total


def nn(left, right):
    return jnp.dot(left, right, preferred_element_type=FLOAT)


def head_rows(ref, head):
    return jnp.concatenate(
        [ref[:, 64 * (3 * head + i) : 64 * (3 * head + i) + 64] for i in range(3)], axis=0
    )


def head_lanes(ref, head):
    return jnp.concatenate(
        [ref[64 * (3 * head + i) : 64 * (3 * head + i) + 64, :] for i in range(3)], axis=1
    )


def turn(value, cosine, sine):
    parts = []
    for head in range(value.shape[0] // 64):
        first = value[64 * head : 64 * head + 32]
        second = value[64 * head + 32 : 64 * head + 64]
        parts.append(first * cosine - second * sine)
        parts.append(second * cosine + first * sine)
    return jnp.concatenate(parts, axis=0)


def normalize(values, weight):
    return values * lax.rsqrt(jnp.mean(values * values, axis=-1, keepdims=True) + EPS_NORM) * weight


def normalize_back(values, weight, grad_out):
    inverse = lax.rsqrt(jnp.mean(values * values, axis=-1, keepdims=True) + EPS_NORM)
    weighted = grad_out * weight
    grad_values = inverse * weighted - values * (inverse * inverse * inverse) * jnp.mean(
        weighted * values, axis=-1, keepdims=True
    )
    return grad_values, jnp.sum(grad_out * values * inverse, axis=0, keepdims=True)


def joined(refs, part, first):
    return jnp.concatenate(
        [ref[:, first : first + 64] for ref in refs[4 * part : 4 * part + 4]], axis=0
    )


def attend_kernel(query_ref, *refs):
    kv_refs, (bias_ref, out_ref, log_ref) = refs[:16], refs[16:]
    for head in range(KV_HEADS):
        queries = head_lanes(query_ref, head)
        top = None
        for part in range(4):
            keys = joined(kv_refs, part, 64 * head)
            values = joined(kv_refs, part, 320 + 64 * head)
            bias = bias_ref[512 * part : 512 * part + 512, :]
            scores = nn(keys, queries) + jnp.concatenate([bias, bias, bias], axis=1)
            part_top = jnp.max(scores, axis=0, keepdims=True)
            new_top = part_top if top is None else jnp.maximum(top, part_top)
            expo = jnp.exp(scores - new_top)
            part_total = jnp.sum(expo, axis=0, keepdims=True)
            part_out = contract_rows(values, expo.astype(BFLOAT))
            if top is None:
                total, out = part_total, part_out
            else:
                shrink = jnp.exp(top - new_top)
                total, out = total * shrink + part_total, out * shrink + part_out
            top = new_top
        out = (out / total).T.astype(BFLOAT)
        for i in range(3):
            place = 64 * (3 * head + i)
            out_ref[:, place : place + 64] = out[128 * i : 128 * i + 128]
        log_ref[head : head + 1, :] = top + jnp.log(total)


def params(mib):
    return pltpu.CompilerParams(vmem_limit_bytes=mib * 1024 * 1024)


def whole(*shape):
    return pl.BlockSpec(shape, lambda i: (0,) * len(shape))


def struct(kind, *shape):
    return jax.ShapeDtypeStruct(shape, kind)


def attend(queries, pairs, bias):
    return pl.pallas_call(
        attend_kernel,
        out_shape=(struct(BFLOAT, TOK_DEV, D), struct(FLOAT, 8, 3 * TOK_DEV)),
        cost_estimate=pl.CostEstimate(
            flops=12_000_000_000, bytes_accessed=5_000_000, transcendentals=4_000_000
        ),
        compiler_params=params(24),
    )(queries, *pairs, bias)


def attend_back_kernel(query_ref, *refs):
    kv_refs, refs = refs[:16], refs[16:]
    bias_ref, log_ref, att_ref, grad_ref, cos_ref, sin_ref, dq_ref = refs[:7]
    d_refs = refs[7:]
    cosine = jnp.concatenate([cos_ref[...]] * 3, axis=1)
    sine = jnp.concatenate([sin_ref[...]] * 3, axis=1)
    for head in range(KV_HEADS):
        queries = head_lanes(query_ref, head)
        grads = head_rows(grad_ref, head)
        outs = head_rows(att_ref, head)
        delta = jnp.sum((grads.astype(FLOAT) * outs.astype(FLOAT)).T, axis=0, keepdims=True)
        log_total = log_ref[head : head + 1, :]
        back = None
        for part, d_ref in enumerate(d_refs):
            keys = joined(kv_refs, part, 64 * head)
            values = joined(kv_refs, part, 320 + 64 * head)
            bias = bias_ref[512 * part : 512 * part + 512, :]
            probs = jnp.exp(
                nn(keys, queries) + jnp.concatenate([bias, bias, bias], axis=1) - log_total
            )
            grad_scores = (probs * (contract_cols(values, grads) - delta)).astype(BFLOAT)
            d_ref[:, 64 * head : 64 * head + 64] = contract_cols(grad_scores, queries).astype(BFLOAT)
            d_ref[:, 320 + 64 * head : 320 + 64 * head + 64] = nn(
                probs.astype(BFLOAT), grads
            ).astype(BFLOAT)
            part_back = contract_rows(keys, grad_scores)
            back = part_back if back is None else back + part_back
        back = turn(back * (HEAD_DIM**-0.5), cosine, -sine).T.astype(BFLOAT)
        for i in range(3):
            place = 64 * (3 * head + i)
            dq_ref[:, place : place + 64] = back[128 * i : 128 * i + 128]


def attend_back(queries, pairs, bias, log_total, attended, grads, cosine, sine):
    side = struct(BFLOAT, 4 * TOK_DEV, 640)
    return pl.pallas_call(
        attend_back_kernel,
        out_shape=(struct(BFLOAT, TOK_DEV, D), side, side, side, side),
        cost_estimate=pl.CostEstimate(
            flops=20_000_000_000, bytes_accessed=9_000_000, transcendentals=4_000_000
        ),
        compiler_params=params(BIG),
    )(queries, *pairs, bias, log_total, attended, grads, cosine, sine)


def project(hidden, gain, wq_ref, wk_ref, wv_ref, cos_ref, sin_ref, normed_ref, query_ref, pair_ref):
    normed = normalize(hidden, gain).astype(BFLOAT)
    normed_ref[...] = normed
    cosine, sine = cos_ref[...], sin_ref[...]
    keys = turn(nn(normed, wk_ref[...]).T, cosine, sine).T
    pair_ref[:, 0:320] = keys.astype(BFLOAT)
    pair_ref[:, 320:640] = nn(normed, wv_ref[...]).astype(BFLOAT)
    queries = turn(nn(normed, wq_ref[...]).T, cosine, sine)
    query_ref[...] = (queries * (HEAD_DIM**-0.5)).astype(BFLOAT)


PROJECTED = (
    struct(BFLOAT, TOK_DEV, D),
    struct(BFLOAT, D, TOK_DEV),
    struct(BFLOAT, TOK_DEV, 640),
)


def spread_kernel(place_ref, rows_ref, *out_refs):
    place = lax.broadcasted_iota(jnp.int32, (TOK_DEV, DP * CAP), 1)
    for part, ref in enumerate(out_refs):
        hot = (place_ref[128 * part : 128 * part + 128, :] == place).astype(FLOAT).astype(BFLOAT)
        ref[...] = nn(hot, rows_ref[...]).astype(BFLOAT)


def spread(place, rows):
    return pl.pallas_call(
        spread_kernel,
        out_shape=[struct(BFLOAT, TOK_DEV, D)] * MP,
        compiler_params=params(24),
    )(place, rows)


def collect_kernel(place_ref, *refs):
    place = lax.broadcasted_iota(jnp.int32, (TOK_DEV, DP * CAP), 1)
    total = None
    for part, ref in enumerate(refs[:-1]):
        hot = (place_ref[128 * part : 128 * part + 128, :] == place).astype(FLOAT).astype(BFLOAT)
        sums = contract_rows(hot, ref[...])
        total = sums if total is None else total + sums
    refs[-1][...] = total.astype(BFLOAT)


def collect(place, blocks):
    return pl.pallas_call(
        collect_kernel, out_shape=struct(BFLOAT, DP * CAP, D), compiler_params=params(24)
    )(place, *blocks)


def enter_kernel(hidden_ref, gain_ref, *refs):
    project(hidden_ref[...], gain_ref[0:1, :], *refs)


def enter(hidden, gains, wq, wk, wv, cosine, sine):
    return pl.pallas_call(enter_kernel, out_shape=PROJECTED, compiler_params=params(24))(
        hidden, gains, wq, wk, wv, cosine, sine
    )


BIG = 56
FF_BLOCK = 640
FF_STEPS = FF // FF_BLOCK


def weight(ref, which):
    return ref[:, which].reshape(FF_BLOCK, D)


def block_kernel(
    more, att_ref, hidden_ref, sel_ref, gain_ref, router_ref, wo_ref, weight_ref, *refs
):
    proj_in, refs = (refs[:5], refs[5:]) if more else ((), refs)
    mixed_ref, input_ref, gate_ref, up_ref, inner_ref, branch_ref, logit_ref, new_ref = refs[:8]
    proj_out, refs = (refs[8:11], refs[11:]) if more else ((), refs[8:])
    acc_ref = refs[0]
    step = pl.program_id(0)
    copies = [
        pltpu.make_async_copy(source, target, refs[4].at[i])
        for i, (source, target) in enumerate(zip(proj_in[:3], refs[1:4]))
    ]

    @pl.when(step == 0)
    def first():
        for copy in copies:
            copy.start()
        mixed = hidden_ref[...] + nn(att_ref[...], wo_ref[...])
        mixed_ref[...] = mixed
        input_ref[...] = normalize(mixed, gain_ref[1:2, :]).astype(BFLOAT)
        acc_ref[...] = mixed

    rows = input_ref[...]
    gate = contract_cols(rows, weight(weight_ref, 0))
    up = contract_cols(rows, weight(weight_ref, 1))
    gate_ref[...] = gate
    up_ref[...] = up
    inner = (gate * jax.nn.sigmoid(gate) * up).astype(BFLOAT)
    inner_ref[...] = inner
    acc_ref[...] += nn(inner, weight(weight_ref, 2))

    @pl.when(step == FF_STEPS - 1)
    def last():
        hidden = hidden_ref[...]
        branch = acc_ref[...]
        branch_ref[...] = branch
        logit = jnp.sum(hidden * router_ref[...], axis=1, keepdims=True)
        logit_ref[...] = logit
        new = hidden + sel_ref[...] * jax.nn.sigmoid(logit) * (branch - hidden)
        new_ref[...] = new
        for copy in copies:
            copy.wait()
        if more:
            project(new, gain_ref[0:1, :], *refs[1:4], *proj_in[3:], *proj_out)


WEIGHT_SPEC = pl.BlockSpec((FF_BLOCK // 80, 3, 80, D), lambda i: (i, 0, 0, 0))


def block(att, hidden, sel, gains, router, wo, weights, projections):
    more = projections is not None
    proj_specs = [pl.BlockSpec(memory_space=pl.ANY)] * 3 + [whole(32, 128), whole(32, 128)]
    rows = pl.BlockSpec((TOK_DEV, FF_BLOCK), lambda i: (0, i))
    return pl.pallas_call(
        functools.partial(block_kernel, more),
        grid=(FF_STEPS,),
        in_specs=[
            whole(TOK_DEV, D),
            whole(TOK_DEV, D),
            whole(TOK_DEV, 1),
            whole(8, D),
            whole(1, D),
            whole(D, D),
            WEIGHT_SPEC,
        ]
        + proj_specs * more,
        out_specs=[
            whole(TOK_DEV, D),
            whole(TOK_DEV, D),
            rows,
            rows,
            rows,
            whole(TOK_DEV, D),
            whole(TOK_DEV, 1),
            whole(TOK_DEV, D),
        ]
        + [whole(TOK_DEV, D), whole(D, TOK_DEV), whole(TOK_DEV, 640)] * more,
        out_shape=(
            struct(FLOAT, TOK_DEV, D),
            struct(BFLOAT, TOK_DEV, D),
            struct(FLOAT, TOK_DEV, FF),
            struct(FLOAT, TOK_DEV, FF),
            struct(BFLOAT, TOK_DEV, FF),
            struct(FLOAT, TOK_DEV, D),
            struct(FLOAT, TOK_DEV, 1),
            struct(FLOAT, TOK_DEV, D),
        )
        + (PROJECTED if more else ()),
        scratch_shapes=[pltpu.VMEM((TOK_DEV, D), FLOAT)]
        + [
            pltpu.VMEM((D, D), BFLOAT),
            pltpu.VMEM((D, 320), BFLOAT),
            pltpu.VMEM((D, 320), BFLOAT),
            pltpu.SemaphoreType.DMA((3,)),
        ]
        * more,
        cost_estimate=pl.CostEstimate(
            flops=4_000_000_000, bytes_accessed=20_000_000, transcendentals=400_000
        ),
        compiler_params=params(BIG),
    )(att, hidden, sel, gains, router, wo, weights, *(projections if more else ()))


def block_back_kernel(
    new_ref, sel_ref, logit_ref, hidden_ref, branch_ref, mixed_ref, gain_ref, router_ref, wo_ref,
    gate_ref, up_ref, weight_ref,
    rows_ref, dgate_ref, dup_ref, in_ref, attn_ref, back_ref, small_ref, acc_ref, held_ref, sem
):
    step = pl.program_id(0)
    sigma = jax.nn.sigmoid(logit_ref[...])
    chosen = sel_ref[...] * sigma
    copy = pltpu.make_async_copy(wo_ref, held_ref, sem)

    @pl.when(step == 0)
    def first():
        copy.start()
        rows_ref[...] = (chosen * new_ref[...]).astype(BFLOAT)
        acc_ref[...] = jnp.zeros_like(acc_ref)

    inner = contract_cols(rows_ref[...], weight(weight_ref, 2))
    gate = gate_ref[...]
    shape = jax.nn.sigmoid(gate)
    dgate = (inner * up_ref[...] * shape * (1.0 + gate * (1.0 - shape))).astype(BFLOAT)
    dup = (inner * gate * shape).astype(BFLOAT)
    dgate_ref[...] = dgate
    dup_ref[...] = dup
    acc_ref[...] += nn(dgate, weight(weight_ref, 0)) + nn(dup, weight(weight_ref, 1))

    @pl.when(step == FF_STEPS - 1)
    def last():
        grad_new = new_ref[...]
        hidden = hidden_ref[...]
        grad_branch = chosen * grad_new
        grad_weight = jnp.sum(grad_new * (branch_ref[...] - hidden), axis=1, keepdims=True)
        grad_logit = grad_weight * sel_ref[...] * sigma * (1.0 - sigma) + ROUTER_LOSS / TOK_DEV * (
            sigma - sel_ref[...]
        )
        grad_norm, gain_row = normalize_back(mixed_ref[...], gain_ref[1:2, :], acc_ref[...])
        grad_mixed = grad_branch + grad_norm
        in_ref[...] = grad_new - grad_branch + grad_logit * router_ref[...] + grad_mixed
        attn = grad_mixed.astype(BFLOAT)
        attn_ref[...] = attn
        copy.wait()
        back_ref[...] = contract_cols(attn, held_ref[...]).astype(BFLOAT)
        small_ref[0:1, :] = gain_row
        small_ref[1:2, :] = jnp.sum(grad_logit * hidden, axis=0, keepdims=True)
        small_ref[2:8, :] = jnp.zeros((6, D), FLOAT)


def block_back(new, sel, logit, hidden, branch, mixed, gains, router, wo, gate, up, weights):
    rows = pl.BlockSpec((TOK_DEV, FF_BLOCK), lambda i: (0, i))
    full = whole(TOK_DEV, D)
    return pl.pallas_call(
        block_back_kernel,
        grid=(FF_STEPS,),
        in_specs=[
            full,
            whole(TOK_DEV, 1),
            whole(TOK_DEV, 1),
            full,
            full,
            full,
            whole(8, D),
            whole(1, D),
            pl.BlockSpec(memory_space=pl.ANY),
            rows,
            rows,
            WEIGHT_SPEC,
        ],
        out_specs=[full, rows, rows, full, full, full, whole(8, D)],
        out_shape=(
            struct(BFLOAT, TOK_DEV, D),
            struct(BFLOAT, TOK_DEV, FF),
            struct(BFLOAT, TOK_DEV, FF),
            struct(FLOAT, TOK_DEV, D),
            struct(BFLOAT, TOK_DEV, D),
            struct(BFLOAT, TOK_DEV, D),
            struct(FLOAT, 8, D),
        ),
        scratch_shapes=[
            pltpu.VMEM((TOK_DEV, D), FLOAT),
            pltpu.VMEM((D, D), BFLOAT),
            pltpu.SemaphoreType.DMA,
        ],
        cost_estimate=pl.CostEstimate(
            flops=4_000_000_000, bytes_accessed=20_000_000, transcendentals=400_000
        ),
        compiler_params=params(BIG),
    )(new, sel, logit, hidden, branch, mixed, gains, router, wo, gate, up, weights)


def enter_back_kernel(
    in_ref, dq_ref, own_ref, hidden_ref, gain_ref, wq_ref, wk_ref, wv_ref, cos_ref, sin_ref,
    pair_ref, out_ref, small_ref
):
    keys = turn(own_ref[:, 0:320].T, cos_ref[...], -sin_ref[...]).T.astype(BFLOAT)
    values = own_ref[:, 320:640].astype(BFLOAT)
    pair_ref[:, 0:320] = keys
    pair_ref[:, 320:640] = values
    grad_normed = (
        contract_cols(dq_ref[...], wq_ref[...])
        + contract_cols(keys, wk_ref[...])
        + contract_cols(values, wv_ref[...])
    )
    grad_hidden, gain_row = normalize_back(hidden_ref[...], gain_ref[0:1, :], grad_normed)
    out_ref[...] = in_ref[...] + grad_hidden
    small_ref[...] = jnp.concatenate([gain_row, jnp.zeros((7, D), FLOAT)], axis=0)


def enter_back(grad_in, dq, own, hidden, gains, wq, wk, wv, cosine, sine):
    return pl.pallas_call(
        enter_back_kernel,
        out_shape=(
            struct(BFLOAT, TOK_DEV, 640),
            struct(FLOAT, TOK_DEV, D),
            struct(FLOAT, 8, D),
        ),
        compiler_params=params(24),
    )(grad_in, dq, own, hidden, gains, wq, wk, wv, cosine, sine)


HEAD_BLOCK = 1024


def head_kernel(rows_ref, near_ref, *refs):
    block_refs, (target_ref, table_ref, logit_ref, pick_ref, out_ref, stat_ref) = refs[:8], refs[8:]
    step = pl.program_id(0)

    @pl.when(step == 0)
    def first():
        picked = None
        for i, ref in enumerate(block_refs):
            hot = rows_ref[...] == near_ref[:, 128 * i : 128 * i + 128]
            part = nn(hot.astype(FLOAT).astype(BFLOAT), ref[...])
            picked = part if picked is None else picked + part
        pick_ref[...] = picked.astype(BFLOAT)
        lane = lax.broadcasted_iota(jnp.int32, (256, 128), 1)
        stat_ref[...] = jnp.where(lane == 0, MASKED, 0.0)

    logits = contract_cols(pick_ref[...], table_ref[...])
    logit_ref[...] = logits
    place = step * HEAD_BLOCK + lax.broadcasted_iota(jnp.int32, (256, HEAD_BLOCK), 1)
    hit = jnp.sum(jnp.where(place == target_ref[...], logits, 0.0), axis=1, keepdims=True)
    old = stat_ref[:, 0:1]
    top = jnp.maximum(old, jnp.max(logits, axis=1, keepdims=True))
    total = stat_ref[:, 1:2] * jnp.exp(old - top) + jnp.sum(
        jnp.exp(logits - top), axis=1, keepdims=True
    )
    stat_ref[:, 1:2] = total
    stat_ref[:, 2:3] = stat_ref[:, 2:3] + hit
    stat_ref[:, 0:1] = top

    @pl.when(step == pl.num_programs(0) - 1)
    def last():
        out_ref[...] = stat_ref[...].T[0:8]


def head(loss_rows, near_rows, blocks, local_targets, table):
    return pl.pallas_call(
        head_kernel,
        grid=(VOCAB_MP // HEAD_BLOCK,),
        in_specs=[whole(256, 1), whole(1, ROWS)]
        + [whole(TOK_DEV, D)] * MP
        + [whole(256, 1), pl.BlockSpec((HEAD_BLOCK, D), lambda i: (i, 0))],
        out_specs=[
            pl.BlockSpec((256, HEAD_BLOCK), lambda i: (0, i)),
            whole(256, D),
            whole(8, 256),
        ],
        out_shape=(
            struct(FLOAT, 256, VOCAB_MP),
            struct(BFLOAT, 256, D),
            struct(FLOAT, 8, 256),
        ),
        scratch_shapes=[pltpu.VMEM((256, 128), FLOAT)],
        compiler_params=params(BIG),
    )(loss_rows, near_rows, *blocks, local_targets, table)


def head_back_kernel(
    rows_ref, near_ref, target_ref, stat_ref, logit_ref, table_ref, grad_ref, *refs
):
    block_refs, (sum_ref, norm_ref) = refs[:8], refs[8:]
    step = pl.program_id(0)

    @pl.when(step == 0)
    def first():
        norm = stat_ref[0:1, :] + jnp.log(stat_ref[1:2, :])
        norm_ref[:, 0:8] = jnp.concatenate([norm] * 8, axis=0).T
        sum_ref[...] = jnp.zeros((256, D), FLOAT)

    place = step * HEAD_BLOCK + lax.broadcasted_iota(jnp.int32, (256, HEAD_BLOCK), 1)
    probs = jnp.exp(logit_ref[...] - norm_ref[:, 0:1])
    hit = jnp.where(place == target_ref[...], 1.0, 0.0)
    grads = ((probs - hit) * (1.0 / TOK_DEV)).astype(BFLOAT)
    grad_ref[...] = grads
    sum_ref[...] += nn(grads, table_ref[...])

    @pl.when(step == pl.num_programs(0) - 1)
    def last():
        total = sum_ref[...].astype(BFLOAT)
        for i, ref in enumerate(block_refs):
            hot = rows_ref[...] == near_ref[:, 128 * i : 128 * i + 128]
            ref[...] = contract_rows(hot.astype(FLOAT).astype(BFLOAT), total).astype(BFLOAT)


def head_back(loss_rows, near_rows, local_targets, stats, logits, table):
    cols = pl.BlockSpec((256, HEAD_BLOCK), lambda i: (0, i))
    return pl.pallas_call(
        head_back_kernel,
        grid=(VOCAB_MP // HEAD_BLOCK,),
        in_specs=[
            whole(256, 1),
            whole(1, ROWS),
            whole(256, 1),
            whole(8, 256),
            cols,
            pl.BlockSpec((HEAD_BLOCK, D), lambda i: (i, 0)),
        ],
        out_specs=[cols] + [whole(TOK_DEV, D)] * MP,
        out_shape=[struct(BFLOAT, 256, VOCAB_MP)] + [struct(BFLOAT, TOK_DEV, D)] * MP,
        scratch_shapes=[pltpu.VMEM((256, D), FLOAT), pltpu.VMEM((256, 128), FLOAT)],
        compiler_params=params(BIG),
    )(loss_rows, near_rows, local_targets, stats, logits, table)


def head_table_kernel(grad_ref, pick_ref, out_ref):
    out_ref[...] = contract_rows(grad_ref[...], pick_ref[...]).astype(BFLOAT)


def head_table(grads, picked):
    return pl.pallas_call(
        head_table_kernel,
        grid=(VOCAB_MP // HEAD_BLOCK,),
        in_specs=[pl.BlockSpec((256, HEAD_BLOCK), lambda i: (0, i)), whole(256, D)],
        out_specs=pl.BlockSpec((HEAD_BLOCK, D), lambda i: (i, 0)),
        out_shape=struct(BFLOAT, VOCAB_MP, D),
        compiler_params=params(BIG),
    )(grads, picked)


def mlp_grad_kernel(which_ref, *refs):
    out_ref = refs[-1]

    def joined(first):
        return jnp.concatenate([ref[...] for ref in refs[first:-1:10]], axis=0)

    def both(first):
        return jnp.concatenate([joined(first), joined(first + 5)], axis=0)

    rights = both(3), both(3), both(4)
    for i in range(3):
        out_ref[:, i] = contract_rows(both(i), rights[i]).reshape(8, 80, D).astype(BFLOAT)


def mlp_grads(which, kept, received):
    def cols(width, place):
        return pl.BlockSpec((TOK_DEV, width), place)

    rights = [cols(D, lambda i, half: (0, 0))] * 2
    own = [cols(640, lambda i, half: (0, half[0] * 2 + i))] * 3 + rights
    far = [cols(640, lambda i, half: (0, i))] * 3 + rights
    args = []
    for parts, other in zip(kept, received):
        args += [*parts, *other]
    return pl.pallas_call(
        mlp_grad_kernel,
        grid_spec=pltpu.PrefetchScalarGridSpec(
            num_scalar_prefetch=1,
            grid=(2,),
            in_specs=(own + far) * RECUR,
            out_specs=pl.BlockSpec((8, 3, 80, D), lambda i, half: (i, 0, 0, 0)),
        ),
        out_shape=struct(BFLOAT, 16, 3, 80, D),
        compiler_params=params(BIG),
    )(which.reshape(1), *args)


def square_grad_kernel(*refs):
    wq_ref, wo_ref = refs[-2:]
    ins = refs[:-2]

    def joined(first):
        return jnp.concatenate([ref[...] for ref in ins[first::8]], axis=0)

    def both(first):
        return jnp.concatenate([joined(first), joined(first + 4)], axis=0)

    wq_ref[...] = contract_rows(both(2), both(3)).astype(BFLOAT)
    wo_ref[...] = contract_rows(both(0), both(1)).astype(BFLOAT)


def square_grads(kept, received):
    args = []
    for parts, other in zip(kept, received):
        args += [*parts, *other]
    return pl.pallas_call(
        square_grad_kernel,
        grid=(1,),
        in_specs=[whole(TOK_DEV, D)] * (8 * RECUR),
        out_specs=[whole(D, D), whole(D, D)],
        out_shape=(struct(BFLOAT, D, D), struct(BFLOAT, D, D)),
        compiler_params=params(BIG),
    )(*args)


def pack_grad_kernel(starts_ref, *refs):
    wq_ref, wo_ref, rows_ref = refs[:3]
    ins = refs[3:-2]
    out_ref, buf = refs[-2:]
    buf[0:960, :] = wq_ref[...]
    buf[1600:2560, :] = wo_ref[...]
    buf[2560:2576, :] = rows_ref[...].astype(BFLOAT)
    buf[2576:2688, :] = jnp.zeros((112, D), BFLOAT)
    normed = jnp.concatenate([ref[...] for ref in ins[0::4] + ins[1::4]], axis=0)
    grads = jnp.concatenate([ref[...] for ref in ins[2::4] + ins[3::4]], axis=0)
    line = lax.broadcasted_iota(jnp.int32, (960, 320), 0)
    place = lax.broadcasted_iota(jnp.int32, (960, 320), 1)
    full = contract_rows(normed, grads).astype(BFLOAT)
    for i in range(3):
        chosen = (line == 3 * place + i).astype(FLOAT).astype(BFLOAT)
        rows = contract_rows(chosen, full).astype(BFLOAT)
        buf[960:1280, 320 * i : 320 * i + 320] = rows[:, 0:320]
        buf[1280:1600, 320 * i : 320 * i + 320] = rows[:, 320:640]
    for i in range(4):
        start = pl.multiple_of(starts_ref[i], 16)
        out_ref[i] = buf[pl.ds(start, 352), :]


def pack_grads(starts, wq, wo, small, kept, received):
    args = []
    for (normed, pair), (far_normed, far_pair) in zip(kept, received):
        args += [normed, far_normed, pair, far_pair]
    specs = [whole(TOK_DEV, D)] * 2 + [whole(TOK_DEV, 640)] * 2
    return pl.pallas_call(
        pack_grad_kernel,
        grid=(1,),
        in_specs=[pl.BlockSpec(memory_space=pltpu.SMEM), whole(D, D), whole(D, D), whole(16, D)]
        + specs * RECUR,
        out_specs=whole(4, 352, D),
        out_shape=struct(BFLOAT, 4, 352, D),
        scratch_shapes=[pltpu.VMEM((PACK_PAD, D), BFLOAT)],
        compiler_params=params(BIG),
    )(starts, wq, wo, small, *args)


def adam_update(master, first, second, grad, clip):
    grad = grad * clip
    first_new = BETA_ONE * first + (1.0 - BETA_ONE) * grad
    second_new = BETA_TWO * second + (1.0 - BETA_TWO) * grad * grad
    corr_one = 1.0 - BETA_ONE**STEP
    corr_two = 1.0 - BETA_TWO**STEP
    master_new = master - LEARN_RATE * (
        first_new / corr_one / (jnp.sqrt(second_new / corr_two) + ADAM_EPS) + DECAY * master
    )
    return (master_new, first_new, second_new)


def pack_row(device):
    return (1283 * device) // 64


def join_kernel(blocks_ref, wq_ref, wk_ref, wv_ref, wo_ref, small_ref, buf):
    row = lax.broadcasted_iota(jnp.int32, (128, 240), 0)
    place = lax.broadcasted_iota(jnp.int32, (128, 240), 1)
    device = (place * 2731) >> 16
    for step in range(PACK_PAD // 128):
        first = min(step * 128 * 64 // 1283, 118) // 2 * 2
        source = ((1283 * (first + device)) >> 6) + place - 24 * device
        chosen = (source == row + 128 * step).astype(FLOAT).astype(BFLOAT)
        buf[128 * step : 128 * step + 128, :] = nn(
            chosen, blocks_ref[24 * first : 24 * first + 240, :]
        ).astype(BFLOAT)
    wq_ref[...] = buf[0:960, :]
    wo_ref[...] = buf[1600:2560, :]
    small_ref[...] = buf[2560:2576, :]
    line = lax.broadcasted_iota(jnp.int32, (960, 320), 0)
    place = lax.broadcasted_iota(jnp.int32, (960, 320), 1)
    for first, ref in ((960, wk_ref), (1280, wv_ref)):
        total = None
        for i in range(3):
            chosen = (line == 3 * place + i).astype(FLOAT).astype(BFLOAT)
            part = nn(chosen, buf[first : first + 320, 320 * i : 320 * i + 320])
            total = part if total is None else total + part
        ref[...] = total.astype(BFLOAT)


def join_pack(blocks):
    return pl.pallas_call(
        join_kernel,
        out_shape=(
            struct(BFLOAT, D, D),
            struct(BFLOAT, D, 320),
            struct(BFLOAT, D, 320),
            struct(BFLOAT, D, D),
            struct(BFLOAT, 16, D),
        ),
        scratch_shapes=[pltpu.VMEM((PACK_PAD, D), BFLOAT)],
        compiler_params=params(32),
    )(blocks)


def stage(value, axis, index):
    total = lax.dynamic_index_in_dim(value, index, 0, False).astype(FLOAT)
    for k in (1, 2, 3):
        sent = lax.dynamic_index_in_dim(value, (index + k) % 4, 0, False)
        total = total + shift(sent, axis, k).astype(FLOAT)
    return total


def gradients(
    dense,
    token_ids,
    targets,
    loss_rows,
    selections,
    boundary,
    pack_master,
    mlp_master,
    table_master,
):
    z = lax.axis_index("z")
    core = lax.axis_index("core")
    y = lax.axis_index("y")
    x = lax.axis_index("x")
    model_index = z * 2 + core
    data_index = y * 4 + x
    device = model_index * DP + data_index
    own_table = table_master.astype(BFLOAT)

    near = jnp.stack([((z + k) % 4) * 2 + (core ^ j) for j in (0, 1) for k in range(4)])
    near_rows = (near[:, None] * TOK_DEV + jnp.arange(TOK_DEV, dtype=jnp.int32)[None, :]).reshape(-1)

    pack_offset = PACK_DEV * device - D * pack_row(device)
    pack_block = lax.dynamic_update_slice(
        jnp.zeros((24 * D,), BFLOAT), pack_master.astype(BFLOAT), (pack_offset,)
    ).reshape(24, D)
    pack_quad = [pack_block] + [shift(pack_block, "x", k) for k in (1, 2, 3)]
    pack_rows = []
    for i in range(4):
        part = pack_quad[3]
        for k in (2, 1, 0):
            part = jnp.where(x == (i + k) % 4, pack_quad[k], part)
        pack_rows.append(part)
    pack_blocks = lax.all_gather(
        jnp.concatenate(pack_rows, axis=0), ("z", "core", "y"), axis=0, tiled=True
    )
    mlp_own = mlp_master.astype(BFLOAT)
    mlp_quad = jnp.concatenate([mlp_own] + [shift(mlp_own, "z", k) for k in (1, 2, 3)], axis=1)

    group_ids = token_ids[0]
    near_ids = reorder(group_ids.reshape(MP, TOK_DEV), near).reshape(-1)
    local_ids = near_ids - model_index * VOCAB_MP
    inside = (local_ids >= 0) & (local_ids < VOCAB_MP)
    high = local_ids >> 7
    low = local_ids & 127
    high_hot = (high[:, None] == jnp.arange(48)[None, :]).astype(BFLOAT)
    low_hot = (low[:, None] == jnp.arange(128)[None, :]).astype(BFLOAT)
    present = (contract_rows(high_hot, low_hot) > 0).reshape(DP, VOCAB_DEV)
    before = (jnp.arange(VOCAB_DEV)[:, None] < jnp.arange(VOCAB_DEV)[None, :]).astype(BFLOAT)
    slots = mm(present.astype(BFLOAT), before)
    asked = present & (slots < CAP)
    over = jnp.max(jnp.where(present & (slots >= CAP), 1.0, 0.0))
    slot_table = jnp.where(asked, slots, 255.0).reshape(48, 128).astype(BFLOAT)
    token_slot = jnp.sum(mm(high_hot, slot_table) * low_hot.astype(FLOAT), axis=-1)
    token_place = jnp.where(
        inside & (token_slot < CAP), (high // 3) * CAP + token_slot.astype(jnp.int32), -1
    )
    token_place = token_place[:, None]
    match = asked[:, None, :] & (slots[:, None, :] == jnp.arange(CAP, dtype=FLOAT)[None, :, None])
    request = (
        jnp.sum(jnp.where(match, jnp.arange(1, VOCAB_DEV + 1, dtype=FLOAT)[None, None, :], 0.0), axis=-1)
        - 1.0
    )
    request = jnp.concatenate([request, jnp.full((DP, 8), over, FLOAT)], axis=1)
    request = lax.all_to_all(request, DP_AXES, 0, 0, tiled=True)
    over = jnp.max(request[:, CAP:])
    owner_hot = (
        request[:, :CAP].reshape(-1)[:, None] == jnp.arange(VOCAB_DEV, dtype=FLOAT)[None, :]
    ).astype(BFLOAT)
    mlp_quad, owner_hot = tie(mlp_quad, owner_hot)
    mlp_weights = lax.all_gather(
        mlp_quad.reshape(3 * 80, D), ("core", "y", "x"), axis=0, tiled=True
    )
    mlp_weights = mlp_weights.reshape(32, 3, 80, D)
    asked_rows = lax.all_to_all(mm(owner_hot, own_table).astype(BFLOAT), DP_AXES, 0, 0, tiled=True)
    own_table, asked_rows = tie(own_table, asked_rows)
    table = lax.all_gather(own_table, DP_AXES, axis=0, tiled=True)
    if dense:
        rows = jnp.take(table, jnp.clip(local_ids, 0, VOCAB_MP - 1), axis=0)
        looked = jnp.where(inside[:, None], rows, jnp.zeros_like(rows))
        looked = [looked[128 * i : 128 * i + 128] for i in range(MP)]
    else:
        looked = spread(token_place, asked_rows)
    hidden, pack_blocks = scatter_group(looked, pack_blocks)

    w_query, w_key, w_value, w_out, last_rows = join_pack(pack_blocks)
    gains = jnp.concatenate([last_rows[:3].astype(FLOAT), jnp.zeros((5, D), FLOAT)])
    router = last_rows[3:6].astype(FLOAT)

    half_dim = HEAD_DIM // 2
    freqs = ROPE_BASE ** (-jnp.arange(half_dim, dtype=FLOAT) / half_dim)
    first_row = data_index * ROWS + model_index * TOK_DEV
    angles = freqs[:, None] * (first_row + jnp.arange(TOK_DEV, dtype=jnp.int32)).astype(FLOAT)[None, :]
    turns = (jnp.cos(angles), jnp.sin(angles))
    projections = (w_query, w_key, w_value) + turns
    group_sel = selections.reshape(RECUR, DP, MP, TOK_DEV)
    prev_index = jnp.maximum(data_index - 1, 0)
    here_sel = lax.dynamic_index_in_dim(group_sel, data_index, 1, False)
    own_sel = lax.dynamic_index_in_dim(here_sel, model_index, 1, False)
    near_sel = reorder(here_sel, near).reshape(RECUR, ROWS)
    prev_sel = reorder(lax.dynamic_index_in_dim(group_sel, prev_index, 1, False), near)
    prev_sel = prev_sel.reshape(RECUR, ROWS)
    start = lax.dynamic_index_in_dim(boundary, data_index, 0, False)
    prev_start = lax.dynamic_index_in_dim(boundary, prev_index, 0, False)
    place = (model_index * TOK_DEV + jnp.arange(TOK_DEV, dtype=jnp.int32))[None, :]
    key_place = near_rows[:, None]
    biases = []
    for step in range(RECUR):
        own_seen = (
            (key_place <= place)
            & ((key_place < start) == (place < start))
            & ((near_sel[step][:, None] > 0) | (key_place == place))
        )
        prev_seen = (
            (data_index > 0)
            & (place < start)
            & (key_place >= prev_start)
            & (prev_sel[step][:, None] > 0)
        )
        seen = [prev_seen[:512], own_seen[:512], prev_seen[512:], own_seen[512:]]
        biases.append(jnp.where(jnp.concatenate(seen, axis=0), 0.0, MASKED))

    sel_cols = own_sel.astype(FLOAT)[:, :, None]
    saves = []
    logits_all = []
    normed, queries, pair = enter(hidden, gains, *projections)
    for step in range(RECUR):
        pairs = group_gather(pair)
        attended, log_total = attend(queries, pairs, biases[step])
        mixed, mlp_input, gate, up, inner, branch, logit, new_hidden, *nexts = block(
            attended,
            hidden,
            sel_cols[step],
            gains,
            router[step : step + 1],
            w_out,
            mlp_weights,
            projections if step < RECUR - 1 else None,
        )
        logits_all.append(logit[:, 0])
        saves.append(
            (
                hidden,
                normed,
                queries,
                pairs,
                attended,
                log_total,
                mixed,
                mlp_input,
                gate,
                up,
                inner,
                branch,
                logit,
            )
        )
        hidden = new_hidden
        if nexts:
            normed, queries, pair = nexts
    logits_all = jnp.stack(logits_all)
    penalty_total = jnp.sum(jax.nn.softplus(logits_all) - own_sel.astype(FLOAT) * logits_all)

    normed_final = rms_scale(hidden, gains[2]).astype(BFLOAT)
    final_rows = gather_group(normed_final)
    row_targets = lax.dynamic_index_in_dim(targets, data_index, 0, keepdims=False)
    head_args = (loss_rows[0][:, None], near_rows[None, :])
    local_targets = (row_targets - model_index * VOCAB_MP)[:, None]
    logits, picked, stats = head(*head_args, final_rows, local_targets, table)
    flag_row = lax.broadcasted_iota(jnp.int32, (8, 256), 0) == 3
    stats = jnp.where(flag_row, over, stats)

    def join_stats(parts):
        top = parts[0][0]
        for part in parts[1:]:
            top = jnp.maximum(top, part[0])
        total = sum(part[1] * jnp.exp(part[0] - top) for part in parts)
        over = parts[0][3]
        for part in parts[1:]:
            over = jnp.maximum(over, part[3])
        rest = [jnp.zeros_like(top)] * 4
        return jnp.stack([top, total, sum(part[2] for part in parts), over] + rest)

    stats = join_stats([stats, swap(stats)])
    stats = join_stats([stats] + [shift(stats, "z", k) for k in (1, 2, 3)])
    log_norm = stats[0] + jnp.log(stats[1])
    cross = log_norm - stats[2]
    per_device = cross.shape[0] // MP
    loss_part = (
        jnp.sum(lax.dynamic_slice_in_dim(cross, model_index * per_device, per_device))
        + ROUTER_LOSS * penalty_total
    )
    grad_logits, *scattered = head_back(*head_args, local_targets, stats, logits, table)
    grad_final, grad_logits = scatter_group(scattered, grad_logits)
    head_grad = head_table(grad_logits, picked)
    grad_hidden, grad_gain_final = rms_back(hidden, gains[2], grad_final)
    if not dense:
        head_grad = lax.psum_scatter(head_grad, DP_AXES, scatter_dimension=0, tiled=True)

    mlp_kept, mlp_far, square_kept, square_far, pack_kept, pack_far = [], [], [], [], [], []
    loss_part, flag, grad_hidden = tie(loss_part, stats[3, 0], grad_hidden)
    router_rows = [None] * RECUR
    gain_one = jnp.zeros((1, D), FLOAT)
    gain_two = jnp.zeros((1, D), FLOAT)
    for step in reversed(range(RECUR)):
        (
            hidden_in,
            normed,
            queries,
            pairs,
            attended,
            log_total,
            mixed,
            mlp_input,
            gate,
            up,
            inner,
            branch,
            logit,
        ) = saves[step]
        grad_rows, grad_gate, grad_up, grad_in, grad_attn, grad_attended, small = block_back(
            grad_hidden,
            sel_cols[step],
            logit,
            hidden_in,
            branch,
            mixed,
            gains,
            router[step : step + 1],
            w_out,
            gate,
            up,
            mlp_weights,
        )
        gain_two = gain_two + small[0:1]
        router_rows[step] = small[1:2]
        mlp_kept.append((grad_gate, grad_up, inner, mlp_input, grad_rows))

        def far_half(value):
            return lax.dynamic_slice_in_dim(value, (1 - core) * (FF // 2), FF // 2, 1)

        mlp_far.append(
            [swap(far_half(part)) for part in (grad_gate, grad_up, inner)]
            + [swap(mlp_input), swap(grad_rows)]
        )
        grad_query, *grad_sides = attend_back(
            queries, pairs, biases[step], log_total, attended, grad_attended, *turns
        )
        far_normed, far_attended = early if step == 0 else (swap(normed), swap(attended))
        square_kept.append((attended, grad_attn, normed, grad_query))
        square_far.append((far_attended, swap(grad_attn), far_normed, swap(grad_query)))
        if step == 0:
            tied = tie(*grad_sides, *mlp_kept[-1])
            grad_sides, mlp_kept[-1] = tied[:4], tied[4:]
        grad_own = group_scatter(*grad_sides)
        if step == 0:
            mlp_half = mlp_grads(core.astype(jnp.int32), mlp_kept, mlp_far)
            mlp_sum = lax.psum_scatter(
                mlp_half.reshape(16 * 240, D), DP_AXES, scatter_dimension=0, tiled=True
            )
            squares = square_grads(square_kept, square_far)
            grad_own, mlp_half, *squares = tie(grad_own, mlp_half, *squares)
        grad_pair, grad_hidden, small = enter_back(
            grad_in, grad_query, grad_own, hidden_in, gains, *projections
        )
        gain_one = gain_one + small[0:1]
        pack_kept.append((normed, grad_pair))
        pack_far.append((far_normed, swap(grad_pair)))
        if step > 0:
            count = len(mlp_far[-1])
            tied = tie(grad_hidden, *mlp_far[-1], *square_far[-1])
            grad_hidden, mlp_far[-1] = tied[0], tied[1 : 1 + count]
            square_far[-1] = tied[1 + count :]
            pack_far[-1] = (square_far[-1][2], pack_far[-1][1])
        if step == 1:
            early = swap(saves[0][1]), swap(saves[0][4])
            if dense:
                *early, grad_hidden = tie(*early, grad_hidden)
            else:
                *early, head_grad, grad_hidden = tie(*early, head_grad, grad_hidden)

    sent = grad_hidden.astype(BFLOAT)
    grad_embed = [sent] + [shift(sent, "z", -k) for k in (1, 2, 3)]
    grad_embed[1], grad_embed[3], gain_one = tie(grad_embed[1], grad_embed[3], gain_one)
    grad_embed += [swap(part) for part in grad_embed]

    def aligned_row(which):
        return (pack_row(which) // 16) * 16

    small = jnp.concatenate(
        [
            gain_one,
            gain_two,
            grad_gain_final[None],
            *router_rows,
            jnp.zeros((10, D), FLOAT),
        ]
    )
    small = small + swap(small)
    starts = jnp.stack([aligned_row(DP * (2 * i + core)) for i in range(4)]).astype(jnp.int32)
    part = pack_grads(starts, *squares, small, pack_kept, pack_far)

    def y_windows(value):
        return jnp.stack([value[..., 80 * i : 80 * i + 112, :] for i in range(4)])

    def x_windows(value):
        return jnp.stack([value[..., i : i + 48, :] for i in (0, 16, 40, 56)])

    part = stage(part, "z", z).astype(BFLOAT)
    part = stage(y_windows(part), "y", y).astype(BFLOAT)
    part, mlp_sum = tie(x_windows(part), mlp_sum)
    mlp_sum = mlp_sum.reshape(3, 4, UNITS, D).transpose(1, 0, 2, 3)
    mlp_grad = mlp_sum[0].astype(FLOAT)
    for k in (1, 2, 3):
        mlp_grad = mlp_grad + shift(mlp_sum[k], "z", -k).astype(FLOAT)
    part = stage(part, "x", x).reshape(-1)
    begin = aligned_row(DP * model_index) + 80 * y + (20 * x) // 8 * 8
    pack_grad = lax.dynamic_slice(part, (PACK_DEV * device - D * begin,), (PACK_DEV,))

    if dense:
        kept_rows = jnp.concatenate(grad_embed).astype(FLOAT) * inside.astype(FLOAT)[:, None]
        sums = jax.ops.segment_sum(
            kept_rows, jnp.clip(local_ids, 0, VOCAB_MP - 1), num_segments=VOCAB_MP
        )
        table_grad = lax.psum_scatter(
            (head_grad.astype(FLOAT) + sums).astype(BFLOAT),
            DP_AXES,
            scatter_dimension=0,
            tiled=True,
        ).astype(FLOAT)
    else:
        unique = collect(token_place, grad_embed)
        unique = lax.all_to_all(unique, DP_AXES, 0, 0, tiled=True)
        table_grad = head_grad.astype(FLOAT) + contract_rows(owner_hot, unique)
    table_grad = by_cols(table_grad)
    squares = (
        jnp.sum(pack_grad * pack_grad)
        + jnp.sum(mlp_grad * mlp_grad)
        + jnp.sum(table_grad * table_grad)
    )
    return pack_grad, mlp_grad, table_grad, squares, loss_part, flag


def shards(
    token_ids,
    targets,
    loss_rows,
    selections,
    boundary,
    pack_master,
    pack_first,
    pack_second,
    mlp_master,
    mlp_first,
    mlp_second,
    table_master,
    table_first,
    table_second,
):
    args = (
        token_ids,
        targets,
        loss_rows,
        selections,
        boundary,
        pack_master,
        mlp_master,
        table_master,
    )
    *found, over = tie(*gradients(False, *args))
    pack_grad, mlp_grad, table_grad, squares, loss_part = lax.cond(
        over > 0, lambda: gradients(True, *args)[:5], lambda: tuple(found)
    )
    lane = lax.broadcasted_iota(jnp.int32, (128, 128), 1)
    sums = lax.all_to_all(
        jnp.where(lane == 0, squares, loss_part), ALL_AXES, 0, 0, tiled=True
    )
    sums = jnp.sum(sums, axis=0, keepdims=True)
    total_squares = sums[0, 0]
    loss_sum = sums[0, 1]
    grad_norm = jnp.sqrt(total_squares)
    clip = CLIP_NORM / jnp.maximum(grad_norm, CLIP_NORM)
    pack_new, pack_first_new, pack_second_new = adam_update(
        pack_master, pack_first, pack_second, pack_grad, clip
    )
    mlp_new, mlp_first_new, mlp_second_new = adam_update(
        mlp_master, mlp_first, mlp_second, mlp_grad, clip
    )
    table_new, table_first_new, table_second_new = adam_update(
        table_master, table_first, table_second, table_grad, clip
    )
    return (
        pack_new,
        pack_first_new,
        pack_second_new,
        mlp_new,
        mlp_first_new,
        mlp_second_new,
        table_new,
        table_first_new,
        table_second_new,
        loss_sum,
        grad_norm,
    )


def solution(mesh):
    grid = Mesh(mesh.devices.reshape(4, 2, 4, 4), ALL_AXES)
    owners = (P(ALL_AXES), P(None, ALL_AXES, None), P(ALL_AXES, None))
    group = P(DP_AXES, None)
    masters = tuple(spec for spec in owners for _ in range(3))
    return jax.shard_map(
        shards,
        mesh=grid,
        in_specs=(group, P(), group, P(), P()) + masters,
        out_specs=masters + (P(), P()),
        check_vma=False,
    )
```

```python
import functools

import jax
import jax.numpy as jnp
from jax import lax
from jax.experimental import pallas as pl
from jax.experimental.layout import Layout, with_layout_constraint
from jax.experimental.pallas import tpu as pltpu
from jax.sharding import Mesh
from jax.sharding import PartitionSpec as P

D = 960
HEADS = 15
KV_HEADS = 5
HEAD_DIM = 64
FF = 2560
RECUR = 3
STEP = 10
TOK_DEV = 128
ROWS = 1024
MP = 8
DP = 16
VOCAB_MP = 6144
VOCAB_DEV = 384
UNITS = 20
PACK_DEV = 19245
PACK_ROWS = 2566
PACK_PAD = 2688
CAP = 24

EPS_NORM = 1e-05
ROPE_BASE = 10000.0
ROUTER_LOSS = 0.1
CLIP_NORM = 1.0
LEARN_RATE = 0.05
BETA_ONE = 0.9
BETA_TWO = 0.95
ADAM_EPS = 1e-08
DECAY = 0.1
MASKED = -1e30
HIGHEST = lax.Precision.HIGHEST
BFLOAT = jnp.bfloat16
FLOAT = jnp.float32
DP_AXES = ("y", "x")
ALL_AXES = ("z", "core", "y", "x")


def shift(value, axis, steps):
    return lax.ppermute(value, axis, [(i, (i + steps) % 4) for i in range(4)])


def swap(value):
    return lax.ppermute(value, "core", [(0, 1), (1, 0)])


def gather_group(value):
    near = [value] + [shift(value, "z", -k) for k in (1, 2, 3)]
    return near + [swap(part) for part in near]


def scatter_group(blocks, other=None):
    half = [near.astype(FLOAT) + swap(far).astype(FLOAT) for near, far in zip(blocks[:4], blocks[4:])]
    total = half[0]
    sent = [part.astype(BFLOAT) for part in half[1:]]
    if other is not None:
        *sent, other = tie(*sent, other)
    for k in (1, 2, 3):
        total = total + shift(sent[k - 1], "z", k).astype(FLOAT)
    return total if other is None else (total, other)


def rms_scale(values, weight):
    return values * lax.rsqrt(jnp.mean(values * values, axis=-1, keepdims=True) + EPS_NORM) * weight


def rms_back(values, weight, grad_out):
    inverse = lax.rsqrt(jnp.mean(values * values, axis=-1, keepdims=True) + EPS_NORM)
    weighted = grad_out * weight
    grad_values = inverse * weighted - values * (inverse * inverse * inverse) * jnp.mean(
        weighted * values, axis=-1, keepdims=True
    )
    return (grad_values, jnp.sum(grad_out * values * inverse, axis=0))


def mm(left, right):
    return jnp.dot(left, right, preferred_element_type=FLOAT)


def contract_rows(left, right):
    return lax.dot_general(left, right, (((0,), (0,)), ((), ())), preferred_element_type=FLOAT)


def contract_cols(left, right):
    return lax.dot_general(left, right, (((1,), (1,)), ((), ())), preferred_element_type=FLOAT)


def reorder(blocks, order):
    hit = order[:, None] == jnp.arange(MP)[None, :]
    return jnp.sum(jnp.where(hit[:, :, None], blocks[..., None, :, :], 0), axis=-2)


def by_cols(value):
    return with_layout_constraint(value, Layout((1, 0)))


def tie(*values):
    return lax.optimization_barrier(values)


def group_gather(pair):
    own = [pair]
    for k in (1, 2, 3):
        own.append(lax.ppermute(pair, "z", [((i + k) % 4, i) for i in range(4) if (i + k) % 4 < i]))
    prev = []
    for k in range(4):
        pairs = []
        for i in range(3):
            for g in range(1, DP):
                pairs.append((((i + k) % 4) * DP + g - 1, i * DP + g))
        prev.append(lax.ppermute(pair, ("z",) + DP_AXES, pairs))
    return prev + own + [swap(part) for part in prev] + [swap(part) for part in own]


def group_scatter(prev, own, prev_far, own_far):
    own = (own.astype(FLOAT) + swap(own_far).astype(FLOAT)).astype(BFLOAT).reshape(4, TOK_DEV, -1)
    prev = (prev.astype(FLOAT) + swap(prev_far).astype(FLOAT)).astype(BFLOAT).reshape(4, TOK_DEV, -1)
    total = own[0].astype(FLOAT)
    for k in (1, 2, 3):
        pairs = [(i, (i + k) % 4) for i in range(4) if (i + k) % 4 < i]
        total = total + lax.ppermute(own[k], "z", pairs).astype(FLOAT)
    for k in range(4):
        pairs = []
        for i in range(3):
            for g in range(1, DP):
                pairs.append((i * DP + g, ((i + k) % 4) * DP + g - 1))
        total = total + lax.ppermute(prev[k], ("z",) + DP_AXES, pairs).astype(FLOAT)
    return total


def nn(left, right):
    return jnp.dot(left, right, preferred_element_type=FLOAT)


def head_rows(ref, head):
    return jnp.concatenate(
        [ref[:, 64 * (3 * head + i) : 64 * (3 * head + i) + 64] for i in range(3)], axis=0
    )


def head_lanes(ref, head):
    return jnp.concatenate(
        [ref[64 * (3 * head + i) : 64 * (3 * head + i) + 64, :] for i in range(3)], axis=1
    )


def turn(value, cosine, sine):
    parts = []
    for head in range(value.shape[0] // 64):
        first = value[64 * head : 64 * head + 32]
        second = value[64 * head + 32 : 64 * head + 64]
        parts.append(first * cosine - second * sine)
        parts.append(second * cosine + first * sine)
    return jnp.concatenate(parts, axis=0)


def normalize(values, weight):
    return values * lax.rsqrt(jnp.mean(values * values, axis=-1, keepdims=True) + EPS_NORM) * weight


def normalize_back(values, weight, grad_out):
    inverse = lax.rsqrt(jnp.mean(values * values, axis=-1, keepdims=True) + EPS_NORM)
    weighted = grad_out * weight
    grad_values = inverse * weighted - values * (inverse * inverse * inverse) * jnp.mean(
        weighted * values, axis=-1, keepdims=True
    )
    return grad_values, jnp.sum(grad_out * values * inverse, axis=0, keepdims=True)


def joined(refs, part, first):
    return jnp.concatenate(
        [ref[:, first : first + 64] for ref in refs[4 * part : 4 * part + 4]], axis=0
    )


def attend_kernel(query_ref, *refs):
    kv_refs, (bias_ref, out_ref, log_ref) = refs[:16], refs[16:]
    for head in range(KV_HEADS):
        queries = head_lanes(query_ref, head)
        top = None
        for part in range(4):
            keys = joined(kv_refs, part, 64 * head)
            values = joined(kv_refs, part, 320 + 64 * head)
            bias = bias_ref[512 * part : 512 * part + 512, :]
            scores = nn(keys, queries) + jnp.concatenate([bias, bias, bias], axis=1)
            part_top = jnp.max(scores, axis=0, keepdims=True)
            new_top = part_top if top is None else jnp.maximum(top, part_top)
            expo = jnp.exp(scores - new_top)
            part_total = jnp.sum(expo, axis=0, keepdims=True)
            part_out = contract_rows(values, expo.astype(BFLOAT))
            if top is None:
                total, out = part_total, part_out
            else:
                shrink = jnp.exp(top - new_top)
                total, out = total * shrink + part_total, out * shrink + part_out
            top = new_top
        out = (out / total).T.astype(BFLOAT)
        for i in range(3):
            place = 64 * (3 * head + i)
            out_ref[:, place : place + 64] = out[128 * i : 128 * i + 128]
        log_ref[head : head + 1, :] = top + jnp.log(total)


def params(mib):
    return pltpu.CompilerParams(vmem_limit_bytes=mib * 1024 * 1024)


def whole(*shape):
    return pl.BlockSpec(shape, lambda i: (0,) * len(shape))


def struct(kind, *shape):
    return jax.ShapeDtypeStruct(shape, kind)


def attend(queries, pairs, bias):
    return pl.pallas_call(
        attend_kernel,
        out_shape=(struct(BFLOAT, TOK_DEV, D), struct(FLOAT, 8, 3 * TOK_DEV)),
        cost_estimate=pl.CostEstimate(
            flops=12_000_000_000, bytes_accessed=5_000_000, transcendentals=4_000_000
        ),
        compiler_params=params(24),
    )(queries, *pairs, bias)


def attend_back_kernel(query_ref, *refs):
    kv_refs, refs = refs[:16], refs[16:]
    bias_ref, log_ref, att_ref, grad_ref, cos_ref, sin_ref, dq_ref = refs[:7]
    d_refs = refs[7:]
    cosine = jnp.concatenate([cos_ref[...]] * 3, axis=1)
    sine = jnp.concatenate([sin_ref[...]] * 3, axis=1)
    for head in range(KV_HEADS):
        queries = head_lanes(query_ref, head)
        grads = head_rows(grad_ref, head)
        outs = head_rows(att_ref, head)
        delta = jnp.sum((grads.astype(FLOAT) * outs.astype(FLOAT)).T, axis=0, keepdims=True)
        log_total = log_ref[head : head + 1, :]
        back = None
        for part, d_ref in enumerate(d_refs):
            keys = joined(kv_refs, part, 64 * head)
            values = joined(kv_refs, part, 320 + 64 * head)
            bias = bias_ref[512 * part : 512 * part + 512, :]
            probs = jnp.exp(
                nn(keys, queries) + jnp.concatenate([bias, bias, bias], axis=1) - log_total
            )
            grad_scores = (probs * (contract_cols(values, grads) - delta)).astype(BFLOAT)
            d_ref[:, 64 * head : 64 * head + 64] = contract_cols(grad_scores, queries).astype(BFLOAT)
            d_ref[:, 320 + 64 * head : 320 + 64 * head + 64] = nn(
                probs.astype(BFLOAT), grads
            ).astype(BFLOAT)
            part_back = contract_rows(keys, grad_scores)
            back = part_back if back is None else back + part_back
        back = turn(back * (HEAD_DIM**-0.5), cosine, -sine).T.astype(BFLOAT)
        for i in range(3):
            place = 64 * (3 * head + i)
            dq_ref[:, place : place + 64] = back[128 * i : 128 * i + 128]


def attend_back(mib, queries, pairs, bias, log_total, attended, grads, cosine, sine):
    side = struct(BFLOAT, 4 * TOK_DEV, 640)
    return pl.pallas_call(
        attend_back_kernel,
        out_shape=(struct(BFLOAT, TOK_DEV, D), side, side, side, side),
        cost_estimate=pl.CostEstimate(
            flops=20_000_000_000, bytes_accessed=9_000_000, transcendentals=4_000_000
        ),
        compiler_params=params(mib),
    )(queries, *pairs, bias, log_total, attended, grads, cosine, sine)


def project(hidden, gain, wq_ref, wk_ref, wv_ref, cos_ref, sin_ref, normed_ref, query_ref, pair_ref):
    normed = normalize(hidden, gain).astype(BFLOAT)
    normed_ref[...] = normed
    cosine, sine = cos_ref[...], sin_ref[...]
    keys = turn(nn(normed, wk_ref[...]).T, cosine, sine).T
    pair_ref[:, 0:320] = keys.astype(BFLOAT)
    pair_ref[:, 320:640] = nn(normed, wv_ref[...]).astype(BFLOAT)
    queries = turn(nn(normed, wq_ref[...]).T, cosine, sine)
    query_ref[...] = (queries * (HEAD_DIM**-0.5)).astype(BFLOAT)


PROJECTED = (
    struct(BFLOAT, TOK_DEV, D),
    struct(BFLOAT, D, TOK_DEV),
    struct(BFLOAT, TOK_DEV, 640),
)


def spread_kernel(place_ref, rows_ref, *out_refs):
    place = lax.broadcasted_iota(jnp.int32, (TOK_DEV, DP * CAP), 1)
    for part, ref in enumerate(out_refs):
        hot = (place_ref[128 * part : 128 * part + 128, :] == place).astype(FLOAT).astype(BFLOAT)
        ref[...] = nn(hot, rows_ref[...]).astype(BFLOAT)


def spread(place, rows):
    return pl.pallas_call(
        spread_kernel,
        out_shape=[struct(BFLOAT, TOK_DEV, D)] * MP,
        compiler_params=params(24),
    )(place, rows)


def collect_kernel(place_ref, *refs):
    place = lax.broadcasted_iota(jnp.int32, (TOK_DEV, DP * CAP), 1)
    total = None
    for part, ref in enumerate(refs[:-1]):
        hot = (place_ref[128 * part : 128 * part + 128, :] == place).astype(FLOAT).astype(BFLOAT)
        sums = contract_rows(hot, ref[...])
        total = sums if total is None else total + sums
    refs[-1][...] = total.astype(BFLOAT)


def collect(place, blocks):
    return pl.pallas_call(
        collect_kernel, out_shape=struct(BFLOAT, DP * CAP, D), compiler_params=params(24)
    )(place, *blocks)


def enter_kernel(hidden_ref, gain_ref, *refs):
    project(hidden_ref[...], gain_ref[0:1, :], *refs)


def enter(hidden, gains, wq, wk, wv, cosine, sine):
    return pl.pallas_call(enter_kernel, out_shape=PROJECTED, compiler_params=params(24))(
        hidden, gains, wq, wk, wv, cosine, sine
    )


BIG = 56
FF_BLOCK = 640
FF_STEPS = FF // FF_BLOCK


def weight(ref, which):
    return ref[:, which].reshape(FF_BLOCK, D)


def block_kernel(
    more, att_ref, hidden_ref, sel_ref, gain_ref, router_ref, wo_ref, weight_ref, *refs
):
    proj_in, refs = (refs[:5], refs[5:]) if more else ((), refs)
    mixed_ref, input_ref, gate_ref, up_ref, inner_ref, branch_ref, logit_ref, new_ref = refs[:8]
    proj_out, refs = (refs[8:11], refs[11:]) if more else ((), refs[8:])
    acc_ref = refs[0]
    step = pl.program_id(0)
    copies = [
        pltpu.make_async_copy(source, target, refs[4].at[i])
        for i, (source, target) in enumerate(zip(proj_in[:3], refs[1:4]))
    ]

    @pl.when(step == 0)
    def first():
        for copy in copies:
            copy.start()
        mixed = hidden_ref[...] + nn(att_ref[...], wo_ref[...])
        mixed_ref[...] = mixed
        input_ref[...] = normalize(mixed, gain_ref[1:2, :]).astype(BFLOAT)
        acc_ref[...] = mixed

    rows = input_ref[...]
    gate = contract_cols(rows, weight(weight_ref, 0))
    up = contract_cols(rows, weight(weight_ref, 1))
    gate_ref[...] = gate
    up_ref[...] = up
    inner = (gate * jax.nn.sigmoid(gate) * up).astype(BFLOAT)
    inner_ref[...] = inner
    acc_ref[...] += nn(inner, weight(weight_ref, 2))

    @pl.when(step == FF_STEPS - 1)
    def last():
        hidden = hidden_ref[...]
        branch = acc_ref[...]
        branch_ref[...] = branch
        logit = jnp.sum(hidden * router_ref[...], axis=1, keepdims=True)
        logit_ref[...] = logit
        new = hidden + sel_ref[...] * jax.nn.sigmoid(logit) * (branch - hidden)
        new_ref[...] = new
        for copy in copies:
            copy.wait()
        if more:
            project(new, gain_ref[0:1, :], *refs[1:4], *proj_in[3:], *proj_out)


WEIGHT_SPEC = pl.BlockSpec((FF_BLOCK // 80, 3, 80, D), lambda i: (i, 0, 0, 0))


def block(att, hidden, sel, gains, router, wo, weights, projections):
    more = projections is not None
    proj_specs = [pl.BlockSpec(memory_space=pl.ANY)] * 3 + [whole(32, 128), whole(32, 128)]
    rows = pl.BlockSpec((TOK_DEV, FF_BLOCK), lambda i: (0, i))
    return pl.pallas_call(
        functools.partial(block_kernel, more),
        grid=(FF_STEPS,),
        in_specs=[
            whole(TOK_DEV, D),
            whole(TOK_DEV, D),
            whole(TOK_DEV, 1),
            whole(8, D),
            whole(1, D),
            whole(D, D),
            WEIGHT_SPEC,
        ]
        + proj_specs * more,
        out_specs=[
            whole(TOK_DEV, D),
            whole(TOK_DEV, D),
            rows,
            rows,
            rows,
            whole(TOK_DEV, D),
            whole(TOK_DEV, 1),
            whole(TOK_DEV, D),
        ]
        + [whole(TOK_DEV, D), whole(D, TOK_DEV), whole(TOK_DEV, 640)] * more,
        out_shape=(
            struct(FLOAT, TOK_DEV, D),
            struct(BFLOAT, TOK_DEV, D),
            struct(FLOAT, TOK_DEV, FF),
            struct(FLOAT, TOK_DEV, FF),
            struct(BFLOAT, TOK_DEV, FF),
            struct(FLOAT, TOK_DEV, D),
            struct(FLOAT, TOK_DEV, 1),
            struct(FLOAT, TOK_DEV, D),
        )
        + (PROJECTED if more else ()),
        scratch_shapes=[pltpu.VMEM((TOK_DEV, D), FLOAT)]
        + [
            pltpu.VMEM((D, D), BFLOAT),
            pltpu.VMEM((D, 320), BFLOAT),
            pltpu.VMEM((D, 320), BFLOAT),
            pltpu.SemaphoreType.DMA((3,)),
        ]
        * more,
        cost_estimate=pl.CostEstimate(
            flops=4_000_000_000, bytes_accessed=20_000_000, transcendentals=400_000
        ),
        compiler_params=params(BIG),
    )(att, hidden, sel, gains, router, wo, weights, *(projections if more else ()))


def block_back_kernel(
    new_ref, sel_ref, logit_ref, hidden_ref, branch_ref, mixed_ref, gain_ref, router_ref, wo_ref,
    gate_ref, up_ref, weight_ref,
    rows_ref, dgate_ref, dup_ref, in_ref, attn_ref, back_ref, small_ref, acc_ref, held_ref, sem
):
    step = pl.program_id(0)
    sigma = jax.nn.sigmoid(logit_ref[...])
    chosen = sel_ref[...] * sigma
    copy = pltpu.make_async_copy(wo_ref, held_ref, sem)

    @pl.when(step == 0)
    def first():
        copy.start()
        rows_ref[...] = (chosen * new_ref[...]).astype(BFLOAT)
        acc_ref[...] = jnp.zeros_like(acc_ref)

    inner = contract_cols(rows_ref[...], weight(weight_ref, 2))
    gate = gate_ref[...]
    shape = jax.nn.sigmoid(gate)
    dgate = (inner * up_ref[...] * shape * (1.0 + gate * (1.0 - shape))).astype(BFLOAT)
    dup = (inner * gate * shape).astype(BFLOAT)
    dgate_ref[...] = dgate
    dup_ref[...] = dup
    acc_ref[...] += nn(dgate, weight(weight_ref, 0)) + nn(dup, weight(weight_ref, 1))

    @pl.when(step == FF_STEPS - 1)
    def last():
        grad_new = new_ref[...]
        hidden = hidden_ref[...]
        grad_branch = chosen * grad_new
        grad_weight = jnp.sum(grad_new * (branch_ref[...] - hidden), axis=1, keepdims=True)
        grad_logit = grad_weight * sel_ref[...] * sigma * (1.0 - sigma) + ROUTER_LOSS / TOK_DEV * (
            sigma - sel_ref[...]
        )
        grad_norm, gain_row = normalize_back(mixed_ref[...], gain_ref[1:2, :], acc_ref[...])
        grad_mixed = grad_branch + grad_norm
        in_ref[...] = grad_new - grad_branch + grad_logit * router_ref[...] + grad_mixed
        attn = grad_mixed.astype(BFLOAT)
        attn_ref[...] = attn
        copy.wait()
        back_ref[...] = contract_cols(attn, held_ref[...]).astype(BFLOAT)
        small_ref[0:1, :] = gain_row
        small_ref[1:2, :] = jnp.sum(grad_logit * hidden, axis=0, keepdims=True)
        small_ref[2:8, :] = jnp.zeros((6, D), FLOAT)


def block_back(new, sel, logit, hidden, branch, mixed, gains, router, wo, gate, up, weights):
    rows = pl.BlockSpec((TOK_DEV, FF_BLOCK), lambda i: (0, i))
    full = whole(TOK_DEV, D)
    return pl.pallas_call(
        block_back_kernel,
        grid=(FF_STEPS,),
        in_specs=[
            full,
            whole(TOK_DEV, 1),
            whole(TOK_DEV, 1),
            full,
            full,
            full,
            whole(8, D),
            whole(1, D),
            pl.BlockSpec(memory_space=pl.ANY),
            rows,
            rows,
            WEIGHT_SPEC,
        ],
        out_specs=[full, rows, rows, full, full, full, whole(8, D)],
        out_shape=(
            struct(BFLOAT, TOK_DEV, D),
            struct(BFLOAT, TOK_DEV, FF),
            struct(BFLOAT, TOK_DEV, FF),
            struct(FLOAT, TOK_DEV, D),
            struct(BFLOAT, TOK_DEV, D),
            struct(BFLOAT, TOK_DEV, D),
            struct(FLOAT, 8, D),
        ),
        scratch_shapes=[
            pltpu.VMEM((TOK_DEV, D), FLOAT),
            pltpu.VMEM((D, D), BFLOAT),
            pltpu.SemaphoreType.DMA,
        ],
        cost_estimate=pl.CostEstimate(
            flops=4_000_000_000, bytes_accessed=20_000_000, transcendentals=400_000
        ),
        compiler_params=params(BIG),
    )(new, sel, logit, hidden, branch, mixed, gains, router, wo, gate, up, weights)


def enter_back_kernel(
    in_ref, dq_ref, own_ref, hidden_ref, gain_ref, wq_ref, wk_ref, wv_ref, cos_ref, sin_ref,
    pair_ref, out_ref, small_ref
):
    keys = turn(own_ref[:, 0:320].T, cos_ref[...], -sin_ref[...]).T.astype(BFLOAT)
    values = own_ref[:, 320:640].astype(BFLOAT)
    pair_ref[:, 0:320] = keys
    pair_ref[:, 320:640] = values
    grad_normed = (
        contract_cols(dq_ref[...], wq_ref[...])
        + contract_cols(keys, wk_ref[...])
        + contract_cols(values, wv_ref[...])
    )
    grad_hidden, gain_row = normalize_back(hidden_ref[...], gain_ref[0:1, :], grad_normed)
    out_ref[...] = in_ref[...] + grad_hidden
    small_ref[...] = jnp.concatenate([gain_row, jnp.zeros((7, D), FLOAT)], axis=0)


def enter_back(grad_in, dq, own, hidden, gains, wq, wk, wv, cosine, sine):
    return pl.pallas_call(
        enter_back_kernel,
        out_shape=(
            struct(BFLOAT, TOK_DEV, 640),
            struct(FLOAT, TOK_DEV, D),
            struct(FLOAT, 8, D),
        ),
        compiler_params=params(24),
    )(grad_in, dq, own, hidden, gains, wq, wk, wv, cosine, sine)


HEAD_BLOCK = 1024


def head_kernel(rows_ref, near_ref, *refs):
    block_refs, (target_ref, table_ref, logit_ref, pick_ref, out_ref, stat_ref) = refs[:8], refs[8:]
    step = pl.program_id(0)

    @pl.when(step == 0)
    def first():
        picked = None
        for i, ref in enumerate(block_refs):
            hot = rows_ref[...] == near_ref[:, 128 * i : 128 * i + 128]
            part = nn(hot.astype(FLOAT).astype(BFLOAT), ref[...])
            picked = part if picked is None else picked + part
        pick_ref[...] = picked.astype(BFLOAT)
        lane = lax.broadcasted_iota(jnp.int32, (256, 128), 1)
        stat_ref[...] = jnp.where(lane == 0, MASKED, 0.0)

    logits = contract_cols(pick_ref[...], table_ref[...])
    logit_ref[...] = logits
    place = step * HEAD_BLOCK + lax.broadcasted_iota(jnp.int32, (256, HEAD_BLOCK), 1)
    hit = jnp.sum(jnp.where(place == target_ref[...], logits, 0.0), axis=1, keepdims=True)
    old = stat_ref[:, 0:1]
    top = jnp.maximum(old, jnp.max(logits, axis=1, keepdims=True))
    total = stat_ref[:, 1:2] * jnp.exp(old - top) + jnp.sum(
        jnp.exp(logits - top), axis=1, keepdims=True
    )
    stat_ref[:, 1:2] = total
    stat_ref[:, 2:3] = stat_ref[:, 2:3] + hit
    stat_ref[:, 0:1] = top

    @pl.when(step == pl.num_programs(0) - 1)
    def last():
        out_ref[...] = stat_ref[...].T[0:8]


def head(loss_rows, near_rows, blocks, local_targets, table):
    return pl.pallas_call(
        head_kernel,
        grid=(VOCAB_MP // HEAD_BLOCK,),
        in_specs=[whole(256, 1), whole(1, ROWS)]
        + [whole(TOK_DEV, D)] * MP
        + [whole(256, 1), pl.BlockSpec((HEAD_BLOCK, D), lambda i: (i, 0))],
        out_specs=[
            pl.BlockSpec((256, HEAD_BLOCK), lambda i: (0, i)),
            whole(256, D),
            whole(8, 256),
        ],
        out_shape=(
            struct(FLOAT, 256, VOCAB_MP),
            struct(BFLOAT, 256, D),
            struct(FLOAT, 8, 256),
        ),
        scratch_shapes=[pltpu.VMEM((256, 128), FLOAT)],
        compiler_params=params(BIG),
    )(loss_rows, near_rows, *blocks, local_targets, table)


def head_back_kernel(
    rows_ref, near_ref, target_ref, stat_ref, logit_ref, pick_ref, table_ref, grad_ref, *refs
):
    block_refs, (sum_ref, norm_ref) = refs[:8], refs[8:]
    step = pl.program_id(0)

    @pl.when(step == 0)
    def first():
        norm = stat_ref[0:1, :] + jnp.log(stat_ref[1:2, :])
        norm_ref[:, 0:8] = jnp.concatenate([norm] * 8, axis=0).T
        sum_ref[...] = jnp.zeros((256, D), FLOAT)

    place = step * HEAD_BLOCK + lax.broadcasted_iota(jnp.int32, (256, HEAD_BLOCK), 1)
    probs = jnp.exp(logit_ref[...] - norm_ref[:, 0:1])
    hit = jnp.where(place == target_ref[...], 1.0, 0.0)
    grads = ((probs - hit) * (1.0 / TOK_DEV)).astype(BFLOAT)
    grad_ref[...] = contract_rows(grads, pick_ref[...]).astype(BFLOAT)
    sum_ref[...] += nn(grads, table_ref[...])

    @pl.when(step == pl.num_programs(0) - 1)
    def last():
        total = sum_ref[...].astype(BFLOAT)
        for i, ref in enumerate(block_refs):
            hot = rows_ref[...] == near_ref[:, 128 * i : 128 * i + 128]
            ref[...] = contract_rows(hot.astype(FLOAT).astype(BFLOAT), total).astype(BFLOAT)


def head_back(loss_rows, near_rows, local_targets, stats, logits, picked, table):
    return pl.pallas_call(
        head_back_kernel,
        grid=(VOCAB_MP // HEAD_BLOCK,),
        in_specs=[
            whole(256, 1),
            whole(1, ROWS),
            whole(256, 1),
            whole(8, 256),
            pl.BlockSpec((256, HEAD_BLOCK), lambda i: (0, i)),
            whole(256, D),
            pl.BlockSpec((HEAD_BLOCK, D), lambda i: (i, 0)),
        ],
        out_specs=[pl.BlockSpec((HEAD_BLOCK, D), lambda i: (i, 0))] + [whole(TOK_DEV, D)] * MP,
        out_shape=[struct(BFLOAT, VOCAB_MP, D)] + [struct(BFLOAT, TOK_DEV, D)] * MP,
        scratch_shapes=[pltpu.VMEM((256, D), FLOAT), pltpu.VMEM((256, 128), FLOAT)],
        compiler_params=params(BIG),
    )(loss_rows, near_rows, local_targets, stats, logits, picked, table)


def mlp_grad_kernel(which_ref, *refs):
    out_ref = refs[-1]

    def joined(first):
        return jnp.concatenate([ref[...] for ref in refs[first:-1:10]], axis=0)

    def both(first):
        return jnp.concatenate([joined(first), joined(first + 5)], axis=0)

    rights = both(3), both(3), both(4)
    for i in range(3):
        out_ref[:, i] = contract_rows(both(i), rights[i]).reshape(8, 80, D).astype(BFLOAT)


def mlp_grads(which, kept, received):
    def cols(width, place):
        return pl.BlockSpec((TOK_DEV, width), place)

    rights = [cols(D, lambda i, half: (0, 0))] * 2
    own = [cols(640, lambda i, half: (0, half[0] * 2 + i))] * 3 + rights
    far = [cols(640, lambda i, half: (0, i))] * 3 + rights
    args = []
    for parts, other in zip(kept, received):
        args += [*parts, *other]
    return pl.pallas_call(
        mlp_grad_kernel,
        grid_spec=pltpu.PrefetchScalarGridSpec(
            num_scalar_prefetch=1,
            grid=(2,),
            in_specs=(own + far) * RECUR,
            out_specs=pl.BlockSpec((8, 3, 80, D), lambda i, half: (i, 0, 0, 0)),
        ),
        out_shape=struct(BFLOAT, 16, 3, 80, D),
        compiler_params=params(BIG),
    )(which.reshape(1), *args)


def square_grad_kernel(*refs):
    wq_ref, wo_ref = refs[-2:]
    ins = refs[:-2]

    def joined(first):
        return jnp.concatenate([ref[...] for ref in ins[first::8]], axis=0)

    def both(first):
        return jnp.concatenate([joined(first), joined(first + 4)], axis=0)

    wq_ref[...] = contract_rows(both(2), both(3)).astype(BFLOAT)
    wo_ref[...] = contract_rows(both(0), both(1)).astype(BFLOAT)


def square_grads(kept, received):
    args = []
    for parts, other in zip(kept, received):
        args += [*parts, *other]
    return pl.pallas_call(
        square_grad_kernel,
        grid=(1,),
        in_specs=[whole(TOK_DEV, D)] * (8 * RECUR),
        out_specs=[whole(D, D), whole(D, D)],
        out_shape=(struct(BFLOAT, D, D), struct(BFLOAT, D, D)),
        compiler_params=params(BIG),
    )(*args)


def pack_grad_kernel(starts_ref, *refs):
    wq_ref, wo_ref, rows_ref = refs[:3]
    ins = refs[3:-2]
    out_ref, buf = refs[-2:]
    buf[0:960, :] = wq_ref[...]
    buf[1600:2560, :] = wo_ref[...]
    buf[2560:2576, :] = rows_ref[...].astype(BFLOAT)
    buf[2576:2688, :] = jnp.zeros((112, D), BFLOAT)
    normed = jnp.concatenate([ref[...] for ref in ins[0::4] + ins[1::4]], axis=0)
    grads = jnp.concatenate([ref[...] for ref in ins[2::4] + ins[3::4]], axis=0)
    line = lax.broadcasted_iota(jnp.int32, (960, 320), 0)
    place = lax.broadcasted_iota(jnp.int32, (960, 320), 1)
    full = contract_rows(normed, grads).astype(BFLOAT)
    for i in range(3):
        chosen = (line == 3 * place + i).astype(FLOAT).astype(BFLOAT)
        rows = contract_rows(chosen, full).astype(BFLOAT)
        buf[960:1280, 320 * i : 320 * i + 320] = rows[:, 0:320]
        buf[1280:1600, 320 * i : 320 * i + 320] = rows[:, 320:640]
    for i in range(4):
        start = pl.multiple_of(starts_ref[i], 16)
        out_ref[i] = buf[pl.ds(start, 352), :]


def pack_grads(starts, wq, wo, small, kept, received):
    args = []
    for (normed, pair), (far_normed, far_pair) in zip(kept, received):
        args += [normed, far_normed, pair, far_pair]
    specs = [whole(TOK_DEV, D)] * 2 + [whole(TOK_DEV, 640)] * 2
    return pl.pallas_call(
        pack_grad_kernel,
        grid=(1,),
        in_specs=[pl.BlockSpec(memory_space=pltpu.SMEM), whole(D, D), whole(D, D), whole(16, D)]
        + specs * RECUR,
        out_specs=whole(4, 352, D),
        out_shape=struct(BFLOAT, 4, 352, D),
        scratch_shapes=[pltpu.VMEM((PACK_PAD, D), BFLOAT)],
        compiler_params=params(BIG),
    )(starts, wq, wo, small, *args)


def adam_update(master, first, second, grad, clip):
    grad = grad * clip
    first_new = BETA_ONE * first + (1.0 - BETA_ONE) * grad
    second_new = BETA_TWO * second + (1.0 - BETA_TWO) * grad * grad
    corr_one = 1.0 - BETA_ONE**STEP
    corr_two = 1.0 - BETA_TWO**STEP
    master_new = master - LEARN_RATE * (
        first_new / corr_one / (jnp.sqrt(second_new / corr_two) + ADAM_EPS) + DECAY * master
    )
    return (master_new, first_new, second_new)


def pack_row(device):
    return (1283 * device) // 64


def join_kernel(blocks_ref, wq_ref, wk_ref, wv_ref, wo_ref, small_ref, buf):
    row = lax.broadcasted_iota(jnp.int32, (128, 240), 0)
    place = lax.broadcasted_iota(jnp.int32, (128, 240), 1)
    device = (place * 2731) >> 16
    for step in range(PACK_PAD // 128):
        first = min(step * 128 * 64 // 1283, 118) // 2 * 2
        source = ((1283 * (first + device)) >> 6) + place - 24 * device
        chosen = (source == row + 128 * step).astype(FLOAT).astype(BFLOAT)
        buf[128 * step : 128 * step + 128, :] = nn(
            chosen, blocks_ref[24 * first : 24 * first + 240, :]
        ).astype(BFLOAT)
    wq_ref[...] = buf[0:960, :]
    wo_ref[...] = buf[1600:2560, :]
    small_ref[...] = buf[2560:2576, :]
    line = lax.broadcasted_iota(jnp.int32, (960, 320), 0)
    place = lax.broadcasted_iota(jnp.int32, (960, 320), 1)
    for first, ref in ((960, wk_ref), (1280, wv_ref)):
        total = None
        for i in range(3):
            chosen = (line == 3 * place + i).astype(FLOAT).astype(BFLOAT)
            part = nn(chosen, buf[first : first + 320, 320 * i : 320 * i + 320])
            total = part if total is None else total + part
        ref[...] = total.astype(BFLOAT)


def join_pack(blocks):
    return pl.pallas_call(
        join_kernel,
        out_shape=(
            struct(BFLOAT, D, D),
            struct(BFLOAT, D, 320),
            struct(BFLOAT, D, 320),
            struct(BFLOAT, D, D),
            struct(BFLOAT, 16, D),
        ),
        scratch_shapes=[pltpu.VMEM((PACK_PAD, D), BFLOAT)],
        compiler_params=params(32),
    )(blocks)


def stage(value, axis, index):
    total = lax.dynamic_index_in_dim(value, index, 0, False).astype(FLOAT)
    for k in (1, 2, 3):
        sent = lax.dynamic_index_in_dim(value, (index + k) % 4, 0, False)
        total = total + shift(sent, axis, k).astype(FLOAT)
    return total


def gradients(
    dense,
    token_ids,
    targets,
    loss_rows,
    selections,
    boundary,
    pack_master,
    mlp_master,
    table_master,
):
    z = lax.axis_index("z")
    core = lax.axis_index("core")
    y = lax.axis_index("y")
    x = lax.axis_index("x")
    model_index = z * 2 + core
    data_index = y * 4 + x
    device = model_index * DP + data_index
    own_table = table_master.astype(BFLOAT)

    near = jnp.stack([((z + k) % 4) * 2 + (core ^ j) for j in (0, 1) for k in range(4)])
    near_rows = (near[:, None] * TOK_DEV + jnp.arange(TOK_DEV, dtype=jnp.int32)[None, :]).reshape(-1)

    pack_offset = PACK_DEV * device - D * pack_row(device)
    pack_block = lax.dynamic_update_slice(
        jnp.zeros((24 * D,), BFLOAT), pack_master.astype(BFLOAT), (pack_offset,)
    ).reshape(24, D)
    pack_quad = [pack_block] + [shift(pack_block, "x", k) for k in (1, 2, 3)]
    pack_rows = []
    for i in range(4):
        part = pack_quad[3]
        for k in (2, 1, 0):
            part = jnp.where(x == (i + k) % 4, pack_quad[k], part)
        pack_rows.append(part)
    pack_blocks = lax.all_gather(
        jnp.concatenate(pack_rows, axis=0), ("z", "core", "y"), axis=0, tiled=True
    )
    mlp_own = mlp_master.astype(BFLOAT)
    mlp_quad = jnp.concatenate([mlp_own] + [shift(mlp_own, "z", k) for k in (1, 2, 3)], axis=1)

    group_ids = token_ids[0]
    near_ids = reorder(group_ids.reshape(MP, TOK_DEV), near).reshape(-1)
    local_ids = near_ids - model_index * VOCAB_MP
    inside = (local_ids >= 0) & (local_ids < VOCAB_MP)
    high = local_ids >> 7
    low = local_ids & 127
    high_hot = (high[:, None] == jnp.arange(48)[None, :]).astype(BFLOAT)
    low_hot = (low[:, None] == jnp.arange(128)[None, :]).astype(BFLOAT)
    present = (contract_rows(high_hot, low_hot) > 0).reshape(DP, VOCAB_DEV)
    before = (jnp.arange(VOCAB_DEV)[:, None] < jnp.arange(VOCAB_DEV)[None, :]).astype(BFLOAT)
    slots = mm(present.astype(BFLOAT), before)
    asked = present & (slots < CAP)
    over = jnp.max(jnp.where(present & (slots >= CAP), 1.0, 0.0))
    slot_table = jnp.where(asked, slots, 255.0).reshape(48, 128).astype(BFLOAT)
    token_slot = jnp.sum(mm(high_hot, slot_table) * low_hot.astype(FLOAT), axis=-1)
    token_place = jnp.where(
        inside & (token_slot < CAP), (high // 3) * CAP + token_slot.astype(jnp.int32), -1
    )
    token_place = token_place[:, None]
    match = asked[:, None, :] & (slots[:, None, :] == jnp.arange(CAP, dtype=FLOAT)[None, :, None])
    request = (
        jnp.sum(jnp.where(match, jnp.arange(1, VOCAB_DEV + 1, dtype=FLOAT)[None, None, :], 0.0), axis=-1)
        - 1.0
    )
    request = jnp.concatenate([request, jnp.full((DP, 8), over, FLOAT)], axis=1)
    request = lax.all_to_all(request, DP_AXES, 0, 0, tiled=True)
    over = jnp.max(request[:, CAP:])
    owner_hot = (
        request[:, :CAP].reshape(-1)[:, None] == jnp.arange(VOCAB_DEV, dtype=FLOAT)[None, :]
    ).astype(BFLOAT)
    mlp_quad, owner_hot = tie(mlp_quad, owner_hot)
    mlp_weights = lax.all_gather(
        mlp_quad.reshape(3 * 80, D), ("core", "y", "x"), axis=0, tiled=True
    )
    mlp_weights = mlp_weights.reshape(32, 3, 80, D)
    asked_rows = lax.all_to_all(mm(owner_hot, own_table).astype(BFLOAT), DP_AXES, 0, 0, tiled=True)
    own_table, asked_rows = tie(own_table, asked_rows)
    table = lax.all_gather(own_table, DP_AXES, axis=0, tiled=True)
    if dense:
        rows = jnp.take(table, jnp.clip(local_ids, 0, VOCAB_MP - 1), axis=0)
        looked = jnp.where(inside[:, None], rows, jnp.zeros_like(rows))
        looked = [looked[128 * i : 128 * i + 128] for i in range(MP)]
    else:
        looked = spread(token_place, asked_rows)
    hidden, pack_blocks = scatter_group(looked, pack_blocks)

    w_query, w_key, w_value, w_out, last_rows = join_pack(pack_blocks)
    gains = jnp.concatenate([last_rows[:3].astype(FLOAT), jnp.zeros((5, D), FLOAT)])
    router = last_rows[3:6].astype(FLOAT)

    half_dim = HEAD_DIM // 2
    freqs = ROPE_BASE ** (-jnp.arange(half_dim, dtype=FLOAT) / half_dim)
    first_row = data_index * ROWS + model_index * TOK_DEV
    angles = freqs[:, None] * (first_row + jnp.arange(TOK_DEV, dtype=jnp.int32)).astype(FLOAT)[None, :]
    turns = (jnp.cos(angles), jnp.sin(angles))
    projections = (w_query, w_key, w_value) + turns
    group_sel = selections.reshape(RECUR, DP, MP, TOK_DEV)
    prev_index = jnp.maximum(data_index - 1, 0)
    here_sel = lax.dynamic_index_in_dim(group_sel, data_index, 1, False)
    own_sel = lax.dynamic_index_in_dim(here_sel, model_index, 1, False)
    near_sel = reorder(here_sel, near).reshape(RECUR, ROWS)
    prev_sel = reorder(lax.dynamic_index_in_dim(group_sel, prev_index, 1, False), near)
    prev_sel = prev_sel.reshape(RECUR, ROWS)
    start = lax.dynamic_index_in_dim(boundary, data_index, 0, False)
    prev_start = lax.dynamic_index_in_dim(boundary, prev_index, 0, False)
    place = (model_index * TOK_DEV + jnp.arange(TOK_DEV, dtype=jnp.int32))[None, :]
    key_place = near_rows[:, None]
    biases = []
    for step in range(RECUR):
        own_seen = (
            (key_place <= place)
            & ((key_place < start) == (place < start))
            & ((near_sel[step][:, None] > 0) | (key_place == place))
        )
        prev_seen = (
            (data_index > 0)
            & (place < start)
            & (key_place >= prev_start)
            & (prev_sel[step][:, None] > 0)
        )
        seen = [prev_seen[:512], own_seen[:512], prev_seen[512:], own_seen[512:]]
        biases.append(jnp.where(jnp.concatenate(seen, axis=0), 0.0, MASKED))

    sel_cols = own_sel.astype(FLOAT)[:, :, None]
    saves = []
    logits_all = []
    normed, queries, pair = enter(hidden, gains, *projections)
    for step in range(RECUR):
        pairs = group_gather(pair)
        attended, log_total = attend(queries, pairs, biases[step])
        mixed, mlp_input, gate, up, inner, branch, logit, new_hidden, *nexts = block(
            attended,
            hidden,
            sel_cols[step],
            gains,
            router[step : step + 1],
            w_out,
            mlp_weights,
            projections if step < RECUR - 1 else None,
        )
        logits_all.append(logit[:, 0])
        saves.append(
            (
                hidden,
                normed,
                queries,
                pairs,
                attended,
                log_total,
                mixed,
                mlp_input,
                gate,
                up,
                inner,
                branch,
                logit,
            )
        )
        hidden = new_hidden
        if nexts:
            normed, queries, pair = nexts
    logits_all = jnp.stack(logits_all)
    penalty_total = jnp.sum(jax.nn.softplus(logits_all) - own_sel.astype(FLOAT) * logits_all)

    normed_final = rms_scale(hidden, gains[2]).astype(BFLOAT)
    final_rows = gather_group(normed_final)
    row_targets = lax.dynamic_index_in_dim(targets, data_index, 0, keepdims=False)
    head_args = (loss_rows[0][:, None], near_rows[None, :])
    local_targets = (row_targets - model_index * VOCAB_MP)[:, None]
    logits, picked, stats = head(*head_args, final_rows, local_targets, table)
    flag_row = lax.broadcasted_iota(jnp.int32, (8, 256), 0) == 3
    stats = jnp.where(flag_row, over, stats)

    def join_stats(parts):
        top = parts[0][0]
        for part in parts[1:]:
            top = jnp.maximum(top, part[0])
        total = sum(part[1] * jnp.exp(part[0] - top) for part in parts)
        over = parts[0][3]
        for part in parts[1:]:
            over = jnp.maximum(over, part[3])
        rest = [jnp.zeros_like(top)] * 4
        return jnp.stack([top, total, sum(part[2] for part in parts), over] + rest)

    stats = join_stats([stats, swap(stats)])
    stats = join_stats([stats] + [shift(stats, "z", k) for k in (1, 2, 3)])
    log_norm = stats[0] + jnp.log(stats[1])
    cross = log_norm - stats[2]
    per_device = cross.shape[0] // MP
    loss_part = (
        jnp.sum(lax.dynamic_slice_in_dim(cross, model_index * per_device, per_device))
        + ROUTER_LOSS * penalty_total
    )
    head_grad, *scattered = head_back(*head_args, local_targets, stats, logits, picked, table)
    grad_final = scatter_group(scattered)
    grad_hidden, grad_gain_final = rms_back(hidden, gains[2], grad_final)
    if not dense:
        head_grad = lax.psum_scatter(head_grad, DP_AXES, scatter_dimension=0, tiled=True)

    mlp_kept, mlp_far, square_kept, square_far, pack_kept, pack_far = [], [], [], [], [], []
    loss_part, flag, grad_hidden = tie(loss_part, stats[3, 0], grad_hidden)
    router_rows = [None] * RECUR
    gain_one = jnp.zeros((1, D), FLOAT)
    gain_two = jnp.zeros((1, D), FLOAT)
    for step in reversed(range(RECUR)):
        (
            hidden_in,
            normed,
            queries,
            pairs,
            attended,
            log_total,
            mixed,
            mlp_input,
            gate,
            up,
            inner,
            branch,
            logit,
        ) = saves[step]
        grad_rows, grad_gate, grad_up, grad_in, grad_attn, grad_attended, small = block_back(
            grad_hidden,
            sel_cols[step],
            logit,
            hidden_in,
            branch,
            mixed,
            gains,
            router[step : step + 1],
            w_out,
            gate,
            up,
            mlp_weights,
        )
        gain_two = gain_two + small[0:1]
        router_rows[step] = small[1:2]
        mlp_kept.append((grad_gate, grad_up, inner, mlp_input, grad_rows))

        def far_half(value):
            return lax.dynamic_slice_in_dim(value, (1 - core) * (FF // 2), FF // 2, 1)

        mlp_far.append(
            [swap(far_half(part)) for part in (grad_gate, grad_up, inner)]
            + [swap(mlp_input), swap(grad_rows)]
        )
        grad_query, *grad_sides = attend_back(
            24 if step == RECUR - 1 else BIG,
            queries, pairs, biases[step], log_total, attended, grad_attended, *turns
        )
        far_normed = swap(normed)
        square_kept.append((attended, grad_attn, normed, grad_query))
        square_far.append((swap(attended), swap(grad_attn), far_normed, swap(grad_query)))
        grad_own = group_scatter(*grad_sides)
        grad_pair, grad_hidden, small = enter_back(
            grad_in, grad_query, grad_own, hidden_in, gains, *projections
        )
        gain_one = gain_one + small[0:1]
        if step == 0:
            _, *mlp_kept[-1] = tie(grad_hidden, *mlp_kept[-1])
            mlp_half = mlp_grads(core.astype(jnp.int32), mlp_kept, mlp_far)
            mlp_sum = lax.psum_scatter(
                mlp_half.reshape(16 * 240, D), DP_AXES, scatter_dimension=0, tiled=True
            )
            squares = square_grads(square_kept, square_far)
        pack_kept.append((normed, grad_pair))
        pack_far.append((far_normed, swap(grad_pair)))
        if step == 1 and not dense:
            head_grad, grad_hidden = tie(head_grad, grad_hidden)

    sent = grad_hidden.astype(BFLOAT)
    grad_embed = [sent] + [shift(sent, "z", -k) for k in (1, 2, 3)]
    grad_embed[1], grad_embed[3], gain_one = tie(grad_embed[1], grad_embed[3], gain_one)
    grad_embed += [swap(part) for part in grad_embed]

    def aligned_row(which):
        return (pack_row(which) // 16) * 16

    small = jnp.concatenate(
        [
            gain_one,
            gain_two,
            grad_gain_final[None],
            *router_rows,
            jnp.zeros((10, D), FLOAT),
        ]
    )
    small = small + swap(small)
    starts = jnp.stack([aligned_row(DP * (2 * i + core)) for i in range(4)]).astype(jnp.int32)
    part = pack_grads(starts, *squares, small, pack_kept, pack_far)

    def y_windows(value):
        return jnp.stack([value[..., 80 * i : 80 * i + 112, :] for i in range(4)])

    def x_windows(value):
        return jnp.stack([value[..., i : i + 48, :] for i in (0, 16, 40, 56)])

    part = stage(part, "z", z).astype(BFLOAT)
    part = stage(y_windows(part), "y", y).astype(BFLOAT)
    part, mlp_sum = tie(x_windows(part), mlp_sum)
    mlp_sum = mlp_sum.reshape(3, 4, UNITS, D).transpose(1, 0, 2, 3)
    mlp_grad = mlp_sum[0].astype(FLOAT)
    for k in (1, 2, 3):
        mlp_grad = mlp_grad + shift(mlp_sum[k], "z", -k).astype(FLOAT)
    part = stage(part, "x", x).reshape(-1)
    begin = aligned_row(DP * model_index) + 80 * y + (20 * x) // 8 * 8
    pack_grad = lax.dynamic_slice(part, (PACK_DEV * device - D * begin,), (PACK_DEV,))

    if dense:
        kept_rows = jnp.concatenate(grad_embed).astype(FLOAT) * inside.astype(FLOAT)[:, None]
        sums = jax.ops.segment_sum(
            kept_rows, jnp.clip(local_ids, 0, VOCAB_MP - 1), num_segments=VOCAB_MP
        )
        table_grad = lax.psum_scatter(
            (head_grad.astype(FLOAT) + sums).astype(BFLOAT),
            DP_AXES,
            scatter_dimension=0,
            tiled=True,
        ).astype(FLOAT)
    else:
        unique = collect(token_place, grad_embed)
        unique = lax.all_to_all(unique, DP_AXES, 0, 0, tiled=True)
        table_grad = head_grad.astype(FLOAT) + contract_rows(owner_hot, unique)
    table_grad = by_cols(table_grad)
    squares = (
        jnp.sum(pack_grad * pack_grad)
        + jnp.sum(mlp_grad * mlp_grad)
        + jnp.sum(table_grad * table_grad)
    )
    return pack_grad, mlp_grad, table_grad, squares, loss_part, flag


def shards(
    token_ids,
    targets,
    loss_rows,
    selections,
    boundary,
    pack_master,
    pack_first,
    pack_second,
    mlp_master,
    mlp_first,
    mlp_second,
    table_master,
    table_first,
    table_second,
):
    args = (
        token_ids,
        targets,
        loss_rows,
        selections,
        boundary,
        pack_master,
        mlp_master,
        table_master,
    )
    *found, over = tie(*gradients(False, *args))
    pack_grad, mlp_grad, table_grad, squares, loss_part = lax.cond(
        over > 0, lambda: gradients(True, *args)[:5], lambda: tuple(found)
    )
    lane = lax.broadcasted_iota(jnp.int32, (128, 128), 1)
    sums = lax.all_to_all(
        jnp.where(lane == 0, squares, loss_part), ALL_AXES, 0, 0, tiled=True
    )
    sums = jnp.sum(sums, axis=0, keepdims=True)
    total_squares = sums[0, 0]
    loss_sum = sums[0, 1]
    grad_norm = jnp.sqrt(total_squares)
    clip = CLIP_NORM / jnp.maximum(grad_norm, CLIP_NORM)
    pack_new, pack_first_new, pack_second_new = adam_update(
        pack_master, pack_first, pack_second, pack_grad, clip
    )
    mlp_new, mlp_first_new, mlp_second_new = adam_update(
        mlp_master, mlp_first, mlp_second, mlp_grad, clip
    )
    table_new, table_first_new, table_second_new = adam_update(
        table_master, table_first, table_second, table_grad, clip
    )
    return (
        pack_new,
        pack_first_new,
        pack_second_new,
        mlp_new,
        mlp_first_new,
        mlp_second_new,
        table_new,
        table_first_new,
        table_second_new,
        loss_sum,
        grad_norm,
    )


def solution(mesh):
    grid = Mesh(mesh.devices.reshape(4, 2, 4, 4), ALL_AXES)
    owners = (P(ALL_AXES), P(None, ALL_AXES, None), P(ALL_AXES, None))
    group = P(DP_AXES, None)
    masters = tuple(spec for spec in owners for _ in range(3))
    return jax.shard_map(
        shards,
        mesh=grid,
        in_specs=(group, P(), group, P(), P()) + masters,
        out_specs=masters + (P(), P()),
        check_vma=False,
    )
```
